32 devices in a mesh: dp: 2 (over core), context: 4 (over y, x), tensor: 4 (over z).
Axes of the slice: x: 2, y: 2, z: 4, core: 2. Of those that a mesh axis runs over, the one named last changes fastest.
Arguments:
- tokens_in: bfloat16 [8192, 768], P(('dp', 'context')), may hold values from -6 to 6
- query_weight: bfloat16 [768, 768], P(('dp', 'context'), 'tensor'), may hold values from -0.21875 to 0.21875
- key_weight: bfloat16 [768, 768], P(('dp', 'context'), 'tensor'), may hold values from -0.21875 to 0.21875
- value_weight: bfloat16 [768, 768], P(('dp', 'context'), 'tensor'), may hold values from -0.21875 to 0.21875
- output_weight: bfloat16 [768, 768], P('tensor', ('dp', 'context')), may hold values from -0.875 to 0.875
- bias_table: float32 [32, 12], P(None, 'tensor'), may hold values from -4 to 4
- attention_gain: bfloat16 [768], P(('dp', 'context')), may hold values from 0.5 to 1.5
- router_weight: bfloat16 [768, 8], P(('dp', 'context')), may hold values from -0.21875 to 0.21875
- expert_gain: bfloat16 [768], P(('dp', 'context')), may hold values from 0.5 to 1.5
- expert_in: bfloat16 [8, 768, 3072], P(('dp', 'context'), None, 'tensor'), may hold values from -0.21875 to 0.21875
- expert_out: bfloat16 [8, 3072, 768], P(('dp', 'context'), 'tensor'), may hold values from -0.15625 to 0.15625
- routes: int32 [8192, 2], P(('dp', 'context')), may hold values from 0 to 7, all different within a row
- pair_order: int32 [8, 2048], P(('dp', 'context')), may hold values from 0 to 2047, each once within a row
- seq_lengths: int32 [2, 2], P('dp'), may hold values from 1 to 4095, as said below
- cotangent: bfloat16 [8192, 768], P(('dp', 'context')), may hold values from -6 to 6
Outputs:
- layer_out: bfloat16 [8192, 768], P(('dp', 'context'))
- input_grad: float32 [8192, 768], P(('dp', 'context'))
- query_grad: float32 [768, 768], P(('dp', 'context'), 'tensor')
- key_grad: float32 [768, 768], P(('dp', 'context'), 'tensor')
- value_grad: float32 [768, 768], P(('dp', 'context'), 'tensor')
- output_grad: float32 [768, 768], P('tensor', ('dp', 'context'))
- table_grad: float32 [32, 12], P(None, 'tensor')
- attention_gain_grad: float32 [768], P(('dp', 'context'))
- router_grad: float32 [768, 8], P(('dp', 'context'))
- expert_gain_grad: float32 [768], P(('dp', 'context'))
- expert_in_grad: float32 [8, 768, 3072], P(('dp', 'context'), None, 'tensor')
- expert_out_grad: float32 [8, 3072, 768], P(('dp', 'context'), 'tensor')
The draws below stay inside these ranges and needn't reach their ends.
Inputs may be any that keep to these rules, and one draw needn't show every extreme that they name: `pair_order`: row b lists the (2048) pairs of block b of tokens, pair 2 t + k for local token t and route k, in the order in which they take slots. `seq_lengths`: row g gives the lengths of the two sequences of token group g, packed from the group's first position, with padding after them; their sum is at most 4096; one of them (which one is drawn) is longer than (3) * 1024, the other at most 512.
All inputs are finite; a program needn't handle non-finite values.
Results may differ from the reference program's by a relative error of at most 0.014.
Values may be sent and summed in bfloat16 or wider, within the bound.
No kernel may reach another device: no remote copies, remote signals or barrier semaphores. Data moves between devices by JAX's collectives and lax.ppermute only.
A program may use at most 448 MiB of HBM per device.

```python
import jax
import jax.numpy as jnp
import numpy as np
from jax import lax

D = 768
HEADS = 12
HEAD_DIM = 64
FF = 3072
BUCKETS = 32
TOK_DEV = 1024
GROUP = 4096
TOKENS = 8192
EXPERTS = 8
CAP = 288
N_DP = 2
N_CONTEXT = 4


def draw_seq_lengths(key, part):
    key = jax.random.fold_in(key, 7)
    short_key, long_key, side_key, pick_key = jax.random.split(key, 4)
    short_len = jax.random.randint(short_key, (N_DP,), 1, TOK_DEV // 2 + 1)
    least_long = (N_CONTEXT - 1) * TOK_DEV + 1
    long_len = jax.random.randint(long_key, (N_DP,), least_long, GROUP - short_len + 1)
    chosen = jax.random.randint(pick_key, (), 0, N_DP)
    forced = jnp.arange(N_DP, dtype=jnp.int32) == chosen
    short_len = jnp.where(forced, 1, short_len)
    long_len = jnp.where(forced, GROUP - 1, long_len)
    long_first = jax.random.randint(side_key, (N_DP,), 0, 2) == 1
    first_len = jnp.where(long_first, long_len, short_len)
    second_len = jnp.where(long_first, short_len, long_len)
    return jnp.stack([first_len, second_len], axis=1).astype(jnp.int32)


def raised(entries, own_key, source, target, shards_of, factor):
    owner, partner = [(jnp.arange(entries.shape[position]) // (entries.shape[position] // shards_of)).reshape([-1 if axis == position else 1 for axis in range(entries.ndim)]) for position in (source, target)]
    chosen = jax.random.permutation(own_key, shards_of)[partner]
    strong = (owner == chosen) | (owner == (partner + shards_of // 2) % shards_of)
    return jnp.where(strong, factor * entries, entries)


def shard_levels(own_key, shape, cuts, low, largest):
    def one(dim, shards_of):
        heights = jax.random.uniform(jax.random.fold_in(jax.random.fold_in(own_key, 6), dim), (shards_of,), jnp.float32, low / len(cuts), largest / len(cuts))
        return jnp.repeat(jnp.exp(heights), shape[dim] // shards_of).reshape((-1,) + (1,) * (len(shape) - dim - 1))

    gain = one(*cuts[0])
    for cut in cuts[1:]:
        gain = gain * one(*cut)
    return gain


def different_ones(key, rows, number_of, top, lift):
    ranking = jax.random.permutation(jax.random.fold_in(key, 1), number_of)
    pull = ranking
    for power in range(3):
        pull = pull * pull // number_of
    pull = pull * lift // number_of
    tickets = jax.random.randint(jax.random.fold_in(key, 2), (rows, number_of), 0, 4096) + pull
    fixed_rows = jax.random.permutation(jax.random.fold_in(key, 3), rows)[jnp.arange(number_of) % rows]
    tickets = jnp.where(jnp.arange(rows)[:, None] == fixed_rows[None, :], 1 << 14, tickets)
    priority = tickets * number_of + jnp.arange(number_of)
    return lax.top_k(priority.astype(jnp.int32), top)[1].astype(jnp.int32)


def bell_draw(stream_key, extent, width, most, shards=(), held_as=jnp.bfloat16):
    values = jax.random.normal(stream_key, extent, jnp.float32) * width
    if len(shards) > 0:
        values = shard_levels(stream_key, extent, shards, -0.22, 0.18) * values
    return jnp.clip(values, min=-most, max=most).astype(held_as)


def heavy_noise(own_key, dims, deviation, reach, shards, heavy, kind=jnp.bfloat16):
    values = deviation * jax.random.normal(own_key, dims, jnp.float32)
    if shards:
        values = values * shard_levels(own_key, dims, shards, -0.22, 0.18)
    return jnp.clip(raised(values, jax.random.fold_in(own_key, 3), *heavy), -reach, reach).astype(kind)


def setup_inputs(seed: int = 0) -> dict:
    seeds = jax.random.split(jax.random.key(seed), 16)
    return {
        "tokens_in": bell_draw(seeds[0], (TOKENS, D), 1.0, 6.0, ((0, 8),)),
        "query_weight": bell_draw(seeds[1], (D, D), D ** -0.5, 0.21875, ((0, 8), (1, 4))),
        "key_weight": bell_draw(seeds[2], (D, D), D ** -0.5, 0.21875, ((0, 8), (1, 4))),
        "value_weight": bell_draw(seeds[3], (D, D), D ** -0.5, 0.21875, ((0, 8), (1, 4))),
        "output_weight": bell_draw(seeds[4], (D, D), (D // 16) ** -0.5, 0.875, ((0, 4), (1, 8))),
        "bias_table": bell_draw(seeds[5], (BUCKETS, HEADS), 1.0, 4.0, ((1, 4),), jnp.float32),
        "attention_gain": jnp.clip(1.0 + 0.1 * jax.random.normal(seeds[6], (D,), jnp.float32), 0.5, 1.5).astype(jnp.bfloat16),
        "router_weight": bell_draw(seeds[7], (D, EXPERTS), D ** -0.5, 0.21875, ((0, 8),)),
        "expert_gain": jnp.clip(1.0 + 0.1 * jax.random.normal(seeds[8], (D,), jnp.float32), 0.5, 1.5).astype(jnp.bfloat16),
        "expert_in": bell_draw(seeds[9], (EXPERTS, D, FF), D ** -0.5, 0.21875, ((0, 8), (2, 4))),
        "expert_out": bell_draw(seeds[10], (EXPERTS, FF, D), (FF // 2) ** -0.5, 0.15625, ((0, 8), (1, 4))),
        "routes": different_ones(seeds[11], TOKENS, EXPERTS, 2, 2048),
        "pair_order": jax.vmap(lambda own: jax.random.permutation(own, 2 * TOK_DEV))(jax.random.split(seeds[12], (N_DP * N_CONTEXT))).reshape((N_DP * N_CONTEXT, 2 * TOK_DEV)).astype(jnp.int32),
        "seq_lengths": draw_seq_lengths(jax.random.fold_in(seeds[15], 71), 0),
        "cotangent": heavy_noise(seeds[14], (TOKENS, D), 1.0, 6.0, ((0, 8),), (0, 1, 8, 2.0)),
    }


@jax.custom_vjp
def low(v):
    return lax.optimization_barrier(v.astype(jnp.bfloat16)).astype(jnp.float32)

@jax.custom_vjp
def low_back(v):
    return v

def low_keep(v):
    return (low(v), None)

def low_pass(kept, grad):
    return (grad,)

def back_keep(v):
    return (v, None)

def back_low(kept, grad):
    return (low(grad),)
low.defvjp(low_keep, low_pass)
low_back.defvjp(back_keep, back_low)
bucket_edges = np.array([19, 21, 24, 27, 31, 35, 40, 46, 52, 59, 67, 77, 87, 99, 113], dtype=np.int32)
epsilon = 1e-06
highest = lax.Precision.HIGHEST
masked_value = -1e+30

def bucket_of(distance):
    clipped = jnp.maximum(distance, 0)
    counted = lax.optimization_barrier(jnp.sum((clipped[..., None] >= jnp.asarray(bucket_edges)).astype(jnp.int32), axis=-1))
    return jnp.where(clipped < 16, clipped, 16 + counted)

def slot_of(pair_expert, pair_live, order_row):
    ordered_expert = pair_expert[order_row]
    ordered_live = pair_live[order_row]
    ordered_hot = ((ordered_expert[:, None] == jnp.arange(EXPERTS, dtype=jnp.int32)[None, :]) & ordered_live[:, None]).astype(jnp.int32)
    earlier = jnp.cumsum(ordered_hot, axis=0) - ordered_hot
    ordered_slot = lax.optimization_barrier(jnp.sum(earlier * ordered_hot, axis=1))
    return jnp.zeros(order_row.shape, jnp.int32).at[order_row].set(ordered_slot)

def reference(tokens_in, query_weight, key_weight, value_weight, output_weight, bias_table, attention_gain, router_weight, expert_gain, expert_in, expert_out, routes, pair_order, seq_lengths, cotangent):
    block_count = N_DP * N_CONTEXT
    positions = jnp.arange(GROUP, dtype=jnp.int32)
    first_end = seq_lengths[:, 0:1]
    second_end = first_end + seq_lengths[:, 1:2]
    segments = (positions[None, :] >= first_end).astype(jnp.int32) + (positions[None, :] >= second_end).astype(jnp.int32)
    token_live = (segments < 2).reshape(block_count, TOK_DEV)
    pair_expert = routes.reshape(block_count, 2 * TOK_DEV)
    pair_live = jnp.repeat(token_live, 2, axis=1)
    slots = jax.vmap(slot_of)(pair_expert, pair_live, pair_order)
    pair_kept = pair_live & (slots < CAP)
    source = jnp.arange(block_count, dtype=jnp.int32)[:, None]
    rows_total = EXPERTS * block_count * CAP
    pair_place = jnp.where(pair_kept, pair_expert * (block_count * CAP) + source * CAP + slots, rows_total)
    token_global = source * TOK_DEV + jnp.arange(2 * TOK_DEV, dtype=jnp.int32)[None, :] // 2
    slot_token = jnp.full((rows_total,), TOKENS, jnp.int32).at[pair_place.reshape(-1)].set(token_global.reshape(-1), mode='drop')
    place_tokens = pair_place.reshape(TOKENS, 2)
    route_hot = (routes[:, :, None] == jnp.arange(EXPERTS, dtype=jnp.int32)[None, None, :]).astype(jnp.float32)
    head_scale = HEAD_DIM ** (-0.5)

    def attention(queries, keys, values, table):

        def group_fn(packed):
            group_queries, group_keys, group_values, group_segments = packed

            def block_fn(inner):
                query_block, start = inner
                query_positions = start + jnp.arange(TOK_DEV, dtype=jnp.int32)
                raw = jnp.einsum('qhd,khd->hqk', query_block, group_keys, precision=highest) * head_scale
                buckets = bucket_of(query_positions[:, None] - positions[None, :])
                bias = jnp.transpose(table[buckets], (2, 0, 1))
                scores = low_back(raw + bias)
                query_segments = lax.dynamic_slice_in_dim(group_segments, start, TOK_DEV)
                visible = (query_segments[:, None] == group_segments[None, :]) & (positions[None, :] <= query_positions[:, None])
                masked = jnp.where(visible[None], scores, masked_value)
                top_score = lax.optimization_barrier(jnp.max(masked, axis=-1, keepdims=True))
                exponent = jnp.where(visible[None], jnp.exp(masked - top_score), 0.0)
                probs = exponent / lax.optimization_barrier(jnp.sum(exponent, axis=-1, keepdims=True))
                return jnp.einsum('hqk,khd->qhd', low(probs), group_values, precision=highest)
            starts = jnp.arange(N_CONTEXT, dtype=jnp.int32) * TOK_DEV
            blocks = group_queries.reshape(N_CONTEXT, TOK_DEV, HEADS, HEAD_DIM)
            return lax.map(jax.checkpoint(block_fn), (blocks, starts)).reshape(GROUP, HEADS, HEAD_DIM)
        shaped = (queries.reshape(N_DP, GROUP, HEADS, HEAD_DIM), keys.reshape(N_DP, GROUP, HEADS, HEAD_DIM), values.reshape(N_DP, GROUP, HEADS, HEAD_DIM), segments)
        return lax.map(group_fn, shaped).reshape(TOKENS, D)

    def forward(inputs, query_w, key_w, value_w, output_w, table, gain_one, router_w, gain_two, inner_w, outer_w):
        scale_one = lax.rsqrt(lax.optimization_barrier(jnp.mean(inputs * inputs, axis=-1, keepdims=True)) + epsilon)
        hidden_one = low(inputs * scale_one * gain_one)
        queries = low_back(low(jnp.dot(hidden_one, query_w, precision=highest)))
        keys = low_back(low(jnp.dot(hidden_one, key_w, precision=highest)))
        values = low_back(low(jnp.dot(hidden_one, value_w, precision=highest)))
        attended = low_back(low(attention(queries, keys, values, table)))
        branch = low_back(jnp.dot(attended, output_w, precision=highest))
        residual_one = inputs + branch
        scale_two = lax.rsqrt(lax.optimization_barrier(jnp.mean(residual_one * residual_one, axis=-1, keepdims=True)) + epsilon)
        hidden_two = low(residual_one * scale_two * gain_two)
        logits = low_back(jnp.dot(hidden_two, router_w, precision=highest))
        router_probs = jax.nn.softmax(logits, axis=-1)
        picked = lax.optimization_barrier(jnp.sum(router_probs[:, None, :] * route_hot, axis=-1))
        gate_values = picked / lax.optimization_barrier(jnp.sum(picked, axis=-1, keepdims=True))
        padded = jnp.concatenate([hidden_two, jnp.zeros((1, D), jnp.float32)], axis=0)
        expert_rows = low_back(padded[slot_token]).reshape(EXPERTS, block_count * CAP, D)

        def one_expert(packed):
            rows_in, inner, outer = packed
            pre_act = low_back(jnp.dot(rows_in, inner, precision=highest))
            acted = low(jax.nn.gelu(pre_act))
            return low_back(low(jnp.dot(acted, outer, precision=highest)))
        expert_outs = lax.map(one_expert, (expert_rows, inner_w, outer_w)).reshape(rows_total, D)
        out_pad = jnp.concatenate([expert_outs, jnp.zeros((1, D), jnp.float32)], axis=0)
        pair_outs = out_pad[place_tokens]
        mixture = lax.optimization_barrier(jnp.sum(gate_values[:, :, None] * pair_outs, axis=1))
        return residual_one + mixture
    floats = (tokens_in.astype(jnp.float32), query_weight.astype(jnp.float32), key_weight.astype(jnp.float32), value_weight.astype(jnp.float32), output_weight.astype(jnp.float32), bias_table.astype(jnp.float32), attention_gain.astype(jnp.float32), router_weight.astype(jnp.float32), expert_gain.astype(jnp.float32), expert_in.astype(jnp.float32), expert_out.astype(jnp.float32))
    result, pullback = jax.vjp(forward, *floats)
    grads = pullback(cotangent.astype(jnp.float32))
    return (result.astype(jnp.bfloat16), grads[0], grads[1], grads[2], grads[3], grads[4], grads[5], grads[6], grads[7], grads[8], grads[9], grads[10])
```

```python
import functools
import jax
import jax.numpy as jnp
import numpy as np
from jax import lax
from jax.experimental import pallas as pl
from jax.experimental.pallas import tpu as pltpu
from jax.sharding import PartitionSpec as P

bf16 = jnp.bfloat16
f32 = jnp.float32
epsilon = 1e-06
masked_value = -1e30
tile = 256
VMEM = pl.BlockSpec(memory_space=pltpu.VMEM)
SMEM = pl.BlockSpec(memory_space=pltpu.SMEM)


def dot_nn(a, b):
    return lax.dot_general(a, b, (((1,), (0,)), ((), ())), preferred_element_type=f32)


def dot_nt(a, b):
    return lax.dot_general(a, b, (((1,), (1,)), ((), ())), preferred_element_type=f32)


def dot_tn(a, b):
    return lax.dot_general(a, b, (((0,), (0,)), ((), ())), preferred_element_type=f32)


def start_of(position, first_end, second_end):
    return jnp.where(
        position >= second_end, second_end, jnp.where(position >= first_end, first_end, 0)
    )


def aligned(value, size):
    return pl.multiple_of(value, size)


def attention_forward_kernel(
    heads, width, scalars, far_bias, offsets, query_ref, bias_ref, *rest
):
    piece_count = len(rest) - 9
    pieces = rest[:piece_count]
    packed_one, packed_two, lse_ref, keys_values = rest[piece_count : piece_count + 4]
    values_t, best, running, side_one, side_two = rest[piece_count + 4 :]
    rows = query_ref.shape[0]
    context, first_end, second_end = scalars[0], scalars[1], scalars[2]
    for index, piece in enumerate(pieces):
        size = piece.shape[0]
        keys_values[pl.ds(aligned(offsets[index], 128), size), :] = piece[...]
    lane_q = lax.broadcasted_iota(jnp.int32, (tile, 256), 1)

    def transpose_values(index, carry):
        start = aligned(index * tile, tile)
        upper = keys_values[pl.ds(start, tile), 256:384].astype(f32).T.astype(bf16)
        lower = keys_values[pl.ds(start, tile), 128:256].astype(f32).T.astype(bf16)
        values_t[0, 0:width, pl.ds(start, tile)] = upper[0:width]
        values_t[1, 0:width, pl.ds(start, tile)] = upper[width:]
        values_t[2, 0:width, pl.ds(start, tile)] = lower[width:]
        for head in range(heads):
            values_t[head, width:, pl.ds(start, tile)] = jnp.ones((16, tile), bf16)
        return carry

    lax.fori_loop(0, (context + 1) * (rows // tile), transpose_values, 0)

    def query_tile(index, carry):
        local = aligned(index * tile, tile)
        first = aligned(context * rows + local, tile)
        positions = first + lax.broadcasted_iota(jnp.int32, (1, tile), 1)
        row_start = start_of(positions, first_end, second_end)
        start_first = start_of(first, first_end, second_end)
        start_last = start_of(first + tile - 1, first_end, second_end)
        queries = query_ref[pl.ds(local, tile), :]
        masked_queries = [
            jnp.where(lane_q // width == head, queries, jnp.zeros_like(queries))
            for head in range(heads)
        ]

        def absorb(key_start, size, bias_index, masked, first_time):
            keys = keys_values[pl.ds(key_start, size), 0:256]
            if masked:
                key_positions = key_start + lax.broadcasted_iota(jnp.int32, (size, tile), 0)
                seen = key_positions >= row_start
                if bias_index == 0:
                    seen = seen & (key_positions <= positions)
            for head in range(heads):
                scores = dot_nt(keys, masked_queries[head])
                shift = 0.0
                if bias_index is None:
                    shift = far_bias[head]
                else:
                    scores = scores + bias_ref[bias_index, head]
                if masked:
                    scores = jnp.where(seen, scores, masked_value)
                top = jnp.max(scores, axis=0, keepdims=True) + shift
                values = values_t[head, :, pl.ds(key_start, size)]
                if first_time:
                    weights = jnp.exp(scores - top).astype(bf16)
                    running[head] = dot_nn(values, weights)
                    best[head] = jnp.broadcast_to(top, (8, tile))
                else:
                    old = best[head, 0:1]
                    new = jnp.maximum(old, top)
                    weights = jnp.exp(scores - (new - shift)).astype(bf16)
                    running[head] = running[head] * jnp.exp(old - new) + dot_nn(values, weights)
                    best[head] = jnp.broadcast_to(new, (8, tile))

        absorb(first, tile, 0, True, True)

        @pl.when(first > 0)
        def _():
            absorb(aligned(first - tile, tile), tile, 1, True, False)

        far_rows = jnp.maximum(first - tile, 0)
        big = 2 * tile
        big_count = far_rows // big
        low = jnp.minimum(start_first // big, big_count)
        middle = jnp.clip((start_last + big - 1) // big, low, big_count)

        def masked_step(step, carry):
            absorb(aligned(step * big, big), big, None, True, False)
            return carry

        def plain_step(step, carry):
            absorb(aligned(step * big, big), big, None, False, False)
            return carry

        lax.fori_loop(low, middle, masked_step, 0)
        lax.fori_loop(middle, big_count, plain_step, 0)

        @pl.when(far_rows > big_count * big)
        def _():
            absorb(aligned(big_count * big, tile), tile, None, True, False)

        outs = []
        for head in range(heads):
            total = running[head, width : width + 1]
            outs.append(running[head, 0:width] / total)
            lse_ref[pl.ds(head, 1), pl.ds(local, tile)] = best[head, 0:1] + jnp.log(total)
        side_one[pl.ds(local, tile), :] = jnp.concatenate([outs[0], outs[1]], axis=0).T
        side_two[pl.ds(local, tile), :] = jnp.concatenate([outs[2], outs[2]], axis=0).T
        return carry

    lax.fori_loop(0, rows // tile, query_tile, 0)
    half, quarter = rows // 2, rows // 4
    lane = lax.broadcasted_iota(jnp.int32, (quarter, 128), 1)
    for part, packed in enumerate((packed_one, packed_two)):
        near = slice(part * quarter, (part + 1) * quarter)
        later = slice(half + part * quarter, half + (part + 1) * quarter)
        packed[:, 0:128] = side_one[near, :].astype(bf16)
        packed[:, 128:256] = jnp.where(
            lane < width, side_two[near, :], side_two[later, :]
        ).astype(bf16)
        packed[:, 256:384] = side_one[later, :].astype(bf16)


def attention_forward(scalars, far_bias, offsets, queries, bias_tiles, pieces, group_rows, heads, width):
    rows = queries.shape[0]
    return pl.pallas_call(
        functools.partial(attention_forward_kernel, heads, width),
        out_shape=(
            jax.ShapeDtypeStruct((rows // 4, 384), bf16),
            jax.ShapeDtypeStruct((rows // 4, 384), bf16),
            jax.ShapeDtypeStruct((8, rows), f32),
            jax.ShapeDtypeStruct((group_rows, 384), bf16),
        ),
        in_specs=[SMEM, SMEM, SMEM, VMEM, VMEM] + [VMEM] * len(pieces),
        out_specs=(VMEM,) * 4,
        scratch_shapes=[
            pltpu.VMEM((heads, width + 16, group_rows), bf16),
            pltpu.VMEM((heads, 8, tile), f32),
            pltpu.VMEM((heads, width + 16, tile), f32),
            pltpu.VMEM((rows, 128), f32),
            pltpu.VMEM((rows, 128), f32),
        ],
        compiler_params=pltpu.CompilerParams(vmem_limit_bytes=56 * 2**20),
        cost_estimate=pl.CostEstimate(
            flops=4 * rows * group_rows * 256 * heads,
            bytes_accessed=10 * 2**20,
            transcendentals=rows * group_rows * heads,
        ),
        name="attention_forward",
    )(scalars, far_bias, offsets, queries, bias_tiles, *pieces)


def attention_backward_kernel(
    heads, width, piece_count, scalars, far_bias, offsets,
    query_ref, keys_values, bias_ref, lse_ref, packed_one, packed_two, output_ref, *rest
):
    pieces = rest[:piece_count]
    (
        dq_ref, own_ref, beside_one, beside_two, across_one, across_two, far_one, far_two, fold_ref
    ) = rest[piece_count : piece_count + 9]
    grad_branch, dout, masked_q, masked_o, keys_t, deltas, dq_t, dk, dv, dkv, band_ref = rest[
        piece_count + 9 :
    ]
    rows = query_ref.shape[0]
    half, quarter = rows // 2, rows // 4
    context, first_end, second_end = scalars[0], scalars[1], scalars[2]
    tiles_here = rows // tile
    for index, piece in enumerate(pieces):
        grad_branch[pl.ds(aligned(offsets[index], 128), piece.shape[0]), :] = piece[...]
    lane_low = lax.broadcasted_iota(jnp.int32, (output_ref.shape[0], 128), 1)
    last_head = jnp.where(lane_low < width, output_ref[:, 128:256].astype(f32), 0.0)
    ordered = jnp.concatenate(
        [pltpu.roll(last_head, width, 1).astype(bf16), output_ref[:, 0:128]], axis=1
    )
    dout[...] = dot_nn(grad_branch[...], ordered).astype(bf16)
    head_row = lax.broadcasted_iota(jnp.int32, (16, 256), 0)
    head_lane = lax.broadcasted_iota(jnp.int32, (16, 256), 1) // width
    head_hot = (head_row == jnp.where(head_lane == 1, 2, head_lane - 2)).astype(bf16)
    for part in range(4):
        span = slice(part * quarter, (part + 1) * quarter)
        packed = packed_one if part % 2 == 0 else packed_two
        lower = packed[:, 128:256].astype(f32)
        if part < 2:
            upper, lower = packed[:, 0:128], pltpu.roll(lower, width, 1)
        else:
            upper = packed[:, 256:384]
        product = dout[span, :].astype(f32) * jnp.concatenate([lower, upper.astype(f32)], axis=1)
        high = product.astype(bf16)
        rest_part = (product - high.astype(f32)).astype(bf16)
        deltas[:, span] = dot_nt(head_hot, high) + dot_nt(head_hot, rest_part)
    lane = lax.broadcasted_iota(jnp.int32, (rows, 256), 1) // width
    for head in range(heads):
        masked_q[head] = jnp.where(lane == head, query_ref[...], jnp.zeros((rows, 256), bf16))
        slot = 1 if head == 2 else head + 2
        masked_o[head] = jnp.where(lane == slot, dout[...], jnp.zeros((rows, 256), bf16))

    def transpose_keys(index, carry):
        start = aligned(index * tile, tile)
        lower = keys_values[pl.ds(start, tile), 0:128].astype(f32).T.astype(bf16)
        upper = keys_values[pl.ds(start, tile), 128:256].astype(f32).T.astype(bf16)
        keys_t[0, :, pl.ds(start, tile)] = lower[0:width]
        keys_t[1, :, pl.ds(start, tile)] = lower[width:]
        keys_t[2, :, pl.ds(start, tile)] = upper[0:width]
        return carry

    lax.fori_loop(0, (context + 1) * tiles_here, transpose_keys, 0)
    dq_t[...] = jnp.zeros_like(dq_t)
    dkv[...] = jnp.zeros_like(dkv)
    band_ref[...] = jnp.zeros_like(band_ref)
    first = context * rows
    all_positions = first + lax.broadcasted_iota(jnp.int32, (1, rows), 1)
    all_starts = start_of(all_positions, first_end, second_end)
    start_first = start_of(first, first_end, second_end)
    start_last = start_of(first + rows - 1, first_end, second_end)

    def block(key_start, query_start, size, bias_index, masked, near):
        keys = keys_values[pl.ds(key_start, tile), 0:256]
        values = keys_values[pl.ds(key_start, tile), 128:384]
        key_sum, value_sum = None, None
        if masked:
            key_positions = key_start + lax.broadcasted_iota(jnp.int32, (tile, size), 0)
            if near:
                positions = (
                    first + query_start + lax.broadcasted_iota(jnp.int32, (1, size), 1)
                )
                seen = (key_positions >= start_of(positions, first_end, second_end)) & (
                    key_positions <= positions
                )
            else:
                seen = key_positions >= all_starts
        span = pl.ds(query_start, size)
        for head in range(heads):
            queries = masked_q[head, span, :]
            grads = masked_o[head, span, :]
            scores = dot_nt(keys, queries)
            lse = lse_ref[pl.ds(head, 1), span]
            if near:
                scores = scores + bias_ref[bias_index, head]
            else:
                lse = lse - far_bias[head]
            probs = jnp.exp(scores - lse)
            if masked:
                probs = jnp.where(seen, probs, 0.0)
            grad_probs = dot_nt(values, grads)
            grad_scores = probs * (grad_probs - deltas[pl.ds(head, 1), span])
            if near:

                @pl.when(bias_index < 2)
                def _():
                    band_ref[bias_index, head] += grad_scores

            low_scores = grad_scores.astype(bf16)
            value_part = dot_nn(probs.astype(bf16), grads)
            key_part = dot_nn(low_scores, queries)
            dq_t[head, :, span] += dot_nn(keys_t[head, :, pl.ds(key_start, tile)], low_scores)
            key_sum = key_part if key_sum is None else key_sum + key_part
            value_sum = value_part if value_sum is None else value_sum + value_part
        return key_sum, value_sum

    lane_tile = lax.broadcasted_iota(jnp.int32, (tile, 128), 1)

    def write(key_start, key_sum, value_sum):
        span = pl.ds(key_start, tile)
        dkv[span, 0:128] = key_sum[:, 0:128].astype(bf16)
        dkv[span, 128:256] = jnp.where(
            lane_tile < width, key_sum[:, 128:256], value_sum[:, 0:128]
        ).astype(bf16)
        dkv[span, 256:384] = value_sum[:, 128:256].astype(bf16)

    far_count = jnp.maximum(context * tiles_here - 1, 0)
    low = jnp.minimum(start_first // tile, far_count)
    middle = jnp.clip((start_last + tile - 1) // tile, low, far_count)

    def masked_step(index, carry):
        start = aligned(index * tile, tile)
        write(start, *block(start, 0, rows, None, True, False))
        return carry

    def plain_step(index, carry):
        start = aligned(index * tile, tile)
        write(start, *block(start, 0, rows, None, False, False))
        return carry

    lax.fori_loop(low, middle, masked_step, 0)
    lax.fori_loop(middle, far_count, plain_step, 0)

    def near_keys(index, carry):
        start = aligned(index * tile, tile)
        lag = index - context * tiles_here
        dk[...] = jnp.zeros_like(dk)
        dv[...] = jnp.zeros_like(dv)

        def near_queries(query, inner):
            bias_index = jnp.minimum(query - lag, 2)
            key_sum, value_sum = block(
                start, aligned(query * tile, tile), tile, bias_index, True, True
            )
            dk[...] += key_sum
            dv[...] += value_sum
            return inner

        lax.fori_loop(jnp.maximum(lag, 0), tiles_here, near_queries, 0)
        write(start, dk[...], dv[...])
        return carry

    lax.fori_loop(far_count, (context + 1) * tiles_here, near_keys, 0)

    def block_rows(which):
        return pl.ds(aligned(which * rows, rows), rows)

    own_ref[...] = dkv[block_rows(context), :]
    for which, first_half, second_half in (
        (1, beside_one, beside_two), (2, across_one, across_two), (3, far_one, far_two)
    ):
        start = (context ^ which) * rows
        first_half[...] = dkv[pl.ds(aligned(start, half), half), :]
        second_half[...] = dkv[pl.ds(aligned(start + half, half), half), :]
    key_index = lax.broadcasted_iota(jnp.int32, (tile, tile), 0)
    query_index = lax.broadcasted_iota(jnp.int32, (tile, tile), 1)
    fold_ref[...] = jnp.zeros_like(fold_ref)
    for head in range(heads):
        both = jnp.where(key_index > query_index, band_ref[1, head], band_ref[0, head])
        by_row = both[0:8]
        for first_row in range(8, tile, 8):
            by_row = by_row + pltpu.roll(both[first_row : first_row + 8], tile - first_row, 1)
        folded = by_row[0:1]
        for row in range(1, 8):
            folded = folded + pltpu.roll(by_row, tile - row, 1)[row : row + 1]
        fold_ref[head : head + 1, :] = folded
    upper = jnp.concatenate([dq_t[0], dq_t[1]], axis=0)
    lower = jnp.concatenate([dq_t[2], jnp.zeros((width, rows), f32)], axis=0)
    scale = width ** (-0.5)
    dq_ref[:, 0:128] = (upper.T * scale).astype(bf16)
    dq_ref[:, 128:256] = (lower.T * scale).astype(bf16)


def attention_backward(
    scalars, far_bias, offsets, queries, keys_values, bias_tiles, lse, packed, output_part, pieces, heads, width
):
    rows = queries.shape[0]
    half = rows // 2
    group_rows = keys_values.shape[0]
    model = output_part.shape[0]
    shape = jax.ShapeDtypeStruct
    return pl.pallas_call(
        functools.partial(attention_backward_kernel, heads, width, len(pieces)),
        out_shape=(
            shape((rows, 256), bf16),
            shape((rows, 384), bf16),
        )
        + (shape((half, 384), bf16),) * 6
        + (shape((8, tile), f32),),
        in_specs=[SMEM, SMEM, SMEM] + [VMEM] * (7 + len(pieces)),
        out_specs=(VMEM,) * 9,
        scratch_shapes=[
            pltpu.VMEM((rows, model), bf16),
            pltpu.VMEM((rows, 256), bf16),
            pltpu.VMEM((heads, rows, 256), bf16),
            pltpu.VMEM((heads, rows, 256), bf16),
            pltpu.VMEM((heads, width, group_rows), bf16),
            pltpu.VMEM((16, rows), f32),
            pltpu.VMEM((heads, width, rows), f32),
            pltpu.VMEM((tile, 256), f32),
            pltpu.VMEM((tile, 256), f32),
            pltpu.VMEM((group_rows, 384), bf16),
            pltpu.VMEM((2, heads, tile, tile), f32),
        ],
        compiler_params=pltpu.CompilerParams(vmem_limit_bytes=60 * 2**20),
        cost_estimate=pl.CostEstimate(
            flops=10 * rows * group_rows * 256 * heads,
            bytes_accessed=16 * 2**20,
            transcendentals=rows * group_rows * heads,
        ),
        name="attention_backward",
    )(scalars, far_bias, offsets, queries, keys_values, bias_tiles, lse, *packed, output_part, *pieces)


bucket_edges = np.array(
    [19, 21, 24, 27, 31, 35, 40, 46, 52, 59, 67, 77, 87, 99, 113], dtype=np.int32
)


def bucket_tiles():
    key = np.arange(tile)[None, :, None]
    query = np.arange(tile)[None, None, :]
    lag = np.arange(3)[:, None, None] * tile + query - key
    clipped = np.maximum(lag, 0)
    counted = (clipped[..., None] >= bucket_edges).sum(-1)
    return np.where(clipped < 16, clipped, 16 + counted).astype(np.int32)


def bias_of(table, buckets):
    out = jnp.broadcast_to(table[0][None, :, None, None], (buckets.shape[0], table.shape[1]) + buckets.shape[1:])
    for b in range(1, table.shape[0]):
        out = jnp.where(buckets[:, None] >= b, table[b][None, :, None, None], out)
    return out


def shape(dims, dtype):
    return jax.ShapeDtypeStruct(dims, dtype)


def params(mebibytes):
    return pltpu.CompilerParams(vmem_limit_bytes=mebibytes * 2**20)


def cost(flops, bytes_accessed):
    return pl.CostEstimate(flops=flops, bytes_accessed=bytes_accessed, transcendentals=0)


def gelu_constants():
    return 0.7978845608028654, 0.044715


def place_kernel(capacity, scalars, route_ref, order_ref, rows_ref, columns_ref, ranks, hot_ref, tall):
    pair_count = order_ref.shape[1]
    rows = pair_count // 2
    expert_pad = hot_ref.shape[0]
    step = 256
    live_end = scalars[2] - scalars[0] * rows
    order = order_ref[...]
    index_row = lax.broadcasted_iota(jnp.int32, (pair_count, 128), 0)
    index_lane = lax.broadcasted_iota(jnp.int32, (pair_count, 128), 1)
    digits = jnp.where(
        index_lane == 0, index_row // 64, jnp.where(index_lane == 1, index_row % 64, 0)
    ).astype(f32).astype(bf16)

    def rank_step(index, carry):
        start = aligned(index * step, step)
        pair = start + lax.broadcasted_iota(jnp.int32, (step, pair_count), 0)
        hit = (pair == order).astype(f32).astype(bf16)
        found = dot_nn(hit, digits)
        rank = found[:, 0:1] * 64.0 + found[:, 1:2]
        ranks[pl.ds(start, step), :] = jnp.broadcast_to(rank, (step, 128))
        return carry

    lax.fori_loop(0, pair_count // step, rank_step, 0)
    rank_row = ranks[...].T[0:1, :]
    position = lax.broadcasted_iota(jnp.int32, (1, rows), 1)
    live = position < live_end
    expert_row = jnp.concatenate([route_ref[0:1, :], route_ref[1:2, :]], axis=1)
    live_row = jnp.concatenate([live, live], axis=1)
    expert_index = lax.broadcasted_iota(jnp.int32, (expert_pad, pair_count), 0)
    hot = ((expert_index == expert_row) & live_row).astype(f32)
    hot_ref[...] = hot.astype(bf16)

    def count_step(index, counts):
        start = aligned(index * step, step)
        earlier = (ranks[pl.ds(start, step), 0:1] < rank_row).astype(f32).astype(bf16)
        return counts + dot_nn(hot_ref[:, pl.ds(start, step)], earlier)

    counts = lax.fori_loop(
        0, pair_count // step, count_step, jnp.zeros((expert_pad, pair_count), f32)
    )
    slot = jnp.sum(counts * hot, axis=0, keepdims=True).astype(jnp.int32)
    place = jnp.where(live_row & (slot < capacity), expert_row * capacity + slot, -1)
    rows_ref[...] = jnp.full_like(rows_ref, -1)
    rows_ref[0:1, :] = place[:, 0:rows]
    rows_ref[1:2, :] = place[:, rows:]
    tall[...] = jnp.full_like(tall, -1.0)
    tall[0:1, :] = place[:, 0:rows].astype(f32)
    tall[1:2, :] = place[:, rows:].astype(f32)
    columns_ref[...] = tall[...].T.astype(jnp.int32)


def find_places(scalars, route_rows, order_row, expert_count, capacity):
    rows = route_rows.shape[1]
    expert_pad = max(16, expert_count)
    return pl.pallas_call(
        functools.partial(place_kernel, capacity),
        out_shape=(shape((8, rows), jnp.int32), shape((rows, 128), jnp.int32)),
        in_specs=[SMEM, VMEM, VMEM],
        out_specs=(VMEM, VMEM),
        scratch_shapes=[
            pltpu.VMEM((2 * rows, 128), f32),
            pltpu.VMEM((expert_pad, 2 * rows), bf16),
            pltpu.VMEM((128, rows), f32),
        ],
        compiler_params=params(40),
        cost_estimate=cost(4 * 4 * rows * rows * 128, 2**20),
        name="find_places",
    )(scalars, route_rows, order_row)


def project_kernel(piece_count, offsets, token_ref, *rest):
    pieces = rest[:piece_count]
    hidden_ref, query_ref, kv_one, kv_two, weight_ref, gain_ref = rest[piece_count:]
    for index, piece in enumerate(pieces):
        weight_ref[pl.ds(aligned(offsets[index], 16), piece.shape[0]), :] = piece[...]
    rows = token_ref.shape[0]
    half = rows // 2
    gains = weight_ref[:, 128:256].astype(f32).T
    gain_ref[0:1, :] = gains[64:65, :]
    gain_ref[1:2, :] = gains[65:66, :]
    step = 256
    lane = lax.broadcasted_iota(jnp.int32, (step, 256), 1)
    for start in range(0, rows, step):
        inputs = token_ref[start : start + step, :].astype(f32)
        scale = lax.rsqrt(jnp.mean(inputs * inputs, axis=-1, keepdims=True) + epsilon)
        hidden = (inputs * scale * gain_ref[0:1, :]).astype(bf16)
        hidden_ref[start : start + step, :] = hidden
        queries = dot_nn(hidden, weight_ref[:, 0:256]).astype(bf16)
        query_ref[start : start + step, :] = jnp.where(
            lane < 192, queries * bf16(0.125), jnp.zeros_like(queries)
        )
        target, base = (kv_one, 0) if start < half else (kv_two, half)
        target[start - base : start - base + step, :] = dot_nn(
            hidden, weight_ref[:, 256:640]
        ).astype(bf16)


def project(offsets, tokens, pieces):
    rows, model = tokens.shape
    return pl.pallas_call(
        functools.partial(project_kernel, len(pieces)),
        out_shape=(
            shape((rows, model), bf16),
            shape((rows, 256), bf16),
            shape((rows // 2, 384), bf16),
            shape((rows // 2, 384), bf16),
            shape((model, 640), bf16),
            shape((8, model), f32),
        ),
        in_specs=[SMEM, VMEM] + [VMEM] * len(pieces),
        out_specs=(VMEM,) * 6,
        compiler_params=params(40),
        cost_estimate=cost(2 * rows * model * 640, 6 * 2**20),
        name="project",
    )(offsets, tokens, *pieces)


def assemble_kernel(piece_count, offsets, *rest):
    pieces = rest[:piece_count]
    out_ref = rest[piece_count]
    for index, piece in enumerate(pieces):
        size = piece.shape[0]
        out_ref[pl.ds(aligned(offsets[index], 16), size), :] = piece[...].astype(out_ref.dtype)


def assemble(offsets, pieces, dtype):
    total = sum(piece.shape[0] for piece in pieces)
    width = pieces[0].shape[1]
    return pl.pallas_call(
        functools.partial(assemble_kernel, len(pieces)),
        out_shape=shape((total, width), dtype),
        in_specs=[SMEM] + [VMEM] * len(pieces),
        out_specs=VMEM,
        compiler_params=params(40),
        cost_estimate=cost(0, 6 * total * width),
        name="assemble",
    )(offsets, *pieces)


def dispatch_kernel(
    heads, width, capacity, expert_count, chunk_count, scalars, starts,
    token_ref, gain_ref, route_ref, row_place, *rest
):
    attended = rest[0:8]
    weights = rest[8:12]
    residual_ref, hidden_ref, info_ref = rest[12:15]
    chunks = rest[15 : 15 + chunk_count]
    packed, joined, column = rest[15 + chunk_count :]
    rows, model = token_ref.shape
    quarter = rows // 4
    lane_low = lax.broadcasted_iota(jnp.int32, (quarter, 128), 1)
    for source in range(4):
        for part in range(2):
            piece = attended[2 * source + part]
            span = slice(part * quarter, (part + 1) * quarter)
            middle = piece[:, 128:256].astype(f32)
            packed[source, span, 0:128] = piece[:, 0:128]
            packed[source, span, 128:256] = jnp.where(lane_low < width, middle, 0.0).astype(bf16)
            span = slice((part + 2) * quarter, (part + 3) * quarter)
            packed[source, span, 0:128] = piece[:, 256:384]
            packed[source, span, 128:256] = jnp.where(
                lane_low < width, pltpu.roll(middle, 64, 1), 0.0
            ).astype(bf16)
    step = 256
    lane = lax.broadcasted_iota(jnp.int32, (step, 128), 1)
    valid = (lane >= 64) & (lane < 64 + expert_count)

    def token_step(index, carry):
        start = aligned(index * step, step)
        span = pl.ds(start, step)
        residual = token_ref[span, :].astype(f32)
        for source in range(4):
            residual = residual + dot_nt(packed[source, span, :], weights[source][...])
        joined[span, :] = residual
        scale = lax.rsqrt(jnp.mean(residual * residual, axis=-1, keepdims=True) + epsilon)
        hidden = (residual * scale * gain_ref[1:2, :]).astype(bf16)
        hidden_ref[span, :] = hidden
        logits = dot_nn(hidden, weights[0][:, 128:256])
        logits = jnp.where(valid, logits, masked_value)
        powers = jnp.where(valid, jnp.exp(logits - jnp.max(logits, axis=-1, keepdims=True)), 0.0)
        probs = powers / jnp.sum(powers, axis=-1, keepdims=True)
        first = jnp.sum(
            jnp.where(lane == route_ref[span, 0:1] + 64, probs, 0.0), axis=-1, keepdims=True
        )
        second = jnp.sum(
            jnp.where(lane == route_ref[span, 1:2] + 64, probs, 0.0), axis=-1, keepdims=True
        )
        total = first + second
        info_ref[span, :] = jnp.where(
            lane == 0,
            first / total,
            jnp.where(lane == 1, second / total, jnp.where(lane == 2, total, probs)),
        )
        return carry

    lax.fori_loop(0, rows // step, token_step, 0)
    residual_ref[...] = joined[pl.ds(aligned(scalars[3] * quarter, quarter), quarter), :]
    gates = info_ref[...].T
    gate_one, gate_two = gates[0:1, :], gates[1:2, :]
    place_one, place_two = row_place[0:1, :], row_place[1:2, :]
    slot = lax.broadcasted_iota(jnp.int32, (capacity, rows), 0)
    column[...] = jnp.zeros_like(column)

    def fill(chunk, entry, expert):
        base = expert * capacity
        hit_one = slot == place_one - base
        hit_two = slot == place_two - base
        picked = jnp.where(hit_one | hit_two, 1.0, 0.0).astype(bf16)
        chunk[entry, 16:, :] = dot_nn(picked, hidden_ref[...]).astype(bf16)
        gate = jnp.where(hit_one, gate_one, 0.0) + jnp.where(hit_two, gate_two, 0.0)
        gate = jnp.sum(gate, axis=-1, keepdims=True)
        column[0:capacity, :] = jnp.broadcast_to(gate, (capacity, 128))
        write_head(chunk, entry, column[...].T[0:1, :])

    for chunk_index, chunk in enumerate(chunks):
        if chunk.shape[0] == 1:
            fill(chunk, 0, starts[chunk_index])
        else:

            def one(entry, carry):
                fill(chunk, entry, starts[chunk_index] + entry)
                return carry

            lax.fori_loop(0, chunk.shape[0], one, 0)


def write_head(chunk, entry, row):
    high = row.astype(bf16)
    left = row - high.astype(f32)
    middle = left.astype(bf16)
    low = (left - middle.astype(f32)).astype(bf16)
    size = row.shape[1]
    index = lax.broadcasted_iota(jnp.int32, (16, size), 0)
    block = jnp.where(
        index == 0,
        high.astype(f32),
        jnp.where(index == 1, middle.astype(f32), jnp.where(index == 2, low.astype(f32), 0.0)),
    )
    chunk[entry, 0:16, :] = jnp.zeros((16, chunk.shape[2]), bf16)
    chunk[entry, 0:16, 0:size] = block.astype(bf16)


def dispatch(
    scalars, starts, tokens, gains, routes, row_place, attended, weights, chunk_shapes,
    heads, width, capacity, expert_count
):
    rows, model = tokens.shape
    pad = (capacity + 127) // 128 * 128
    return pl.pallas_call(
        functools.partial(
            dispatch_kernel, heads, width, capacity, expert_count, len(chunk_shapes)
        ),
        out_shape=(
            shape((rows // 4, model), f32),
            shape((rows, model), bf16),
            shape((rows, 128), f32),
        )
        + tuple(shape((per, capacity + 16, model), bf16) for per in chunk_shapes),
        in_specs=[SMEM, SMEM] + [VMEM] * 16,
        out_specs=(VMEM,) * (3 + len(chunk_shapes)),
        scratch_shapes=[
            pltpu.VMEM((4, rows, 256), bf16),
            pltpu.VMEM((rows, model), f32),
            pltpu.VMEM((pad, 128), f32),
        ],
        compiler_params=params(56),
        cost_estimate=cost(2 * rows * model * (1024 + 2304), 16 * 2**20),
        name="dispatch",
    )(scalars, starts, tokens, gains, routes, row_place, *attended, *weights)


def scatter_kernel(capacity, chunk_count, starts, value_ref, row_place, *chunks):
    rows = value_ref.shape[0]
    place_one, place_two = row_place[0:1, :], row_place[1:2, :]
    slot = lax.broadcasted_iota(jnp.int32, (capacity, rows), 0)

    def fill(chunk, entry, expert):
        base = expert * capacity
        hit = (slot == place_one - base) | (slot == place_two - base)
        picked = jnp.where(hit, 1.0, 0.0).astype(bf16)
        chunk[entry] = dot_nn(picked, value_ref[...]).astype(bf16)

    for chunk_index, chunk in enumerate(chunks):
        if chunk.shape[0] == 1:
            fill(chunk, 0, starts[chunk_index])
        else:

            def one(entry, carry):
                fill(chunk, entry, starts[chunk_index] + entry)
                return carry

            lax.fori_loop(0, chunk.shape[0], one, 0)


def scatter_rows(starts, values, row_place, chunk_shapes, capacity):
    rows, model = values.shape
    return pl.pallas_call(
        functools.partial(scatter_kernel, capacity, len(chunk_shapes)),
        out_shape=tuple(shape((per, capacity, model), bf16) for per in chunk_shapes),
        in_specs=[SMEM, VMEM, VMEM],
        out_specs=(VMEM,) * len(chunk_shapes),
        compiler_params=params(40),
        cost_estimate=cost(2 * rows * model * 2304, 6 * 2**20),
        name="scatter_rows",
    )(starts, values, row_place)


def expert_kernel(chunk_count, in_ref, out_ref, *rest):
    row_chunks = rest[:chunk_count]
    grad_chunks = rest[chunk_count : 2 * chunk_count]
    rows_all, grads_all, acted_all, pre_all = rest[2 * chunk_count : 2 * chunk_count + 4]
    returns = rest[2 * chunk_count + 4 : 3 * chunk_count + 4]
    held, column = rest[3 * chunk_count + 4 :]
    source_count, capacity, model = rows_all.shape
    root, cubic = gelu_constants()
    at = 0
    for chunk, grads in zip(row_chunks, grad_chunks):
        per = chunk.shape[0]
        rows_all[at : at + per] = chunk[:, 16:, :]
        grads_all[at : at + per] = grads[...]
        at += per
    column[...] = jnp.zeros_like(column)

    def one(source, carry):
        pre = dot_nn(rows_all[source], in_ref[0])
        square = pre * pre
        bent = jnp.tanh(root * pre * (1.0 + cubic * square))
        acted = (0.5 * pre * (1.0 + bent)).astype(bf16)
        slope = 0.5 * (1.0 + bent) + 0.5 * pre * (1.0 - bent * bent) * root * (
            1.0 + 3.0 * cubic * square
        )
        grad_acted = dot_nt(grads_all[source], out_ref[0])
        acted_all[source] = acted
        gate_grad = jnp.sum(grad_acted * acted.astype(f32), axis=-1, keepdims=True)
        column[0:capacity, :] = jnp.broadcast_to(gate_grad, (capacity, 128))
        grad_pre = (grad_acted * slope).astype(bf16)
        pre_all[source] = grad_pre
        held[source, 16:, :] = dot_nt(grad_pre, in_ref[0]).astype(bf16)
        write_head(held, source, column[...].T[0:1, :])
        return carry

    lax.fori_loop(0, source_count, one, 0)
    at = 0
    for returned in returns:
        per = returned.shape[0]
        returned[...] = held[at : at + per]
        at += per


def expert_step(weight_in, weight_out, row_chunks, grad_chunks):
    count = len(row_chunks)
    sources = sum(chunk.shape[0] for chunk in row_chunks)
    _, capacity, model = grad_chunks[0].shape
    hidden = weight_in.shape[2]
    pad = (capacity + 127) // 128 * 128
    return pl.pallas_call(
        functools.partial(expert_kernel, count),
        out_shape=(
            shape((sources, capacity, model), bf16),
            shape((sources, capacity, model), bf16),
            shape((sources, capacity, hidden), bf16),
            shape((sources, capacity, hidden), bf16),
        )
        + tuple(shape(chunk.shape, bf16) for chunk in row_chunks),
        in_specs=[VMEM] * (2 + 2 * count),
        out_specs=(VMEM,) * (4 + count),
        scratch_shapes=[
            pltpu.VMEM((sources, capacity + 16, model), bf16),
            pltpu.VMEM((pad, 128), f32),
        ],
        compiler_params=params(60),
        cost_estimate=cost(6 * sources * capacity * model * hidden, 30 * 2**20),
        name="expert_step",
    )(weight_in, weight_out, *row_chunks, *grad_chunks)


def expert_out_kernel(acted_all, out_ref, *rest):
    chunks, held = rest[:-1], rest[-1]

    def one(source, carry):
        held[source] = dot_nn(acted_all[source], out_ref[0]).astype(bf16)
        return carry

    lax.fori_loop(0, held.shape[0], one, 0)
    at = 0
    for chunk in chunks:
        per = chunk.shape[0]
        chunk[...] = held[at : at + per]
        at += per


def expert_outputs(acted_all, weight_out, chunk_shapes):
    sources, capacity, hidden = acted_all.shape
    model = weight_out.shape[2]
    return pl.pallas_call(
        expert_out_kernel,
        out_shape=tuple(shape((per, capacity, model), bf16) for per in chunk_shapes),
        in_specs=[VMEM, VMEM],
        out_specs=(VMEM,) * len(chunk_shapes),
        scratch_shapes=[pltpu.VMEM((sources, capacity, model), bf16)],
        compiler_params=params(40),
        cost_estimate=cost(2 * sources * capacity * model * hidden, 10 * 2**20),
        name="expert_outputs",
    )(acted_all, weight_out)


def gather_rows(chunks, head, starts, place, info, capacity):
    tokens = place.shape[0]
    slot = lax.broadcasted_iota(jnp.int32, (tokens, capacity), 1)
    gate_one, gate_two = info[:, 0:1], info[:, 1:2]
    place_one, place_two = place[:, 0:1], place[:, 1:2]
    total, grad_one, grad_two = None, None, None

    def one(chunk, entry, expert):
        base = expert * capacity
        hit_one = slot == place_one - base
        hit_two = slot == place_two - base
        weights = jnp.where(hit_one, gate_one, jnp.where(hit_two, gate_two, 0.0)).astype(bf16)
        out = dot_nn(weights, chunk[entry, head:, :])
        if head == 0:
            return (out,)
        row = jnp.sum(chunk[entry, 0:16, 0:capacity].astype(f32), axis=0, keepdims=True)
        first = jnp.sum(jnp.where(hit_one, row, 0.0), axis=-1, keepdims=True)
        second = jnp.sum(jnp.where(hit_two, row, 0.0), axis=-1, keepdims=True)
        return out, first, second

    sums = None
    for index, chunk in enumerate(chunks):
        if chunk.shape[0] == 1:
            parts = one(chunk, 0, starts[index])
        else:

            def step(entry, carry, chunk=chunk, index=index):
                found = one(chunk, entry, starts[index] + entry)
                return tuple(a + b for a, b in zip(carry, found))

            zero = (jnp.zeros((tokens, chunk.shape[2]), f32),)
            if head:
                zero = zero + (jnp.zeros((tokens, 1), f32),) * 2
            parts = lax.fori_loop(0, chunk.shape[0], step, zero)
        sums = parts if sums is None else tuple(a + b for a, b in zip(sums, parts))
    return sums


def write_ring(scalars, joined, own, next_one, next_two, last_one, last_two, far_one, far_two):
    quarter = own.shape[0]
    eighth = quarter // 2
    rank = scalars[3]

    def rows_of(which):
        return aligned(lax.rem(rank + which, 4) * quarter, quarter)

    own[...] = joined[pl.ds(rows_of(0), quarter), :]
    for which, one, two in ((1, next_one, next_two), (3, last_one, last_two), (2, far_one, far_two)):
        start = rows_of(which)
        one[...] = joined[pl.ds(start, eighth), :].astype(bf16)
        two[...] = joined[pl.ds(aligned(start + eighth, eighth), eighth), :].astype(bf16)


def ring_shapes(rows, model):
    return (shape((rows // 4, model), f32),) + (shape((rows // 8, model), bf16),) * 6


def combine_grads_kernel(
    capacity, expert_count, chunk_count, scalars, starts, place_ref, info_ref, route_ref, router_ref, *rest
):
    chunks = rest[:chunk_count]
    logit_ref = rest[chunk_count]
    ring = rest[chunk_count + 1 : chunk_count + 8]
    joined = rest[chunk_count + 8]
    rows = place_ref.shape[0]
    step = 256
    lane = lax.broadcasted_iota(jnp.int32, (step, 128), 1)

    def token_step(index, carry):
        start = aligned(index * step, step)
        span = pl.ds(start, step)
        info = info_ref[span, :]
        total, first, second = gather_rows(
            chunks, 16, starts, place_ref[span, :], info, capacity
        )
        mix = first * info[:, 0:1] + second * info[:, 1:2]
        pair_total = info[:, 2:3]
        picked = jnp.where(
            lane == route_ref[span, 0:1] + 64,
            (first - mix) / pair_total,
            jnp.where(lane == route_ref[span, 1:2] + 64, (second - mix) / pair_total, 0.0),
        )
        probs = jnp.where((lane >= 64) & (lane < 64 + expert_count), info, 0.0)
        grads = probs * (picked - jnp.sum(probs * picked, axis=-1, keepdims=True))
        grads = grads.astype(bf16)
        logit_ref[span, :] = grads
        joined[span, :] = total + dot_nt(grads, router_ref[:, 128:256])
        return carry

    lax.fori_loop(0, rows // step, token_step, 0)
    write_ring(scalars, joined, *ring)


def combine_grads(scalars, starts, place, info, routes, router, chunks, capacity, expert_count):
    rows = place.shape[0]
    model = router.shape[0]
    return pl.pallas_call(
        functools.partial(combine_grads_kernel, capacity, expert_count, len(chunks)),
        out_shape=(shape((rows, 128), bf16),) + ring_shapes(rows, model),
        in_specs=[SMEM, SMEM] + [VMEM] * (4 + len(chunks)),
        out_specs=(VMEM,) * 8,
        scratch_shapes=[pltpu.VMEM((rows, model), f32)],
        compiler_params=params(56),
        cost_estimate=cost(2 * rows * model * 2304, 10 * 2**20),
        name="combine_grads",
    )(scalars, starts, place, info, routes, router, *chunks)


def combine_outs_kernel(capacity, chunk_count, scalars, starts, place_ref, info_ref, *rest):
    chunks = rest[:chunk_count]
    ring = rest[chunk_count : chunk_count + 7]
    joined = rest[chunk_count + 7]
    rows = place_ref.shape[0]
    step = 256

    def token_step(index, carry):
        span = pl.ds(aligned(index * step, step), step)
        (total,) = gather_rows(
            chunks, 0, starts, place_ref[span, :], info_ref[span, :], capacity
        )
        joined[span, :] = total
        return carry

    lax.fori_loop(0, rows // step, token_step, 0)
    write_ring(scalars, joined, *ring)


def combine_outs(scalars, starts, place, info, chunks, capacity):
    rows = place.shape[0]
    model = chunks[0].shape[2]
    return pl.pallas_call(
        functools.partial(combine_outs_kernel, capacity, len(chunks)),
        out_shape=ring_shapes(rows, model),
        in_specs=[SMEM, SMEM] + [VMEM] * (2 + len(chunks)),
        out_specs=(VMEM,) * 7,
        scratch_shapes=[pltpu.VMEM((rows, model), f32)],
        compiler_params=params(56),
        cost_estimate=cost(2 * rows * model * 2304, 10 * 2**20),
        name="combine_outs",
    )(scalars, starts, place, info, *chunks)


def received(own, next_one, next_two, last_one, last_two):
    eighth = next_one.shape[0]
    first = own[0:eighth, :] + next_one[...].astype(f32) + last_one[...].astype(f32)
    second = own[eighth:, :] + next_two[...].astype(f32) + last_two[...].astype(f32)
    return jnp.concatenate([first, second], axis=0)


def norm_back_kernel(gain_index, has_bypass_rows, scalars, value_ref, gain_ref, bypass_ref, *rest):
    grads = received(*rest[:5])
    full_ref, one_ref, two_ref, gain_grad = rest[5:]
    quarter = grads.shape[0]
    eighth = quarter // 2
    here = pl.ds(aligned(scalars[3] * quarter, quarter), quarter)
    values = (value_ref[here, :] if gain_index == 0 else value_ref[...]).astype(f32)
    bypass = (bypass_ref[here, :] if has_bypass_rows else bypass_ref[...]).astype(f32)
    scale = lax.rsqrt(jnp.mean(values * values, axis=-1, keepdims=True) + epsilon)
    normed = values * scale
    scaled = grads * gain_ref[gain_index : gain_index + 1, :]
    gain_grad[...] = jnp.broadcast_to(
        jnp.sum(grads * normed, axis=0, keepdims=True), gain_grad.shape
    )
    out = bypass + scale * (scaled - normed * jnp.mean(scaled * normed, axis=-1, keepdims=True))
    full_ref[...] = out
    one_ref[...] = out[0:eighth].astype(bf16)
    two_ref[...] = out[eighth:].astype(bf16)


def norm_back(gain_index, has_bypass_rows, scalars, values, gains, bypass, parts):
    quarter, model = parts[0].shape
    return pl.pallas_call(
        functools.partial(norm_back_kernel, gain_index, has_bypass_rows),
        out_shape=(
            shape((quarter, model), f32),
            shape((quarter // 2, model), bf16),
            shape((quarter // 2, model), bf16),
            shape((8, model), f32),
        ),
        in_specs=[SMEM] + [VMEM] * 8,
        out_specs=(VMEM,) * 4,
        compiler_params=params(40),
        cost_estimate=cost(quarter * model * 16, 6 * 2**20),
        name="norm_back",
    )(scalars, values, gains, bypass, *parts)


def finish_kernel(residual_ref, *rest):
    total = residual_ref[...] + received(*rest[:5])
    one_ref, two_ref = rest[5:]
    eighth = one_ref.shape[0]
    one_ref[...] = total[0:eighth].astype(bf16)
    two_ref[...] = total[eighth:].astype(bf16)


def finish(residual, parts):
    quarter, model = residual.shape
    return pl.pallas_call(
        finish_kernel,
        out_shape=(shape((quarter // 2, model), bf16),) * 2,
        in_specs=[VMEM] * 6,
        out_specs=(VMEM,) * 2,
        compiler_params=params(40),
        cost_estimate=cost(quarter * model * 4, 4 * 2**20),
        name="finish",
    )(residual, *parts)


def hidden_grad_kernel(scalars, dq_ref, weight_ref, own, from_one, from_two, dkv_ref, *rest):
    ring, joined = rest[:7], rest[7]
    half = own.shape[0] // 2
    for part in range(2):
        span = slice(part * half, (part + 1) * half)
        total = (
            own[span, :].astype(f32)
            + from_one[part][...].astype(f32)
            + from_two[part][...].astype(f32)
        ).astype(bf16)
        dkv_ref[span, :] = total
        joined[span, :] = dot_nt(dq_ref[span, :], weight_ref[:, 0:256]) + dot_nt(
            total, weight_ref[:, 256:640]
        )
    write_ring(scalars, joined, *ring)


def hidden_grad(scalars, dq, weights, own, from_one, from_two):
    rows = dq.shape[0]
    model = weights.shape[0]

    def kernel(scal, dq_ref, weight_ref, own_ref, a, b, c, d, *rest):
        hidden_grad_kernel(scal, dq_ref, weight_ref, own_ref, (a, b), (c, d), *rest)

    return pl.pallas_call(
        kernel,
        out_shape=(shape((rows, 384), bf16),) + ring_shapes(rows, model),
        in_specs=[SMEM] + [VMEM] * 7,
        out_specs=(VMEM,) * 8,
        scratch_shapes=[pltpu.VMEM((rows, model), f32)],
        compiler_params=params(40),
        cost_estimate=cost(2 * rows * model * 640, 8 * 2**20),
        name="hidden_grad",
    )(scalars, dq, weights, own, *from_one, *from_two)


def shift(value, amount):
    size = lax.axis_size("tensor")
    return lax.ppermute(value, "tensor", [(i, (i + amount) % size) for i in range(size)])


def cross(value, mask):
    size = lax.axis_size("context")
    return lax.ppermute(value, "context", [(i, i ^ mask) for i in range(size)])


def ring_gather(one, two):
    last_one, next_two = shift(one, 1), shift(two, -1)
    last_two, next_one = shift(two, 1), shift(one, -1)
    far_one, far_two = shift(last_one, 1), shift(next_two, -1)
    return (one, two, last_one, last_two, next_one, next_two, far_one, far_two)


def ring_ranks(rank):
    return [lax.rem(rank + step, 4) for step in (0, 3, 1, 2)]


def added(first, second):
    return (first.astype(f32) + second.astype(f32)).astype(bf16)


def ring_reduce(own, next_one, next_two, last_one, last_two, far_one, far_two):
    arrived_one, arrived_two = shift(far_one, 1), shift(far_two, -1)
    from_last_two, from_next_one = shift(next_two, 1), shift(last_one, -1)
    from_last_one = shift(added(next_one, arrived_one), 1)
    from_next_two = shift(added(last_two, arrived_two), -1)
    return (own, from_last_one, from_last_two, from_next_one, from_next_two)


def square_gather(one, two):
    beside_one, across_two = cross(one, 1), cross(two, 2)
    beside_two, across_one = cross(two, 1), cross(one, 2)
    far_one, far_two = cross(beside_one, 2), cross(across_two, 1)
    return (one, two, beside_one, beside_two, across_one, across_two, far_one, far_two)


def square_reduce(beside_one, beside_two, across_one, across_two, far_one, far_two):
    arrived_one, arrived_two = cross(far_one, 1), cross(far_two, 2)
    from_beside_one, from_across_two = cross(beside_one, 1), cross(across_two, 2)
    from_across_one = cross(added(across_one, arrived_one), 2)
    from_beside_two = cross(added(beside_two, arrived_two), 1)
    return (from_beside_one, from_beside_two), (from_across_one, from_across_two)


ALL_ROWS = ("dp", "context")


def exchange(chunks):
    count = lax.axis_size("dp") * lax.axis_size("context")
    if len(chunks) == 1:
        return [lax.all_to_all(chunks[0], ALL_ROWS, split_axis=0, concat_axis=0, tiled=True)]
    return [
        chunk if j == 0 else lax.ppermute(chunk, ALL_ROWS, [(d, d ^ j) for d in range(count)])
        for j, chunk in enumerate(chunks)
    ]


def gather_weights(block, here, small):
    count = lax.axis_size("dp") * lax.axis_size("context")
    size = block.shape[0]
    if not small:
        whole = lax.all_gather(block, ALL_ROWS, axis=0, tiled=True)
        return [whole], jnp.zeros((1,), jnp.int32)
    pieces = [
        block if j == 0 else lax.ppermute(block, ALL_ROWS, [(d, d ^ j) for d in range(count)])
        for j in range(count)
    ]
    return pieces, jnp.stack([(here ^ j) * size for j in range(count)])


def scatter_weights(whole, small):
    if not small:
        return lax.psum_scatter(whole, ALL_ROWS, scatter_dimension=0, tiled=True)
    side, context = lax.axis_index("dp"), lax.axis_index("context")
    halves = whole.reshape((2, whole.shape[0] // 2) + whole.shape[1:])
    mine = lax.dynamic_index_in_dim(halves, side, 0, keepdims=False)
    other = lax.dynamic_index_in_dim(halves, 1 - side, 0, keepdims=False)
    mine = mine + lax.ppermute(other, "dp", [(0, 1), (1, 0)])
    blocks = mine.reshape((4, mine.shape[0] // 4) + mine.shape[1:])
    total = lax.dynamic_index_in_dim(blocks, context, 0, keepdims=False)
    for mask in (1, 2, 3):
        part = lax.dynamic_index_in_dim(blocks, context ^ mask, 0, keepdims=False)
        total = total + cross(part, mask)
    return total


def on_device(
    tokens_in, query_weight, key_weight, value_weight, output_weight, bias_table, attention_gain,
    router_weight, expert_gain, expert_in, expert_out, routes, pair_order, seq_lengths, cotangent,
):
    rows, model = tokens_in.shape
    heads = bias_table.shape[1]
    width = query_weight.shape[1] // heads
    group_rows = rows * lax.axis_size("context")
    expert_count = router_weight.shape[1]
    capacity = (9 * rows + 4 * expert_count - 1) // (4 * expert_count)
    count = lax.axis_size("dp") * lax.axis_size("context")
    small = count == 8
    context, rank = lax.axis_index("context"), lax.axis_index("tensor")
    here = lax.axis_index("dp") * lax.axis_size("context") + context
    first_end = seq_lengths[0, 0]
    second_end = first_end + seq_lengths[0, 1]
    scalars = jnp.stack([context, first_end, second_end, rank]).astype(jnp.int32)
    chunk_shapes = [1] * count if small else [expert_count]
    starts = jnp.stack([here ^ j for j in range(count)]) if small else jnp.zeros((1,), jnp.int32)
    starts = starts.astype(jnp.int32)
    shard = query_weight.shape[0]
    first_block = jnp.concatenate(
        [
            query_weight,
            attention_gain[:, None],
            expert_gain[:, None],
            jnp.zeros((shard, 62), bf16),
            key_weight,
            value_weight[:, 2 * width :],
            value_weight[:, : 2 * width],
        ],
        axis=1,
    )
    second_block = jnp.concatenate(
        [output_weight.T, router_weight, jnp.zeros((shard, 64 - expert_count), bf16)], axis=1
    )
    first_pieces, first_offsets = gather_weights(first_block, here, small)
    buckets = jnp.asarray(bucket_tiles())
    bias_tiles = bias_of(bias_table, buckets)
    far_bias = bias_table[-1]
    order_row = (pair_order & 1) * rows + (pair_order >> 1)
    row_place, column_place = find_places(scalars, routes.T, order_row, expert_count, capacity)
    hidden_one, queries, kv_one, kv_two, weights, gains = project(
        first_offsets, tokens_in, first_pieces
    )
    kv_pieces = square_gather(kv_one, kv_two)
    second_pieces, second_offsets = gather_weights(second_block, here, small)
    output_own = assemble(second_offsets, second_pieces, bf16)
    output_parts = [output_own] + [shift(output_own, step) for step in (1, -1, 2)]
    cotangent_chunks = exchange(
        scatter_rows(starts, cotangent, row_place, chunk_shapes, capacity)
    )
    half = rows // 2
    kv_offsets = jnp.stack(
        [(context ^ mask) * rows + part * half for mask in range(4) for part in range(2)]
    )
    packed_one, packed_two, lse, keys_values = attention_forward(
        scalars, far_bias, kv_offsets, queries, bias_tiles, kv_pieces, group_rows, heads, width
    )
    attended = ring_gather(packed_one, packed_two)
    residual, hidden_two, info, *row_chunks = dispatch(
        scalars, starts, tokens_in, gains, routes, row_place, attended, output_parts, chunk_shapes,
        heads, width, capacity, expert_count,
    )
    row_chunks = exchange(row_chunks)
    rows_all, grads_all, acted_all, pre_all, *returns = expert_step(
        expert_in, expert_out, row_chunks, cotangent_chunks
    )
    returns = exchange(returns)
    grad_logits, *ring = combine_grads(
        scalars, starts, column_place, info, routes, output_own, returns, capacity, expert_count
    )
    grad_one, branch_one, branch_two, gain_two_grad = norm_back(
        1, True, scalars, residual, gains, cotangent, ring_reduce(*ring)
    )
    branch_pieces = ring_gather(branch_one, branch_two)
    eighth = rows // 8
    token_offsets = jnp.stack(
        [which * 2 * eighth + part * eighth for which in ring_ranks(rank) for part in range(2)]
    )
    dq, own, *sent, fold = attention_backward(
        scalars, far_bias, token_offsets, queries, keys_values, bias_tiles, lse,
        (packed_one, packed_two), output_own, branch_pieces, heads, width,
    )
    dkv, *ring = hidden_grad(scalars, dq, weights, own, *square_reduce(*sent))
    input_full, input_one, input_two, gain_one_grad = norm_back(
        0, False, scalars, tokens_in, gains, grad_one, ring_reduce(*ring)
    )
    input_grad = assemble(token_offsets, ring_gather(input_one, input_two), f32)
    out_chunks = exchange(expert_outputs(acted_all, expert_out, chunk_shapes))
    ring = combine_outs(scalars, starts, column_place, info, out_chunks, capacity)
    layer_one, layer_two = finish(residual, ring_reduce(*ring))
    layer_out = assemble(token_offsets, ring_gather(layer_one, layer_two), bf16)
    gate_rows = jnp.concatenate([chunk[:, 0:16, 0:capacity] for chunk in row_chunks], axis=0)
    gates = jnp.sum(gate_rows.astype(f32), axis=1).reshape(-1, 1)
    total_rows = gates.shape[0]
    acted_flat = acted_all.reshape(total_rows, -1)
    pre_flat = pre_all.reshape(total_rows, -1)
    expert_out_grad = dot_tn(
        (acted_flat.astype(f32) * gates).astype(bf16), grads_all.reshape(total_rows, -1)
    )[None]
    expert_in_grad = dot_tn(
        rows_all.reshape(total_rows, -1), (pre_flat.astype(f32) * gates).astype(bf16)
    )[None]
    grad_branch = assemble(token_offsets, branch_pieces, bf16)
    quarter = rows // 4
    attended_own = jnp.concatenate(
        [
            jnp.concatenate([packed_one[:, :192], packed_two[:, :192]], axis=0),
            jnp.concatenate(
                [
                    jnp.concatenate([packed_one[:, 256:], packed_one[:, 192:256]], axis=1),
                    jnp.concatenate([packed_two[:, 256:], packed_two[:, 192:256]], axis=1),
                ],
                axis=0,
            ),
        ],
        axis=0,
    )
    output_grad = scatter_weights(dot_tn(grad_branch, attended_own), small).T
    projected = jnp.concatenate([dot_tn(hidden_one, dq), dot_tn(hidden_one, dkv)], axis=1)
    projected = scatter_weights(projected, small)
    router_grad = dot_tn(hidden_two, grad_logits)[:, 64 : 64 + expert_count]
    vectors = jnp.concatenate([router_grad, gain_two_grad[0][:, None]], axis=1)
    vectors = lax.psum(vectors, ("dp", "context", "tensor"))
    vectors = lax.dynamic_slice_in_dim(vectors, here * shard, shard, 0)
    gain_one_grad = lax.psum(gain_one_grad[0], ("dp", "context", "tensor"))
    gain_one_grad = lax.dynamic_slice_in_dim(gain_one_grad, here * shard, shard, 0)
    bucket_row = jnp.asarray(bucket_tiles()[0, 0])
    bucket_hot = (bucket_row[None, :] == jnp.arange(bias_table.shape[0] - 1)[:, None]).astype(f32)
    near_grad = jnp.sum(bucket_hot[:, None, :] * fold[None, :heads, :], axis=-1)
    table_grad = jnp.concatenate([near_grad, -jnp.sum(near_grad, axis=0, keepdims=True)], axis=0)
    table_grad = lax.psum(table_grad, ALL_ROWS)
    return (
        layer_out,
        input_grad,
        projected[:, :192],
        projected[:, 256:448],
        jnp.concatenate([projected[:, 512:], projected[:, 448:512]], axis=1),
        output_grad,
        table_grad,
        gain_one_grad,
        vectors[:, :expert_count],
        vectors[:, expert_count],
        expert_in_grad,
        expert_out_grad,
    )


def solution(mesh):
    rows = P(("dp", "context"), None)
    return jax.shard_map(
        on_device,
        mesh=mesh,
        in_specs=(
            rows,
            P(("dp", "context"), "tensor"),
            P(("dp", "context"), "tensor"),
            P(("dp", "context"), "tensor"),
            P("tensor", ("dp", "context")),
            P(None, "tensor"),
            P(("dp", "context")),
            rows,
            P(("dp", "context")),
            P(("dp", "context"), None, "tensor"),
            P(("dp", "context"), "tensor", None),
            rows,
            rows,
            P("dp", None),
            rows,
        ),
        out_specs=(
            rows,
            rows,
            P(("dp", "context"), "tensor"),
            P(("dp", "context"), "tensor"),
            P(("dp", "context"), "tensor"),
            P("tensor", ("dp", "context")),
            P(None, "tensor"),
            P(("dp", "context")),
            rows,
            P(("dp", "context")),
            P(("dp", "context"), None, "tensor"),
            P(("dp", "context"), "tensor", None),
        ),
        check_vma=False,
    )
```

```python
import functools
import jax
import jax.numpy as jnp
import numpy as np
from jax import lax
from jax.experimental import pallas as pl
from jax.experimental.pallas import tpu as pltpu
from jax.sharding import PartitionSpec as P

bf16 = jnp.bfloat16
f32 = jnp.float32
epsilon = 1e-06
masked_value = -1e30
tile = 256
VMEM = pl.BlockSpec(memory_space=pltpu.VMEM)
SMEM = pl.BlockSpec(memory_space=pltpu.SMEM)


def dot_nn(a, b):
    return lax.dot_general(a, b, (((1,), (0,)), ((), ())), preferred_element_type=f32)


def dot_nt(a, b):
    return lax.dot_general(a, b, (((1,), (1,)), ((), ())), preferred_element_type=f32)


def dot_tn(a, b):
    return lax.dot_general(a, b, (((0,), (0,)), ((), ())), preferred_element_type=f32)


def start_of(position, first_end, second_end):
    return jnp.where(
        position >= second_end, second_end, jnp.where(position >= first_end, first_end, 0)
    )


def aligned(value, size):
    return pl.multiple_of(value, size)


def attention_forward_kernel(
    heads, width, scalars, far_bias, offsets, query_ref, bias_ref, *rest
):
    piece_count = len(rest) - 9
    pieces = rest[:piece_count]
    packed_one, packed_two, lse_ref, keys_values = rest[piece_count : piece_count + 4]
    values_t, best, running, side_one, side_two = rest[piece_count + 4 :]
    rows = query_ref.shape[0]
    context, first_end, second_end = scalars[0], scalars[1], scalars[2]
    for index, piece in enumerate(pieces):
        size = piece.shape[0]
        keys_values[pl.ds(aligned(offsets[index], 128), size), :] = piece[...]
    lane_q = lax.broadcasted_iota(jnp.int32, (tile, 256), 1)

    def transpose_values(index, carry):
        start = aligned(index * tile, tile)
        upper = keys_values[pl.ds(start, tile), 256:384].astype(f32).T.astype(bf16)
        lower = keys_values[pl.ds(start, tile), 128:256].astype(f32).T.astype(bf16)
        values_t[0, 0:width, pl.ds(start, tile)] = upper[0:width]
        values_t[1, 0:width, pl.ds(start, tile)] = upper[width:]
        values_t[2, 0:width, pl.ds(start, tile)] = lower[width:]
        for head in range(heads):
            values_t[head, width:, pl.ds(start, tile)] = jnp.ones((16, tile), bf16)
        return carry

    lax.fori_loop(0, (context + 1) * (rows // tile), transpose_values, 0)

    def query_tile(index, carry):
        local = aligned(index * tile, tile)
        first = aligned(context * rows + local, tile)
        positions = first + lax.broadcasted_iota(jnp.int32, (1, tile), 1)
        row_start = start_of(positions, first_end, second_end)
        start_first = start_of(first, first_end, second_end)
        start_last = start_of(first + tile - 1, first_end, second_end)
        queries = query_ref[pl.ds(local, tile), :]
        masked_queries = [
            jnp.where(lane_q // width == head, queries, jnp.zeros_like(queries))
            for head in range(heads)
        ]

        def absorb(key_start, size, bias_index, masked, first_time):
            keys = keys_values[pl.ds(key_start, size), 0:256]
            if masked:
                key_positions = key_start + lax.broadcasted_iota(jnp.int32, (size, tile), 0)
                seen = key_positions >= row_start
                if bias_index == 0:
                    seen = seen & (key_positions <= positions)
            for head in range(heads):
                scores = dot_nt(keys, masked_queries[head])
                shift = 0.0
                if bias_index is None:
                    shift = far_bias[head]
                else:
                    scores = scores + bias_ref[bias_index, head]
                if masked:
                    scores = jnp.where(seen, scores, masked_value)
                top = jnp.max(scores, axis=0, keepdims=True) + shift
                values = values_t[head, :, pl.ds(key_start, size)]
                if first_time:
                    weights = jnp.exp(scores - top).astype(bf16)
                    running[head] = dot_nn(values, weights)
                    best[head] = jnp.broadcast_to(top, (8, tile))
                else:
                    old = best[head, 0:1]
                    new = jnp.maximum(old, top)
                    weights = jnp.exp(scores - (new - shift)).astype(bf16)
                    running[head] = running[head] * jnp.exp(old - new) + dot_nn(values, weights)
                    best[head] = jnp.broadcast_to(new, (8, tile))

        absorb(first, tile, 0, True, True)

        @pl.when(first > 0)
        def _():
            absorb(aligned(first - tile, tile), tile, 1, True, False)

        far_rows = jnp.maximum(first - tile, 0)
        big = 2 * tile
        big_count = far_rows // big
        low = jnp.minimum(start_first // big, big_count)
        middle = jnp.clip((start_last + big - 1) // big, low, big_count)

        def masked_step(step, carry):
            absorb(aligned(step * big, big), big, None, True, False)
            return carry

        def plain_step(step, carry):
            absorb(aligned(step * big, big), big, None, False, False)
            return carry

        lax.fori_loop(low, middle, masked_step, 0)
        lax.fori_loop(middle, big_count, plain_step, 0)

        @pl.when(far_rows > big_count * big)
        def _():
            absorb(aligned(big_count * big, tile), tile, None, True, False)

        outs = []
        for head in range(heads):
            total = running[head, width : width + 1]
            outs.append(running[head, 0:width] / total)
            lse_ref[pl.ds(head, 1), pl.ds(local, tile)] = best[head, 0:1] + jnp.log(total)
        side_one[pl.ds(local, tile), :] = jnp.concatenate([outs[0], outs[1]], axis=0).T
        side_two[pl.ds(local, tile), :] = jnp.concatenate([outs[2], outs[2]], axis=0).T
        return carry

    lax.fori_loop(0, rows // tile, query_tile, 0)
    half, quarter = rows // 2, rows // 4
    lane = lax.broadcasted_iota(jnp.int32, (quarter, 128), 1)
    for part, packed in enumerate((packed_one, packed_two)):
        near = slice(part * quarter, (part + 1) * quarter)
        later = slice(half + part * quarter, half + (part + 1) * quarter)
        packed[:, 0:128] = side_one[near, :].astype(bf16)
        packed[:, 128:256] = jnp.where(
            lane < width, side_two[near, :], side_two[later, :]
        ).astype(bf16)
        packed[:, 256:384] = side_one[later, :].astype(bf16)


def attention_forward(scalars, far_bias, offsets, queries, bias_tiles, pieces, group_rows, heads, width):
    rows = queries.shape[0]
    return pl.pallas_call(
        functools.partial(attention_forward_kernel, heads, width),
        out_shape=(
            jax.ShapeDtypeStruct((rows // 4, 384), bf16),
            jax.ShapeDtypeStruct((rows // 4, 384), bf16),
            jax.ShapeDtypeStruct((8, rows), f32),
            jax.ShapeDtypeStruct((group_rows, 384), bf16),
        ),
        in_specs=[SMEM, SMEM, SMEM, VMEM, VMEM] + [VMEM] * len(pieces),
        out_specs=(VMEM,) * 4,
        scratch_shapes=[
            pltpu.VMEM((heads, width + 16, group_rows), bf16),
            pltpu.VMEM((heads, 8, tile), f32),
            pltpu.VMEM((heads, width + 16, tile), f32),
            pltpu.VMEM((rows, 128), f32),
            pltpu.VMEM((rows, 128), f32),
        ],
        compiler_params=pltpu.CompilerParams(vmem_limit_bytes=56 * 2**20),
        cost_estimate=pl.CostEstimate(
            flops=4 * rows * group_rows * 256 * heads,
            bytes_accessed=10 * 2**20,
            transcendentals=rows * group_rows * heads,
        ),
        name="attention_forward",
    )(scalars, far_bias, offsets, queries, bias_tiles, *pieces)


def attention_backward_kernel(
    heads, width, piece_count, scalars, far_bias, offsets,
    query_ref, keys_values, bias_ref, lse_ref, packed_one, packed_two, *rest
):
    pieces = rest[:piece_count]
    (
        dq_ref, own_ref, beside_one, beside_two, across_one, across_two, far_one, far_two, fold_ref
    ) = rest[piece_count : piece_count + 9]
    dout, masked_q, masked_o, keys_t, deltas, dq_t, dk, dv, dkv, band_ref = rest[
        piece_count + 9 :
    ]
    rows = query_ref.shape[0]
    half, quarter = rows // 2, rows // 4
    context, first_end, second_end = scalars[0], scalars[1], scalars[2]
    tiles_here = rows // tile
    for index, piece in enumerate(pieces):
        span = pl.ds(aligned(offsets[index], 128), piece.shape[0])
        dout[span, 0:128] = pltpu.roll(piece[:, 128:256].astype(f32), width, 1).astype(bf16)
        dout[span, 128:256] = piece[:, 0:128]
    head_row = lax.broadcasted_iota(jnp.int32, (16, 256), 0)
    head_lane = lax.broadcasted_iota(jnp.int32, (16, 256), 1) // width
    head_hot = (head_row == jnp.where(head_lane == 1, 2, head_lane - 2)).astype(bf16)
    for part in range(4):
        span = slice(part * quarter, (part + 1) * quarter)
        packed = packed_one if part % 2 == 0 else packed_two
        lower = packed[:, 128:256].astype(f32)
        if part < 2:
            upper, lower = packed[:, 0:128], pltpu.roll(lower, width, 1)
        else:
            upper = packed[:, 256:384]
        product = dout[span, :].astype(f32) * jnp.concatenate([lower, upper.astype(f32)], axis=1)
        high = product.astype(bf16)
        rest_part = (product - high.astype(f32)).astype(bf16)
        deltas[:, span] = dot_nt(head_hot, high) + dot_nt(head_hot, rest_part)
    lane = lax.broadcasted_iota(jnp.int32, (rows, 256), 1) // width
    for head in range(heads):
        masked_q[head] = jnp.where(lane == head, query_ref[...], jnp.zeros((rows, 256), bf16))
        slot = 1 if head == 2 else head + 2
        masked_o[head] = jnp.where(lane == slot, dout[...], jnp.zeros((rows, 256), bf16))

    def transpose_keys(index, carry):
        start = aligned(index * tile, tile)
        lower = keys_values[pl.ds(start, tile), 0:128].astype(f32).T.astype(bf16)
        upper = keys_values[pl.ds(start, tile), 128:256].astype(f32).T.astype(bf16)
        keys_t[0, :, pl.ds(start, tile)] = lower[0:width]
        keys_t[1, :, pl.ds(start, tile)] = lower[width:]
        keys_t[2, :, pl.ds(start, tile)] = upper[0:width]
        return carry

    lax.fori_loop(0, (context + 1) * tiles_here, transpose_keys, 0)
    dq_t[...] = jnp.zeros_like(dq_t)
    dkv[...] = jnp.zeros_like(dkv)
    band_ref[...] = jnp.zeros_like(band_ref)
    first = context * rows
    all_positions = first + lax.broadcasted_iota(jnp.int32, (1, rows), 1)
    all_starts = start_of(all_positions, first_end, second_end)
    start_first = start_of(first, first_end, second_end)
    start_last = start_of(first + rows - 1, first_end, second_end)

    def block(key_start, query_start, size, bias_index, masked, near):
        keys = keys_values[pl.ds(key_start, tile), 0:256]
        values = keys_values[pl.ds(key_start, tile), 128:384]
        key_sum, value_sum = None, None
        if masked:
            key_positions = key_start + lax.broadcasted_iota(jnp.int32, (tile, size), 0)
            if near:
                positions = (
                    first + query_start + lax.broadcasted_iota(jnp.int32, (1, size), 1)
                )
                seen = (key_positions >= start_of(positions, first_end, second_end)) & (
                    key_positions <= positions
                )
            else:
                seen = key_positions >= all_starts
        span = pl.ds(query_start, size)
        for head in range(heads):
            queries = masked_q[head, span, :]
            grads = masked_o[head, span, :]
            scores = dot_nt(keys, queries)
            lse = lse_ref[pl.ds(head, 1), span]
            if near:
                scores = scores + bias_ref[bias_index, head]
            else:
                lse = lse - far_bias[head]
            probs = jnp.exp(scores - lse)
            if masked:
                probs = jnp.where(seen, probs, 0.0)
            grad_probs = dot_nt(values, grads)
            grad_scores = probs * (grad_probs - deltas[pl.ds(head, 1), span])
            if near:

                @pl.when(bias_index < 2)
                def _():
                    band_ref[bias_index, head] += grad_scores

            low_scores = grad_scores.astype(bf16)
            value_part = dot_nn(probs.astype(bf16), grads)
            key_part = dot_nn(low_scores, queries)
            dq_t[head, :, span] += dot_nn(keys_t[head, :, pl.ds(key_start, tile)], low_scores)
            key_sum = key_part if key_sum is None else key_sum + key_part
            value_sum = value_part if value_sum is None else value_sum + value_part
        return key_sum, value_sum

    lane_tile = lax.broadcasted_iota(jnp.int32, (tile, 128), 1)

    def write(key_start, key_sum, value_sum):
        span = pl.ds(key_start, tile)
        dkv[span, 0:128] = key_sum[:, 0:128].astype(bf16)
        dkv[span, 128:256] = jnp.where(
            lane_tile < width, key_sum[:, 128:256], value_sum[:, 0:128]
        ).astype(bf16)
        dkv[span, 256:384] = value_sum[:, 128:256].astype(bf16)

    far_count = jnp.maximum(context * tiles_here - 1, 0)
    low = jnp.minimum(start_first // tile, far_count)
    middle = jnp.clip((start_last + tile - 1) // tile, low, far_count)

    def masked_step(index, carry):
        start = aligned(index * tile, tile)
        write(start, *block(start, 0, rows, None, True, False))
        return carry

    def plain_step(index, carry):
        start = aligned(index * tile, tile)
        write(start, *block(start, 0, rows, None, False, False))
        return carry

    lax.fori_loop(low, middle, masked_step, 0)
    lax.fori_loop(middle, far_count, plain_step, 0)

    def near_keys(index, carry):
        start = aligned(index * tile, tile)
        lag = index - context * tiles_here
        dk[...] = jnp.zeros_like(dk)
        dv[...] = jnp.zeros_like(dv)

        def near_queries(query, inner):
            bias_index = jnp.minimum(query - lag, 2)
            key_sum, value_sum = block(
                start, aligned(query * tile, tile), tile, bias_index, True, True
            )
            dk[...] += key_sum
            dv[...] += value_sum
            return inner

        lax.fori_loop(jnp.maximum(lag, 0), tiles_here, near_queries, 0)
        write(start, dk[...], dv[...])
        return carry

    lax.fori_loop(far_count, (context + 1) * tiles_here, near_keys, 0)

    def block_rows(which):
        return pl.ds(aligned(which * rows, rows), rows)

    own_ref[...] = dkv[block_rows(context), :]
    for which, first_half, second_half in (
        (1, beside_one, beside_two), (2, across_one, across_two), (3, far_one, far_two)
    ):
        start = (context ^ which) * rows
        first_half[...] = dkv[pl.ds(aligned(start, half), half), :]
        second_half[...] = dkv[pl.ds(aligned(start + half, half), half), :]
    key_index = lax.broadcasted_iota(jnp.int32, (tile, tile), 0)
    query_index = lax.broadcasted_iota(jnp.int32, (tile, tile), 1)
    fold_ref[...] = jnp.zeros_like(fold_ref)
    for head in range(heads):
        both = jnp.where(key_index > query_index, band_ref[1, head], band_ref[0, head])
        by_row = both[0:8]
        for first_row in range(8, tile, 8):
            by_row = by_row + pltpu.roll(both[first_row : first_row + 8], tile - first_row, 1)
        folded = by_row[0:1]
        for row in range(1, 8):
            folded = folded + pltpu.roll(by_row, tile - row, 1)[row : row + 1]
        fold_ref[head : head + 1, :] = folded
    upper = jnp.concatenate([dq_t[0], dq_t[1]], axis=0)
    lower = jnp.concatenate([dq_t[2], jnp.zeros((width, rows), f32)], axis=0)
    scale = width ** (-0.5)
    dq_ref[:, 0:128] = (upper.T * scale).astype(bf16)
    dq_ref[:, 128:256] = (lower.T * scale).astype(bf16)


def attention_backward(
    scalars, far_bias, offsets, queries, keys_values, bias_tiles, lse, packed, pieces, heads, width
):
    rows = queries.shape[0]
    half = rows // 2
    group_rows = keys_values.shape[0]
    shape = jax.ShapeDtypeStruct
    return pl.pallas_call(
        functools.partial(attention_backward_kernel, heads, width, len(pieces)),
        out_shape=(
            shape((rows, 256), bf16),
            shape((rows, 384), bf16),
        )
        + (shape((half, 384), bf16),) * 6
        + (shape((8, tile), f32),),
        in_specs=[SMEM, SMEM, SMEM] + [VMEM] * (6 + len(pieces)),
        out_specs=(VMEM,) * 9,
        scratch_shapes=[
            pltpu.VMEM((rows, 256), bf16),
            pltpu.VMEM((heads, rows, 256), bf16),
            pltpu.VMEM((heads, rows, 256), bf16),
            pltpu.VMEM((heads, width, group_rows), bf16),
            pltpu.VMEM((16, rows), f32),
            pltpu.VMEM((heads, width, rows), f32),
            pltpu.VMEM((tile, 256), f32),
            pltpu.VMEM((tile, 256), f32),
            pltpu.VMEM((group_rows, 384), bf16),
            pltpu.VMEM((2, heads, tile, tile), f32),
        ],
        compiler_params=pltpu.CompilerParams(vmem_limit_bytes=60 * 2**20),
        cost_estimate=pl.CostEstimate(
            flops=10 * rows * group_rows * 256 * heads,
            bytes_accessed=16 * 2**20,
            transcendentals=rows * group_rows * heads,
        ),
        name="attention_backward",
    )(scalars, far_bias, offsets, queries, keys_values, bias_tiles, lse, *packed, *pieces)


bucket_edges = np.array(
    [19, 21, 24, 27, 31, 35, 40, 46, 52, 59, 67, 77, 87, 99, 113], dtype=np.int32
)


def bucket_tiles():
    key = np.arange(tile)[None, :, None]
    query = np.arange(tile)[None, None, :]
    lag = np.arange(3)[:, None, None] * tile + query - key
    clipped = np.maximum(lag, 0)
    counted = (clipped[..., None] >= bucket_edges).sum(-1)
    return np.where(clipped < 16, clipped, 16 + counted).astype(np.int32)


def shape(dims, dtype):
    return jax.ShapeDtypeStruct(dims, dtype)


def params(mebibytes):
    return pltpu.CompilerParams(vmem_limit_bytes=mebibytes * 2**20)


def cost(flops, bytes_accessed):
    return pl.CostEstimate(flops=flops, bytes_accessed=bytes_accessed, transcendentals=0)


def gelu_constants():
    return 0.7978845608028654, 0.044715


def prepare_kernel(
    capacity, padded, scalars, table, route_ref, order_ref, rows_ref, columns_ref,
    bias_ref, ranks, hot_ref, tall,
):
    pair_count = order_ref.shape[1]
    rows = pair_count // 2
    expert_pad = hot_ref.shape[0]
    step = 256
    live_end = scalars[2] - scalars[0] * rows
    order = order_ref[...]
    index_row = lax.broadcasted_iota(jnp.int32, (pair_count, 128), 0)
    index_lane = lax.broadcasted_iota(jnp.int32, (pair_count, 128), 1)
    digits = jnp.where(
        index_lane == 0, index_row // 64, jnp.where(index_lane == 1, index_row % 64, 0)
    ).astype(f32).astype(bf16)

    def rank_step(index, carry):
        start = aligned(index * step, step)
        pair = start + lax.broadcasted_iota(jnp.int32, (step, pair_count), 0)
        hit = (pair == order).astype(f32).astype(bf16)
        found = dot_nn(hit, digits)
        position = found[:, 0:1] * 64.0 + found[:, 1:2]
        ranks[pl.ds(start, step), :] = jnp.broadcast_to(position, (step, 128))
        return carry

    lax.fori_loop(0, pair_count // step, rank_step, 0)
    rank_row = ranks[...].T[0:1, :]
    position = lax.broadcasted_iota(jnp.int32, (1, rows), 1)
    live = position < live_end
    expert_row = jnp.concatenate([route_ref[0:1, :], route_ref[1:2, :]], axis=1)
    live_row = jnp.concatenate([live, live], axis=1)
    expert_index = lax.broadcasted_iota(jnp.int32, (expert_pad, pair_count), 0)
    hot = ((expert_index == expert_row) & live_row).astype(f32)
    hot_ref[...] = hot.astype(bf16)

    def count_step(index, counts):
        start = aligned(index * step, step)
        earlier = (ranks[pl.ds(start, step), 0:1] < rank_row).astype(f32).astype(bf16)
        return counts + dot_nn(hot_ref[:, pl.ds(start, step)], earlier)

    counts = lax.fori_loop(
        0, pair_count // step, count_step, jnp.zeros((expert_pad, pair_count), f32)
    )
    slot = jnp.sum(counts * hot, axis=0, keepdims=True).astype(jnp.int32)
    place = jnp.where(live_row & (slot < capacity), expert_row * padded + slot, -1)
    rows_ref[...] = jnp.full_like(rows_ref, -1)
    rows_ref[0:1, :] = place[:, 0:rows]
    rows_ref[1:2, :] = place[:, rows:]
    tall[...] = jnp.full_like(tall, -1.0)
    tall[0:1, :] = place[:, 0:rows].astype(f32)
    tall[1:2, :] = place[:, rows:].astype(f32)
    columns_ref[...] = tall[...].T.astype(jnp.int32)
    key = lax.broadcasted_iota(jnp.int32, (8, tile), 0)
    query = lax.broadcasted_iota(jnp.int32, (8, tile), 1)
    heads = bias_ref.shape[1]
    for head in range(heads):
        bias_ref[2, head] = jnp.full((tile, tile), table[31, head], f32)

    def bias_step(index, carry):
        start = aligned(index * 8, 8)
        for band in range(2):
            lag = band * tile + query - key - start
            found = [jnp.full((8, tile), table[0, head], f32) for head in range(heads)]
            for bucket, edge in enumerate(list(range(1, 17)) + list(bucket_edges), start=1):
                beyond = lag >= int(edge)
                found = [
                    jnp.where(beyond, table[bucket, head], found[head]) for head in range(heads)
                ]
            for head in range(heads):
                bias_ref[band, head, pl.ds(start, 8), :] = found[head]
        return carry

    lax.fori_loop(0, tile // 8, bias_step, 0)


def prepare(scalars, table, route_rows, order_row, expert_count, capacity, padded):
    rows = route_rows.shape[1]
    heads = table.shape[1]
    expert_pad = max(16, expert_count)
    return pl.pallas_call(
        functools.partial(prepare_kernel, capacity, padded),
        out_shape=(
            shape((8, rows), jnp.int32),
            shape((rows, 128), jnp.int32),
            shape((3, heads, tile, tile), f32),
        ),
        in_specs=[SMEM, SMEM, VMEM, VMEM],
        out_specs=(VMEM,) * 3,
        scratch_shapes=[
            pltpu.VMEM((2 * rows, 128), f32),
            pltpu.VMEM((expert_pad, 2 * rows), bf16),
            pltpu.VMEM((128, rows), f32),
        ],
        compiler_params=params(40),
        cost_estimate=cost(10 * 10**9, 3 * 2**20),
        name="prepare",
    )(scalars, table, route_rows, order_row)


def project_kernel(piece_count, offsets, token_ref, *rest):
    pieces = rest[:piece_count]
    hidden_ref, query_ref, kv_one, kv_two, weight_ref, gain_ref = rest[piece_count:]
    for index, piece in enumerate(pieces):
        weight_ref[pl.ds(aligned(offsets[index], 16), piece.shape[0]), :] = piece[...]
    rows = token_ref.shape[0]
    half = rows // 2
    gains = weight_ref[:, 128:256].astype(f32).T
    gain_ref[0:1, :] = gains[64:65, :]
    gain_ref[1:2, :] = gains[65:66, :]
    step = 256
    lane = lax.broadcasted_iota(jnp.int32, (step, 256), 1)
    for start in range(0, rows, step):
        inputs = token_ref[start : start + step, :].astype(f32)
        scale = lax.rsqrt(jnp.mean(inputs * inputs, axis=-1, keepdims=True) + epsilon)
        hidden = (inputs * scale * gain_ref[0:1, :]).astype(bf16)
        hidden_ref[start : start + step, :] = hidden
        queries = dot_nn(hidden, weight_ref[:, 0:256]).astype(bf16)
        query_ref[start : start + step, :] = jnp.where(
            lane < 192, queries * bf16(0.125), jnp.zeros_like(queries)
        )
        target, base = (kv_one, 0) if start < half else (kv_two, half)
        target[start - base : start - base + step, :] = dot_nn(
            hidden, weight_ref[:, 256:640]
        ).astype(bf16)


def project(offsets, tokens, pieces):
    rows, model = tokens.shape
    return pl.pallas_call(
        functools.partial(project_kernel, len(pieces)),
        out_shape=(
            shape((rows, model), bf16),
            shape((rows, 256), bf16),
            shape((rows // 2, 384), bf16),
            shape((rows // 2, 384), bf16),
            shape((model, 640), bf16),
            shape((8, model), f32),
        ),
        in_specs=[SMEM, VMEM] + [VMEM] * len(pieces),
        out_specs=(VMEM,) * 6,
        compiler_params=params(40),
        cost_estimate=cost(2 * rows * model * 640, 6 * 2**20),
        name="project",
    )(offsets, tokens, *pieces)


def assemble_kernel(piece_count, offsets, *rest):
    pieces = rest[:piece_count]
    out_ref = rest[piece_count]
    for index, piece in enumerate(pieces):
        size = piece.shape[0]
        out_ref[pl.ds(aligned(offsets[index], 16), size), :] = piece[...].astype(out_ref.dtype)


def assemble(offsets, pieces, dtype):
    total = sum(piece.shape[0] for piece in pieces)
    width = pieces[0].shape[1]
    return pl.pallas_call(
        functools.partial(assemble_kernel, len(pieces)),
        out_shape=shape((total, width), dtype),
        in_specs=[SMEM] + [VMEM] * len(pieces),
        out_specs=VMEM,
        compiler_params=params(40),
        cost_estimate=cost(0, 6 * total * width),
        name="assemble",
    )(offsets, *pieces)


def dispatch_kernel(
    heads, width, expert_count, padded, piece_count, scalars, offsets,
    token_ref, gain_ref, route_ref, row_place, *rest
):
    attended = rest[0:8]
    pieces = rest[8 : 8 + piece_count]
    rest = rest[8 + piece_count :]
    residual_ref, hidden_ref, info_ref, output_own, output_all, sent = rest[0:6]
    packed, joined, weights, column = rest[6:]
    for index, piece in enumerate(pieces):
        weights[:, pl.ds(aligned(offsets[index], 16), piece.shape[1]), :] = piece[...]
    output_own[...] = weights[0]
    lane_weight = lax.broadcasted_iota(jnp.int32, (weights.shape[1], 128), 1)
    for source in range(4):
        output_all[source, :, 0:128] = weights[source, :, 0:128]
        output_all[source, :, 128:256] = jnp.where(
            lane_weight < width, weights[source, :, 128:256], jnp.zeros_like(lane_weight, bf16)
        )
    rows, model = token_ref.shape
    quarter = rows // 4
    lane_low = lax.broadcasted_iota(jnp.int32, (quarter, 128), 1)
    for source in range(4):
        for part in range(2):
            piece = attended[2 * source + part]
            span = slice(part * quarter, (part + 1) * quarter)
            middle = piece[:, 128:256].astype(f32)
            packed[source, span, 0:128] = piece[:, 0:128]
            packed[source, span, 128:256] = jnp.where(lane_low < width, middle, 0.0).astype(bf16)
            span = slice((part + 2) * quarter, (part + 3) * quarter)
            packed[source, span, 0:128] = piece[:, 256:384]
            packed[source, span, 128:256] = jnp.where(
                lane_low < width, pltpu.roll(middle, 64, 1), 0.0
            ).astype(bf16)
    step = 256
    lane = lax.broadcasted_iota(jnp.int32, (step, 128), 1)
    valid = (lane >= 64) & (lane < 64 + expert_count)

    def token_step(index, carry):
        start = aligned(index * step, step)
        span = pl.ds(start, step)
        residual = token_ref[span, :].astype(f32)
        for source in range(4):
            residual = residual + dot_nt(packed[source, span, :], weights[source])
        joined[span, :] = residual
        scale = lax.rsqrt(jnp.mean(residual * residual, axis=-1, keepdims=True) + epsilon)
        hidden = (residual * scale * gain_ref[1:2, :]).astype(bf16)
        hidden_ref[span, :] = hidden
        logits = dot_nn(hidden, weights[0, :, 128:256])
        logits = jnp.where(valid, logits, masked_value)
        powers = jnp.where(valid, jnp.exp(logits - jnp.max(logits, axis=-1, keepdims=True)), 0.0)
        probs = powers / jnp.sum(powers, axis=-1, keepdims=True)
        first = jnp.sum(
            jnp.where(lane == route_ref[span, 0:1] + 64, probs, 0.0), axis=-1, keepdims=True
        )
        second = jnp.sum(
            jnp.where(lane == route_ref[span, 1:2] + 64, probs, 0.0), axis=-1, keepdims=True
        )
        total = first + second
        info_ref[span, :] = jnp.where(
            lane == 0,
            first / total,
            jnp.where(lane == 1, second / total, jnp.where(lane == 2, total, probs)),
        )
        return carry

    lax.fori_loop(0, rows // step, token_step, 0)
    residual_ref[...] = joined[pl.ds(aligned(scalars[3] * quarter, quarter), quarter), :]
    gates = info_ref[...].T
    gate_one, gate_two = gates[0:1, :], gates[1:2, :]
    place_one, place_two = row_place[0:1, :], row_place[1:2, :]
    column[...] = jnp.zeros_like(column)

    def expert_rows(index, carry):
        start = aligned(index * padded, 16)
        slot = start + lax.broadcasted_iota(jnp.int32, (padded, rows), 0)
        hit_one, hit_two = slot == place_one, slot == place_two
        picked = jnp.where(hit_one | hit_two, 1.0, 0.0).astype(bf16)
        sent[pl.ds(start, padded), :] = dot_nn(picked, hidden_ref[...]).astype(bf16)
        gate = jnp.where(hit_one, gate_one, 0.0) + jnp.where(hit_two, gate_two, 0.0)
        write_digits(sent, column, start, padded, jnp.sum(gate, axis=-1, keepdims=True))
        return carry

    lax.fori_loop(0, expert_count, expert_rows, 0)


def write_digits(rows_ref, column, start, padded, values):
    column[0:padded, :] = jnp.broadcast_to(values, (padded, 128))
    row = column[...].T[0:1, :]
    high = row.astype(bf16).astype(f32)
    middle = (row - high).astype(bf16).astype(f32)
    low = row - high - middle
    size = row.shape[1]
    index = lax.broadcasted_iota(jnp.int32, (16, size), 0)
    block = jnp.where(
        index == 0, high, jnp.where(index == 1, middle, jnp.where(index == 2, low, 0.0))
    )
    span = pl.ds(aligned(start + padded - 16, 16), 16)
    rows_ref[span, 0:size] = block.astype(bf16)
    rows_ref[span, size:] = jnp.zeros((16, rows_ref.shape[1] - size), bf16)


def read_digits(rows_ref, start, padded):
    wide = (padded + 127) // 128 * 128
    span = pl.ds(aligned(start + padded - 16, 16), 16)
    return jnp.sum(rows_ref[span, 0:wide].astype(f32), axis=0, keepdims=True)


def dispatch(
    scalars, offsets, tokens, gains, routes, row_place, attended, pieces,
    heads, width, expert_count, padded
):
    rows, model = tokens.shape
    slots = expert_count * padded
    wide = (padded + 127) // 128 * 128
    return pl.pallas_call(
        functools.partial(dispatch_kernel, heads, width, expert_count, padded, len(pieces)),
        out_shape=(
            shape((rows // 4, model), f32),
            shape((rows, model), bf16),
            shape((rows, 128), f32),
            shape((model, 256), bf16),
            shape((4, model, 256), bf16),
            shape((slots, model), bf16),
        ),
        in_specs=[SMEM, SMEM] + [VMEM] * (12 + len(pieces)),
        out_specs=(VMEM,) * 6,
        scratch_shapes=[
            pltpu.VMEM((4, rows, 256), bf16),
            pltpu.VMEM((rows, model), f32),
            pltpu.VMEM((4, model, 256), bf16),
            pltpu.VMEM((wide, 128), f32),
        ],
        compiler_params=params(56),
        cost_estimate=cost(2 * rows * model * (1024 + slots), 16 * 2**20),
        name="dispatch",
    )(scalars, offsets, tokens, gains, routes, row_place, *attended, *pieces)


def scatter_kernel(value_ref, row_place, sent):
    rows = value_ref.shape[0]
    place_one, place_two = row_place[0:1, :], row_place[1:2, :]
    fill = 128

    def slot_step(index, carry):
        start = aligned(index * fill, fill)
        slot = start + lax.broadcasted_iota(jnp.int32, (fill, rows), 0)
        picked = jnp.where((slot == place_one) | (slot == place_two), 1.0, 0.0).astype(bf16)
        sent[pl.ds(start, fill), :] = dot_nn(picked, value_ref[...]).astype(bf16)
        return carry

    lax.fori_loop(0, sent.shape[0] // fill, slot_step, 0)


def scatter_rows(values, row_place, slots):
    rows, model = values.shape
    return pl.pallas_call(
        scatter_kernel,
        out_shape=shape((slots, model), bf16),
        in_specs=[VMEM, VMEM],
        out_specs=VMEM,
        compiler_params=params(40),
        cost_estimate=cost(2 * rows * model * slots, 6 * 2**20),
        name="scatter_rows",
    )(values, row_place)


def expert_kernel(padded, in_ref, out_ref, rows_ref, grads_ref, acted_ref, pre_ref, gate_ref, back_ref, held, column):
    model = rows_ref.shape[1]
    hidden = in_ref.shape[2]
    root, cubic = gelu_constants()
    wide = column.shape[0]
    column[...] = jnp.zeros_like(column)

    def one(index, carry):
        start = aligned(index * padded, 16)
        span = pl.ds(start, padded)
        gate_part = None
        for first in range(0, hidden, 256):
            part = slice(first, first + 256)
            pre = dot_nn(rows_ref[span, :], in_ref[0, :, part])
            grad_acted = dot_nt(grads_ref[span, :], out_ref[0, part, :])
            square = pre * pre
            bent = jnp.tanh(root * pre * (1.0 + cubic * square))
            acted = (0.5 * pre * (1.0 + bent)).astype(bf16)
            slope = 0.5 * (1.0 + bent) + 0.5 * pre * (1.0 - bent * bent) * root * (
                1.0 + 3.0 * cubic * square
            )
            acted_ref[span, part] = acted
            product = grad_acted * acted.astype(f32)
            folded = product[:, 0:128] + product[:, 128:256]
            gate_part = folded if gate_part is None else gate_part + folded
            held[:, part] = (grad_acted * slope).astype(bf16)
        pre_ref[span, :] = held[...]
        back_ref[span, :] = dot_nt(held[...], in_ref[0]).astype(bf16)
        write_digits(back_ref, column, start, padded, jnp.sum(gate_part, axis=-1, keepdims=True))
        gates = jnp.broadcast_to(read_digits(rows_ref, start, padded), (128, wide))
        gate_ref[span, :] = gates.T[0:padded, :]
        return carry

    lax.fori_loop(0, rows_ref.shape[0] // padded, one, 0)


def expert_step(weight_in, weight_out, rows_in, grads_in, padded):
    slots, model = rows_in.shape
    hidden = weight_in.shape[2]
    wide = (padded + 127) // 128 * 128
    return pl.pallas_call(
        functools.partial(expert_kernel, padded),
        out_shape=(
            shape((slots, hidden), bf16),
            shape((slots, hidden), bf16),
            shape((slots, 128), f32),
            shape((slots, model), bf16),
        ),
        in_specs=[VMEM] * 4,
        out_specs=(VMEM,) * 4,
        scratch_shapes=[pltpu.VMEM((padded, hidden), bf16), pltpu.VMEM((wide, 128), f32)],
        compiler_params=params(60),
        cost_estimate=cost(6 * slots * model * hidden, 24 * 2**20),
        name="expert_step",
    )(weight_in, weight_out, rows_in, grads_in)


def weights_of(place, info, slots):
    slot = lax.broadcasted_iota(jnp.int32, (place.shape[0], slots), 1)
    hit_one, hit_two = slot == place[:, 0:1], slot == place[:, 1:2]
    weights = jnp.where(hit_one, info[:, 0:1], jnp.where(hit_two, info[:, 1:2], 0.0))
    return hit_one, hit_two, weights.astype(bf16)


def write_ring(scalars, joined, own, next_one, next_two, last_one, last_two, far_one, far_two):
    quarter = own.shape[0]
    eighth = quarter // 2
    rank = scalars[3]

    def rows_of(which):
        return aligned(lax.rem(rank + which, 4) * quarter, quarter)

    own[...] = joined[pl.ds(rows_of(0), quarter), :]
    for which, one, two in ((1, next_one, next_two), (3, last_one, last_two), (2, far_one, far_two)):
        start = rows_of(which)
        one[...] = joined[pl.ds(start, eighth), :].astype(bf16)
        two[...] = joined[pl.ds(aligned(start + eighth, eighth), eighth), :].astype(bf16)


def ring_shapes(rows, model):
    return (shape((rows // 4, model), f32),) + (shape((rows // 8, model), bf16),) * 6


def combine_grads_kernel(
    expert_count, padded, scalars, place_ref, info_ref, route_ref, router_ref, back_ref,
    logit_ref, *rest
):
    ring, joined, digits = rest[:7], rest[7], rest[8]
    rows = place_ref.shape[0]
    slots = back_ref.shape[0]
    wide = (padded + 127) // 128 * 128
    lane_digit = lax.broadcasted_iota(jnp.int32, (padded, 128), 1)

    def column_step(expert, carry):
        start = aligned(expert * padded, 16)
        row = jnp.broadcast_to(read_digits(back_ref, start, padded), (128, wide))
        column = row.T[0:padded, :]
        high = column.astype(bf16).astype(f32)
        middle = (column - high).astype(bf16).astype(f32)
        digits[pl.ds(start, padded), :] = jnp.where(
            lane_digit == 0,
            high,
            jnp.where(lane_digit == 1, middle, jnp.where(lane_digit == 2, column - high - middle, 0.0)),
        ).astype(bf16)
        return carry

    lax.fori_loop(0, expert_count, column_step, 0)
    step = 256
    lane = lax.broadcasted_iota(jnp.int32, (step, 128), 1)
    slot = lax.broadcasted_iota(jnp.int32, (step, slots), 1)

    def token_step(index, carry):
        span = pl.ds(aligned(index * step, step), step)
        info, place = info_ref[span, :], place_ref[span, :]
        hit_one, hit_two = slot == place[:, 0:1], slot == place[:, 1:2]
        weights = jnp.where(hit_one, info[:, 0:1], jnp.where(hit_two, info[:, 1:2], 0.0))
        total = dot_nn(weights.astype(bf16), back_ref[...])
        signs = jnp.where(hit_one, 1.0, jnp.where(hit_two, -1.0, 0.0)).astype(bf16)
        difference = jnp.sum(dot_nn(signs, digits[...]), axis=-1, keepdims=True) / info[:, 2:3]
        picked = jnp.where(
            lane == route_ref[span, 0:1] + 64,
            info[:, 1:2] * difference,
            jnp.where(lane == route_ref[span, 1:2] + 64, -info[:, 0:1] * difference, 0.0),
        )
        probs = jnp.where((lane >= 64) & (lane < 64 + expert_count), info, 0.0)
        grads = probs * (picked - jnp.sum(probs * picked, axis=-1, keepdims=True))
        grads = grads.astype(bf16)
        logit_ref[span, :] = grads
        joined[span, :] = total + dot_nt(grads, router_ref[:, 128:256])
        return carry

    lax.fori_loop(0, rows // step, token_step, 0)
    write_ring(scalars, joined, *ring)


def combine_grads(scalars, place, info, routes, router, back, expert_count, padded):
    rows = place.shape[0]
    model = router.shape[0]
    slots = back.shape[0]
    return pl.pallas_call(
        functools.partial(combine_grads_kernel, expert_count, padded),
        out_shape=(shape((rows, 128), bf16),) + ring_shapes(rows, model),
        in_specs=[SMEM] + [VMEM] * 5,
        out_specs=(VMEM,) * 8,
        scratch_shapes=[pltpu.VMEM((rows, model), f32), pltpu.VMEM((slots, 128), bf16)],
        compiler_params=params(56),
        cost_estimate=cost(2 * rows * model * slots, 8 * 2**20),
        name="combine_grads",
    )(scalars, place, info, routes, router, back)


def combine_outs_kernel(place_ref, info_ref, rows_ref, out_ref):
    step = 256

    def token_step(index, carry):
        span = pl.ds(aligned(index * step, step), step)
        weights = weights_of(place_ref[span, :], info_ref[span, :], rows_ref.shape[0])[2]
        out_ref[span, :] = dot_nn(weights, rows_ref[...]).astype(bf16)
        return carry

    lax.fori_loop(0, out_ref.shape[0] // step, token_step, 0)


def combine_outs(place, info, rows_in):
    rows = place.shape[0]
    slots, model = rows_in.shape
    return pl.pallas_call(
        combine_outs_kernel,
        out_shape=shape((rows, model), bf16),
        in_specs=[VMEM] * 3,
        out_specs=VMEM,
        compiler_params=params(56),
        cost_estimate=cost(2 * rows * model * slots, 8 * 2**20),
        name="combine_outs",
    )(place, info, rows_in)


def received(own, next_one, next_two, last_one, last_two):
    eighth = next_one.shape[0]
    first = own[0:eighth, :] + next_one[...].astype(f32) + last_one[...].astype(f32)
    second = own[eighth:, :] + next_two[...].astype(f32) + last_two[...].astype(f32)
    return jnp.concatenate([first, second], axis=0)


def norm_back_kernel(gain_index, has_bypass_rows, scalars, value_ref, gain_ref, bypass_ref, *rest):
    grads = received(*rest[:5])
    rest = rest[5:]
    if gain_index == 1:
        weight_ref, rest = rest[0], rest[1:]
    full_ref, one_ref, two_ref, gain_grad = rest[0:4]
    quarter = grads.shape[0]
    eighth = quarter // 2
    here = pl.ds(aligned(scalars[3] * quarter, quarter), quarter)
    values = (value_ref[here, :] if gain_index == 0 else value_ref[...]).astype(f32)
    bypass = (bypass_ref[here, :] if has_bypass_rows else bypass_ref[...]).astype(f32)
    scale = lax.rsqrt(jnp.mean(values * values, axis=-1, keepdims=True) + epsilon)
    normed = values * scale
    scaled = grads * gain_ref[gain_index : gain_index + 1, :]
    gain_grad[...] = jnp.broadcast_to(
        jnp.sum(grads * normed, axis=0, keepdims=True), gain_grad.shape
    )
    out = bypass + scale * (scaled - normed * jnp.mean(scaled * normed, axis=-1, keepdims=True))
    full_ref[...] = out
    low = out.astype(bf16)
    one_ref[...] = low[0:eighth]
    two_ref[...] = low[eighth:]
    for source, target in enumerate(rest[4:]):
        target[...] = dot_nn(low, weight_ref[source]).astype(bf16)


def norm_back(gain_index, has_bypass_rows, scalars, values, gains, bypass, parts, weights=None):
    quarter, model = parts[0].shape
    extra = () if weights is None else (weights,)
    return pl.pallas_call(
        functools.partial(norm_back_kernel, gain_index, has_bypass_rows),
        out_shape=(
            shape((quarter, model), f32),
            shape((quarter // 2, model), bf16),
            shape((quarter // 2, model), bf16),
            shape((8, model), f32),
        )
        + (shape((quarter, 256), bf16),) * (4 * len(extra)),
        in_specs=[SMEM] + [VMEM] * (8 + len(extra)),
        out_specs=(VMEM,) * (4 + 4 * len(extra)),
        compiler_params=params(40),
        cost_estimate=cost(quarter * model * 16, 6 * 2**20),
        name="norm_back",
    )(scalars, values, gains, bypass, *parts, *extra)


def finish_kernel(residual_ref, part_ref, out_ref):
    total = residual_ref[...]
    quarter = total.shape[0]
    for source in range(4):
        total = total + part_ref[source * quarter : (source + 1) * quarter, :].astype(f32)
    low = total.astype(bf16)
    for target in range(4):
        out_ref[target * quarter : (target + 1) * quarter, :] = low


def finish(residual, parts):
    quarter, model = residual.shape
    return pl.pallas_call(
        finish_kernel,
        out_shape=shape((4 * quarter, model), bf16),
        in_specs=[VMEM] * 2,
        out_specs=VMEM,
        compiler_params=params(40),
        cost_estimate=cost(quarter * model * 4, 4 * 2**20),
        name="finish",
    )(residual, parts)


def hidden_grad_kernel(scalars, dq_ref, weight_ref, own, from_one, from_two, dkv_ref, *rest):
    ring, joined = rest[:7], rest[7]
    half = own.shape[0] // 2
    for part in range(2):
        span = slice(part * half, (part + 1) * half)
        total = (
            own[span, :].astype(f32)
            + from_one[part][...].astype(f32)
            + from_two[part][...].astype(f32)
        ).astype(bf16)
        dkv_ref[span, :] = total
        joined[span, :] = dot_nt(dq_ref[span, :], weight_ref[:, 0:256]) + dot_nt(
            total, weight_ref[:, 256:640]
        )
    write_ring(scalars, joined, *ring)


def hidden_grad(scalars, dq, weights, own, from_one, from_two):
    rows = dq.shape[0]
    model = weights.shape[0]

    def kernel(scal, dq_ref, weight_ref, own_ref, a, b, c, d, *rest):
        hidden_grad_kernel(scal, dq_ref, weight_ref, own_ref, (a, b), (c, d), *rest)

    return pl.pallas_call(
        kernel,
        out_shape=(shape((rows, 384), bf16),) + ring_shapes(rows, model),
        in_specs=[SMEM] + [VMEM] * 7,
        out_specs=(VMEM,) * 8,
        scratch_shapes=[pltpu.VMEM((rows, model), f32)],
        compiler_params=params(40),
        cost_estimate=cost(2 * rows * model * 640, 8 * 2**20),
        name="hidden_grad",
    )(scalars, dq, weights, own, *from_one, *from_two)


def split_by_side(scalars, whole, mine, other):
    half = mine.shape[0]
    side = scalars[5]
    mine[...] = whole[pl.ds(aligned(side * half, 16), half), :]
    other[...] = whole[pl.ds(aligned((1 - side) * half, 16), half), :]


def output_grad_kernel(
    piece_count, width, scalars, offsets, hidden_ref, logit_ref, packed_one, packed_two, *rest
):
    pieces = rest[:piece_count]
    outs = rest[piece_count:-3]
    grads, attended, whole = rest[-3:]
    quarter = packed_one.shape[0]
    for index, piece in enumerate(pieces):
        grads[pl.ds(aligned(offsets[index], 16), piece.shape[0]), :] = piece[...]
    lane = lax.broadcasted_iota(jnp.int32, (quarter, 128), 1)
    for part, packed in enumerate((packed_one, packed_two)):
        span = slice(part * quarter, (part + 1) * quarter)
        middle = packed[:, 128:256].astype(f32)
        attended[span, 0:128] = packed[:, 0:128]
        attended[span, 128:256] = jnp.where(lane < width, middle, 0.0).astype(bf16)
        span = slice((part + 2) * quarter, (part + 3) * quarter)
        attended[span, 0:128] = packed[:, 256:384]
        attended[span, 128:256] = jnp.where(lane < width, pltpu.roll(middle, 64, 1), 0.0).astype(bf16)
    whole[...] = dot_tn(grads[...], attended[...])
    whole[:, 128:256] += dot_tn(hidden_ref[...], logit_ref[...])
    if len(outs) == 2:
        split_by_side(scalars, whole, *outs)
    else:
        outs[0][...] = whole[...]


def output_grads(scalars, offsets, hidden, grad_logits, packed, pieces, width, small):
    rows, model = hidden.shape
    outs = (shape((model // 2, 256), f32),) * 2 if small else (shape((model, 256), f32),)
    return pl.pallas_call(
        functools.partial(output_grad_kernel, len(pieces), width),
        out_shape=outs,
        in_specs=[SMEM, SMEM] + [VMEM] * (4 + len(pieces)),
        out_specs=(VMEM,) * len(outs),
        scratch_shapes=[
            pltpu.VMEM((rows, model), bf16),
            pltpu.VMEM((rows, 256), bf16),
            pltpu.VMEM((model, 256), f32),
        ],
        compiler_params=params(40),
        cost_estimate=cost(2 * rows * model * 384, 6 * 2**20),
        name="output_grads",
    )(scalars, offsets, hidden, grad_logits, *packed, *pieces)


def projection_grad_kernel(scalars, hidden_ref, dq_ref, dkv_ref, gain_ref, *rest):
    outs, whole = rest[:-1], rest[-1]
    hidden = hidden_ref[...]
    whole[:, 0:256] = dot_tn(hidden, dq_ref[...])
    whole[:, 256:640] = dot_tn(hidden, dkv_ref[...])
    lane = lax.broadcasted_iota(jnp.int32, (whole.shape[0], 128), 1)
    column = jnp.broadcast_to(gain_ref[0:1, :], (128, whole.shape[0])).T
    whole[:, 128:256] = jnp.where(lane < 64, whole[:, 128:256], column)
    if len(outs) == 2:
        split_by_side(scalars, whole, *outs)
    else:
        outs[0][...] = whole[...]


def projection_grads(scalars, hidden, dq, dkv, gain_grad, small):
    rows, model = hidden.shape
    outs = (shape((model // 2, 640), f32),) * 2 if small else (shape((model, 640), f32),)
    return pl.pallas_call(
        projection_grad_kernel,
        out_shape=outs,
        in_specs=[SMEM] + [VMEM] * 4,
        out_specs=(VMEM,) * len(outs),
        scratch_shapes=[pltpu.VMEM((model, 640), f32)],
        compiler_params=params(40),
        cost_estimate=cost(2 * rows * model * 640, 6 * 2**20),
        name="projection_grads",
    )(scalars, hidden, dq, dkv, gain_grad)


def share_kernel(scalars, mine, other, *outs):
    size = outs[0].shape[0]
    context = scalars[0]
    for mask, out in enumerate(outs):
        span = pl.ds(aligned((context ^ mask) * size, 16), size)
        out[...] = mine[span, :] + other[span, :]


def share(scalars, mine, other):
    rows, width = mine.shape
    return pl.pallas_call(
        share_kernel,
        out_shape=(shape((rows // 4, width), f32),) * 4,
        in_specs=[SMEM, VMEM, VMEM],
        out_specs=(VMEM,) * 4,
        compiler_params=params(40),
        cost_estimate=cost(rows * width, 12 * rows * width),
        name="share",
    )(scalars, mine, other)


def shift(value, amount):
    size = lax.axis_size("tensor")
    return lax.ppermute(value, "tensor", [(i, (i + amount) % size) for i in range(size)])


def cross(value, mask):
    size = lax.axis_size("context")
    return lax.ppermute(value, "context", [(i, i ^ mask) for i in range(size)])


def ring_gather(one, two):
    last_one, next_two = shift(one, 1), shift(two, -1)
    last_two, next_one = shift(two, 1), shift(one, -1)
    far_one, far_two = shift(last_one, 1), shift(next_two, -1)
    return (one, two, last_one, last_two, next_one, next_two, far_one, far_two)


def ring_ranks(rank):
    return [lax.rem(rank + step, 4) for step in (0, 3, 1, 2)]


def added(first, second):
    return (first.astype(f32) + second.astype(f32)).astype(bf16)


def ring_start(far_one, far_two):
    return shift(far_one, 1), shift(far_two, -1)


def ring_finish(next_one, next_two, last_one, last_two, arrived_one, arrived_two):
    from_last_two, from_next_one = shift(next_two, 1), shift(last_one, -1)
    from_last_one = shift(added(next_one, arrived_one), 1)
    from_next_two = shift(added(last_two, arrived_two), -1)
    return (from_last_one, from_last_two, from_next_one, from_next_two)


def ring_reduce(own, next_one, next_two, last_one, last_two, far_one, far_two):
    arrived = ring_start(far_one, far_two)
    return (own,) + ring_finish(next_one, next_two, last_one, last_two, *arrived)


def square_gather(one, two):
    beside_one, across_two = cross(one, 1), cross(two, 2)
    beside_two, across_one = cross(two, 1), cross(one, 2)
    far_one, far_two = cross(beside_one, 2), cross(across_two, 1)
    return (one, two, beside_one, beside_two, across_one, across_two, far_one, far_two)


def square_reduce(beside_one, beside_two, across_one, across_two, far_one, far_two):
    arrived_one, arrived_two = cross(far_one, 1), cross(far_two, 2)
    from_beside_one, from_across_two = cross(beside_one, 1), cross(across_two, 2)
    from_across_one = cross(added(across_one, arrived_one), 2)
    from_beside_two = cross(added(beside_two, arrived_two), 1)
    return (from_beside_one, from_beside_two), (from_across_one, from_across_two)


def doubled(value, axis, masks):
    for mask in masks:
        size = lax.axis_size(axis)
        value = value + lax.ppermute(value, axis, [(i, i ^ mask) for i in range(size)])
    return value


def sum_rows(value, small):
    if not small:
        return lax.psum(value, ALL_ROWS)
    return doubled(doubled(value, "dp", (1,)), "context", (1, 2))


ALL_ROWS = ("dp", "context")


def exchange(rows_out):
    return lax.all_to_all(rows_out, ALL_ROWS, split_axis=0, concat_axis=0, tiled=True)


def gather_weights(block, small, axis):
    size = block.shape[axis]
    if not small:
        whole = lax.all_gather(block, ALL_ROWS, axis=axis, tiled=True)
        return [whole], jnp.zeros((1,), jnp.int32)
    context, side = lax.axis_index("context"), lax.axis_index("dp")
    pieces = [block] + [cross(block, mask) for mask in (1, 2, 3)]
    pieces = pieces + [lax.ppermute(piece, "dp", [(0, 1), (1, 0)]) for piece in pieces]
    return pieces, jnp.stack(
        [((side ^ far) * 4 + (context ^ mask)) * size for far in range(2) for mask in range(4)]
    )


def scatter_weights(scalars, parts):
    if len(parts) == 1:
        return lax.psum_scatter(parts[0], ALL_ROWS, scatter_dimension=0, tiled=True)
    mine, other = parts
    blocks = share(scalars, mine, lax.ppermute(other, "dp", [(0, 1), (1, 0)]))
    return blocks[0] + cross(blocks[1], 1) + cross(blocks[2], 2) + cross(blocks[3], 3)


def on_device(
    tokens_in, query_weight, key_weight, value_weight, output_weight, bias_table, attention_gain,
    router_weight, expert_gain, expert_in, expert_out, routes, pair_order, seq_lengths, cotangent,
):
    rows, model = tokens_in.shape
    heads = bias_table.shape[1]
    width = query_weight.shape[1] // heads
    group_rows = rows * lax.axis_size("context")
    expert_count = router_weight.shape[1]
    capacity = (9 * rows + 4 * expert_count - 1) // (4 * expert_count)
    count = lax.axis_size("dp") * lax.axis_size("context")
    small = count == 8
    context, rank = lax.axis_index("context"), lax.axis_index("tensor")
    here = lax.axis_index("dp") * lax.axis_size("context") + context
    first_end = seq_lengths[0, 0]
    second_end = first_end + seq_lengths[0, 1]
    side = lax.axis_index("dp")
    scalars = jnp.stack([context, first_end, second_end, rank, here, side]).astype(jnp.int32)
    padded = (capacity + 15) // 16 * 16 + 16
    slots = expert_count * padded
    shard = query_weight.shape[0]
    first_block = jnp.concatenate(
        [
            query_weight,
            attention_gain[:, None],
            expert_gain[:, None],
            jnp.zeros((shard, 62), bf16),
            key_weight,
            value_weight[:, 2 * width :],
            value_weight[:, : 2 * width],
        ],
        axis=1,
    )
    second_block = jnp.concatenate(
        [output_weight.T, router_weight, jnp.zeros((shard, 64 - expert_count), bf16)], axis=1
    )
    tie = lax.optimization_barrier
    half, quarter, eighth = rows // 2, rows // 4, rows // 8
    kv_offsets = jnp.stack(
        [(context ^ mask) * rows + part * half for mask in range(4) for part in range(2)]
    )
    token_offsets = jnp.stack(
        [which * quarter + part * eighth for which in ring_ranks(rank) for part in range(2)]
    )
    far_bias = bias_table[-1]
    order_row = (pair_order & 1) * rows + (pair_order >> 1)
    first_pieces, first_offsets = gather_weights(first_block, small, 0)
    second_block = jnp.stack([second_block] + [shift(second_block, step) for step in (1, -1, 2)])
    hidden_one, queries, kv_one, kv_two, weights, gains = project(
        first_offsets, tokens_in, first_pieces
    )
    kv_pieces = square_gather(kv_one, kv_two)
    order_row, queries = tie((order_row, queries))
    row_place, column_place, bias_tiles = prepare(
        scalars, bias_table, routes.T, order_row, expert_count, capacity, padded
    )
    cotangent_rows = scatter_rows(cotangent, row_place, slots)
    queries, kv_pieces, second_block, cotangent_rows = tie(
        (queries, kv_pieces, second_block, cotangent_rows)
    )
    second_pieces, second_offsets = gather_weights(second_block, small, 1)
    cotangent_rows = exchange(cotangent_rows)
    packed_one, packed_two, lse, keys_values = attention_forward(
        scalars, far_bias, kv_offsets, queries, bias_tiles, kv_pieces, group_rows, heads, width
    )
    attended = ring_gather(packed_one, packed_two)
    residual, hidden_two, info, output_own, output_all, rows_out = dispatch(
        scalars, second_offsets, tokens_in, gains, routes, row_place, attended, second_pieces,
        heads, width, expert_count, padded,
    )
    rows_out, cotangent_rows = tie((rows_out, cotangent_rows))
    expert_rows = exchange(rows_out)
    acted, grad_pre, gates, back = expert_step(
        expert_in, expert_out, expert_rows, cotangent_rows, padded
    )
    back = exchange(back)
    gate_column = gates[:, 0:1]
    outs = dot_nn(acted, expert_out[0]).astype(bf16)
    expert_out_grad = dot_tn((acted.astype(f32) * gate_column).astype(bf16), cotangent_rows)
    expert_in_grad = dot_tn(expert_rows, (grad_pre.astype(f32) * gate_column).astype(bf16))
    back, outs, expert_out_grad, expert_in_grad = tie(
        (back, outs, expert_out_grad, expert_in_grad)
    )
    grad_logits, *ring = combine_grads(
        scalars, column_place, info, routes, output_own, back, expert_count, padded
    )
    ring, outs = ring_reduce(*ring), exchange(outs)
    ring, outs = tie((ring, outs))
    grad_one, branch_one, branch_two, gain_two_grad, *grad_heads = norm_back(
        1, True, scalars, residual, gains, cotangent, ring, output_all
    )
    head_pieces = (
        grad_heads[0], shift(grad_heads[2], 1), shift(grad_heads[1], -1), shift(grad_heads[3], 2)
    )
    mixed = combine_outs(column_place, info, outs)
    head_pieces, branch_one, branch_two, mixed = tie((head_pieces, branch_one, branch_two, mixed))
    mixed = lax.all_to_all(mixed, "tensor", split_axis=0, concat_axis=0, tiled=True)
    branch_pieces = ring_gather(branch_one, branch_two)
    dq, own, *sent, fold = attention_backward(
        scalars, far_bias, token_offsets[::2], queries, keys_values, bias_tiles, lse,
        (packed_one, packed_two), head_pieces, heads, width,
    )
    mixed, sent, branch_pieces = tie((mixed, sent, branch_pieces))
    from_square = square_reduce(*sent)
    layer_out = lax.all_to_all(
        finish(residual, mixed), "tensor", split_axis=0, concat_axis=0, tiled=True
    )
    outer_parts = output_grads(
        scalars, token_offsets, hidden_two, grad_logits, (packed_one, packed_two), branch_pieces,
        width, small,
    )
    dq, from_square, layer_out, outer_parts = tie((dq, from_square, layer_out, outer_parts))
    dkv, *ring = hidden_grad(scalars, dq, weights, own, *from_square)
    ring = ring_reduce(*ring)
    input_full, input_one, input_two, _ = norm_back(
        0, False, scalars, tokens_in, gains, grad_one, ring
    )
    input_pieces = ring_gather(input_one, input_two)
    input_grad = assemble(token_offsets, input_pieces, f32)
    dkv, input_one = tie((dkv, input_one))
    expert_out_grad, expert_in_grad = expert_out_grad[None], expert_in_grad[None]
    outer_grads = scatter_weights(scalars, outer_parts)
    output_grad = outer_grads[:, :192].T
    router_grad = doubled(outer_grads[:, 192 : 192 + expert_count], "tensor", (1, 2))
    projected = scatter_weights(
        scalars, projection_grads(scalars, hidden_one, dq, dkv, gain_two_grad, small)
    )
    query_grad, key_grad = projected[:, :192], projected[:, 256:448]
    value_grad = jnp.concatenate([projected[:, 512:], projected[:, 448:512]], axis=1)
    gain_one_grad = jnp.sum(
        query_weight.astype(f32) * query_grad
        + key_weight.astype(f32) * key_grad
        + value_weight.astype(f32) * value_grad,
        axis=1,
        keepdims=True,
    )
    gain_grads = doubled(
        jnp.concatenate([gain_one_grad, projected[:, 192:193]], axis=1), "tensor", (1, 2)
    )
    bucket_row = jnp.asarray(bucket_tiles()[0, 0])
    bucket_hot = (bucket_row[None, :] == jnp.arange(bias_table.shape[0] - 1)[:, None]).astype(f32)
    near_grad = jnp.sum(bucket_hot[:, None, :] * sum_rows(fold, small)[None, :heads, :], axis=-1)
    table_grad = jnp.concatenate([near_grad, -jnp.sum(near_grad, axis=0, keepdims=True)], axis=0)
    return (
        layer_out,
        input_grad,
        query_grad,
        key_grad,
        value_grad,
        output_grad,
        table_grad,
        gain_grads[:, 0] / attention_gain.astype(f32),
        router_grad,
        gain_grads[:, 1],
        expert_in_grad,
        expert_out_grad,
    )


def solution(mesh):
    rows = P(("dp", "context"), None)
    return jax.shard_map(
        on_device,
        mesh=mesh,
        in_specs=(
            rows,
            P(("dp", "context"), "tensor"),
            P(("dp", "context"), "tensor"),
            P(("dp", "context"), "tensor"),
            P("tensor", ("dp", "context")),
            P(None, "tensor"),
            P(("dp", "context")),
            rows,
            P(("dp", "context")),
            P(("dp", "context"), None, "tensor"),
            P(("dp", "context"), "tensor", None),
            rows,
            rows,
            P("dp", None),
            rows,
        ),
        out_specs=(
            rows,
            rows,
            P(("dp", "context"), "tensor"),
            P(("dp", "context"), "tensor"),
            P(("dp", "context"), "tensor"),
            P("tensor", ("dp", "context")),
            P(None, "tensor"),
            P(("dp", "context")),
            rows,
            P(("dp", "context")),
            P(("dp", "context"), None, "tensor"),
            P(("dp", "context"), "tensor", None),
        ),
        check_vma=False,
    )
```

```python
import functools
import jax
import jax.numpy as jnp
import numpy as np
from jax import lax
from jax.experimental import pallas as pl
from jax.experimental.pallas import tpu as pltpu
from jax.sharding import PartitionSpec as P

bf16 = jnp.bfloat16
f32 = jnp.float32
epsilon = 1e-06
masked_value = -1e30
tile = 256
VMEM = pl.BlockSpec(memory_space=pltpu.VMEM)
SMEM = pl.BlockSpec(memory_space=pltpu.SMEM)


def dot_nn(a, b):
    return lax.dot_general(a, b, (((1,), (0,)), ((), ())), preferred_element_type=f32)


def dot_nt(a, b):
    return lax.dot_general(a, b, (((1,), (1,)), ((), ())), preferred_element_type=f32)


def dot_tn(a, b):
    return lax.dot_general(a, b, (((0,), (0,)), ((), ())), preferred_element_type=f32)


def start_of(position, first_end, second_end):
    return jnp.where(
        position >= second_end, second_end, jnp.where(position >= first_end, first_end, 0)
    )


def aligned(value, size):
    return pl.multiple_of(value, size)


def transpose_values(source, source_start, values_t, start, width):
    span, target = pl.ds(source_start, tile), pl.ds(start, tile)
    upper = source[span, 256:384].astype(f32).T.astype(bf16)
    lower = source[span, 128:256].astype(f32).T.astype(bf16)
    for head, part in enumerate((upper[0:width], upper[width:], lower[width:])):
        values_t[head, 0:width, target] = part
        values_t[head, width:, target] = jnp.ones((16, tile), bf16)


def masked_heads(queries, heads, width):
    lane = lax.broadcasted_iota(jnp.int32, queries.shape, 1) // width
    return [jnp.where(lane == head, queries, jnp.zeros_like(queries)) for head in range(heads)]


def absorb(
    keys_values, values_t, bias_ref, far_bias, best, running, index, masked_queries, heads,
    key_start, size, key_first, positions, row_start, bias_index, masked, first_time,
):
    keys = keys_values[pl.ds(key_start, size), 0:256]
    if masked:
        key_positions = (
            key_first + key_start + lax.broadcasted_iota(jnp.int32, (size, tile), 0)
        )
        seen = key_positions >= row_start
        if bias_index == 0:
            seen = seen & (key_positions <= positions)
    for head in range(heads):
        scores = dot_nt(keys, masked_queries[head])
        shift_by = 0.0
        if bias_index is None:
            shift_by = far_bias[head]
        else:
            scores = scores + bias_ref[bias_index, head]
        if masked:
            scores = jnp.where(seen, scores, masked_value)
        top = jnp.max(scores, axis=0, keepdims=True) + shift_by
        values = values_t[head, :, pl.ds(key_start, size)]
        if first_time:
            weights = jnp.exp(scores - top).astype(bf16)
            running[index, head] = dot_nn(values, weights)
            best[index, head] = jnp.broadcast_to(top, (8, tile))
        else:
            old = best[index, head, 0:1]
            new = jnp.maximum(old, top)
            weights = jnp.exp(scores - (new - shift_by)).astype(bf16)
            running[index, head] = running[index, head] * jnp.exp(old - new) + dot_nn(
                values, weights
            )
            best[index, head] = jnp.broadcast_to(new, (8, tile))


def attention_near_kernel(
    heads, width, scalars, far_bias, query_ref, bias_ref, kv_one, kv_two, running, best,
    keys_values, values_t,
):
    rows = query_ref.shape[0]
    half = rows // 2
    context, first_end, second_end = scalars[0], scalars[1], scalars[2]
    keys_values[0:half, :] = kv_one[...]
    keys_values[half:, :] = kv_two[...]
    base = context * rows

    def values_step(index, carry):
        start = aligned(index * tile, tile)
        transpose_values(keys_values, start, values_t, start, width)
        return carry

    lax.fori_loop(0, rows // tile, values_step, 0)

    def query_tile(index, carry):
        local = aligned(index * tile, tile)
        positions = base + local + lax.broadcasted_iota(jnp.int32, (1, tile), 1)
        row_start = start_of(positions, first_end, second_end)
        masked_queries = masked_heads(query_ref[pl.ds(local, tile), :], heads, width)

        def take(key_start, bias_index, first_time):
            absorb(
                keys_values, values_t, bias_ref, far_bias, best, running, index,
                masked_queries, heads, key_start, tile, base, positions, row_start, bias_index,
                True, first_time,
            )

        take(local, 0, True)

        @pl.when(index > 0)
        def _():
            take(aligned(local - tile, tile), 1, False)

        def far_step(step, inner):
            take(aligned(step * tile, tile), None, False)
            return inner

        lax.fori_loop(0, jnp.maximum(index - 1, 0), far_step, 0)
        return carry

    lax.fori_loop(0, rows // tile, query_tile, 0)


def attention_near(scalars, far_bias, queries, bias_tiles, kv_one, kv_two, heads, width):
    rows = queries.shape[0]
    tiles = rows // tile
    return pl.pallas_call(
        functools.partial(attention_near_kernel, heads, width),
        out_shape=(
            jax.ShapeDtypeStruct((tiles, heads, width + 16, tile), f32),
            jax.ShapeDtypeStruct((tiles, heads, 8, tile), f32),
        ),
        in_specs=[SMEM, SMEM] + [VMEM] * 4,
        out_specs=(VMEM,) * 2,
        scratch_shapes=[
            pltpu.VMEM((rows, 384), bf16),
            pltpu.VMEM((heads, width + 16, rows), bf16),
        ],
        compiler_params=pltpu.CompilerParams(vmem_limit_bytes=40 * 2**20),
        cost_estimate=pl.CostEstimate(
            flops=2 * rows * rows * 256 * heads,
            bytes_accessed=4 * 2**20,
            transcendentals=rows * rows * heads // 2,
        ),
        name="attention_near",
    )(scalars, far_bias, queries, bias_tiles, kv_one, kv_two)


def attention_far_kernel(
    heads, width, part, piece_count, scalars, far_bias, offsets, query_ref, bias_ref,
    running_in, best_in, *rest
):
    pieces = rest[:piece_count]
    if part == 0:
        packed, lse_ref, keys_values, values_t, running, best, side_one, side_two = rest[
            piece_count:
        ]
    else:
        keys_values, values_t, packed, lse_ref, running, best, side_one, side_two = rest
    rows = query_ref.shape[0]
    half, quarter = rows // 2, rows // 4
    context, first_end, second_end = scalars[0], scalars[1], scalars[2]
    base = context * rows
    if part == 0:
        for index, piece in enumerate(pieces):
            size = piece.shape[0]
            keys_values[pl.ds(aligned(offsets[index], 128), size), :] = piece[...]

        def values_step(index, carry):
            start = aligned(index * tile, tile)
            transpose_values(keys_values, start, values_t, start, width)
            return carry

        lax.fori_loop(0, context * (rows // tile), values_step, 0)
    running[...] = running_in[2 * part : 2 * part + 2]
    best[...] = best_in[2 * part : 2 * part + 2]

    def query_tile(index, carry):
        local = aligned(part * half + index * tile, tile)
        first = base + local
        positions = first + lax.broadcasted_iota(jnp.int32, (1, tile), 1)
        row_start = start_of(positions, first_end, second_end)
        start_first = start_of(first, first_end, second_end)
        start_last = start_of(first + tile - 1, first_end, second_end)
        masked_queries = masked_heads(query_ref[pl.ds(local, tile), :], heads, width)

        def take(key_start, size, bias_index, masked):
            absorb(
                keys_values, values_t, bias_ref, far_bias, best, running, index,
                masked_queries, heads, key_start, size, 0, positions, row_start, bias_index,
                masked, False,
            )

        far_rows = base
        if part == 0:
            far_rows = jnp.where(index == 0, jnp.maximum(base - tile, 0), base)

            @pl.when((index == 0) & (context > 0))
            def _():
                take(aligned(base - tile, tile), tile, 1, True)

        big = 2 * tile
        big_count = far_rows // big
        low = jnp.minimum(start_first // big, big_count)
        middle = jnp.clip((start_last + big - 1) // big, low, big_count)

        def masked_step(step, inner):
            take(aligned(step * big, big), big, None, True)
            return inner

        def plain_step(step, inner):
            take(aligned(step * big, big), big, None, False)
            return inner

        lax.fori_loop(low, middle, masked_step, 0)
        lax.fori_loop(middle, big_count, plain_step, 0)
        if part == 0:

            @pl.when(far_rows > big_count * big)
            def _():
                take(aligned(big_count * big, tile), tile, None, True)

        outs = []
        for head in range(heads):
            total = running[index, head, width : width + 1]
            outs.append(running[index, head, 0:width] / total)
            lse_ref[pl.ds(head, 1), pl.ds(aligned(index * tile, tile), tile)] = best[
                index, head, 0:1
            ] + jnp.log(total)
        span = pl.ds(aligned(index * tile, tile), tile)
        side_one[span, :] = jnp.concatenate([outs[0], outs[1]], axis=0).T
        side_two[span, :] = jnp.concatenate([outs[2], outs[2]], axis=0).T
        return carry

    lax.fori_loop(0, half // tile, query_tile, 0)
    lane = lax.broadcasted_iota(jnp.int32, (quarter, 128), 1)
    packed[:, 0:128] = side_one[0:quarter, :].astype(bf16)
    packed[:, 128:256] = jnp.where(
        lane < width, side_two[0:quarter, :], side_two[quarter:, :]
    ).astype(bf16)
    packed[:, 256:384] = side_one[quarter:, :].astype(bf16)


def attention_far(
    part, scalars, far_bias, offsets, queries, bias_tiles, states, kv, group_rows, heads, width
):
    rows = queries.shape[0]
    half = rows // 2
    shape = jax.ShapeDtypeStruct
    made = (
        shape((group_rows, 384), bf16),
        shape((heads, width + 16, group_rows), bf16),
    )
    outs = (shape((rows // 4, 384), bf16), shape((8, half), f32)) + (made if part == 0 else ())
    return pl.pallas_call(
        functools.partial(attention_far_kernel, heads, width, part, len(kv) if part == 0 else 0),
        out_shape=outs,
        in_specs=[SMEM, SMEM, SMEM] + [VMEM] * (4 + len(kv)),
        out_specs=(VMEM,) * len(outs),
        scratch_shapes=[
            pltpu.VMEM((2, heads, width + 16, tile), f32),
            pltpu.VMEM((2, heads, 8, tile), f32),
            pltpu.VMEM((half, 128), f32),
            pltpu.VMEM((half, 128), f32),
        ],
        compiler_params=pltpu.CompilerParams(vmem_limit_bytes=60 * 2**20),
        cost_estimate=pl.CostEstimate(
            flops=2 * rows * group_rows * 256 * heads,
            bytes_accessed=8 * 2**20,
            transcendentals=rows * group_rows * heads // 2,
        ),
        name="attention_far",
    )(scalars, far_bias, offsets, queries, bias_tiles, *states, *kv)


def attention_backward_kernel(heads, width, masks, piece_count, scalars, far_bias, offsets, *rest):
    query_ref, keys_values, bias_ref, lse_one, lse_two = rest[0:5]
    rest = rest[5:]
    first_call, last_call = masks[0] == 3, masks[0] == 0
    if first_call:
        packed_one, packed_two = rest[0:2]
        pieces = rest[2 : 2 + piece_count]
        rest = rest[2 + piece_count :]
        dout, deltas, dq_t = rest[0:3]
        rest = rest[3:]
    else:
        dout, deltas, dq_in, fold_in = rest[0:4]
        dq_t = rest[4]
        rest = rest[5:]
    out_count = 1 if last_call else 2 * len(masks)
    outs, rest = rest[:out_count], rest[out_count:]
    if last_call:
        dq_ref, rest = rest[0], rest[1:]
    fold_ref, masked_q, masked_o, keys_t, dkv, band_ref = rest
    rows = query_ref.shape[0]
    half, quarter = rows // 2, rows // 4
    context, first_end, second_end = scalars[0], scalars[1], scalars[2]
    tiles_here = rows // tile
    if first_call:
        for index, piece in enumerate(pieces):
            span = pl.ds(aligned(offsets[index], 128), piece.shape[0])
            dout[span, 0:128] = pltpu.roll(piece[:, 128:256].astype(f32), width, 1).astype(bf16)
            dout[span, 128:256] = piece[:, 0:128]
        head_row = lax.broadcasted_iota(jnp.int32, (16, 256), 0)
        head_lane = lax.broadcasted_iota(jnp.int32, (16, 256), 1) // width
        head_hot = (head_row == jnp.where(head_lane == 1, 2, head_lane - 2)).astype(bf16)
        for part in range(4):
            span = slice(part * quarter, (part + 1) * quarter)
            packed = packed_one if part < 2 else packed_two
            lower = packed[:, 128:256].astype(f32)
            if part % 2 == 0:
                upper, lower = packed[:, 0:128], pltpu.roll(lower, width, 1)
            else:
                upper = packed[:, 256:384]
            product = dout[span, :].astype(f32) * jnp.concatenate(
                [lower, upper.astype(f32)], axis=1
            )
            high = product.astype(bf16)
            rest_part = (product - high.astype(f32)).astype(bf16)
            deltas[:, span] = dot_nt(head_hot, high) + dot_nt(head_hot, rest_part)
        dq_t[...] = jnp.zeros_like(dq_t)
        fold_ref[...] = jnp.zeros_like(fold_ref)
    else:
        dq_t[...] = dq_in[...]
        fold_ref[...] = fold_in[...]
    lane = lax.broadcasted_iota(jnp.int32, (rows, 256), 1) // width
    for head in range(heads):
        masked_q[head] = jnp.where(lane == head, query_ref[...], jnp.zeros((rows, 256), bf16))
        slot = 1 if head == 2 else head + 2
        masked_o[head] = jnp.where(lane == slot, dout[...], jnp.zeros((rows, 256), bf16))
    first = context * rows
    all_positions = first + lax.broadcasted_iota(jnp.int32, (1, rows), 1)
    all_starts = start_of(all_positions, first_end, second_end)
    start_first = start_of(first, first_end, second_end)
    start_last = start_of(first + rows - 1, first_end, second_end)

    lse_all = jnp.concatenate([lse_one[...], lse_two[...]], axis=1)

    def block(key_start, base, query_start, bands, masked):
        size = rows - query_start
        here = pl.ds(aligned(key_start - base, tile), tile)
        keys = keys_values[pl.ds(key_start, tile), 0:256]
        values = keys_values[pl.ds(key_start, tile), 128:384]
        key_sum, value_sum = None, None
        if masked:
            key_positions = key_start + lax.broadcasted_iota(jnp.int32, (tile, size), 0)
            seen = key_positions >= all_starts[:, query_start:]
            if 0 in bands:
                seen = seen & (key_positions <= all_positions[:, query_start:])
        span = slice(query_start, rows)
        for head in range(heads):
            queries = masked_q[head, span, :]
            grads = masked_o[head, span, :]
            scores = dot_nt(keys, queries)
            lse = lse_all[head : head + 1, span]
            if bands:
                parts = [
                    scores[:, place * tile : (place + 1) * tile] + bias_ref[band, head]
                    for place, band in enumerate(bands)
                ]
                if size > len(bands) * tile:
                    parts.append(scores[:, len(bands) * tile :] + far_bias[head])
                scores = jnp.concatenate(parts, axis=1)
            else:
                lse = lse - far_bias[head]
            probs = jnp.exp(scores - lse)
            if masked:
                probs = jnp.where(seen, probs, 0.0)
            grad_probs = dot_nt(values, grads)
            grad_scores = probs * (grad_probs - deltas[head : head + 1, span])
            for place, band in enumerate(bands):
                band_ref[band, head] += grad_scores[:, place * tile : (place + 1) * tile]
            low_scores = grad_scores.astype(bf16)
            value_part = dot_nn(probs.astype(bf16), grads)
            key_part = dot_nn(low_scores, queries)
            dq_t[head, :, span] += dot_nn(keys_t[head, :, here], low_scores)
            key_sum = key_part if key_sum is None else key_sum + key_part
            value_sum = value_part if value_sum is None else value_sum + value_part
        return key_sum, value_sum

    lane_tile = lax.broadcasted_iota(jnp.int32, (tile, 128), 1)

    def write(local, key_sum, value_sum):
        span = pl.ds(local, tile)
        dkv[span, 0:128] = key_sum[:, 0:128].astype(bf16)
        dkv[span, 128:256] = jnp.where(
            lane_tile < width, key_sum[:, 128:256], value_sum[:, 0:128]
        ).astype(bf16)
        dkv[span, 256:384] = value_sum[:, 128:256].astype(bf16)

    band_ref[...] = jnp.zeros_like(band_ref)
    for place, mask in enumerate(masks):
        which = context ^ mask
        base = aligned(which * rows, rows)
        dkv[...] = jnp.zeros_like(dkv)

        @pl.when(which <= context)
        def _():
            def transpose_keys(index, carry):
                source = pl.ds(aligned(base + index * tile, tile), tile)
                target = pl.ds(aligned(index * tile, tile), tile)
                lower = keys_values[source, 0:128].astype(f32).T.astype(bf16)
                upper = keys_values[source, 128:256].astype(f32).T.astype(bf16)
                keys_t[0, :, target] = lower[0:width]
                keys_t[1, :, target] = lower[width:]
                keys_t[2, :, target] = upper[0:width]
                return carry

            lax.fori_loop(0, tiles_here, transpose_keys, 0)
            low_tile = which * tiles_here
            high_tile = low_tile + tiles_here
            if mask:
                far_end = jnp.minimum(high_tile, context * tiles_here - 1)
                low = jnp.clip(start_first // tile, low_tile, far_end)
                middle = jnp.clip((start_last + tile - 1) // tile, low, far_end)

                def masked_step(index, carry):
                    start = aligned(index * tile, tile)
                    found = block(start, base, 0, (), True)
                    write(aligned(start - base, tile), *found)
                    return carry

                def plain_step(index, carry):
                    start = aligned(index * tile, tile)
                    found = block(start, base, 0, (), False)
                    write(aligned(start - base, tile), *found)
                    return carry

                lax.fori_loop(low, middle, masked_step, 0)
                lax.fori_loop(middle, far_end, plain_step, 0)

                @pl.when(far_end < high_tile)
                def _():
                    start = aligned(far_end * tile, tile)
                    write(aligned(start - base, tile), *block(start, base, 0, (1,), True))

            else:
                for index in range(tiles_here):
                    start = aligned(base + index * tile, tile)
                    bands = (0, 1) if index + 1 < tiles_here else (0,)
                    write(index * tile, *block(start, base, index * tile, bands, True))

        if mask:
            outs[2 * place][...] = dkv[0:half, :]
            outs[2 * place + 1][...] = dkv[half:, :]
        else:
            outs[0][...] = dkv[...]
    key_index = lax.broadcasted_iota(jnp.int32, (tile, tile), 0)
    query_index = lax.broadcasted_iota(jnp.int32, (tile, tile), 1)
    for head in range(heads):
        both = jnp.where(key_index > query_index, band_ref[1, head], band_ref[0, head])
        by_row = both[0:8]
        for first_row in range(8, tile, 8):
            by_row = by_row + pltpu.roll(both[first_row : first_row + 8], tile - first_row, 1)
        folded = by_row[0:1]
        for row in range(1, 8):
            folded = folded + pltpu.roll(by_row, tile - row, 1)[row : row + 1]
        fold_ref[head : head + 1, :] += folded
    if last_call:
        scale = width ** (-0.5)
        upper = jnp.concatenate([dq_t[0], dq_t[1]], axis=0)
        lower = jnp.concatenate([dq_t[2], jnp.zeros((width, rows), f32)], axis=0)
        dq_ref[:, 0:128] = (upper.T * scale).astype(bf16)
        dq_ref[:, 128:256] = (lower.T * scale).astype(bf16)


def attention_backward(
    masks, scalars, far_bias, offsets, queries, keys_values, bias_tiles, lse, given, piece_count,
    heads, width,
):
    rows = queries.shape[0]
    half = rows // 2
    shape = jax.ShapeDtypeStruct
    first_call, last_call = masks[0] == 3, masks[0] == 0
    outs = (shape((heads, width, rows), f32),)
    if first_call:
        outs = (shape((rows, 256), bf16), shape((16, rows), f32)) + outs
    if last_call:
        outs = outs + (shape((rows, 384), bf16),)
    else:
        outs = outs + (shape((half, 384), bf16),) * (2 * len(masks))
    if last_call:
        outs = outs + (shape((rows, 256), bf16),)
    outs = outs + (shape((8, tile), f32),)

    return pl.pallas_call(
        functools.partial(attention_backward_kernel, heads, width, masks, piece_count),
        out_shape=outs,
        in_specs=[SMEM, SMEM, SMEM] + [VMEM] * (5 + len(given)),
        out_specs=(VMEM,) * len(outs),
        scratch_shapes=[
            pltpu.VMEM((heads, rows, 256), bf16),
            pltpu.VMEM((heads, rows, 256), bf16),
            pltpu.VMEM((heads, width, rows), bf16),
            pltpu.VMEM((rows, 384), bf16),
            pltpu.VMEM((2, heads, tile, tile), f32),
        ],
        compiler_params=pltpu.CompilerParams(vmem_limit_bytes=60 * 2**20),
        cost_estimate=pl.CostEstimate(
            flops=10 * rows * rows * 256 * heads if first_call else 0,
            bytes_accessed=10 * 2**20 if first_call else 2**10,
            transcendentals=0,
        ),
        name="attention_backward",
    )(scalars, far_bias, offsets, queries, keys_values, bias_tiles, *lse, *given)


bucket_edges = np.array(
    [19, 21, 24, 27, 31, 35, 40, 46, 52, 59, 67, 77, 87, 99, 113], dtype=np.int32
)


def bucket_tiles():
    key = np.arange(tile)[None, :, None]
    query = np.arange(tile)[None, None, :]
    lag = np.arange(3)[:, None, None] * tile + query - key
    clipped = np.maximum(lag, 0)
    counted = (clipped[..., None] >= bucket_edges).sum(-1)
    return np.where(clipped < 16, clipped, 16 + counted).astype(np.int32)


def shape(dims, dtype):
    return jax.ShapeDtypeStruct(dims, dtype)


def params(mebibytes):
    return pltpu.CompilerParams(vmem_limit_bytes=mebibytes * 2**20)


def cost(flops, bytes_accessed):
    return pl.CostEstimate(flops=flops, bytes_accessed=bytes_accessed, transcendentals=0)


def gelu_constants():
    return 0.7978845608028654, 0.044715


def prepare_kernel(
    part, padded, scalars, table, route_ref, order_ref, rows_ref, columns_ref,
    bias_ref, ranks, hot_ref, tall,
):
    pair_count = order_ref.shape[1]
    rows = pair_count // 2
    expert_pad = hot_ref.shape[0]
    step = 256
    live_end = scalars[2] - scalars[0] * rows
    order = order_ref[...]
    index_row = lax.broadcasted_iota(jnp.int32, (pair_count, 128), 0)
    index_lane = lax.broadcasted_iota(jnp.int32, (pair_count, 128), 1)
    digits = jnp.where(
        index_lane == 0, index_row // 64, jnp.where(index_lane == 1, index_row % 64, 0)
    ).astype(f32).astype(bf16)

    def rank_step(index, carry):
        start = aligned(index * step, step)
        pair = start + lax.broadcasted_iota(jnp.int32, (step, pair_count), 0)
        hit = (pair == order).astype(f32).astype(bf16)
        found = dot_nn(hit, digits)
        position = found[:, 0:1] * 64.0 + found[:, 1:2]
        ranks[pl.ds(start, step), :] = jnp.broadcast_to(position, (step, 128))
        return carry

    lax.fori_loop(0, pair_count // step, rank_step, 0)
    rank_row = ranks[...].T[0:1, :]
    position = lax.broadcasted_iota(jnp.int32, (1, rows), 1)
    live = position < live_end
    expert_row = jnp.concatenate([route_ref[0:1, :], route_ref[1:2, :]], axis=1)
    live_row = jnp.concatenate([live, live], axis=1)
    expert_index = lax.broadcasted_iota(jnp.int32, (expert_pad, pair_count), 0)
    hot = ((expert_index == expert_row) & live_row).astype(f32)
    hot_ref[...] = hot.astype(bf16)

    def count_step(index, counts):
        start = aligned(index * step, step)
        earlier = (ranks[pl.ds(start, step), 0:1] < rank_row).astype(f32).astype(bf16)
        return counts + dot_nn(hot_ref[:, pl.ds(start, step)], earlier)

    counts = lax.fori_loop(
        0, pair_count // step, count_step, jnp.zeros((expert_pad, pair_count), f32)
    )
    slot = jnp.sum(counts * hot, axis=0, keepdims=True).astype(jnp.int32)
    own = slot - (scalars[3] & 1) * part
    place = jnp.where(live_row & (own >= 0) & (own < part), expert_row * padded + own, -1)
    rows_ref[...] = jnp.full_like(rows_ref, -1)
    rows_ref[0:1, :] = place[:, 0:rows]
    rows_ref[1:2, :] = place[:, rows:]
    tall[...] = jnp.full_like(tall, -1.0)
    tall[0:1, :] = place[:, 0:rows].astype(f32)
    tall[1:2, :] = place[:, rows:].astype(f32)
    columns_ref[...] = tall[...].T.astype(jnp.int32)
    key = lax.broadcasted_iota(jnp.int32, (8, tile), 0)
    query = lax.broadcasted_iota(jnp.int32, (8, tile), 1)
    heads = bias_ref.shape[1]
    for head in range(heads):
        bias_ref[2, head] = jnp.full((tile, tile), table[31, head], f32)

    def bias_step(index, carry):
        start = aligned(index * 8, 8)
        for band in range(2):
            lag = band * tile + query - key - start
            found = [jnp.full((8, tile), table[0, head], f32) for head in range(heads)]
            for bucket, edge in enumerate(list(range(1, 17)) + list(bucket_edges), start=1):
                beyond = lag >= int(edge)
                found = [
                    jnp.where(beyond, table[bucket, head], found[head]) for head in range(heads)
                ]
            for head in range(heads):
                bias_ref[band, head, pl.ds(start, 8), :] = found[head]
        return carry

    lax.fori_loop(0, tile // 8, bias_step, 0)


def prepare(scalars, table, route_rows, order_row, expert_count, part, padded):
    rows = route_rows.shape[1]
    heads = table.shape[1]
    expert_pad = max(16, expert_count)
    return pl.pallas_call(
        functools.partial(prepare_kernel, part, padded),
        out_shape=(
            shape((8, rows), jnp.int32),
            shape((rows, 128), jnp.int32),
            shape((3, heads, tile, tile), f32),
        ),
        in_specs=[SMEM, SMEM, VMEM, VMEM],
        out_specs=(VMEM,) * 3,
        scratch_shapes=[
            pltpu.VMEM((2 * rows, 128), f32),
            pltpu.VMEM((expert_pad, 2 * rows), bf16),
            pltpu.VMEM((128, rows), f32),
        ],
        compiler_params=params(40),
        cost_estimate=cost(10 * 10**9, 3 * 2**20),
        name="prepare",
    )(scalars, table, route_rows, order_row)


def pack_kernel(query, key, value, output, gain_one, gain_two, router, block):
    size = query.shape[0]
    experts = router.shape[1]
    block[...] = jnp.zeros_like(block)
    block[:, 0:192] = query[...]
    gains = jnp.concatenate([gain_one[...], gain_two[...]], axis=0).astype(f32)
    block[:, 192:194] = gains.T.astype(bf16)
    block[:, 256:448] = key[...]
    block[:, 448:512] = value[:, 128:192]
    block[:, 512:640] = value[:, 0:128]
    block[:, 640:832] = output[...].astype(f32).T.astype(bf16)
    block[:, 832 : 832 + experts] = router[...]


def pack_weights(query, key, value, output, gain_one, gain_two, router):
    size = query.shape[0]
    return pl.pallas_call(
        pack_kernel,
        out_shape=shape((size, 896), bf16),
        in_specs=[VMEM] * 7,
        out_specs=VMEM,
        compiler_params=params(60),
        cost_estimate=cost(0, 2**19),
        name="pack_weights",
    )(query, key, value, output, gain_one[None], gain_two[None], router)


def project_kernel(piece_count, offsets, token_ref, *rest):
    pieces = rest[:piece_count]
    hidden_ref, query_ref, kv_one, kv_two, weight_ref, output_ref, gain_ref = rest[piece_count:]
    for index, piece in enumerate(pieces):
        span = pl.ds(aligned(offsets[index], 16), piece.shape[0])
        weight_ref[span, :] = piece[:, 0:640]
        output_ref[span, :] = piece[:, 640:896]
    rows = token_ref.shape[0]
    half = rows // 2
    gains = weight_ref[:, 128:256].astype(f32).T
    gain_ref[0:1, :] = gains[64:65, :]
    gain_ref[1:2, :] = gains[65:66, :]
    step = 256
    lane = lax.broadcasted_iota(jnp.int32, (step, 256), 1)
    for start in range(0, rows, step):
        inputs = token_ref[start : start + step, :].astype(f32)
        scale = lax.rsqrt(jnp.mean(inputs * inputs, axis=-1, keepdims=True) + epsilon)
        hidden = (inputs * scale * gain_ref[0:1, :]).astype(bf16)
        hidden_ref[start : start + step, :] = hidden
        queries = dot_nn(hidden, weight_ref[:, 0:256]).astype(bf16)
        query_ref[start : start + step, :] = jnp.where(
            lane < 192, queries * bf16(0.125), jnp.zeros_like(queries)
        )
        target, base = (kv_one, 0) if start < half else (kv_two, half)
        target[start - base : start - base + step, :] = dot_nn(
            hidden, weight_ref[:, 256:640]
        ).astype(bf16)


def project(offsets, tokens, pieces):
    rows, model = tokens.shape
    return pl.pallas_call(
        functools.partial(project_kernel, len(pieces)),
        out_shape=(
            shape((rows, model), bf16),
            shape((rows, 256), bf16),
            shape((rows // 2, 384), bf16),
            shape((rows // 2, 384), bf16),
            shape((model, 640), bf16),
            shape((model, 256), bf16),
            shape((8, model), f32),
        ),
        in_specs=[SMEM, VMEM] + [VMEM] * len(pieces),
        out_specs=(VMEM,) * 7,
        compiler_params=params(40),
        cost_estimate=cost(2 * rows * model * 640, 6 * 2**20),
        name="project",
    )(offsets, tokens, *pieces)


def assemble_kernel(piece_count, offsets, *rest):
    pieces = rest[:piece_count]
    out_ref = rest[piece_count]
    for index, piece in enumerate(pieces):
        size = piece.shape[0]
        out_ref[pl.ds(aligned(offsets[index], 16), size), :] = piece[...].astype(out_ref.dtype)


def assemble(offsets, pieces, dtype):
    total = sum(piece.shape[0] for piece in pieces)
    width = pieces[0].shape[1]
    return pl.pallas_call(
        functools.partial(assemble_kernel, len(pieces)),
        out_shape=shape((total, width), dtype),
        in_specs=[SMEM] + [VMEM] * len(pieces),
        out_specs=VMEM,
        compiler_params=params(40),
        cost_estimate=cost(0, 6 * total * width),
        name="assemble",
    )(offsets, *pieces)


def dispatch_kernel(
    width, expert_count, padded, scalars, token_ref, gain_ref, route_ref, row_place, *rest
):
    attended = rest[0:8]
    weights = rest[8:12]
    residual_ref, hidden_ref, info_ref, attended_ref, sent = rest[12:17]
    packed, joined, column = rest[17:]
    rows, model = token_ref.shape
    half, quarter = rows // 2, rows // 4
    lane_low = lax.broadcasted_iota(jnp.int32, (quarter, 128), 1)
    for source in range(4):
        for part in range(2):
            piece = attended[2 * source + part]
            middle = piece[:, 128:256].astype(f32)
            span = slice(part * half, part * half + quarter)
            packed[source, span, 0:128] = piece[:, 0:128]
            packed[source, span, 128:256] = jnp.where(lane_low < width, middle, 0.0).astype(bf16)
            span = slice(part * half + quarter, (part + 1) * half)
            packed[source, span, 0:128] = piece[:, 256:384]
            packed[source, span, 128:256] = jnp.where(
                lane_low < width, pltpu.roll(middle, 64, 1), 0.0
            ).astype(bf16)
    step = 256
    lane = lax.broadcasted_iota(jnp.int32, (step, 128), 1)
    valid = (lane >= 64) & (lane < 64 + expert_count)

    def token_step(index, carry):
        start = aligned(index * step, step)
        span = pl.ds(start, step)
        residual = token_ref[span, :].astype(f32)
        for source in range(4):
            residual = residual + dot_nt(packed[source, span, :], weights[source][...])
        joined[span, :] = residual
        scale = lax.rsqrt(jnp.mean(residual * residual, axis=-1, keepdims=True) + epsilon)
        hidden = (residual * scale * gain_ref[1:2, :]).astype(bf16)
        hidden_ref[span, :] = hidden
        logits = dot_nn(hidden, weights[0][:, 128:256])
        logits = jnp.where(valid, logits, masked_value)
        powers = jnp.where(valid, jnp.exp(logits - jnp.max(logits, axis=-1, keepdims=True)), 0.0)
        probs = powers / jnp.sum(powers, axis=-1, keepdims=True)
        first = jnp.sum(
            jnp.where(lane == route_ref[span, 0:1] + 64, probs, 0.0), axis=-1, keepdims=True
        )
        second = jnp.sum(
            jnp.where(lane == route_ref[span, 1:2] + 64, probs, 0.0), axis=-1, keepdims=True
        )
        total = first + second
        info_ref[span, :] = jnp.where(
            lane == 0,
            first / total,
            jnp.where(lane == 1, second / total, jnp.where(lane == 2, total, probs)),
        )
        return carry

    lax.fori_loop(0, rows // step, token_step, 0)
    here = pl.ds(aligned(scalars[3] * quarter, quarter), quarter)
    residual_ref[...] = joined[here, :]
    for source in range(4):
        attended_ref[:, source * 256 : (source + 1) * 256] = packed[source, here, :]
    gates = info_ref[...].T
    gate_one, gate_two = gates[0:1, :], gates[1:2, :]
    place_one, place_two = row_place[0:1, :], row_place[1:2, :]
    column[...] = jnp.zeros_like(column)

    taken = 4 * padded

    def expert_rows(index, carry):
        start = aligned(index * taken, 64)
        slot = start + lax.broadcasted_iota(jnp.int32, (taken, rows), 0)
        hit_one, hit_two = slot == place_one, slot == place_two
        picked = jnp.where(hit_one | hit_two, 1.0, 0.0).astype(bf16)
        sent[pl.ds(start, taken), :] = dot_nn(picked, hidden_ref[...]).astype(bf16)
        gate = jnp.where(hit_one, gate_one, jnp.where(hit_two, gate_two, 0.0))
        gate = jnp.sum(gate, axis=-1, keepdims=True)
        for chunk in range(4):
            write_digits(
                sent, column, start + chunk * padded, padded,
                gate[chunk * padded : (chunk + 1) * padded],
            )
        return carry

    lax.fori_loop(0, expert_count // 4, expert_rows, 0)


def write_digits(rows_ref, column, start, padded, values):
    column[0:padded, :] = jnp.broadcast_to(values, (padded, 128))
    row = column[...].T[0:1, :]
    high = row.astype(bf16).astype(f32)
    middle = (row - high).astype(bf16).astype(f32)
    low = row - high - middle
    size = row.shape[1]
    index = lax.broadcasted_iota(jnp.int32, (16, size), 0)
    block = jnp.where(
        index == 0, high, jnp.where(index == 1, middle, jnp.where(index == 2, low, 0.0))
    )
    span = pl.ds(aligned(start + padded - 16, 16), 16)
    rows_ref[span, 0:size] = block.astype(bf16)
    rows_ref[span, size:] = jnp.zeros((16, rows_ref.shape[1] - size), bf16)


def read_digits(rows_ref, start, padded):
    wide = (padded + 127) // 128 * 128
    span = pl.ds(aligned(start + padded - 16, 16), 16)
    return jnp.sum(rows_ref[span, 0:wide].astype(f32), axis=0, keepdims=True)


def dispatch(
    scalars, tokens, gains, routes, row_place, attended, weights, width, expert_count, padded
):
    rows, model = tokens.shape
    slots = expert_count * padded
    wide = (padded + 127) // 128 * 128
    return pl.pallas_call(
        functools.partial(dispatch_kernel, width, expert_count, padded),
        out_shape=(
            shape((rows // 4, model), f32),
            shape((rows, model), bf16),
            shape((rows, 128), f32),
            shape((rows // 4, 1024), bf16),
            shape((slots, model), bf16),
        ),
        in_specs=[SMEM] + [VMEM] * 16,
        out_specs=(VMEM,) * 5,
        scratch_shapes=[
            pltpu.VMEM((4, rows, 256), bf16),
            pltpu.VMEM((rows, model), f32),
            pltpu.VMEM((wide, 128), f32),
        ],
        compiler_params=params(60),
        cost_estimate=cost(2 * rows * model * (1024 + slots), 16 * 2**20),
        name="dispatch",
    )(scalars, tokens, gains, routes, row_place, *attended, *weights)


def scatter_kernel(value_ref, row_place, sent):
    rows = value_ref.shape[0]
    place_one, place_two = row_place[0:1, :], row_place[1:2, :]
    fill = sent.shape[0] // 2

    def slot_step(index, carry):
        start = aligned(index * fill, fill)
        slot = start + lax.broadcasted_iota(jnp.int32, (fill, rows), 0)
        picked = jnp.where((slot == place_one) | (slot == place_two), 1.0, 0.0).astype(bf16)
        sent[pl.ds(start, fill), :] = dot_nn(picked, value_ref[...]).astype(bf16)
        return carry

    lax.fori_loop(0, sent.shape[0] // fill, slot_step, 0)


def scatter_rows(values, row_place, slots):
    rows, model = values.shape
    return pl.pallas_call(
        scatter_kernel,
        out_shape=shape((slots, model), bf16),
        in_specs=[VMEM, VMEM],
        out_specs=VMEM,
        compiler_params=params(40),
        cost_estimate=cost(2 * rows * model * slots, 6 * 2**20),
        name="scatter_rows",
    )(values, row_place)


def expert_kernel(
    padded, in_own, in_partner, out_own, out_partner, rows_ref, grads_ref, acted_ref, pre_ref,
    back_ref, column, gate_ref,
):
    hidden = in_own.shape[1]
    root, cubic = gelu_constants()
    wide = column.shape[0]
    column[...] = jnp.zeros_like(column)
    slots = rows_ref.shape[0]
    taken = 4 * padded

    def one(index, carry):
        start = aligned(index * taken, 64)
        span = pl.ds(start, taken)
        for chunk in range(4):
            gates = read_digits(rows_ref, start + chunk * padded, padded)
            gates = jnp.broadcast_to(gates, (128, wide)).T[0:padded, :]
            gate_ref[chunk * padded : (chunk + 1) * padded, :] = gates
        gate = jnp.concatenate([gate_ref[...], gate_ref[...]], axis=1)
        gate_part = None
        for side, (in_ref, out_ref) in enumerate(((in_own, out_own), (in_partner, out_partner))):
            for first in range(0, hidden, 256):
                part = slice(first, first + 256)
                pre = dot_nn(rows_ref[span, :], in_ref[:, part])
                grad_acted = dot_nt(grads_ref[span, :], out_ref[part, :])
                square = pre * pre
                bent = jnp.tanh(root * pre * (1.0 + cubic * square))
                acted = 0.5 * pre * (1.0 + bent)
                slope = 0.5 * (1.0 + bent) + 0.5 * pre * (1.0 - bent * bent) * root * (
                    1.0 + 3.0 * cubic * square
                )
                acted_ref[side, span, part] = (acted * gate).astype(bf16)
                product = grad_acted * acted
                folded = product[:, 0:128] + product[:, 128:256]
                gate_part = folded if gate_part is None else gate_part + folded
                pre_ref[side, span, part] = (grad_acted * slope * gate).astype(bf16)
        back = dot_nt(pre_ref[0, span, :], in_own[...])
        back = back + dot_nt(pre_ref[1, span, :], in_partner[...])
        back_ref[span, :] = back.astype(bf16)
        gate_part = jnp.sum(gate_part, axis=-1, keepdims=True)
        for chunk in range(4):
            write_digits(
                back_ref, column, start + chunk * padded, padded,
                gate_part[chunk * padded : (chunk + 1) * padded],
            )
        return carry

    lax.fori_loop(0, slots // taken, one, 0)


def expert_step(in_parts, out_parts, rows_in, grads_in, padded):
    slots, model = rows_in.shape
    hidden = in_parts[0].shape[1]
    wide = (padded + 127) // 128 * 128
    return pl.pallas_call(
        functools.partial(expert_kernel, padded),
        out_shape=(
            shape((2, slots, hidden), bf16),
            shape((2, slots, hidden), bf16),
            shape((slots, model), bf16),
        ),
        in_specs=[VMEM] * 6,
        out_specs=(VMEM,) * 3,
        scratch_shapes=[pltpu.VMEM((wide, 128), f32), pltpu.VMEM((4 * padded, 128), f32)],
        compiler_params=params(60),
        cost_estimate=cost(12 * slots * model * hidden, 24 * 2**20),
        name="expert_step",
    )(*in_parts, *out_parts, rows_in, grads_in)


def expert_out_kernel(acted_ref, out_own, out_partner, out_ref):
    step = out_ref.shape[0] // 4

    def one(index, carry):
        span = pl.ds(aligned(index * step, 16), step)
        total = dot_nn(acted_ref[0, span, :], out_own[...])
        total = total + dot_nn(acted_ref[1, span, :], out_partner[...])
        out_ref[span, :] = total.astype(bf16)
        return carry

    lax.fori_loop(0, 4, one, 0)


def expert_outputs(acted, out_parts):
    _, slots, hidden = acted.shape
    model = out_parts[0].shape[1]
    return pl.pallas_call(
        expert_out_kernel,
        out_shape=shape((slots, model), bf16),
        in_specs=[VMEM] * 3,
        out_specs=VMEM,
        compiler_params=params(60),
        cost_estimate=cost(4 * slots * model * hidden, 10 * 2**20),
        name="expert_outputs",
    )(acted, *out_parts)


def write_ring(scalars, joined, own, next_ref, last_ref, far_one, far_two):
    quarter = own.shape[0]
    eighth = quarter // 2
    rank = scalars[3]

    def rows_of(which):
        return aligned(lax.rem(rank + which, 4) * quarter, quarter)

    own[...] = joined[pl.ds(rows_of(0), quarter), :]
    next_ref[...] = joined[pl.ds(rows_of(1), quarter), :].astype(bf16)
    last_ref[...] = joined[pl.ds(rows_of(3), quarter), :].astype(bf16)
    far = rows_of(2)
    far_one[...] = joined[pl.ds(far, eighth), :].astype(bf16)
    far_two[...] = joined[pl.ds(aligned(far + eighth, eighth), eighth), :].astype(bf16)


def ring_shapes(rows, model):
    quarter, eighth = shape((rows // 4, model), bf16), shape((rows // 8, model), bf16)
    return (shape((rows // 4, model), f32), quarter, quarter, eighth, eighth)


def combine_grads_kernel(
    expert_count, padded, far, scalars, place_ref, info_ref, route_ref, router_ref, back_ref, *rest
):
    if far:
        logit_ref, far_one, far_two, digits = rest
    else:
        far_logits, logit_ref, own, next_ref, last_ref, digits = rest
    rows = place_ref.shape[0]
    quarter, eighth = rows // 4, rows // 8
    slots = back_ref.shape[0]
    rank = scalars[3]
    wide = (padded + 127) // 128 * 128
    lane_digit = lax.broadcasted_iota(jnp.int32, (padded, 128), 1)

    def column_step(expert, carry):
        start = aligned(expert * padded, 16)
        row = jnp.broadcast_to(read_digits(back_ref, start, padded), (128, wide))
        column = row.T[0:padded, :]
        high = column.astype(bf16).astype(f32)
        middle = (column - high).astype(bf16).astype(f32)
        digits[pl.ds(start, padded), :] = jnp.where(
            lane_digit == 0,
            high,
            jnp.where(lane_digit == 1, middle, jnp.where(lane_digit == 2, column - high - middle, 0.0)),
        ).astype(bf16)
        return carry

    lax.fori_loop(0, expert_count, column_step, 0)
    lane = lax.broadcasted_iota(jnp.int32, (quarter, 128), 1)
    slot = lax.broadcasted_iota(jnp.int32, (quarter, slots), 1)

    def rows_of(which):
        return pl.ds(aligned(lax.rem(rank + which, 4) * quarter, quarter), quarter)

    def tokens(which):
        span = rows_of(which)
        info, place = info_ref[span, :], place_ref[span, :]
        hit_one, hit_two = slot == place[:, 0:1], slot == place[:, 1:2]
        ones = jnp.where(hit_one | hit_two, 1.0, 0.0).astype(bf16)
        total = dot_nn(ones, back_ref[...])
        signs = jnp.where(hit_one, 1.0, jnp.where(hit_two, -1.0, 0.0)).astype(bf16)
        difference = jnp.sum(dot_nn(signs, digits[...]), axis=-1, keepdims=True) / info[:, 2:3]
        picked = jnp.where(
            lane == route_ref[span, 0:1] + 64,
            info[:, 1:2] * difference,
            jnp.where(lane == route_ref[span, 1:2] + 64, -info[:, 0:1] * difference, 0.0),
        )
        probs = jnp.where((lane >= 64) & (lane < 64 + expert_count), info, 0.0)
        grads = probs * (picked - jnp.sum(probs * picked, axis=-1, keepdims=True))
        grads = grads.astype(bf16)
        return grads, total + dot_nt(grads, router_ref[:, 128:256])

    if far:
        grads, total = tokens(2)
        logit_ref[...] = grads
        far_one[...] = total[0:eighth].astype(bf16)
        far_two[...] = total[eighth:].astype(bf16)
    else:
        logit_ref[rows_of(2), :] = far_logits[...]
        for which, target in ((1, next_ref), (3, last_ref)):
            grads, total = tokens(which)
            logit_ref[rows_of(which), :] = grads
            target[...] = total.astype(bf16)
        grads, total = tokens(0)
        logit_ref[rows_of(0), :] = grads
        own[...] = total


def combine_grads(far, scalars, place, info, routes, router, back, given, expert_count, padded):
    rows = place.shape[0]
    model = router.shape[0]
    slots = back.shape[0]
    half = shape((rows // 8, model), bf16)
    if far:
        outs = (shape((rows // 4, 128), bf16), half, half)
    else:
        outs = (shape((rows, 128), bf16), shape((rows // 4, model), f32))
        outs = outs + (shape((rows // 4, model), bf16),) * 2
    return pl.pallas_call(
        functools.partial(combine_grads_kernel, expert_count, padded, far),
        out_shape=outs,
        in_specs=[SMEM] + [VMEM] * (5 + len(given)),
        out_specs=(VMEM,) * len(outs),
        scratch_shapes=[pltpu.VMEM((slots, 128), bf16)],
        compiler_params=params(60),
        cost_estimate=cost(2 * rows * model * slots, 8 * 2**20),
        name="combine_grads",
    )(scalars, place, info, routes, router, back, *given)


def combine_outs_kernel(place_ref, rows_ref, out_ref):
    step = 256
    slot = lax.broadcasted_iota(jnp.int32, (step, rows_ref.shape[0]), 1)

    def token_step(index, carry):
        span = pl.ds(aligned(index * step, step), step)
        place = place_ref[span, :]
        hit = (slot == place[:, 0:1]) | (slot == place[:, 1:2])
        out_ref[span, :] = dot_nn(jnp.where(hit, 1.0, 0.0).astype(bf16), rows_ref[...]).astype(bf16)
        return carry

    lax.fori_loop(0, out_ref.shape[0] // step, token_step, 0)


def combine_outs(place, rows_in):
    rows = place.shape[0]
    slots, model = rows_in.shape
    return pl.pallas_call(
        combine_outs_kernel,
        out_shape=shape((rows, model), bf16),
        in_specs=[VMEM] * 2,
        out_specs=VMEM,
        compiler_params=params(60),
        cost_estimate=cost(2 * rows * model * slots, 8 * 2**20),
        name="combine_outs",
    )(place, rows_in)


def received(own, from_last, from_next):
    return own[...] + from_last[...].astype(f32) + from_next[...].astype(f32)


def norm_back_kernel(gain_index, has_bypass_rows, scalars, value_ref, gain_ref, bypass_ref, *rest):
    grads = received(*rest[:3])
    rest = rest[3:]
    weights = ()
    if gain_index == 1:
        weights, rest = rest[0:4], rest[4:]
    else:
        blocks_ref, rest = rest[0], rest[1:]
    full_ref, low_ref, gain_grad = rest[0:3]
    quarter = grads.shape[0]
    here = pl.ds(aligned(scalars[3] * quarter, quarter), quarter)
    values = (value_ref[here, :] if gain_index == 0 else value_ref[...]).astype(f32)
    bypass = (bypass_ref[here, :] if has_bypass_rows else bypass_ref[...]).astype(f32)
    scale = lax.rsqrt(jnp.mean(values * values, axis=-1, keepdims=True) + epsilon)
    normed = values * scale
    scaled = grads * gain_ref[gain_index : gain_index + 1, :]
    gain_grad[...] = jnp.broadcast_to(
        jnp.sum(grads * normed, axis=0, keepdims=True), gain_grad.shape
    )
    out = bypass + scale * (scaled - normed * jnp.mean(scaled * normed, axis=-1, keepdims=True))
    full_ref[...] = out
    low = out.astype(bf16)
    if weights:
        low_ref[...] = low
    else:
        block = blocks_ref.shape[0] // 3
        for place, step in enumerate((0, 3, 1, 2)):
            target = lax.rem(scalars[3] + step, 4)
            low_ref[target, 0:quarter, :] = low
            columns = slice(place * 256, (place + 1) * 256)
            for third in range(3):
                low_ref[target, quarter:, third * 256 : (third + 1) * 256] = blocks_ref[
                    third * block : (third + 1) * block, columns
                ].astype(bf16)
    lane = lax.broadcasted_iota(jnp.int32, (quarter, 256), 1)
    for weight, target in zip(weights, rest[3:]):
        target[...] = jnp.where(lane < 192, dot_nn(low, weight[...]), 0.0).astype(bf16)


def norm_back(gain_index, has_bypass_rows, scalars, values, gains, bypass, parts, weights=(), blocks=None):
    quarter, model = parts[0].shape
    low = shape((quarter, model), bf16)
    if blocks is not None:
        low = shape((4, quarter + blocks.shape[0] // 3, model), bf16)
    extra = tuple(weights) if blocks is None else (blocks,)
    return pl.pallas_call(
        functools.partial(norm_back_kernel, gain_index, has_bypass_rows),
        out_shape=(shape((quarter, model), f32), low, shape((8, model), f32))
        + (shape((quarter, 256), bf16),) * len(weights),
        in_specs=[SMEM] + [VMEM] * (6 + len(extra)),
        out_specs=(VMEM,) * (3 + len(weights)),
        compiler_params=params(60),
        cost_estimate=cost(quarter * model * 16, 6 * 2**20),
        name="norm_back",
    )(scalars, values, gains, bypass, *parts, *extra)


def unpack_kernel(arrived, input_ref, outer_ref):
    quarter = input_ref.shape[0] // 4
    block = outer_ref.shape[0] // 3
    for source in range(4):
        input_ref[source * quarter : (source + 1) * quarter, :] = arrived[
            source, 0:quarter, :
        ].astype(f32)
    total = arrived[0, quarter:, :].astype(f32)
    for source in range(1, 4):
        total = total + arrived[source, quarter:, :].astype(f32)
    for third in range(3):
        outer_ref[third * block : (third + 1) * block, :] = total[:, third * 256 : third * 256 + 256]


def unpack(arrived, rows, shard):
    return pl.pallas_call(
        unpack_kernel,
        out_shape=(shape((rows, arrived.shape[2]), f32), shape((shard, 256), f32)),
        in_specs=[VMEM],
        out_specs=(VMEM,) * 2,
        compiler_params=params(40),
        cost_estimate=cost(0, 5 * 2**20),
        name="unpack",
    )(arrived)


def finish_kernel(residual_ref, part_ref, out_ref):
    total = residual_ref[...]
    quarter = total.shape[0]
    for source in range(4):
        total = total + part_ref[source * quarter : (source + 1) * quarter, :].astype(f32)
    low = total.astype(bf16)
    for target in range(4):
        out_ref[target * quarter : (target + 1) * quarter, :] = low


def finish(residual, parts):
    quarter, model = residual.shape
    return pl.pallas_call(
        finish_kernel,
        out_shape=shape((4 * quarter, model), bf16),
        in_specs=[VMEM] * 2,
        out_specs=VMEM,
        compiler_params=params(40),
        cost_estimate=cost(quarter * model * 4, 4 * 2**20),
        name="finish",
    )(residual, parts)


def hidden_grad_kernel(
    scalars, dq_ref, weight_ref, own, beside_one, beside_two, across_one, across_two, dkv_ref, *rest
):
    ring, joined = rest[:5], rest[5]
    half = own.shape[0] // 2
    for part, (beside, across) in enumerate(
        ((beside_one, across_one), (beside_two, across_two))
    ):
        span = slice(part * half, (part + 1) * half)
        total = own[span, :].astype(f32) + beside[...].astype(f32) + across[...].astype(f32)
        total = total.astype(bf16)
        dkv_ref[span, :] = total
        joined[span, :] = dot_nt(dq_ref[span, :], weight_ref[:, 0:256]) + dot_nt(
            total, weight_ref[:, 256:640]
        )
    write_ring(scalars, joined, *ring)


def hidden_grad(scalars, dq, weights, own, beside, across):
    rows = dq.shape[0]
    model = weights.shape[0]
    return pl.pallas_call(
        hidden_grad_kernel,
        out_shape=(shape((rows, 384), bf16),) + ring_shapes(rows, model),
        in_specs=[SMEM] + [VMEM] * 7,
        out_specs=(VMEM,) * 6,
        scratch_shapes=[pltpu.VMEM((rows, model), f32)],
        compiler_params=params(40),
        cost_estimate=cost(2 * rows * model * 640, 8 * 2**20),
        name="hidden_grad",
    )(scalars, dq, weights, own, *beside, *across)


def split_by_side(scalars, whole, mine, other):
    half = mine.shape[0]
    side = scalars[5]
    mine[...] = whole[pl.ds(aligned(side * half, 16), half), :]
    other[...] = whole[pl.ds(aligned((1 - side) * half, 16), half), :].astype(other.dtype)


def output_grad_kernel(scalars, branch_ref, attended_ref, hidden_ref, logit_ref, *rest):
    outs, whole = rest[:-1], rest[-1]
    whole[...] = dot_tn(branch_ref[...], attended_ref[...])
    router = dot_tn(hidden_ref[...], logit_ref[...])
    for source in range(4):
        whole[:, source * 256 + 128 : source * 256 + 256] += router
    if len(outs) == 1:
        outs[0][...] = whole[...]
    else:
        size = outs[0].shape[0] // 4
        context, side = scalars[0], scalars[5]
        for out, masks in zip(outs, ((0, 2), (1, 3))):
            for place, mask in enumerate(masks):
                for far in range(2):
                    start = aligned((4 * (side ^ far) + (context ^ mask)) * size, 16)
                    target = slice((2 * place + far) * size, (2 * place + far + 1) * size)
                    out[target, :] = whole[pl.ds(start, size), :].astype(out.dtype)


def output_grads(scalars, branch, attended, hidden, grad_logits, small):
    rows, model = hidden.shape
    outs = (shape((model, 1024), f32),)
    if small:
        outs = (shape((model // 2, 1024), f32), shape((model // 2, 1024), bf16))
    return pl.pallas_call(
        output_grad_kernel,
        out_shape=outs,
        in_specs=[SMEM] + [VMEM] * 4,
        out_specs=(VMEM,) * len(outs),
        scratch_shapes=[pltpu.VMEM((model, 1024), f32)],
        compiler_params=params(60),
        cost_estimate=cost(2 * rows * model * 384, 6 * 2**20),
        name="output_grads",
    )(scalars, branch, attended, hidden, grad_logits)


def projection_grad_kernel(scalars, hidden_ref, dq_ref, dkv_ref, gain_ref, fold_ref, *rest):
    outs, whole = rest[:-1], rest[-1]
    hidden = hidden_ref[...]
    whole[:, 0:256] = dot_tn(hidden, dq_ref[...])
    whole[:, 256:640] = dot_tn(hidden, dkv_ref[...])
    lane = lax.broadcasted_iota(jnp.int32, (whole.shape[0], 128), 1)
    column = jnp.broadcast_to(gain_ref[0:1, :], (128, whole.shape[0])).T
    whole[:, 128:256] = jnp.where(lane < 64, whole[:, 128:256], column)
    if len(outs) == 2:
        side = scalars[5]
        block = outs[0].shape[0] // 4
        size = block - 8
        for which, out in ((side, outs[0]), (1 - side, outs[1])):
            for context in range(4):
                start = aligned((which * 4 + context) * size, 8)
                out[context * block : context * block + size, :] = whole[pl.ds(start, size), :]
                tail = slice(context * block + size, (context + 1) * block)
                out[tail, 0:256] = fold_ref[...]
                out[tail, 256:640] = jnp.zeros((8, 384), f32)
    else:
        outs[0][...] = whole[...]


def projection_grads(scalars, hidden, dq, dkv, gain_grad, fold, small):
    rows, model = hidden.shape
    outs = (shape((model // 2 + 32, 640), f32),) * 2 if small else (shape((model, 640), f32),)
    return pl.pallas_call(
        projection_grad_kernel,
        out_shape=outs,
        in_specs=[SMEM] + [VMEM] * 5,
        out_specs=(VMEM,) * len(outs),
        scratch_shapes=[pltpu.VMEM((model, 640), f32)],
        compiler_params=params(40),
        cost_estimate=cost(2 * rows * model * 640, 6 * 2**20),
        name="projection_grads",
    )(scalars, hidden, dq, dkv, gain_grad, fold)


def share_kernel(scalars, mine, other, *outs):
    size = outs[0].shape[0]
    context = scalars[0]
    for mask, out in enumerate(outs):
        span = pl.ds(aligned((context ^ mask) * size, 8), size)
        total = mine[span, :] + other[span, :].astype(f32)
        out[...] = total.astype(out.dtype)


def share(scalars, mine, other):
    rows, width = mine.shape
    return pl.pallas_call(
        share_kernel,
        out_shape=(shape((rows // 4, width), f32),) + (shape((rows // 4, width), other.dtype),) * 3,
        in_specs=[SMEM, VMEM, VMEM],
        out_specs=(VMEM,) * 4,
        compiler_params=params(40),
        cost_estimate=cost(rows * width, 12 * rows * width),
        name="share",
    )(scalars, mine, other)


def shift(value, amount):
    size = lax.axis_size("tensor")
    return lax.ppermute(value, "tensor", [(i, (i + amount) % size) for i in range(size)])


def cross(value, mask):
    size = lax.axis_size("context")
    return lax.ppermute(value, "context", [(i, i ^ mask) for i in range(size)])


def partner(value):
    return lax.ppermute(value, "tensor", [(i, i ^ 1) for i in range(lax.axis_size("tensor"))])


def spread(value):
    return [value] + [shift(value, step) for step in (1, -1, 2)]


def sum_ranks(value):
    total = value
    for step in (1, 2, 3):
        total = total + shift(value, step)
    return total


def ring_gather(one, two):
    last_one, next_two = shift(one, 1), shift(two, -1)
    last_two, next_one = shift(two, 1), shift(one, -1)
    far_one, far_two = shift(last_one, 1), shift(next_two, -1)
    return (one, two, last_one, last_two, next_one, next_two, far_one, far_two)


def ring_ranks(rank):
    return [lax.rem(rank + step, 4) for step in (0, 3, 1, 2)]


def added(first, second):
    return (first.astype(f32) + second.astype(f32)).astype(bf16)


def ring_start(far_one, far_two):
    return shift(far_one, 1), shift(far_two, -1)


def with_first(whole, arrived):
    half = arrived.shape[0]
    return jnp.concatenate([added(whole[:half], arrived), whole[half:]], axis=0)


def with_second(whole, arrived):
    half = arrived.shape[0]
    return jnp.concatenate([whole[:half], added(whole[half:], arrived)], axis=0)


def ring_finish(next_block, last_block, arrived_one, arrived_two):
    from_last = shift(with_first(next_block, arrived_one), 1)
    from_next = shift(with_second(last_block, arrived_two), -1)
    return from_last, from_next


ALL_ROWS = ("dp", "context")


def exchange(rows_out):
    return lax.all_to_all(rows_out, ALL_ROWS, split_axis=0, concat_axis=0, tiled=True)


def gather_weights(block, small, axis):
    size = block.shape[axis]
    if not small:
        whole = lax.all_gather(block, ALL_ROWS, axis=axis, tiled=True)
        return [whole], jnp.zeros((1,), jnp.int32)
    context, side = lax.axis_index("context"), lax.axis_index("dp")
    pieces = [block] + [cross(block, mask) for mask in (1, 2, 3)]
    pieces = pieces + [lax.ppermute(piece, "dp", [(0, 1), (1, 0)]) for piece in pieces]
    return pieces, jnp.stack(
        [((side ^ far) * 4 + (context ^ mask)) * size for far in range(2) for mask in range(4)]
    )


def swap_sides(parts):
    if len(parts) == 1:
        return parts
    return parts[0], lax.ppermute(parts[1], "dp", [(0, 1), (1, 0)])


def share_blocks(scalars, parts):
    return parts if len(parts) == 1 else share(scalars, *parts)


def halve(mine, arrived):
    total = mine + arrived.astype(f32)
    half = total.shape[0] // 2
    return total[:half], total[half:].astype(bf16)


def scatter_blocks(blocks):
    if len(blocks) == 1:
        return lax.psum_scatter(blocks[0], ALL_ROWS, scatter_dimension=0, tiled=True)
    total = blocks[0]
    for mask in (1, 2, 3):
        total = total + cross(blocks[mask], mask).astype(f32)
    return total


def on_device(
    tokens_in, query_weight, key_weight, value_weight, output_weight, bias_table, attention_gain,
    router_weight, expert_gain, expert_in, expert_out, routes, pair_order, seq_lengths, cotangent,
):
    rows, model = tokens_in.shape
    heads = bias_table.shape[1]
    width = query_weight.shape[1] // heads
    group_rows = rows * lax.axis_size("context")
    expert_count = router_weight.shape[1]
    capacity = (9 * rows + 4 * expert_count - 1) // (4 * expert_count)
    count = lax.axis_size("dp") * lax.axis_size("context")
    small = count == 8
    context, rank = lax.axis_index("context"), lax.axis_index("tensor")
    here = lax.axis_index("dp") * lax.axis_size("context") + context
    first_end = seq_lengths[0, 0]
    second_end = first_end + seq_lengths[0, 1]
    side = lax.axis_index("dp")
    scalars = jnp.stack([context, first_end, second_end, rank, here, side]).astype(jnp.int32)
    part = capacity // 2
    padded = (part + 15) // 16 * 16 + 16
    slots = expert_count * padded
    shard = query_weight.shape[0]
    block = pack_weights(
        query_weight, key_weight, value_weight, output_weight, attention_gain, expert_gain, router_weight
    )
    tie = lax.optimization_barrier
    half, quarter = rows // 2, rows // 4
    kv_offsets = jnp.stack(
        [(context ^ mask) * rows + part * half for mask in range(4) for part in range(2)]
    )
    token_offsets = jnp.stack([which * quarter for which in ring_ranks(rank)])
    far_bias = bias_table[-1]
    order_row = (pair_order & 1) * rows + (pair_order >> 1)
    pieces, offsets = gather_weights(block, small, 0)
    in_parts = (expert_in[0], partner(expert_in[0]))
    out_parts = (expert_out[0], partner(expert_out[0]))
    hidden_one, queries, kv_one, kv_two, weights, output_own, gains = project(
        offsets, tokens_in, pieces
    )
    output_parts = [output_own] + [shift(output_own, step) for step in (1, -1, 2)]
    beside_one, across_two = cross(kv_one, 1), cross(kv_two, 2)
    beside_two, across_one = cross(kv_two, 1), cross(kv_one, 2)
    order_row, queries = tie((order_row, queries))
    row_place, column_place, bias_tiles = prepare(
        scalars, bias_table, routes.T, order_row, expert_count, part, padded
    )
    beside_one, across_two, row_place = tie((beside_one, across_two, row_place))
    kv_far = cross(beside_one, 2), cross(across_two, 1)
    kv_pieces = (kv_one, kv_two, beside_one, beside_two, across_one, across_two) + kv_far
    cotangent_rows = scatter_rows(cotangent, row_place, slots)
    states = attention_near(
        scalars, far_bias, queries, bias_tiles, kv_one, kv_two, heads, width
    )
    states, kv_pieces, cotangent_rows, in_parts, out_parts = tie(
        (states, kv_pieces, cotangent_rows, in_parts, out_parts)
    )
    packed_one, lse_one, *made = attention_far(
        0, scalars, far_bias, kv_offsets, queries, bias_tiles, states, kv_pieces, group_rows,
        heads, width,
    )
    attended_one = spread(packed_one)
    packed_two, lse_two = attention_far(
        1, scalars, far_bias, kv_offsets, queries, bias_tiles, states, made, group_rows,
        heads, width,
    )
    packed_two, attended_one, output_parts, cotangent_rows = tie(
        (packed_two, attended_one, output_parts, cotangent_rows)
    )
    attended_two = spread(packed_two)
    cotangent_rows = exchange(cotangent_rows)
    attended = [piece for pair in zip(attended_one, attended_two) for piece in pair]
    attended, cotangent_rows = tie((attended, cotangent_rows))
    residual, hidden_two, info, attended_here, rows_out = dispatch(
        scalars, tokens_in, gains, routes, row_place, attended, output_parts, width,
        expert_count, padded,
    )
    expert_rows = exchange(rows_out)
    acted, grad_pre, back = expert_step(
        in_parts, out_parts, expert_rows, cotangent_rows, padded
    )
    back = exchange(back)
    in_grad_partner = dot_tn(expert_rows, grad_pre[1]).astype(bf16)
    out_grad_partner = dot_tn(acted[1], cotangent_rows).astype(bf16)
    in_grad_partner, out_grad_partner, acted, grad_pre = tie(
        (in_grad_partner, out_grad_partner, acted, grad_pre)
    )
    in_grad_partner = partner(in_grad_partner)
    outs = expert_outputs(acted, out_parts)
    expert_out_grad = dot_tn(acted[0], cotangent_rows)
    expert_in_grad = dot_tn(expert_rows, grad_pre[0])
    back, outs, expert_out_grad, expert_in_grad = tie(
        (back, outs, expert_out_grad, expert_in_grad)
    )
    combine = (scalars, column_place, info, routes, output_own, back)
    far_logits, *far = combine_grads(True, *combine, (), expert_count, padded)
    arrived = ring_start(*far)
    grad_logits, own, *ring = combine_grads(False, *combine, (far_logits,), expert_count, padded)
    arrived, ring, outs, in_grad_partner = tie((arrived, ring, outs, in_grad_partner))
    ring, outs = (own,) + ring_finish(*ring, *arrived), exchange(outs)
    ring, outs = tie((ring, outs))
    grad_one, grad_branch, gain_two_grad, *grad_heads = norm_back(
        1, True, scalars, residual, gains, cotangent, ring, output_parts
    )
    head_pieces = (
        grad_heads[0], shift(grad_heads[2], 1), shift(grad_heads[1], -1), shift(grad_heads[3], 2)
    )
    outer = output_grads(scalars, grad_branch, attended_here, hidden_two, grad_logits, small)
    mixed = combine_outs(column_place, outs)
    head_pieces, mixed, out_grad_partner, outer = tie(
        (head_pieces, mixed, out_grad_partner, outer)
    )
    if small:
        outer = outer[0], cross(outer[1], 1)
    out_grad_partner = partner(out_grad_partner)
    mixed = lax.all_to_all(mixed, "tensor", split_axis=0, concat_axis=0, tiled=True)
    shared = (scalars, far_bias, token_offsets, queries, made[0], bias_tiles)
    lse = (lse_one, lse_two)
    dout, deltas, dq_t, far_one, far_two, fold = attention_backward(
        (3,), *shared, lse, (packed_one, packed_two, *head_pieces), 4, heads, width
    )
    arrived = cross(far_one, 1), cross(far_two, 2)
    dq_t, *beside_across, fold = attention_backward(
        (1, 2), *shared, lse, (dout, deltas, dq_t, fold), 0, heads, width
    )
    beside, across = beside_across[0:2], beside_across[2:4]
    beside_two, across_one = added(beside[1], arrived[1]), added(across[0], arrived[0])
    dq_t, mixed, beside_two, across_one, outer = tie(
        (dq_t, mixed, beside_two, across_one, outer)
    )
    from_square = (
        (cross(beside[0], 1), cross(beside_two, 1)), (cross(across_one, 2), cross(across[1], 2))
    )
    layer_out = finish(residual, mixed)
    dq_t, layer_out = tie((dq_t, layer_out))
    layer_out = lax.all_to_all(layer_out, "tensor", split_axis=0, concat_axis=0, tiled=True)
    dq_t, own, dq, fold = attention_backward(
        (0,), *shared, lse, (dout, deltas, dq_t, fold), 0, heads, width
    )
    dq, from_square, out_grad_partner = tie((dq, from_square, out_grad_partner))
    dkv, own, *ring = hidden_grad(scalars, dq, weights, own, *from_square)
    arrived = ring_start(*ring[2:4])
    inner_parts = projection_grads(scalars, hidden_one, dq, dkv, gain_two_grad, fold, small)
    if small:
        outer = halve(*outer)
    arrived, inner_parts, outer = tie((arrived, inner_parts, outer))
    inner_parts = swap_sides(inner_parts)
    ring = (own,) + ring_finish(*ring[0:2], *arrived)
    if small:
        outer = halve(outer[0], cross(outer[1], 2))
        outer_grads = outer[0] + swap_sides(outer)[1].astype(f32)
    else:
        outer_grads = lax.psum_scatter(outer[0], ALL_ROWS, scatter_dimension=0, tiled=True)
    ring, layer_out, outer_grads = tie((ring, layer_out, outer_grads))
    _, input_low, _ = norm_back(
        0, False, scalars, tokens_in, gains, grad_one, ring, blocks=outer_grads
    )
    arrived = lax.all_to_all(input_low, "tensor", split_axis=0, concat_axis=0, tiled=True)
    inner_parts, layer_out, input_low = tie((inner_parts, layer_out, input_low))
    layer_out = assemble(jnp.zeros((1,), jnp.int32), [layer_out], bf16)
    projected = scatter_blocks(share_blocks(scalars, inner_parts))
    expert_out_grad, expert_in_grad, projected = tie((expert_out_grad, expert_in_grad, projected))
    input_grad, outer_grads = unpack(arrived, rows, shard)
    expert_out_grad = (expert_out_grad + out_grad_partner.astype(f32))[None]
    expert_in_grad = (expert_in_grad + in_grad_partner.astype(f32))[None]
    output_grad = outer_grads[:, :192].T
    router_grad = outer_grads[:, 192 : 192 + expert_count]
    fold = projected[shard:, :256] if small else lax.psum(fold, ALL_ROWS)
    projected = projected[:shard]
    query_grad, key_grad = projected[:, :192], projected[:, 256:448]
    value_grad = jnp.concatenate([projected[:, 512:], projected[:, 448:512]], axis=1)
    gain_one_grad = jnp.sum(
        query_weight.astype(f32) * query_grad
        + key_weight.astype(f32) * key_grad
        + value_weight.astype(f32) * value_grad,
        axis=1,
        keepdims=True,
    )
    gain_grads = sum_ranks(jnp.concatenate([gain_one_grad, projected[:, 192:193]], axis=1))
    bucket_row = jnp.asarray(bucket_tiles()[0, 0])
    bucket_hot = (bucket_row[None, :] == jnp.arange(bias_table.shape[0] - 1)[:, None]).astype(f32)
    near_grad = jnp.sum(bucket_hot[:, None, :] * fold[None, :heads, :], axis=-1)
    table_grad = jnp.concatenate([near_grad, -jnp.sum(near_grad, axis=0, keepdims=True)], axis=0)
    return (
        layer_out,
        input_grad,
        query_grad,
        key_grad,
        value_grad,
        output_grad,
        table_grad,
        gain_grads[:, 0] / attention_gain.astype(f32),
        router_grad,
        gain_grads[:, 1],
        expert_in_grad,
        expert_out_grad,
    )


def solution(mesh):
    rows = P(("dp", "context"), None)
    return jax.shard_map(
        on_device,
        mesh=mesh,
        in_specs=(
            rows,
            P(("dp", "context"), "tensor"),
            P(("dp", "context"), "tensor"),
            P(("dp", "context"), "tensor"),
            P("tensor", ("dp", "context")),
            P(None, "tensor"),
            P(("dp", "context")),
            rows,
            P(("dp", "context")),
            P(("dp", "context"), None, "tensor"),
            P(("dp", "context"), "tensor", None),
            rows,
            rows,
            P("dp", None),
            rows,
        ),
        out_specs=(
            rows,
            rows,
            P(("dp", "context"), "tensor"),
            P(("dp", "context"), "tensor"),
            P(("dp", "context"), "tensor"),
            P("tensor", ("dp", "context")),
            P(None, "tensor"),
            P(("dp", "context")),
            rows,
            P(("dp", "context")),
            P(("dp", "context"), None, "tensor"),
            P(("dp", "context"), "tensor", None),
        ),
        check_vma=False,
    )
```

```python
import functools
import jax
import jax.numpy as jnp
import numpy as np
from jax import lax
from jax.experimental import pallas as pl
from jax.experimental.pallas import tpu as pltpu
from jax.sharding import PartitionSpec as P

bf16 = jnp.bfloat16
f32 = jnp.float32
epsilon = 1e-06
masked_value = -1e30
tile = 256
VMEM = pl.BlockSpec(memory_space=pltpu.VMEM)
SMEM = pl.BlockSpec(memory_space=pltpu.SMEM)


def dot_nn(a, b):
    return lax.dot_general(a, b, (((1,), (0,)), ((), ())), preferred_element_type=f32)


def dot_nt(a, b):
    return lax.dot_general(a, b, (((1,), (1,)), ((), ())), preferred_element_type=f32)


def dot_tn(a, b):
    return lax.dot_general(a, b, (((0,), (0,)), ((), ())), preferred_element_type=f32)


def start_of(position, first_end, second_end):
    return jnp.where(
        position >= second_end, second_end, jnp.where(position >= first_end, first_end, 0)
    )


def aligned(value, size):
    return pl.multiple_of(value, size)


def transpose_values(source, source_start, values_t, start, width):
    span, target = pl.ds(source_start, tile), pl.ds(start, tile)
    upper = source[span, 256:384].astype(f32).T.astype(bf16)
    lower = source[span, 128:256].astype(f32).T.astype(bf16)
    for head, part in enumerate((upper[0:width], upper[width:], lower[width:])):
        values_t[head, 0:width, target] = part
        values_t[head, width:, target] = jnp.ones((16, tile), bf16)


def masked_heads(queries, heads, width):
    lane = lax.broadcasted_iota(jnp.int32, queries.shape, 1) // width
    return [jnp.where(lane == head, queries, jnp.zeros_like(queries)) for head in range(heads)]


def absorb(
    keys_values, values_t, bias_ref, far_bias, best, running, index, masked_queries, heads,
    key_start, size, key_first, positions, row_start, bias_index, masked, first_time,
):
    keys = keys_values[pl.ds(key_start, size), 0:256]
    if masked:
        key_positions = (
            key_first + key_start + lax.broadcasted_iota(jnp.int32, (size, tile), 0)
        )
        seen = key_positions >= row_start
        if bias_index == 0:
            seen = seen & (key_positions <= positions)
    shift_by = [far_bias[head] if bias_index is None else 0.0 for head in range(heads)]
    scores = [dot_nt(keys, masked_queries[head]) for head in range(heads)]
    if bias_index is not None:
        scores = [scores[head] + bias_ref[bias_index][head] for head in range(heads)]
    if masked:
        scores = [jnp.where(seen, part, masked_value) for part in scores]
    tops = [
        jnp.max(scores[head], axis=0, keepdims=True) + shift_by[head] for head in range(heads)
    ]
    if first_time:
        new = tops
    else:
        old = [best[index, head, 0:1] for head in range(heads)]
        new = [jnp.maximum(old[head], tops[head]) for head in range(heads)]
    weights = [
        jnp.exp(scores[head] - (new[head] - shift_by[head])).astype(bf16) for head in range(heads)
    ]
    sums = [
        dot_nn(values_t[head, :, pl.ds(key_start, size)], weights[head]) for head in range(heads)
    ]
    for head in range(heads):
        if first_time:
            running[index, head] = sums[head]
        else:
            running[index, head] = running[index, head] * jnp.exp(old[head] - new[head]) + sums[head]
        best[index, head] = jnp.broadcast_to(new[head], (8, tile))


def attention_near_kernel(
    heads, width, scalars, far_bias, query_ref, bias_own, bias_next, keys_values, running, best,
    values_t,
):
    rows = query_ref.shape[0]
    context, first_end, second_end = scalars[0], scalars[1], scalars[2]
    base = context * rows

    def values_step(index, carry):
        start = aligned(index * tile, tile)
        transpose_values(keys_values, start, values_t, start, width)
        return carry

    lax.fori_loop(0, rows // tile, values_step, 0)

    def query_tile(index, carry):
        local = aligned(index * tile, tile)
        positions = base + local + lax.broadcasted_iota(jnp.int32, (1, tile), 1)
        row_start = start_of(positions, first_end, second_end)
        masked_queries = masked_heads(query_ref[pl.ds(local, tile), :], heads, width)

        def take(key_start, bias_index, first_time):
            absorb(
                keys_values, values_t, (bias_own, bias_next), far_bias, best, running, index,
                masked_queries, heads, key_start, tile, base, positions, row_start, bias_index,
                True, first_time,
            )

        take(local, 0, True)

        @pl.when(index > 0)
        def _():
            take(aligned(local - tile, tile), 1, False)

        def far_step(step, inner):
            take(aligned(step * tile, tile), None, False)
            return inner

        lax.fori_loop(0, jnp.maximum(index - 1, 0), far_step, 0)
        return carry

    lax.fori_loop(0, rows // tile, query_tile, 0)


def attention_near(scalars, far_bias, queries, bias_own, bias_next, keys_values, heads, width):
    rows = queries.shape[0]
    tiles = rows // tile
    return pl.pallas_call(
        functools.partial(attention_near_kernel, heads, width),
        out_shape=(
            jax.ShapeDtypeStruct((tiles, heads, width + 16, tile), f32),
            jax.ShapeDtypeStruct((tiles, heads, 8, tile), f32),
        ),
        in_specs=[SMEM, SMEM] + [VMEM] * 4,
        out_specs=(VMEM,) * 2,
        scratch_shapes=[pltpu.VMEM((heads, width + 16, rows), bf16)],
        compiler_params=pltpu.CompilerParams(vmem_limit_bytes=40 * 2**20),
        cost_estimate=pl.CostEstimate(
            flops=2 * rows * rows * 256 * heads,
            bytes_accessed=4 * 2**20,
            transcendentals=rows * rows * heads // 2,
        ),
        name="attention_near",
    )(scalars, far_bias, queries, bias_own, bias_next, keys_values)


def attention_far_kernel(
    heads, width, piece_count, scalars, far_bias, offsets, query_ref, running_in, best_in,
    bias_next, *rest
):
    pieces = rest[:piece_count]
    packed, lse_ref, keys_values, values_t, running, best, side_one, side_two = rest[piece_count:]
    rows = query_ref.shape[0]
    half, quarter = rows // 2, rows // 4
    context, first_end, second_end = scalars[0], scalars[1], scalars[2]
    base = context * rows
    for index, piece in enumerate(pieces):
        size = piece.shape[0]
        keys_values[pl.ds(aligned(offsets[index], 128), size), :] = piece[...]

    def values_step(index, carry):
        start = aligned(index * tile, tile)
        transpose_values(keys_values, start, values_t, start, width)
        return carry

    lax.fori_loop(0, context * (rows // tile), values_step, 0)
    running[...] = running_in[...]
    best[...] = best_in[...]

    def query_tile(index, carry):
        local = aligned(index * tile, tile)
        first = base + local
        positions = first + lax.broadcasted_iota(jnp.int32, (1, tile), 1)
        row_start = start_of(positions, first_end, second_end)
        start_first = start_of(first, first_end, second_end)
        start_last = start_of(first + tile - 1, first_end, second_end)
        masked_queries = masked_heads(query_ref[pl.ds(local, tile), :], heads, width)

        def take(key_start, size, bias_index, masked):
            absorb(
                keys_values, values_t, (None, bias_next), far_bias, best, running, index,
                masked_queries, heads, key_start, size, 0, positions, row_start, bias_index,
                masked, False,
            )

        far_rows = jnp.where(index == 0, jnp.maximum(base - tile, 0), base)

        @pl.when((index == 0) & (context > 0))
        def _():
            take(aligned(base - tile, tile), tile, 1, True)

        big = 4 * tile
        big_count = far_rows // big
        low = jnp.minimum(start_first // big, big_count)
        middle = jnp.clip((start_last + big - 1) // big, low, big_count)

        def masked_step(step, inner):
            take(aligned(step * big, big), big, None, True)
            return inner

        def plain_step(step, inner):
            take(aligned(step * big, big), big, None, False)
            return inner

        lax.fori_loop(low, middle, masked_step, 0)
        lax.fori_loop(middle, big_count, plain_step, 0)

        def small_step(step, inner):
            take(aligned(step * tile, tile), tile, None, True)
            return inner

        lax.fori_loop(big_count * 4, far_rows // tile, small_step, 0)
        outs = []
        for head in range(heads):
            total = running[index, head, width : width + 1]
            outs.append(running[index, head, 0:width] / total)
            lse_ref[pl.ds(head, 1), pl.ds(aligned(index * tile, tile), tile)] = best[
                index, head, 0:1
            ] + jnp.log(total)
        span = pl.ds(aligned(index * tile, tile), tile)
        side_one[span, :] = jnp.concatenate([outs[0], outs[1]], axis=0).T
        side_two[span, :] = jnp.concatenate([outs[2], outs[2]], axis=0).T
        return carry

    lax.fori_loop(0, rows // tile, query_tile, 0)
    lane = lax.broadcasted_iota(jnp.int32, (quarter, 128), 1)
    for part in range(2):
        target = slice(part * quarter, (part + 1) * quarter)
        first_rows = slice(part * half, part * half + quarter)
        last_rows = slice(part * half + quarter, (part + 1) * half)
        packed[target, 0:128] = side_one[first_rows, :].astype(bf16)
        packed[target, 128:256] = jnp.where(
            lane < width, side_two[first_rows, :], side_two[last_rows, :]
        ).astype(bf16)
        packed[target, 256:384] = side_one[last_rows, :].astype(bf16)


def attention_far(
    scalars, far_bias, offsets, queries, bias_next, state, pieces, group_rows, heads, width
):
    rows = queries.shape[0]
    shape = jax.ShapeDtypeStruct
    return pl.pallas_call(
        functools.partial(attention_far_kernel, heads, width, len(pieces)),
        out_shape=(shape((rows // 2, 384), bf16), shape((8, rows), f32)),
        in_specs=[SMEM, SMEM, SMEM] + [VMEM] * (4 + len(pieces)),
        out_specs=(VMEM,) * 2,
        scratch_shapes=[
            pltpu.VMEM((group_rows, 384), bf16),
            pltpu.VMEM((heads, width + 16, group_rows), bf16),
            pltpu.VMEM((rows // tile, heads, width + 16, tile), f32),
            pltpu.VMEM((rows // tile, heads, 8, tile), f32),
            pltpu.VMEM((rows, 128), f32),
            pltpu.VMEM((rows, 128), f32),
        ],
        compiler_params=pltpu.CompilerParams(vmem_limit_bytes=60 * 2**20),
        cost_estimate=pl.CostEstimate(
            flops=4 * rows * group_rows * 256 * heads,
            bytes_accessed=8 * 2**20,
            transcendentals=rows * group_rows * heads,
        ),
        name="attention_far",
    )(scalars, far_bias, offsets, queries, *state, bias_next, *pieces)


def attention_backward_kernel(heads, width, masks, piece_count, scalars, far_bias, offsets, *rest):
    first_call, last_call = masks[0] == 3, masks[0] == 0
    block_count = 2 if first_call else len(masks)
    blocks, rest = rest[:block_count], rest[block_count:]
    query_ref, lse_ref, bias_next = rest[0:3]
    rest = rest[3:]
    bias_own = None
    if last_call:
        bias_own, rest = rest[0], rest[1:]
    bias_ref = (bias_own, bias_next)
    if first_call:
        packed_ref = rest[0]
        pieces = rest[1 : 1 + piece_count]
        rest = rest[1 + piece_count :]
        dout, deltas, dq_t = rest[0:3]
        rest = rest[3:]
    else:
        dout, deltas, dq_in, fold_in = rest[0:4]
        dq_t = rest[4]
        rest = rest[5:]
    out_count = 1 if last_call else 2 * len(masks)
    outs, rest = rest[:out_count], rest[out_count:]
    if last_call:
        dq_ref, rest = rest[0], rest[1:]
    fold_ref, masked_q, masked_o, keys_t, dkv, band_ref, keys_values, semaphores = rest
    copies = []
    for place, block_ref in enumerate(blocks):
        target = keys_values.at[place]
        if first_call:
            size = block_ref.shape[0]
            target = keys_values.at[0, pl.ds(place * size, size), :]
        copies.append(pltpu.make_async_copy(block_ref, target, semaphores.at[place]))
        copies[-1].start()
    rows = query_ref.shape[0]
    half, quarter = rows // 2, rows // 4
    context, first_end, second_end = scalars[0], scalars[1], scalars[2]
    tiles_here = rows // tile
    if first_call:
        for index, piece in enumerate(pieces):
            span = pl.ds(aligned(offsets[index], 128), piece.shape[0])
            dout[span, 0:128] = pltpu.roll(piece[:, 128:256].astype(f32), width, 1).astype(bf16)
            dout[span, 128:256] = piece[:, 0:128]
        head_row = lax.broadcasted_iota(jnp.int32, (16, 256), 0)
        head_lane = lax.broadcasted_iota(jnp.int32, (16, 256), 1) // width
        head_hot = (head_row == jnp.where(head_lane == 1, 2, head_lane - 2)).astype(bf16)
        for part in range(4):
            span = slice(part * quarter, (part + 1) * quarter)
            packed = packed_ref[part // 2 * quarter : (part // 2 + 1) * quarter, :]
            lower = packed[:, 128:256].astype(f32)
            if part % 2 == 0:
                upper, lower = packed[:, 0:128], pltpu.roll(lower, width, 1)
            else:
                upper = packed[:, 256:384]
            product = dout[span, :].astype(f32) * jnp.concatenate(
                [lower, upper.astype(f32)], axis=1
            )
            high = product.astype(bf16)
            rest_part = (product - high.astype(f32)).astype(bf16)
            deltas[:, span] = dot_nt(head_hot, high) + dot_nt(head_hot, rest_part)
        dq_t[...] = jnp.zeros_like(dq_t)
        fold_ref[...] = jnp.zeros_like(fold_ref)
    else:
        dq_t[...] = dq_in[...]
        fold_ref[...] = fold_in[...]
    lane = lax.broadcasted_iota(jnp.int32, (rows, 256), 1) // width
    for head in range(heads):
        masked_q[head] = jnp.where(lane == head, query_ref[...], jnp.zeros((rows, 256), bf16))
        slot = 1 if head == 2 else head + 2
        masked_o[head] = jnp.where(lane == slot, dout[...], jnp.zeros((rows, 256), bf16))
    first = context * rows
    all_positions = first + lax.broadcasted_iota(jnp.int32, (1, rows), 1)
    all_starts = start_of(all_positions, first_end, second_end)
    start_first = start_of(first, first_end, second_end)
    start_last = start_of(first + rows - 1, first_end, second_end)


    def block(place, key_start, base, query_start, bands, masked):
        size = rows - query_start
        here = pl.ds(aligned(key_start - base, tile), tile)
        keys = keys_values[place, here, 0:256]
        values = keys_values[place, here, 128:384]
        key_sum, value_sum = None, None
        if masked:
            key_positions = key_start + lax.broadcasted_iota(jnp.int32, (tile, size), 0)
            seen = key_positions >= all_starts[:, query_start:]
            if 0 in bands:
                seen = seen & (key_positions <= all_positions[:, query_start:])
        span = slice(query_start, rows)
        every = range(heads)
        queries = [masked_q[head, span, :] for head in every]
        grads = [masked_o[head, span, :] for head in every]
        scores = [dot_nt(keys, queries[head]) for head in every]
        grad_probs = [dot_nt(values, grads[head]) for head in every]
        lse = [lse_ref[head : head + 1, span] for head in every]
        if bands:
            for head in every:
                parts = [
                    scores[head][:, at * tile : (at + 1) * tile] + bias_ref[band][head]
                    for at, band in enumerate(bands)
                ]
                if size > len(bands) * tile:
                    parts.append(scores[head][:, len(bands) * tile :] + far_bias[head])
                scores[head] = jnp.concatenate(parts, axis=1)
        else:
            lse = [lse[head] - far_bias[head] for head in every]
        probs = [jnp.exp(scores[head] - lse[head]) for head in every]
        if masked:
            probs = [jnp.where(seen, part, 0.0) for part in probs]
        grad_scores = [
            probs[head] * (grad_probs[head] - deltas[head : head + 1, span]) for head in every
        ]
        for head in every:
            for at, band in enumerate(bands):
                band_ref[band, head] += grad_scores[head][:, at * tile : (at + 1) * tile]
        low_scores = [part.astype(bf16) for part in grad_scores]
        low_probs = [part.astype(bf16) for part in probs]
        for head in every:
            value_part = dot_nn(low_probs[head], grads[head])
            key_part = dot_nn(low_scores[head], queries[head])
            dq_t[head, :, span] += dot_nn(keys_t[head, :, here], low_scores[head])
            key_sum = key_part if key_sum is None else key_sum + key_part
            value_sum = value_part if value_sum is None else value_sum + value_part
        return key_sum, value_sum

    lane_tile = lax.broadcasted_iota(jnp.int32, (tile, 128), 1)

    def write(local, key_sum, value_sum):
        span = pl.ds(local, tile)
        dkv[span, 0:128] = key_sum[:, 0:128].astype(bf16)
        dkv[span, 128:256] = jnp.where(
            lane_tile < width, key_sum[:, 128:256], value_sum[:, 0:128]
        ).astype(bf16)
        dkv[span, 256:384] = value_sum[:, 128:256].astype(bf16)

    near = jnp.bool_(last_call)
    for mask in masks:
        near = near | ((context ^ mask) == context - 1)

    @pl.when(near)
    def _():
        band_ref[...] = jnp.zeros_like(band_ref)

    for place, mask in enumerate(masks):
        which = context ^ mask
        base = aligned(which * rows, rows)
        for copy in copies if first_call else copies[place : place + 1]:
            copy.wait()

        @pl.when((which > context) | (start_first > base))
        def _():
            dkv[...] = jnp.zeros_like(dkv)

        @pl.when(which <= context)
        def _():
            def transpose_keys(index, carry):
                target = pl.ds(aligned(index * tile, tile), tile)
                lower = keys_values[place, target, 0:128].astype(f32).T.astype(bf16)
                upper = keys_values[place, target, 128:256].astype(f32).T.astype(bf16)
                keys_t[0, :, target] = lower[0:width]
                keys_t[1, :, target] = lower[width:]
                keys_t[2, :, target] = upper[0:width]
                return carry

            lax.fori_loop(0, tiles_here, transpose_keys, 0)
            low_tile = which * tiles_here
            high_tile = low_tile + tiles_here
            if mask:
                far_end = jnp.minimum(high_tile, context * tiles_here - 1)
                low = jnp.clip(start_first // tile, low_tile, far_end)
                middle = jnp.clip((start_last + tile - 1) // tile, low, far_end)

                def masked_step(index, carry):
                    start = aligned(index * tile, tile)
                    found = block(place, start, base, 0, (), True)
                    write(aligned(start - base, tile), *found)
                    return carry

                def plain_step(index, carry):
                    start = aligned(index * tile, tile)
                    found = block(place, start, base, 0, (), False)
                    write(aligned(start - base, tile), *found)
                    return carry

                lax.fori_loop(low, middle, masked_step, 0)
                lax.fori_loop(middle, far_end, plain_step, 0)

                @pl.when(far_end < high_tile)
                def _():
                    start = aligned(far_end * tile, tile)
                    write(aligned(start - base, tile), *block(place, start, base, 0, (1,), True))

            else:
                for index in range(tiles_here):
                    start = aligned(base + index * tile, tile)
                    bands = (0, 1) if index + 1 < tiles_here else (0,)
                    write(index * tile, *block(place, start, base, index * tile, bands, True))

        if mask:
            outs[2 * place][...] = dkv[0:half, :]
            outs[2 * place + 1][...] = dkv[half:, :]
        else:
            outs[0][...] = dkv[...]

    @pl.when(near)
    def _():
        key_index = lax.broadcasted_iota(jnp.int32, (tile, tile), 0)
        query_index = lax.broadcasted_iota(jnp.int32, (tile, tile), 1)
        for head in range(heads):
            both = jnp.where(key_index > query_index, band_ref[1, head], band_ref[0, head])
            by_row = both[0:8]
            for first_row in range(8, tile, 8):
                by_row = by_row + pltpu.roll(both[first_row : first_row + 8], tile - first_row, 1)
            folded = by_row[0:1]
            for row in range(1, 8):
                folded = folded + pltpu.roll(by_row, tile - row, 1)[row : row + 1]
            fold_ref[head : head + 1, :] += folded

    if last_call:
        scale = width ** (-0.5)
        upper = jnp.concatenate([dq_t[0], dq_t[1]], axis=0)
        lower = jnp.concatenate([dq_t[2], jnp.zeros((width, rows), f32)], axis=0)
        dq_ref[:, 0:128] = (upper.T * scale).astype(bf16)
        dq_ref[:, 128:256] = (lower.T * scale).astype(bf16)


def attention_backward(
    masks, scalars, far_bias, offsets, queries, bias_own, bias_next, lse, blocks, given,
    piece_count, heads, width,
):
    rows = queries.shape[0]
    half = rows // 2
    shape = jax.ShapeDtypeStruct
    first_call, last_call = masks[0] == 3, masks[0] == 0
    if last_call:
        given = (bias_own,) + tuple(given)
    outs = (shape((heads, width, rows), f32),)
    if first_call:
        outs = (shape((rows, 256), bf16), shape((16, rows), f32)) + outs
    if last_call:
        outs = outs + (shape((rows, 384), bf16),)
    else:
        outs = outs + (shape((half, 384), bf16),) * (2 * len(masks))
    if last_call:
        outs = outs + (shape((rows, 256), bf16),)
    outs = outs + (shape((8, tile), f32),)

    return pl.pallas_call(
        functools.partial(attention_backward_kernel, heads, width, masks, piece_count),
        out_shape=outs,
        in_specs=[SMEM, SMEM, SMEM]
        + [pl.BlockSpec(memory_space=pl.ANY)] * len(blocks)
        + [VMEM] * (3 + len(given)),
        out_specs=(VMEM,) * len(outs),
        scratch_shapes=[
            pltpu.VMEM((heads, rows, 256), bf16),
            pltpu.VMEM((heads, rows, 256), bf16),
            pltpu.VMEM((heads, width, rows), bf16),
            pltpu.VMEM((rows, 384), bf16),
            pltpu.VMEM((2, heads, tile, tile), f32),
            pltpu.VMEM((len(masks), rows, 384), bf16),
            pltpu.SemaphoreType.DMA((len(blocks),)),
        ],
        compiler_params=pltpu.CompilerParams(vmem_limit_bytes=60 * 2**20),
        cost_estimate=pl.CostEstimate(
            flops=10 * rows * rows * 256 * heads if first_call else 0,
            bytes_accessed=10 * 2**20 if first_call else 2**10,
            transcendentals=0,
        ),
        name="attention_backward",
    )(scalars, far_bias, offsets, *blocks, queries, lse, bias_next, *given)


bucket_edges = np.array(
    [19, 21, 24, 27, 31, 35, 40, 46, 52, 59, 67, 77, 87, 99, 113], dtype=np.int32
)


def bucket_tiles():
    key = np.arange(tile)[None, :, None]
    query = np.arange(tile)[None, None, :]
    lag = np.arange(3)[:, None, None] * tile + query - key
    clipped = np.maximum(lag, 0)
    counted = (clipped[..., None] >= bucket_edges).sum(-1)
    return np.where(clipped < 16, clipped, 16 + counted).astype(np.int32)


def shape(dims, dtype):
    return jax.ShapeDtypeStruct(dims, dtype)


def params(mebibytes):
    return pltpu.CompilerParams(vmem_limit_bytes=mebibytes * 2**20)


def cost(flops, bytes_accessed):
    return pl.CostEstimate(flops=flops, bytes_accessed=bytes_accessed, transcendentals=0)


def gelu_constants():
    return 0.7978845608028654, 0.044715


def prepare_kernel(
    part, padded, scalars, table, route_ref, order_ref, rows_ref, columns_ref,
    bias_own, bias_next, ranks, hot_ref, tall,
):
    pair_count = order_ref.shape[1]
    rows = pair_count // 2
    expert_pad = hot_ref.shape[0]
    step = 256
    live_end = scalars[2] - scalars[0] * rows
    order = order_ref[...]
    index_row = lax.broadcasted_iota(jnp.int32, (pair_count, 128), 0)
    index_lane = lax.broadcasted_iota(jnp.int32, (pair_count, 128), 1)
    digits = jnp.where(
        index_lane == 0, index_row // 64, jnp.where(index_lane == 1, index_row % 64, 0)
    ).astype(f32).astype(bf16)

    def rank_step(index, carry):
        start = aligned(index * step, step)
        pair = start + lax.broadcasted_iota(jnp.int32, (step, pair_count), 0)
        hit = (pair == order).astype(f32).astype(bf16)
        found = dot_nn(hit, digits)
        position = found[:, 0:1] * 64.0 + found[:, 1:2]
        ranks[pl.ds(start, step), :] = jnp.broadcast_to(position, (step, 128))
        return carry

    lax.fori_loop(0, pair_count // step, rank_step, 0)
    rank_row = ranks[...].T[0:1, :]
    position = lax.broadcasted_iota(jnp.int32, (1, rows), 1)
    live = position < live_end
    expert_row = jnp.concatenate([route_ref[0:1, :], route_ref[1:2, :]], axis=1)
    live_row = jnp.concatenate([live, live], axis=1)
    expert_index = lax.broadcasted_iota(jnp.int32, (expert_pad, pair_count), 0)
    hot = ((expert_index == expert_row) & live_row).astype(f32)
    hot_ref[...] = hot.astype(bf16)

    def count_step(index, counts):
        start = aligned(index * step, step)
        earlier = (ranks[pl.ds(start, step), 0:1] < rank_row).astype(f32).astype(bf16)
        return counts + dot_nn(hot_ref[:, pl.ds(start, step)], earlier)

    counts = lax.fori_loop(
        0, pair_count // step, count_step, jnp.zeros((expert_pad, pair_count), f32)
    )
    slot = jnp.sum(counts * hot, axis=0, keepdims=True).astype(jnp.int32)
    own = slot - (scalars[3] & 1) * part
    place = jnp.where(live_row & (own >= 0) & (own < part), expert_row * padded + own, -1)
    rows_ref[...] = jnp.full_like(rows_ref, -1)
    rows_ref[0:1, :] = place[:, 0:rows]
    rows_ref[1:2, :] = place[:, rows:]
    tall[...] = jnp.full_like(tall, -1.0)
    tall[0:1, :] = place[:, 0:rows].astype(f32)
    tall[1:2, :] = place[:, rows:].astype(f32)
    columns_ref[...] = tall[...].T.astype(jnp.int32)
    key = lax.broadcasted_iota(jnp.int32, (8, tile), 0)
    query = lax.broadcasted_iota(jnp.int32, (8, tile), 1)
    heads = bias_own.shape[0]

    def bias_step(index, carry):
        start = aligned(index * 8, 8)
        for band, bias_ref in enumerate((bias_own, bias_next)):
            lag = band * tile + query - key - start
            found = [jnp.full((8, tile), table[0, head], f32) for head in range(heads)]
            for bucket, edge in enumerate(list(range(1, 17)) + list(bucket_edges), start=1):
                beyond = lag >= int(edge)
                found = [
                    jnp.where(beyond, table[bucket, head], found[head]) for head in range(heads)
                ]
            for head in range(heads):
                bias_ref[head, pl.ds(start, 8), :] = found[head]
        return carry

    lax.fori_loop(0, tile // 8, bias_step, 0)


def prepare(scalars, table, route_rows, order_row, expert_count, part, padded):
    rows = route_rows.shape[1]
    heads = table.shape[1]
    expert_pad = max(16, expert_count)
    return pl.pallas_call(
        functools.partial(prepare_kernel, part, padded),
        out_shape=(
            shape((8, rows), jnp.int32),
            shape((rows, 128), jnp.int32),
            shape((heads, tile, tile), f32),
            shape((heads, tile, tile), f32),
        ),
        in_specs=[SMEM, SMEM, VMEM, VMEM],
        out_specs=(VMEM,) * 4,
        scratch_shapes=[
            pltpu.VMEM((2 * rows, 128), f32),
            pltpu.VMEM((expert_pad, 2 * rows), bf16),
            pltpu.VMEM((128, rows), f32),
        ],
        compiler_params=params(40),
        cost_estimate=cost(10 * 10**9, 3 * 2**20),
        name="prepare",
    )(scalars, table, route_rows, order_row)


def pack_kernel(query, key, value, output, gain_one, gain_two, router, block):
    size = query.shape[0]
    experts = router.shape[1]
    block[...] = jnp.zeros_like(block)
    block[:, 0:192] = query[...]
    gains = jnp.concatenate([gain_one[...], gain_two[...]], axis=0).astype(f32)
    block[:, 192:194] = gains.T.astype(bf16)
    block[:, 256:448] = key[...]
    block[:, 448:512] = value[:, 128:192]
    block[:, 512:640] = value[:, 0:128]
    block[:, 640:832] = output[...].astype(f32).T.astype(bf16)
    block[:, 832 : 832 + experts] = router[...]


def pack_weights(query, key, value, output, gain_one, gain_two, router):
    size = query.shape[0]
    return pl.pallas_call(
        pack_kernel,
        out_shape=shape((size, 896), bf16),
        in_specs=[VMEM] * 7,
        out_specs=VMEM,
        compiler_params=params(60),
        cost_estimate=cost(0, 2**19),
        name="pack_weights",
    )(query, key, value, output, gain_one[None], gain_two[None], router)


def project_kernel(piece_count, offsets, token_ref, *rest):
    pieces = rest[:piece_count]
    hidden_ref, query_ref, kv_ref, weight_ref, output_ref, gain_ref = rest[piece_count:]
    for index, piece in enumerate(pieces):
        span = pl.ds(aligned(offsets[index], 16), piece.shape[0])
        weight_ref[span, :] = piece[:, 0:640]
        output_ref[span, :] = piece[:, 640:896]
    rows = token_ref.shape[0]
    gains = weight_ref[:, 128:256].astype(f32).T
    gain_ref[0:1, :] = gains[64:65, :]
    gain_ref[1:2, :] = gains[65:66, :]
    step = 256
    lane = lax.broadcasted_iota(jnp.int32, (step, 256), 1)
    for start in range(0, rows, step):
        inputs = token_ref[start : start + step, :].astype(f32)
        scale = lax.rsqrt(jnp.mean(inputs * inputs, axis=-1, keepdims=True) + epsilon)
        hidden = (inputs * scale * gain_ref[0:1, :]).astype(bf16)
        hidden_ref[start : start + step, :] = hidden
        queries = dot_nn(hidden, weight_ref[:, 0:256]).astype(bf16)
        query_ref[start : start + step, :] = jnp.where(
            lane < 192, queries * bf16(0.125), jnp.zeros_like(queries)
        )
        kv_ref[start : start + step, :] = dot_nn(hidden, weight_ref[:, 256:640]).astype(bf16)


def project(offsets, tokens, pieces):
    rows, model = tokens.shape
    return pl.pallas_call(
        functools.partial(project_kernel, len(pieces)),
        out_shape=(
            shape((rows, model), bf16),
            shape((rows, 256), bf16),
            shape((rows, 384), bf16),
            shape((model, 640), bf16),
            shape((model, 256), bf16),
            shape((8, model), f32),
        ),
        in_specs=[SMEM, VMEM] + [VMEM] * len(pieces),
        out_specs=(VMEM,) * 6,
        compiler_params=params(40),
        cost_estimate=cost(2 * rows * model * 640, 6 * 2**20),
        name="project",
    )(offsets, tokens, *pieces)


def assemble_kernel(piece_count, offsets, *rest):
    pieces = rest[:piece_count]
    out_ref = rest[piece_count]
    for index, piece in enumerate(pieces):
        size = piece.shape[0]
        out_ref[pl.ds(aligned(offsets[index], 16), size), :] = piece[...].astype(out_ref.dtype)


def assemble(offsets, pieces, dtype):
    total = sum(piece.shape[0] for piece in pieces)
    width = pieces[0].shape[1]
    return pl.pallas_call(
        functools.partial(assemble_kernel, len(pieces)),
        out_shape=shape((total, width), dtype),
        in_specs=[SMEM] + [VMEM] * len(pieces),
        out_specs=VMEM,
        compiler_params=params(40),
        cost_estimate=cost(0, 6 * total * width),
        name="assemble",
    )(offsets, *pieces)


def route_half(
    width, expert_count, part, token_ref, gain_ref, route_ref, attended, weights, packed, joined,
    hidden_ref, info_ref,
):
    half = packed.shape[1]
    quarter = half // 2
    lane_low = lax.broadcasted_iota(jnp.int32, (quarter, 128), 1)
    for source in range(4):
        piece = attended[source]
        middle = piece[:, 128:256].astype(f32)
        packed[source, 0:quarter, 0:128] = piece[:, 0:128]
        packed[source, 0:quarter, 128:256] = jnp.where(lane_low < width, middle, 0.0).astype(bf16)
        packed[source, quarter:, 0:128] = piece[:, 256:384]
        packed[source, quarter:, 128:256] = jnp.where(
            lane_low < width, pltpu.roll(middle, 64, 1), 0.0
        ).astype(bf16)
    step = quarter
    lane = lax.broadcasted_iota(jnp.int32, (step, 128), 1)
    valid = (lane >= 64) & (lane < 64 + expert_count)

    def token_step(index, carry):
        span = pl.ds(aligned(index * step, step), step)
        where = pl.ds(aligned(part * half + index * step, step), step)
        residual = token_ref[where, :].astype(f32)
        for source in range(4):
            residual = residual + dot_nt(packed[source, span, :], weights[source][...])
        joined[span, :] = residual
        scale = lax.rsqrt(jnp.mean(residual * residual, axis=-1, keepdims=True) + epsilon)
        hidden = (residual * scale * gain_ref[1:2, :]).astype(bf16)
        hidden_ref[span, :] = hidden
        logits = dot_nn(hidden, weights[0][:, 128:256])
        logits = jnp.where(valid, logits, masked_value)
        powers = jnp.where(valid, jnp.exp(logits - jnp.max(logits, axis=-1, keepdims=True)), 0.0)
        probs = powers / jnp.sum(powers, axis=-1, keepdims=True)
        first = jnp.sum(
            jnp.where(lane == route_ref[where, 0:1] + 64, probs, 0.0), axis=-1, keepdims=True
        )
        second = jnp.sum(
            jnp.where(lane == route_ref[where, 1:2] + 64, probs, 0.0), axis=-1, keepdims=True
        )
        total = first + second
        info_ref[span, :] = jnp.where(
            lane == 0,
            first / total,
            jnp.where(lane == 1, second / total, jnp.where(lane == 2, total, probs)),
        )
        return carry

    lax.fori_loop(0, half // step, token_step, 0)


def dispatch_kernel(
    width, expert_count, padded, scalars, token_ref, gain_ref, route_ref, row_place, *rest
):
    attended, weights = rest[0:4], rest[4:8]
    residual_ref, hidden_ref, info_ref, attended_ref, sent = rest[8:13]
    packed, joined, column = rest[13:]
    rows, model = token_ref.shape
    half, quarter = rows // 2, rows // 4
    for part in range(2):
        span = pl.ds(part * half, half)
        route_half(
            width, expert_count, part, token_ref, gain_ref, route_ref,
            [piece.at[pl.ds(part * quarter, quarter), :] for piece in attended], weights,
            packed.at[part], joined.at[span, :], hidden_ref.at[span, :], info_ref.at[span, :],
        )
    rank = scalars[3]
    here = aligned(lax.rem(rank, 2) * quarter, quarter)
    residual_ref[...] = joined[pl.ds(aligned(rank * quarter, quarter), quarter), :]
    for source in range(4):
        attended_ref[:, source * 256 : (source + 1) * 256] = packed[
            rank // 2, source, pl.ds(here, quarter), :
        ]
    gates = info_ref[...].T
    gate_one, gate_two = gates[0:1, :], gates[1:2, :]
    place_one, place_two = row_place[0:1, :], row_place[1:2, :]
    column[...] = jnp.zeros_like(column)

    taken = 4 * padded

    def expert_rows(index, carry):
        start = aligned(index * taken, 64)
        slot = start + lax.broadcasted_iota(jnp.int32, (taken, rows), 0)
        hit_one, hit_two = slot == place_one, slot == place_two
        picked = jnp.where(hit_one | hit_two, 1.0, 0.0).astype(bf16)
        sent[pl.ds(start, taken), :] = dot_nn(picked, hidden_ref[...]).astype(bf16)
        gate = jnp.where(hit_one, gate_one, jnp.where(hit_two, gate_two, 0.0))
        gate = jnp.sum(gate, axis=-1, keepdims=True)
        for chunk in range(4):
            write_digits(
                sent, column, start + chunk * padded, padded,
                gate[chunk * padded : (chunk + 1) * padded],
            )
        return carry

    lax.fori_loop(0, expert_count // 4, expert_rows, 0)


def write_digits(rows_ref, column, start, padded, values):
    column[0:padded, :] = jnp.broadcast_to(values, (padded, 128))
    row = column[...].T[0:1, :]
    high = row.astype(bf16).astype(f32)
    middle = (row - high).astype(bf16).astype(f32)
    low = row - high - middle
    size = row.shape[1]
    index = lax.broadcasted_iota(jnp.int32, (16, size), 0)
    block = jnp.where(
        index == 0, high, jnp.where(index == 1, middle, jnp.where(index == 2, low, 0.0))
    )
    span = pl.ds(aligned(start + padded - 16, 16), 16)
    rows_ref[span, 0:size] = block.astype(bf16)
    rows_ref[span, size:] = jnp.zeros((16, rows_ref.shape[1] - size), bf16)


def read_digits(rows_ref, start, padded):
    wide = (padded + 127) // 128 * 128
    span = pl.ds(aligned(start + padded - 16, 16), 16)
    return jnp.sum(rows_ref[span, 0:wide].astype(f32), axis=0, keepdims=True)


def dispatch(
    scalars, tokens, gains, routes, row_place, attended, weights, width, expert_count, padded
):
    rows, model = tokens.shape
    slots = expert_count * padded
    wide = (padded + 127) // 128 * 128
    return pl.pallas_call(
        functools.partial(dispatch_kernel, width, expert_count, padded),
        out_shape=(
            shape((rows // 4, model), f32),
            shape((rows, model), bf16),
            shape((rows, 128), f32),
            shape((rows // 4, 1024), bf16),
            shape((slots, model), bf16),
        ),
        in_specs=[SMEM] + [VMEM] * 12,
        out_specs=(VMEM,) * 5,
        scratch_shapes=[
            pltpu.VMEM((2, 4, rows // 2, 256), bf16),
            pltpu.VMEM((rows, model), f32),
            pltpu.VMEM((wide, 128), f32),
        ],
        compiler_params=params(60),
        cost_estimate=cost(2 * rows * model * (1024 + slots), 16 * 2**20),
        name="dispatch",
    )(scalars, tokens, gains, routes, row_place, *attended, *weights)


def scatter_kernel(value_ref, row_place, sent):
    rows = value_ref.shape[0]
    place_one, place_two = row_place[0:1, :], row_place[1:2, :]
    fill = sent.shape[0] // 2

    def slot_step(index, carry):
        start = aligned(index * fill, fill)
        slot = start + lax.broadcasted_iota(jnp.int32, (fill, rows), 0)
        picked = jnp.where((slot == place_one) | (slot == place_two), 1.0, 0.0).astype(bf16)
        sent[pl.ds(start, fill), :] = dot_nn(picked, value_ref[...]).astype(bf16)
        return carry

    lax.fori_loop(0, sent.shape[0] // fill, slot_step, 0)


def scatter_rows(values, row_place, slots):
    rows, model = values.shape
    return pl.pallas_call(
        scatter_kernel,
        out_shape=shape((slots, model), bf16),
        in_specs=[VMEM, VMEM],
        out_specs=VMEM,
        compiler_params=params(40),
        cost_estimate=cost(2 * rows * model * slots, 6 * 2**20),
        name="scatter_rows",
    )(values, row_place)


def expert_kernel(
    padded, in_own, in_partner, out_own, out_first, out_second, rows_ref, grads_ref, acted_ref,
    pre_ref, back_ref, column, gate_ref,
):
    hidden = in_own.shape[1]
    root, cubic = gelu_constants()
    wide = column.shape[0]
    column[...] = jnp.zeros_like(column)
    slots = rows_ref.shape[0]
    taken = 4 * padded

    def one(index, carry):
        start = aligned(index * taken, 64)
        span = pl.ds(start, taken)
        for chunk in range(4):
            gates = read_digits(rows_ref, start + chunk * padded, padded)
            gates = jnp.broadcast_to(gates, (128, wide)).T[0:padded, :]
            gate_ref[chunk * padded : (chunk + 1) * padded, :] = gates
        gate = jnp.concatenate([gate_ref[...], gate_ref[...]], axis=1)
        gate_part = None
        cut = out_first.shape[0]
        for side, in_ref in enumerate((in_own, in_partner)):
            for first in range(0, hidden, 256):
                part = slice(first, first + 256)
                pre = dot_nn(rows_ref[span, :], in_ref[:, part])
                if side == 0:
                    outer = out_own[part, :]
                elif first < cut:
                    outer = out_first[part, :]
                else:
                    outer = out_second[first - cut : first - cut + 256, :]
                grad_acted = dot_nt(grads_ref[span, :], outer)
                square = pre * pre
                bent = jnp.tanh(root * pre * (1.0 + cubic * square))
                acted = 0.5 * pre * (1.0 + bent)
                slope = 0.5 * (1.0 + bent) + 0.5 * pre * (1.0 - bent * bent) * root * (
                    1.0 + 3.0 * cubic * square
                )
                acted_ref[side, span, part] = (acted * gate).astype(bf16)
                product = grad_acted * acted
                folded = product[:, 0:128] + product[:, 128:256]
                gate_part = folded if gate_part is None else gate_part + folded
                pre_ref[side, span, part] = (grad_acted * slope * gate).astype(bf16)
        back = dot_nt(pre_ref[0, span, :], in_own[...])
        back = back + dot_nt(pre_ref[1, span, :], in_partner[...])
        back_ref[span, :] = back.astype(bf16)
        gate_part = jnp.sum(gate_part, axis=-1, keepdims=True)
        for chunk in range(4):
            write_digits(
                back_ref, column, start + chunk * padded, padded,
                gate_part[chunk * padded : (chunk + 1) * padded],
            )
        return carry

    lax.fori_loop(0, slots // taken, one, 0)


def expert_step(in_parts, out_parts, rows_in, grads_in, padded):
    slots, model = rows_in.shape
    hidden = in_parts[0].shape[1]
    wide = (padded + 127) // 128 * 128
    return pl.pallas_call(
        functools.partial(expert_kernel, padded),
        out_shape=(
            shape((2, slots, hidden), bf16),
            shape((2, slots, hidden), bf16),
            shape((slots, model), bf16),
        ),
        in_specs=[VMEM] * 7,
        out_specs=(VMEM,) * 3,
        scratch_shapes=[pltpu.VMEM((wide, 128), f32), pltpu.VMEM((4 * padded, 128), f32)],
        compiler_params=params(60),
        cost_estimate=cost(12 * slots * model * hidden, 24 * 2**20),
        name="expert_step",
    )(*in_parts, *out_parts, rows_in, grads_in)


def expert_out_kernel(acted_ref, out_own, out_first, out_second, out_ref):
    step = out_ref.shape[0] // 4
    cut = out_first.shape[0]

    def one(index, carry):
        span = pl.ds(aligned(index * step, 16), step)
        total = dot_nn(acted_ref[0, span, :], out_own[...])
        total = total + dot_nn(acted_ref[1, span, 0:cut], out_first[...])
        total = total + dot_nn(acted_ref[1, span, cut:], out_second[...])
        out_ref[span, :] = total.astype(bf16)
        return carry

    lax.fori_loop(0, 4, one, 0)


def expert_outputs(acted, out_parts):
    _, slots, hidden = acted.shape
    model = out_parts[0].shape[1]
    return pl.pallas_call(
        expert_out_kernel,
        out_shape=shape((slots, model), bf16),
        in_specs=[VMEM] * 4,
        out_specs=VMEM,
        compiler_params=params(60),
        cost_estimate=cost(4 * slots * model * hidden, 10 * 2**20),
        name="expert_outputs",
    )(acted, *out_parts)


def write_ring(scalars, joined, own, next_ref, last_ref, far_one, far_two):
    quarter = own.shape[0]
    eighth = quarter // 2
    rank = scalars[3]

    def rows_of(which):
        return aligned(lax.rem(rank + which, 4) * quarter, quarter)

    own[...] = joined[pl.ds(rows_of(0), quarter), :]
    next_ref[...] = joined[pl.ds(rows_of(1), quarter), :].astype(bf16)
    last_ref[...] = joined[pl.ds(rows_of(3), quarter), :].astype(bf16)
    far = rows_of(2)
    far_one[...] = joined[pl.ds(far, eighth), :].astype(bf16)
    far_two[...] = joined[pl.ds(aligned(far + eighth, eighth), eighth), :].astype(bf16)


def ring_shapes(rows, model):
    quarter, eighth = shape((rows // 4, model), bf16), shape((rows // 8, model), bf16)
    return (shape((rows // 4, model), f32), quarter, quarter, eighth, eighth)


def combine_grads_kernel(
    expert_count, padded, far, scalars, place_ref, info_ref, route_ref, router_ref, back_ref, *rest
):
    if far:
        logit_ref, far_one, far_two, digits = rest
    else:
        far_logits, logit_ref, own, next_ref, last_ref, digits = rest
    rows = place_ref.shape[0]
    quarter, eighth = rows // 4, rows // 8
    slots = back_ref.shape[0]
    rank = scalars[3]
    wide = (padded + 127) // 128 * 128
    lane_digit = lax.broadcasted_iota(jnp.int32, (padded, 128), 1)

    def column_step(expert, carry):
        start = aligned(expert * padded, 16)
        row = jnp.broadcast_to(read_digits(back_ref, start, padded), (128, wide))
        column = row.T[0:padded, :]
        high = column.astype(bf16).astype(f32)
        middle = (column - high).astype(bf16).astype(f32)
        digits[pl.ds(start, padded), :] = jnp.where(
            lane_digit == 0,
            high,
            jnp.where(lane_digit == 1, middle, jnp.where(lane_digit == 2, column - high - middle, 0.0)),
        ).astype(bf16)
        return carry

    lax.fori_loop(0, expert_count, column_step, 0)
    lane = lax.broadcasted_iota(jnp.int32, (quarter, 128), 1)
    slot = lax.broadcasted_iota(jnp.int32, (quarter, slots), 1)

    def rows_of(which):
        return pl.ds(aligned(lax.rem(rank + which, 4) * quarter, quarter), quarter)

    def tokens(which):
        span = rows_of(which)
        info, place = info_ref[span, :], place_ref[span, :]
        hit_one, hit_two = slot == place[:, 0:1], slot == place[:, 1:2]
        ones = jnp.where(hit_one | hit_two, 1.0, 0.0).astype(bf16)
        total = dot_nn(ones, back_ref[...])
        signs = jnp.where(hit_one, 1.0, jnp.where(hit_two, -1.0, 0.0)).astype(bf16)
        difference = jnp.sum(dot_nn(signs, digits[...]), axis=-1, keepdims=True) / info[:, 2:3]
        picked = jnp.where(
            lane == route_ref[span, 0:1] + 64,
            info[:, 1:2] * difference,
            jnp.where(lane == route_ref[span, 1:2] + 64, -info[:, 0:1] * difference, 0.0),
        )
        probs = jnp.where((lane >= 64) & (lane < 64 + expert_count), info, 0.0)
        grads = probs * (picked - jnp.sum(probs * picked, axis=-1, keepdims=True))
        grads = grads.astype(bf16)
        return grads, total + dot_nt(grads, router_ref[:, 128:256])

    if far:
        grads, total = tokens(2)
        logit_ref[...] = grads
        far_one[...] = total[0:eighth].astype(bf16)
        far_two[...] = total[eighth:].astype(bf16)
    else:
        logit_ref[rows_of(2), :] = far_logits[...]
        for which, target in ((1, next_ref), (3, last_ref)):
            grads, total = tokens(which)
            logit_ref[rows_of(which), :] = grads
            target[...] = total.astype(bf16)
        grads, total = tokens(0)
        logit_ref[rows_of(0), :] = grads
        own[...] = total


def combine_grads(far, scalars, place, info, routes, router, back, given, expert_count, padded):
    rows = place.shape[0]
    model = router.shape[0]
    slots = back.shape[0]
    half = shape((rows // 8, model), bf16)
    if far:
        outs = (shape((rows // 4, 128), bf16), half, half)
    else:
        outs = (shape((rows, 128), bf16), shape((rows // 4, model), f32))
        outs = outs + (shape((rows // 4, model), bf16),) * 2
    return pl.pallas_call(
        functools.partial(combine_grads_kernel, expert_count, padded, far),
        out_shape=outs,
        in_specs=[SMEM] + [VMEM] * (5 + len(given)),
        out_specs=(VMEM,) * len(outs),
        scratch_shapes=[pltpu.VMEM((slots, 128), bf16)],
        compiler_params=params(60),
        cost_estimate=cost(2 * rows * model * slots, 8 * 2**20),
        name="combine_grads",
    )(scalars, place, info, routes, router, back, *given)


def combine_outs_kernel(place_ref, rows_ref, out_ref):
    step = 256
    slot = lax.broadcasted_iota(jnp.int32, (step, rows_ref.shape[0]), 1)

    def token_step(index, carry):
        span = pl.ds(aligned(index * step, step), step)
        place = place_ref[span, :]
        hit = (slot == place[:, 0:1]) | (slot == place[:, 1:2])
        out_ref[span, :] = dot_nn(jnp.where(hit, 1.0, 0.0).astype(bf16), rows_ref[...]).astype(bf16)
        return carry

    lax.fori_loop(0, out_ref.shape[0] // step, token_step, 0)


def combine_outs(place, rows_in):
    rows = place.shape[0]
    slots, model = rows_in.shape
    return pl.pallas_call(
        combine_outs_kernel,
        out_shape=shape((rows, model), bf16),
        in_specs=[VMEM] * 2,
        out_specs=VMEM,
        compiler_params=params(60),
        cost_estimate=cost(2 * rows * model * slots, 8 * 2**20),
        name="combine_outs",
    )(place, rows_in)


def received(own, from_last, from_next):
    return own[...] + from_last[...].astype(f32) + from_next[...].astype(f32)


def norm_back_kernel(gain_index, has_bypass_rows, scalars, value_ref, gain_ref, bypass_ref, *rest):
    grads = received(*rest[:3])
    rest = rest[3:]
    weights = ()
    if gain_index == 1:
        weights, rest = rest[0:4], rest[4:]
    else:
        blocks_ref, rest = rest[0], rest[1:]
    full_ref, low_ref, gain_grad = rest[0:3]
    quarter = grads.shape[0]
    here = pl.ds(aligned(scalars[3] * quarter, quarter), quarter)
    values = (value_ref[here, :] if gain_index == 0 else value_ref[...]).astype(f32)
    bypass = (bypass_ref[here, :] if has_bypass_rows else bypass_ref[...]).astype(f32)
    scale = lax.rsqrt(jnp.mean(values * values, axis=-1, keepdims=True) + epsilon)
    normed = values * scale
    scaled = grads * gain_ref[gain_index : gain_index + 1, :]
    gain_grad[...] = jnp.broadcast_to(
        jnp.sum(grads * normed, axis=0, keepdims=True), gain_grad.shape
    )
    out = bypass + scale * (scaled - normed * jnp.mean(scaled * normed, axis=-1, keepdims=True))
    full_ref[...] = out
    low = out.astype(bf16)
    if weights:
        low_ref[...] = low
    else:
        low_ref[...] = low
        for place in range(4):
            target = scalars[3] ^ place
            rest[3][target] = blocks_ref[:, place * 256 : (place + 1) * 256].astype(bf16)
    lane = lax.broadcasted_iota(jnp.int32, (quarter, 256), 1)
    for weight, target in zip(weights, rest[3:]):
        target[...] = jnp.where(lane < 192, dot_nn(low, weight[...]), 0.0).astype(bf16)


def norm_back(gain_index, has_bypass_rows, scalars, values, gains, bypass, parts, weights=(), blocks=None):
    quarter, model = parts[0].shape
    low = shape((quarter, model), bf16)
    extra, more = tuple(weights), (shape((quarter, 256), bf16),) * len(weights)
    if blocks is not None:
        extra, more = (blocks,), (shape((4, blocks.shape[0], 256), bf16),)
    return pl.pallas_call(
        functools.partial(norm_back_kernel, gain_index, has_bypass_rows),
        out_shape=(shape((quarter, model), f32), low, shape((8, model), f32)) + more,
        in_specs=[SMEM] + [VMEM] * (6 + len(extra)),
        out_specs=(VMEM,) * (3 + len(more)),
        compiler_params=params(60),
        cost_estimate=cost(quarter * model * 16, 6 * 2**20),
        name="norm_back",
    )(scalars, values, gains, bypass, *parts, *extra)


def finish_kernel(residual_ref, part_ref, out_ref):
    total = residual_ref[...]
    quarter = total.shape[0]
    for source in range(4):
        total = total + part_ref[source * quarter : (source + 1) * quarter, :].astype(f32)
    low = total.astype(bf16)
    for target in range(4):
        out_ref[target * quarter : (target + 1) * quarter, :] = low


def finish(residual, parts):
    quarter, model = residual.shape
    return pl.pallas_call(
        finish_kernel,
        out_shape=shape((4 * quarter, model), bf16),
        in_specs=[VMEM] * 2,
        out_specs=VMEM,
        compiler_params=params(40),
        cost_estimate=cost(quarter * model * 4, 4 * 2**20),
        name="finish",
    )(residual, parts)


def hidden_grad_kernel(
    scalars, dq_ref, weight_ref, own, beside_one, beside_two, across_one, across_two, dkv_ref, *rest
):
    ring, joined = rest[:5], rest[5]
    half = own.shape[0] // 2
    for part, (beside, across) in enumerate(
        ((beside_one, across_one), (beside_two, across_two))
    ):
        span = slice(part * half, (part + 1) * half)
        total = own[span, :].astype(f32) + beside[...].astype(f32) + across[...].astype(f32)
        total = total.astype(bf16)
        dkv_ref[span, :] = total
        joined[span, :] = dot_nt(dq_ref[span, :], weight_ref[:, 0:256]) + dot_nt(
            total, weight_ref[:, 256:640]
        )
    write_ring(scalars, joined, *ring)


def hidden_grad(scalars, dq, weights, own, beside, across):
    rows = dq.shape[0]
    model = weights.shape[0]
    return pl.pallas_call(
        hidden_grad_kernel,
        out_shape=(shape((rows, 384), bf16),) + ring_shapes(rows, model),
        in_specs=[SMEM] + [VMEM] * 7,
        out_specs=(VMEM,) * 6,
        scratch_shapes=[pltpu.VMEM((rows, model), f32)],
        compiler_params=params(40),
        cost_estimate=cost(2 * rows * model * 640, 8 * 2**20),
        name="hidden_grad",
    )(scalars, dq, weights, own, *beside, *across)


def split_by_side(scalars, whole, mine, other):
    half = mine.shape[0]
    side = scalars[5]
    mine[...] = whole[pl.ds(aligned(side * half, 16), half), :]
    other[...] = whole[pl.ds(aligned((1 - side) * half, 16), half), :].astype(other.dtype)


def output_grad_kernel(scalars, branch_ref, attended_ref, hidden_ref, logit_ref, *rest):
    outs, whole = rest[:-1], rest[-1]
    whole[...] = dot_tn(branch_ref[...], attended_ref[...])
    router = dot_tn(hidden_ref[...], logit_ref[...])
    for source in range(4):
        whole[:, source * 256 + 128 : source * 256 + 256] += router
    if len(outs) == 1:
        outs[0][...] = whole[...]
    else:
        size = outs[0].shape[0] // 4
        context, side = scalars[0], scalars[5]
        for out, masks in zip(outs, ((0, 2), (1, 3))):
            for place, mask in enumerate(masks):
                for far in range(2):
                    start = aligned((4 * (side ^ far) + (context ^ mask)) * size, 16)
                    target = slice((2 * place + far) * size, (2 * place + far + 1) * size)
                    out[target, :] = whole[pl.ds(start, size), :].astype(out.dtype)


def output_grads(scalars, branch, attended, hidden, grad_logits, small):
    rows, model = hidden.shape
    outs = (shape((model, 1024), f32),)
    if small:
        outs = (shape((model // 2, 1024), f32), shape((model // 2, 1024), bf16))
    return pl.pallas_call(
        output_grad_kernel,
        out_shape=outs,
        in_specs=[SMEM] + [VMEM] * 4,
        out_specs=(VMEM,) * len(outs),
        scratch_shapes=[pltpu.VMEM((model, 1024), f32)],
        compiler_params=params(60),
        cost_estimate=cost(2 * rows * model * 384, 6 * 2**20),
        name="output_grads",
    )(scalars, branch, attended, hidden, grad_logits)


def projection_grad_kernel(scalars, hidden_ref, dq_ref, dkv_ref, gain_ref, fold_ref, *rest):
    outs, whole = rest[:-1], rest[-1]
    hidden = hidden_ref[...]
    whole[:, 0:256] = dot_tn(hidden, dq_ref[...])
    whole[:, 256:640] = dot_tn(hidden, dkv_ref[...])
    lane = lax.broadcasted_iota(jnp.int32, (whole.shape[0], 128), 1)
    column = jnp.broadcast_to(gain_ref[0:1, :], (128, whole.shape[0])).T
    whole[:, 128:256] = jnp.where(lane < 64, whole[:, 128:256], column)
    if len(outs) == 2:
        side = scalars[5]
        block = outs[0].shape[0] // 4
        size = block - 8
        for which, out in ((side, outs[0]), (1 - side, outs[1])):
            for context in range(4):
                start = aligned((which * 4 + context) * size, 8)
                out[context * block : context * block + size, :] = whole[pl.ds(start, size), :]
                tail = slice(context * block + size, (context + 1) * block)
                out[tail, 0:256] = fold_ref[...]
                out[tail, 256:640] = jnp.zeros((8, 384), f32)
    else:
        outs[0][...] = whole[...]


def projection_grads(scalars, hidden, dq, dkv, gain_grad, fold, small):
    rows, model = hidden.shape
    outs = (shape((model // 2 + 32, 640), f32),) * 2 if small else (shape((model, 640), f32),)
    return pl.pallas_call(
        projection_grad_kernel,
        out_shape=outs,
        in_specs=[SMEM] + [VMEM] * 5,
        out_specs=(VMEM,) * len(outs),
        scratch_shapes=[pltpu.VMEM((model, 640), f32)],
        compiler_params=params(40),
        cost_estimate=cost(2 * rows * model * 640, 6 * 2**20),
        name="projection_grads",
    )(scalars, hidden, dq, dkv, gain_grad, fold)


def share_kernel(scalars, mine, other, *outs):
    size = outs[0].shape[0]
    context = scalars[0]
    for mask, out in enumerate(outs):
        span = pl.ds(aligned((context ^ mask) * size, 8), size)
        total = mine[span, :] + other[span, :].astype(f32)
        out[...] = total.astype(out.dtype)


def share(scalars, mine, other):
    rows, width = mine.shape
    return pl.pallas_call(
        share_kernel,
        out_shape=(shape((rows // 4, width), f32),) + (shape((rows // 4, width), other.dtype),) * 3,
        in_specs=[SMEM, VMEM, VMEM],
        out_specs=(VMEM,) * 4,
        compiler_params=params(40),
        cost_estimate=cost(rows * width, 12 * rows * width),
        name="share",
    )(scalars, mine, other)


def shift(value, amount):
    size = lax.axis_size("tensor")
    return lax.ppermute(value, "tensor", [(i, (i + amount) % size) for i in range(size)])


def cross(value, mask):
    size = lax.axis_size("context")
    return lax.ppermute(value, "context", [(i, i ^ mask) for i in range(size)])


def trade(value, mask):
    return lax.ppermute(value, "tensor", [(i, i ^ mask) for i in range(lax.axis_size("tensor"))])


def spread(value):
    across, beside = trade(value, 2), trade(value, 1)
    return [value, beside, across, trade(across, 1)]


def sum_ranks(value):
    total = value
    for step in (1, 2, 3):
        total = total + shift(value, step)
    return total


def added(first, second):
    return (first.astype(f32) + second.astype(f32)).astype(bf16)


def ring_start(far_one, far_two):
    return shift(far_one, 1), shift(far_two, -1)


def with_first(whole, arrived):
    half = arrived.shape[0]
    return jnp.concatenate([added(whole[:half], arrived), whole[half:]], axis=0)


def with_second(whole, arrived):
    half = arrived.shape[0]
    return jnp.concatenate([whole[:half], added(whole[half:], arrived)], axis=0)


def ring_finish(next_block, last_block, arrived_one, arrived_two):
    from_last = shift(with_first(next_block, arrived_one), 1)
    from_next = shift(with_second(last_block, arrived_two), -1)
    return from_last, from_next


ALL_ROWS = ("dp", "context")


def exchange(rows_out):
    return lax.all_to_all(rows_out, ALL_ROWS, split_axis=0, concat_axis=0, tiled=True)


def gather_weights(block, small, axis):
    size = block.shape[axis]
    if not small:
        whole = lax.all_gather(block, ALL_ROWS, axis=axis, tiled=True)
        return [whole], jnp.zeros((1,), jnp.int32)
    context, side = lax.axis_index("context"), lax.axis_index("dp")
    pieces = [block] + [cross(block, mask) for mask in (1, 2, 3)]
    pieces = pieces + [lax.ppermute(piece, "dp", [(0, 1), (1, 0)]) for piece in pieces]
    return pieces, jnp.stack(
        [((side ^ far) * 4 + (context ^ mask)) * size for far in range(2) for mask in range(4)]
    )


def swap_sides(parts):
    if len(parts) == 1:
        return parts
    return parts[0], lax.ppermute(parts[1], "dp", [(0, 1), (1, 0)])


def share_blocks(scalars, parts):
    return parts if len(parts) == 1 else share(scalars, *parts)


def halve(mine, arrived):
    total = mine + arrived.astype(f32)
    half = total.shape[0] // 2
    return total[:half], total[half:].astype(bf16)


def scatter_blocks(blocks):
    if len(blocks) == 1:
        return lax.psum_scatter(blocks[0], ALL_ROWS, scatter_dimension=0, tiled=True)
    total = blocks[0]
    for mask in (1, 2, 3):
        total = total + cross(blocks[mask], mask).astype(f32)
    return total


def on_device(
    tokens_in, query_weight, key_weight, value_weight, output_weight, bias_table, attention_gain,
    router_weight, expert_gain, expert_in, expert_out, routes, pair_order, seq_lengths, cotangent,
):
    rows, model = tokens_in.shape
    heads = bias_table.shape[1]
    width = query_weight.shape[1] // heads
    group_rows = rows * lax.axis_size("context")
    expert_count = router_weight.shape[1]
    capacity = (9 * rows + 4 * expert_count - 1) // (4 * expert_count)
    count = lax.axis_size("dp") * lax.axis_size("context")
    small = count == 8
    context, rank = lax.axis_index("context"), lax.axis_index("tensor")
    here = lax.axis_index("dp") * lax.axis_size("context") + context
    first_end = seq_lengths[0, 0]
    second_end = first_end + seq_lengths[0, 1]
    side = lax.axis_index("dp")
    scalars = jnp.stack([context, first_end, second_end, rank, here, side]).astype(jnp.int32)
    part = capacity // 2
    padded = (part + 15) // 16 * 16 + 16
    slots = expert_count * padded
    shard = query_weight.shape[0]
    block = pack_weights(
        query_weight, key_weight, value_weight, output_weight, attention_gain, expert_gain, router_weight
    )
    tie = lax.optimization_barrier
    half, quarter = rows // 2, rows // 4
    far_block = (context ^ 3) * rows
    kv_offsets = jnp.stack(
        [context * rows, (context ^ 1) * rows, (context ^ 2) * rows, far_block, far_block + half]
    )
    token_offsets = jnp.stack([(rank ^ mask) * quarter for mask in range(4)])
    far_bias = bias_table[-1]
    order_row = (pair_order & 1) * rows + (pair_order >> 1)
    pieces, offsets = gather_weights(block, small, 0)
    in_partner, out_first = trade(expert_in[0], 1), trade(expert_out[0, :256], 1)
    hidden_one, queries, kv_own, weights, output_own, gains = project(
        offsets, tokens_in, pieces
    )
    kv_beside, kv_across = cross(kv_own, 1), cross(kv_own, 2)
    output_parts = spread(output_own)
    order_row, queries = tie((order_row, queries))
    row_place, column_place, bias_own, bias_next = prepare(
        scalars, bias_table, routes.T, order_row, expert_count, part, padded
    )
    kv_beside, kv_across, row_place = tie((kv_beside, kv_across, row_place))
    kv_far = cross(kv_beside[:half], 2), cross(kv_across[half:], 1)
    kv_pieces = (kv_own, kv_beside, kv_across) + kv_far
    cotangent_rows = scatter_rows(cotangent, row_place, slots)
    states = attention_near(
        scalars, far_bias, queries, bias_own, bias_next, kv_own, heads, width
    )
    states, kv_pieces, cotangent_rows, in_partner, output_parts = tie(
        (states, kv_pieces, cotangent_rows, in_partner, output_parts)
    )
    packed, lse = attention_far(
        scalars, far_bias, kv_offsets, queries, bias_next, states, kv_pieces, group_rows, heads,
        width,
    )
    packed, output_parts, out_first, cotangent_rows = tie(
        (packed, output_parts, out_first, cotangent_rows)
    )
    attended = spread(packed)
    cotangent_rows = exchange(cotangent_rows)
    attended, cotangent_rows = tie((attended, cotangent_rows))
    out_second, attended = tie((expert_out[0, 256:], attended))
    out_second = trade(out_second, 1)
    residual, hidden_two, info, attended_here, rows_out = dispatch(
        scalars, tokens_in, gains, routes, row_place, attended, output_parts, width, expert_count,
        padded,
    )
    in_parts, out_parts = (expert_in[0], in_partner), (expert_out[0], out_first, out_second)
    expert_rows = exchange(rows_out)
    acted, grad_pre, back = expert_step(
        in_parts, out_parts, expert_rows, cotangent_rows, padded
    )
    back = exchange(back)
    in_grad_partner = dot_tn(expert_rows, grad_pre[1]).astype(bf16)
    out_grad_partner = dot_tn(acted[1], cotangent_rows).astype(bf16)
    in_grad_partner, out_grad_partner, acted, grad_pre = tie(
        (in_grad_partner, out_grad_partner, acted, grad_pre)
    )
    in_grad_partner = trade(in_grad_partner, 1)
    outs = expert_outputs(acted, out_parts)
    expert_out_grad = dot_tn(acted[0], cotangent_rows)
    expert_in_grad = dot_tn(expert_rows, grad_pre[0])
    back, outs, expert_out_grad, expert_in_grad = tie(
        (back, outs, expert_out_grad, expert_in_grad)
    )
    combine = (scalars, column_place, info, routes, output_own, back)
    far_logits, *far = combine_grads(True, *combine, (), expert_count, padded)
    arrived = ring_start(*far)
    grad_logits, own, *ring = combine_grads(False, *combine, (far_logits,), expert_count, padded)
    arrived, ring, outs, in_grad_partner = tie((arrived, ring, outs, in_grad_partner))
    ring, outs = (own,) + ring_finish(*ring, *arrived), exchange(outs)
    ring, outs = tie((ring, outs))
    grad_one, grad_branch, gain_two_grad, *grad_heads = norm_back(
        1, True, scalars, residual, gains, cotangent, ring, output_parts
    )
    head_pieces = (grad_heads[0],) + tuple(trade(grad_heads[mask], mask) for mask in (1, 2, 3))
    outer = output_grads(scalars, grad_branch, attended_here, hidden_two, grad_logits, small)
    mixed = combine_outs(column_place, outs)
    head_pieces, mixed, out_grad_partner, outer = tie(
        (head_pieces, mixed, out_grad_partner, outer)
    )
    if small:
        outer = outer[0], cross(outer[1], 1)
    out_grad_partner = trade(out_grad_partner, 1)
    mixed = lax.all_to_all(mixed, "tensor", split_axis=0, concat_axis=0, tiled=True)
    shared = (scalars, far_bias, token_offsets, queries, bias_own, bias_next, lse)
    dout, deltas, dq_t, far_one, far_two, fold = attention_backward(
        (3,), *shared, kv_far, (packed, *head_pieces), 4, heads, width
    )
    arrived = cross(far_one, 1), cross(far_two, 2)
    dq_t, *beside_across, fold = attention_backward(
        (1, 2), *shared, (kv_beside, kv_across), (dout, deltas, dq_t, fold), 0, heads, width
    )
    beside, across = beside_across[0:2], beside_across[2:4]
    beside_two, across_one = added(beside[1], arrived[1]), added(across[0], arrived[0])
    dq_t, mixed, beside_two, across_one, outer = tie(
        (dq_t, mixed, beside_two, across_one, outer)
    )
    from_square = (
        (cross(beside[0], 1), cross(beside_two, 1)), (cross(across_one, 2), cross(across[1], 2))
    )
    layer_out = finish(residual, mixed)
    dq_t, layer_out = tie((dq_t, layer_out))
    layer_out = lax.all_to_all(layer_out, "tensor", split_axis=0, concat_axis=0, tiled=True)
    dq_t, own, dq, fold = attention_backward(
        (0,), *shared, (kv_own,), (dout, deltas, dq_t, fold), 0, heads, width
    )
    dq, from_square, out_grad_partner = tie((dq, from_square, out_grad_partner))
    dkv, own, *ring = hidden_grad(scalars, dq, weights, own, *from_square)
    arrived = ring_start(*ring[2:4])
    inner_parts = projection_grads(scalars, hidden_one, dq, dkv, gain_two_grad, fold, small)
    if small:
        outer = halve(*outer)
        outer = halve(outer[0], cross(outer[1], 2))
    arrived, inner_parts, outer = tie((arrived, inner_parts, outer))
    inner_parts = swap_sides(inner_parts)
    ring = (own,) + ring_finish(*ring[0:2], *arrived)
    if small:
        outer_grads = outer[0] + swap_sides(outer)[1].astype(f32)
    else:
        outer_grads = lax.psum_scatter(outer[0], ALL_ROWS, scatter_dimension=0, tiled=True)
    inner_parts = share_blocks(scalars, inner_parts)
    ring, layer_out, outer_grads, inner_parts = tie((ring, layer_out, outer_grads, inner_parts))
    _, input_low, _, outer_grads = norm_back(
        0, False, scalars, tokens_in, gains, grad_one, ring, blocks=outer_grads
    )
    input_far, input_beside = trade(input_low, 2), trade(input_low, 1)
    outer_grads = lax.all_to_all(outer_grads, "tensor", split_axis=0, concat_axis=0, tiled=True)
    layer_out, input_far = tie((layer_out, input_far))
    layer_out = assemble(jnp.zeros((1,), jnp.int32), [layer_out], bf16)
    projected = scatter_blocks(inner_parts)
    expert_out_grad, expert_in_grad, projected = tie((expert_out_grad, expert_in_grad, projected))
    input_pieces = [input_low, input_beside, input_far, trade(input_far, 1)]
    input_grad = assemble(token_offsets, input_pieces, f32)
    outer_grads = jnp.sum(outer_grads.astype(f32), axis=0)
    expert_out_grad = (expert_out_grad + out_grad_partner.astype(f32))[None]
    expert_in_grad = (expert_in_grad + in_grad_partner.astype(f32))[None]
    output_grad = outer_grads[:, :192].T
    router_grad = outer_grads[:, 192 : 192 + expert_count]
    fold = projected[shard:, :256] if small else lax.psum(fold, ALL_ROWS)
    projected = projected[:shard]
    query_grad, key_grad = projected[:, :192], projected[:, 256:448]
    value_grad = jnp.concatenate([projected[:, 512:], projected[:, 448:512]], axis=1)
    gain_one_grad = jnp.sum(
        query_weight.astype(f32) * query_grad
        + key_weight.astype(f32) * key_grad
        + value_weight.astype(f32) * value_grad,
        axis=1,
        keepdims=True,
    )
    gain_grads = sum_ranks(jnp.concatenate([gain_one_grad, projected[:, 192:193]], axis=1))
    bucket_row = jnp.asarray(bucket_tiles()[0, 0])
    bucket_hot = (bucket_row[None, :] == jnp.arange(bias_table.shape[0] - 1)[:, None]).astype(f32)
    near_grad = jnp.sum(bucket_hot[:, None, :] * fold[None, :heads, :], axis=-1)
    table_grad = jnp.concatenate([near_grad, -jnp.sum(near_grad, axis=0, keepdims=True)], axis=0)
    return (
        layer_out,
        input_grad,
        query_grad,
        key_grad,
        value_grad,
        output_grad,
        table_grad,
        gain_grads[:, 0] / attention_gain.astype(f32),
        router_grad,
        gain_grads[:, 1],
        expert_in_grad,
        expert_out_grad,
    )


def solution(mesh):
    rows = P(("dp", "context"), None)
    return jax.shard_map(
        on_device,
        mesh=mesh,
        in_specs=(
            rows,
            P(("dp", "context"), "tensor"),
            P(("dp", "context"), "tensor"),
            P(("dp", "context"), "tensor"),
            P("tensor", ("dp", "context")),
            P(None, "tensor"),
            P(("dp", "context")),
            rows,
            P(("dp", "context")),
            P(("dp", "context"), None, "tensor"),
            P(("dp", "context"), "tensor", None),
            rows,
            rows,
            P("dp", None),
            rows,
        ),
        out_specs=(
            rows,
            rows,
            P(("dp", "context"), "tensor"),
            P(("dp", "context"), "tensor"),
            P(("dp", "context"), "tensor"),
            P("tensor", ("dp", "context")),
            P(None, "tensor"),
            P(("dp", "context")),
            rows,
            P(("dp", "context")),
            P(("dp", "context"), None, "tensor"),
            P(("dp", "context"), "tensor", None),
        ),
        check_vma=False,
    )
```

```python
import functools
import jax
import jax.numpy as jnp
import numpy as np
from jax import lax
from jax.experimental import pallas as pl
from jax.experimental.pallas import tpu as pltpu
from jax.sharding import PartitionSpec as P

bf16 = jnp.bfloat16
f32 = jnp.float32
epsilon = 1e-06
masked_value = -1e30
tile = 256
VMEM = pl.BlockSpec(memory_space=pltpu.VMEM)
SMEM = pl.BlockSpec(memory_space=pltpu.SMEM)


def dot_nn(a, b):
    return lax.dot_general(a, b, (((1,), (0,)), ((), ())), preferred_element_type=f32)


def dot_nt(a, b):
    return lax.dot_general(a, b, (((1,), (1,)), ((), ())), preferred_element_type=f32)


def dot_tn(a, b):
    return lax.dot_general(a, b, (((0,), (0,)), ((), ())), preferred_element_type=f32)


def start_of(position, first_end, second_end):
    return jnp.where(
        position >= second_end, second_end, jnp.where(position >= first_end, first_end, 0)
    )


def aligned(value, size):
    return pl.multiple_of(value, size)


def transpose_values(source, source_start, values_t, start, width):
    span, target = pl.ds(source_start, tile), pl.ds(start, tile)
    upper = source[span, 256:384].astype(f32).T.astype(bf16)
    lower = source[span, 128:256].astype(f32).T.astype(bf16)
    for head, part in enumerate((upper[0:width], upper[width:], lower[width:])):
        values_t[head, 0:width, target] = part
        values_t[head, width:, target] = jnp.ones((16, tile), bf16)


def masked_heads(queries, heads, width):
    lane = lax.broadcasted_iota(jnp.int32, queries.shape, 1) // width
    return [jnp.where(lane == head, queries, jnp.zeros_like(queries)) for head in range(heads)]


def absorb(
    keys_values, values_t, bias_ref, far_bias, best, running, index, masked_queries, heads,
    key_start, size, key_first, positions, row_start, bias_index, masked, first_time,
):
    keys = keys_values[pl.ds(key_start, size), 0:256]
    if masked:
        key_positions = (
            key_first + key_start + lax.broadcasted_iota(jnp.int32, (size, tile), 0)
        )
        seen = key_positions >= row_start
        if bias_index == 0:
            seen = seen & (key_positions <= positions)
    shift_by = [far_bias[head] if bias_index is None else 0.0 for head in range(heads)]
    scores = [dot_nt(keys, masked_queries[head]) for head in range(heads)]
    if bias_index is not None:
        scores = [scores[head] + bias_ref[bias_index][head] for head in range(heads)]
    if masked:
        scores = [jnp.where(seen, part, masked_value) for part in scores]
    tops = [
        jnp.max(scores[head], axis=0, keepdims=True) + shift_by[head] for head in range(heads)
    ]
    if first_time:
        new = tops
    else:
        old = [best[index, head, 0:1] for head in range(heads)]
        new = [jnp.maximum(old[head], tops[head]) for head in range(heads)]
    weights = [
        jnp.exp(scores[head] - (new[head] - shift_by[head])).astype(bf16) for head in range(heads)
    ]
    sums = [
        dot_nn(values_t[head, :, pl.ds(key_start, size)], weights[head]) for head in range(heads)
    ]
    for head in range(heads):
        if first_time:
            running[index, head] = sums[head]
        else:
            running[index, head] = running[index, head] * jnp.exp(old[head] - new[head]) + sums[head]
        best[index, head] = jnp.broadcast_to(new[head], (8, tile))


def attention_near_kernel(
    heads, width, scalars, far_bias, query_ref, bias_own, bias_next, keys_values, running, best,
    values_t,
):
    rows = query_ref.shape[0]
    context, first_end, second_end = scalars[0], scalars[1], scalars[2]
    base = context * rows

    def values_step(index, carry):
        start = aligned(index * tile, tile)
        transpose_values(keys_values, start, values_t, start, width)
        return carry

    lax.fori_loop(0, rows // tile, values_step, 0)

    def query_tile(index, carry):
        local = aligned(index * tile, tile)
        positions = base + local + lax.broadcasted_iota(jnp.int32, (1, tile), 1)
        row_start = start_of(positions, first_end, second_end)
        masked_queries = masked_heads(query_ref[pl.ds(local, tile), :], heads, width)

        def take(key_start, bias_index, first_time):
            absorb(
                keys_values, values_t, (bias_own, bias_next), far_bias, best, running, index,
                masked_queries, heads, key_start, tile, base, positions, row_start, bias_index,
                True, first_time,
            )

        take(local, 0, True)

        @pl.when(index > 0)
        def _():
            take(aligned(local - tile, tile), 1, False)

        def far_step(step, inner):
            take(aligned(step * tile, tile), None, False)
            return inner

        lax.fori_loop(0, jnp.maximum(index - 1, 0), far_step, 0)
        return carry

    lax.fori_loop(0, rows // tile, query_tile, 0)


def attention_near(scalars, far_bias, queries, bias_own, bias_next, keys_values, heads, width):
    rows = queries.shape[0]
    tiles = rows // tile
    return pl.pallas_call(
        functools.partial(attention_near_kernel, heads, width),
        out_shape=(
            jax.ShapeDtypeStruct((tiles, heads, width + 16, tile), f32),
            jax.ShapeDtypeStruct((tiles, heads, 8, tile), f32),
        ),
        in_specs=[SMEM, SMEM] + [VMEM] * 4,
        out_specs=(VMEM,) * 2,
        scratch_shapes=[pltpu.VMEM((heads, width + 16, rows), bf16)],
        compiler_params=pltpu.CompilerParams(vmem_limit_bytes=40 * 2**20),
        cost_estimate=pl.CostEstimate(
            flops=2 * rows * rows * 256 * heads,
            bytes_accessed=4 * 2**20,
            transcendentals=rows * rows * heads // 2,
        ),
        name="attention_near",
    )(scalars, far_bias, queries, bias_own, bias_next, keys_values)


def attention_far_kernel(
    heads, width, piece_count, scalars, far_bias, offsets, query_ref, running_in, best_in,
    bias_next, *rest
):
    pieces = rest[:piece_count]
    packed, lse_ref, keys_values, values_t, running, best, side_one, side_two = rest[piece_count:]
    rows = query_ref.shape[0]
    half, quarter = rows // 2, rows // 4
    context, first_end, second_end = scalars[0], scalars[1], scalars[2]
    base = context * rows
    for index, piece in enumerate(pieces):
        size = piece.shape[0]
        keys_values[pl.ds(aligned(offsets[index], 128), size), :] = piece[...]

    def values_step(index, carry):
        start = aligned(index * tile, tile)
        transpose_values(keys_values, start, values_t, start, width)
        return carry

    lax.fori_loop(0, context * (rows // tile), values_step, 0)
    running[...] = running_in[...]
    best[...] = best_in[...]

    def query_tile(index, carry):
        local = aligned(index * tile, tile)
        first = base + local
        positions = first + lax.broadcasted_iota(jnp.int32, (1, tile), 1)
        row_start = start_of(positions, first_end, second_end)
        start_first = start_of(first, first_end, second_end)
        start_last = start_of(first + tile - 1, first_end, second_end)
        masked_queries = masked_heads(query_ref[pl.ds(local, tile), :], heads, width)

        def take(key_start, size, bias_index, masked):
            absorb(
                keys_values, values_t, (None, bias_next), far_bias, best, running, index,
                masked_queries, heads, key_start, size, 0, positions, row_start, bias_index,
                masked, False,
            )

        far_rows = jnp.where(index == 0, jnp.maximum(base - tile, 0), base)

        @pl.when((index == 0) & (context > 0))
        def _():
            take(aligned(base - tile, tile), tile, 1, True)

        big = 4 * tile
        big_count = far_rows // big
        low = jnp.minimum(start_first // big, big_count)
        middle = jnp.clip((start_last + big - 1) // big, low, big_count)

        def masked_step(step, inner):
            take(aligned(step * big, big), big, None, True)
            return inner

        def plain_step(step, inner):
            take(aligned(step * big, big), big, None, False)
            return inner

        lax.fori_loop(low, middle, masked_step, 0)
        lax.fori_loop(middle, big_count, plain_step, 0)

        def small_step(step, inner):
            take(aligned(step * tile, tile), tile, None, True)
            return inner

        lax.fori_loop(big_count * 4, far_rows // tile, small_step, 0)
        outs = []
        for head in range(heads):
            total = running[index, head, width : width + 1]
            outs.append(running[index, head, 0:width] / total)
            lse_ref[pl.ds(head, 1), pl.ds(aligned(index * tile, tile), tile)] = best[
                index, head, 0:1
            ] + jnp.log(total)
        span = pl.ds(aligned(index * tile, tile), tile)
        side_one[span, :] = jnp.concatenate([outs[0], outs[1]], axis=0).T
        side_two[span, :] = jnp.concatenate([outs[2], outs[2]], axis=0).T
        return carry

    lax.fori_loop(0, rows // tile, query_tile, 0)
    lane = lax.broadcasted_iota(jnp.int32, (quarter, 128), 1)
    for part in range(2):
        target = slice(part * quarter, (part + 1) * quarter)
        first_rows = slice(part * half, part * half + quarter)
        last_rows = slice(part * half + quarter, (part + 1) * half)
        packed[target, 0:128] = side_one[first_rows, :].astype(bf16)
        packed[target, 128:256] = jnp.where(
            lane < width, side_two[first_rows, :], side_two[last_rows, :]
        ).astype(bf16)
        packed[target, 256:384] = side_one[last_rows, :].astype(bf16)


def attention_far(
    scalars, far_bias, offsets, queries, bias_next, state, pieces, group_rows, heads, width
):
    rows = queries.shape[0]
    shape = jax.ShapeDtypeStruct
    return pl.pallas_call(
        functools.partial(attention_far_kernel, heads, width, len(pieces)),
        out_shape=(shape((rows // 2, 384), bf16), shape((8, rows), f32)),
        in_specs=[SMEM, SMEM, SMEM] + [VMEM] * (4 + len(pieces)),
        out_specs=(VMEM,) * 2,
        scratch_shapes=[
            pltpu.VMEM((group_rows, 384), bf16),
            pltpu.VMEM((heads, width + 16, group_rows), bf16),
            pltpu.VMEM((rows // tile, heads, width + 16, tile), f32),
            pltpu.VMEM((rows // tile, heads, 8, tile), f32),
            pltpu.VMEM((rows, 128), f32),
            pltpu.VMEM((rows, 128), f32),
        ],
        compiler_params=pltpu.CompilerParams(vmem_limit_bytes=60 * 2**20),
        cost_estimate=pl.CostEstimate(
            flops=4 * rows * group_rows * 256 * heads,
            bytes_accessed=8 * 2**20,
            transcendentals=rows * group_rows * heads,
        ),
        name="attention_far",
    )(scalars, far_bias, offsets, queries, *state, bias_next, *pieces)


def attention_backward_kernel(heads, width, masks, piece_count, scalars, far_bias, offsets, *rest):
    first_call, last_call = masks[0] == 3, masks[0] == 0
    block_count = 2 if first_call else len(masks)
    blocks, rest = rest[:block_count], rest[block_count:]
    query_ref, lse_ref, bias_next = rest[0:3]
    rest = rest[3:]
    bias_own = None
    if last_call:
        bias_own, rest = rest[0], rest[1:]
    bias_ref = (bias_own, bias_next)
    if first_call:
        packed_ref = rest[0]
        pieces = rest[1 : 1 + piece_count]
        rest = rest[1 + piece_count :]
        dout, deltas, dq_t = rest[0:3]
        rest = rest[3:]
    else:
        dout, deltas, dq_in, fold_in = rest[0:4]
        dq_t = rest[4]
        rest = rest[5:]
    out_count = 2 if first_call else len(masks)
    outs, rest = rest[:out_count], rest[out_count:]
    if last_call:
        dq_ref, rest = rest[0], rest[1:]
    fold_ref, masked_q, masked_o, keys_t, dkv, band_ref, keys_values, semaphores = rest
    copies = []
    for place, block_ref in enumerate(blocks):
        target = keys_values.at[place]
        if first_call:
            size = block_ref.shape[0]
            target = keys_values.at[0, pl.ds(place * size, size), :]
        copies.append(pltpu.make_async_copy(block_ref, target, semaphores.at[place]))
        copies[-1].start()
    rows = query_ref.shape[0]
    half, quarter = rows // 2, rows // 4
    context, first_end, second_end = scalars[0], scalars[1], scalars[2]
    tiles_here = rows // tile
    if first_call:
        for index, piece in enumerate(pieces):
            span = pl.ds(aligned(offsets[index], 128), piece.shape[0])
            dout[span, 0:128] = pltpu.roll(piece[:, 128:256].astype(f32), width, 1).astype(bf16)
            dout[span, 128:256] = piece[:, 0:128]
        head_row = lax.broadcasted_iota(jnp.int32, (16, 256), 0)
        head_lane = lax.broadcasted_iota(jnp.int32, (16, 256), 1) // width
        head_hot = (head_row == jnp.where(head_lane == 1, 2, head_lane - 2)).astype(bf16)
        for part in range(4):
            span = slice(part * quarter, (part + 1) * quarter)
            packed = packed_ref[part // 2 * quarter : (part // 2 + 1) * quarter, :]
            lower = packed[:, 128:256].astype(f32)
            if part % 2 == 0:
                upper, lower = packed[:, 0:128], pltpu.roll(lower, width, 1)
            else:
                upper = packed[:, 256:384]
            product = dout[span, :].astype(f32) * jnp.concatenate(
                [lower, upper.astype(f32)], axis=1
            )
            high = product.astype(bf16)
            rest_part = (product - high.astype(f32)).astype(bf16)
            deltas[:, span] = dot_nt(head_hot, high) + dot_nt(head_hot, rest_part)
        dq_t[...] = jnp.zeros_like(dq_t)
        fold_ref[...] = jnp.zeros_like(fold_ref)
    else:
        dq_t[...] = dq_in[...]
        fold_ref[...] = fold_in[...]
    lane = lax.broadcasted_iota(jnp.int32, (rows, 256), 1) // width
    for head in range(heads):
        masked_q[head] = jnp.where(lane == head, query_ref[...], jnp.zeros((rows, 256), bf16))
        slot = 1 if head == 2 else head + 2
        masked_o[head] = jnp.where(lane == slot, dout[...], jnp.zeros((rows, 256), bf16))
    first = context * rows
    all_positions = first + lax.broadcasted_iota(jnp.int32, (1, rows), 1)
    all_starts = start_of(all_positions, first_end, second_end)
    start_first = start_of(first, first_end, second_end)
    start_last = start_of(first + rows - 1, first_end, second_end)


    def block(place, key_start, base, query_start, bands, masked):
        size = rows - query_start
        here = pl.ds(aligned(key_start - base, tile), tile)
        keys = keys_values[place, here, 0:256]
        values = keys_values[place, here, 128:384]
        key_sum, value_sum = None, None
        if masked:
            key_positions = key_start + lax.broadcasted_iota(jnp.int32, (tile, size), 0)
            seen = key_positions >= all_starts[:, query_start:]
            if 0 in bands:
                seen = seen & (key_positions <= all_positions[:, query_start:])
        span = slice(query_start, rows)
        every = range(heads)
        queries = [masked_q[head, span, :] for head in every]
        grads = [masked_o[head, span, :] for head in every]
        scores = [dot_nt(keys, queries[head]) for head in every]
        grad_probs = [dot_nt(values, grads[head]) for head in every]
        lse = [lse_ref[head : head + 1, span] for head in every]
        if bands:
            for head in every:
                parts = [
                    scores[head][:, at * tile : (at + 1) * tile] + bias_ref[band][head]
                    for at, band in enumerate(bands)
                ]
                if size > len(bands) * tile:
                    parts.append(scores[head][:, len(bands) * tile :] + far_bias[head])
                scores[head] = jnp.concatenate(parts, axis=1)
        else:
            lse = [lse[head] - far_bias[head] for head in every]
        probs = [jnp.exp(scores[head] - lse[head]) for head in every]
        if masked:
            probs = [jnp.where(seen, part, 0.0) for part in probs]
        grad_scores = [
            probs[head] * (grad_probs[head] - deltas[head : head + 1, span]) for head in every
        ]
        for head in every:
            for at, band in enumerate(bands):
                band_ref[band, head] += grad_scores[head][:, at * tile : (at + 1) * tile]
        low_scores = [part.astype(bf16) for part in grad_scores]
        low_probs = [part.astype(bf16) for part in probs]
        for head in every:
            value_part = dot_nn(low_probs[head], grads[head])
            key_part = dot_nn(low_scores[head], queries[head])
            dq_t[head, :, span] += dot_nn(keys_t[head, :, here], low_scores[head])
            key_sum = key_part if key_sum is None else key_sum + key_part
            value_sum = value_part if value_sum is None else value_sum + value_part
        return key_sum, value_sum

    lane_tile = lax.broadcasted_iota(jnp.int32, (tile, 128), 1)

    def write(local, key_sum, value_sum):
        span = pl.ds(local, tile)
        dkv[span, 0:128] = key_sum[:, 0:128].astype(bf16)
        dkv[span, 128:256] = jnp.where(
            lane_tile < width, key_sum[:, 128:256], value_sum[:, 0:128]
        ).astype(bf16)
        dkv[span, 256:384] = value_sum[:, 128:256].astype(bf16)

    near = jnp.bool_(last_call)
    for mask in masks:
        near = near | ((context ^ mask) == context - 1)

    @pl.when(near)
    def _():
        band_ref[...] = jnp.zeros_like(band_ref)

    for place, mask in enumerate(masks):
        which = context ^ mask
        base = aligned(which * rows, rows)
        for copy in copies if first_call else copies[place : place + 1]:
            copy.wait()

        @pl.when((which > context) | (start_first > base))
        def _():
            dkv[...] = jnp.zeros_like(dkv)

        @pl.when(which <= context)
        def _():
            def transpose_keys(index, carry):
                target = pl.ds(aligned(index * tile, tile), tile)
                lower = keys_values[place, target, 0:128].astype(f32).T.astype(bf16)
                upper = keys_values[place, target, 128:256].astype(f32).T.astype(bf16)
                keys_t[0, :, target] = lower[0:width]
                keys_t[1, :, target] = lower[width:]
                keys_t[2, :, target] = upper[0:width]
                return carry

            lax.fori_loop(0, tiles_here, transpose_keys, 0)
            low_tile = which * tiles_here
            high_tile = low_tile + tiles_here
            if mask:
                far_end = jnp.minimum(high_tile, context * tiles_here - 1)
                low = jnp.clip(start_first // tile, low_tile, far_end)
                middle = jnp.clip((start_last + tile - 1) // tile, low, far_end)

                def masked_step(index, carry):
                    start = aligned(index * tile, tile)
                    found = block(place, start, base, 0, (), True)
                    write(aligned(start - base, tile), *found)
                    return carry

                def plain_step(index, carry):
                    start = aligned(index * tile, tile)
                    found = block(place, start, base, 0, (), False)
                    write(aligned(start - base, tile), *found)
                    return carry

                lax.fori_loop(low, middle, masked_step, 0)
                lax.fori_loop(middle, far_end, plain_step, 0)

                @pl.when(far_end < high_tile)
                def _():
                    start = aligned(far_end * tile, tile)
                    write(aligned(start - base, tile), *block(place, start, base, 0, (1,), True))

            else:
                for index in range(tiles_here):
                    start = aligned(base + index * tile, tile)
                    bands = (0, 1) if index + 1 < tiles_here else (0,)
                    write(index * tile, *block(place, start, base, index * tile, bands, True))

        if mask == 3:
            outs[0][...] = dkv[0:half, :]
            outs[1][...] = dkv[half:, :]
        else:
            outs[place][...] = dkv[...]

    @pl.when(near)
    def _():
        key_index = lax.broadcasted_iota(jnp.int32, (tile, tile), 0)
        query_index = lax.broadcasted_iota(jnp.int32, (tile, tile), 1)
        for head in range(heads):
            both = jnp.where(key_index > query_index, band_ref[1, head], band_ref[0, head])
            by_row = both[0:8]
            for first_row in range(8, tile, 8):
                by_row = by_row + pltpu.roll(both[first_row : first_row + 8], tile - first_row, 1)
            folded = by_row[0:1]
            for row in range(1, 8):
                folded = folded + pltpu.roll(by_row, tile - row, 1)[row : row + 1]
            fold_ref[head : head + 1, :] += folded

    if last_call:
        scale = width ** (-0.5)
        upper = jnp.concatenate([dq_t[0], dq_t[1]], axis=0)
        lower = jnp.concatenate([dq_t[2], jnp.zeros((width, rows), f32)], axis=0)
        dq_ref[:, 0:128] = (upper.T * scale).astype(bf16)
        dq_ref[:, 128:256] = (lower.T * scale).astype(bf16)


def attention_backward(
    masks, scalars, far_bias, offsets, queries, bias_own, bias_next, lse, blocks, given,
    piece_count, heads, width,
):
    rows = queries.shape[0]
    half = rows // 2
    shape = jax.ShapeDtypeStruct
    first_call, last_call = masks[0] == 3, masks[0] == 0
    if last_call:
        given = (bias_own,) + tuple(given)
    outs = (shape((heads, width, rows), f32),)
    if first_call:
        outs = (shape((rows, 256), bf16), shape((16, rows), f32)) + outs
    if first_call:
        outs = outs + (shape((half, 384), bf16),) * 2
    else:
        outs = outs + (shape((rows, 384), bf16),) * len(masks)
    if last_call:
        outs = outs + (shape((rows, 256), bf16),)
    outs = outs + (shape((8, tile), f32),)

    return pl.pallas_call(
        functools.partial(attention_backward_kernel, heads, width, masks, piece_count),
        out_shape=outs,
        in_specs=[SMEM, SMEM, SMEM]
        + [pl.BlockSpec(memory_space=pl.ANY)] * len(blocks)
        + [VMEM] * (3 + len(given)),
        out_specs=(VMEM,) * len(outs),
        scratch_shapes=[
            pltpu.VMEM((heads, rows, 256), bf16),
            pltpu.VMEM((heads, rows, 256), bf16),
            pltpu.VMEM((heads, width, rows), bf16),
            pltpu.VMEM((rows, 384), bf16),
            pltpu.VMEM((2, heads, tile, tile), f32),
            pltpu.VMEM((len(masks), rows, 384), bf16),
            pltpu.SemaphoreType.DMA((len(blocks),)),
        ],
        compiler_params=pltpu.CompilerParams(vmem_limit_bytes=60 * 2**20),
        cost_estimate=pl.CostEstimate(
            flops=10 * rows * rows * 256 * heads if first_call else 0,
            bytes_accessed=10 * 2**20 if first_call else 2**10,
            transcendentals=0,
        ),
        name="attention_backward",
    )(scalars, far_bias, offsets, *blocks, queries, lse, bias_next, *given)


bucket_edges = np.array(
    [19, 21, 24, 27, 31, 35, 40, 46, 52, 59, 67, 77, 87, 99, 113], dtype=np.int32
)


def bucket_tiles():
    key = np.arange(tile)[None, :, None]
    query = np.arange(tile)[None, None, :]
    lag = np.arange(3)[:, None, None] * tile + query - key
    clipped = np.maximum(lag, 0)
    counted = (clipped[..., None] >= bucket_edges).sum(-1)
    return np.where(clipped < 16, clipped, 16 + counted).astype(np.int32)


def shape(dims, dtype):
    return jax.ShapeDtypeStruct(dims, dtype)


def params(mebibytes):
    return pltpu.CompilerParams(vmem_limit_bytes=mebibytes * 2**20)


def cost(flops, bytes_accessed):
    return pl.CostEstimate(flops=flops, bytes_accessed=bytes_accessed, transcendentals=0)


def gelu_constants():
    return 0.7978845608028654, 0.044715


def prepare_kernel(
    part, padded, scalars, route_ref, order_ref, rows_ref, columns_ref, ranks, hot_ref, tall,
):
    pair_count = order_ref.shape[1]
    rows = pair_count // 2
    expert_pad = hot_ref.shape[0]
    step = 256
    live_end = scalars[2] - scalars[0] * rows
    order = order_ref[...]
    index_row = lax.broadcasted_iota(jnp.int32, (pair_count, 128), 0)
    index_lane = lax.broadcasted_iota(jnp.int32, (pair_count, 128), 1)
    digits = jnp.where(
        index_lane == 0, index_row // 64, jnp.where(index_lane == 1, index_row % 64, 0)
    ).astype(f32).astype(bf16)

    def rank_step(index, carry):
        start = aligned(index * step, step)
        pair = start + lax.broadcasted_iota(jnp.int32, (step, pair_count), 0)
        hit = (pair == order).astype(f32).astype(bf16)
        found = dot_nn(hit, digits)
        position = found[:, 0:1] * 64.0 + found[:, 1:2]
        ranks[pl.ds(start, step), :] = jnp.broadcast_to(position, (step, 128))
        return carry

    lax.fori_loop(0, pair_count // step, rank_step, 0)
    rank_row = ranks[...].T[0:1, :]
    position = lax.broadcasted_iota(jnp.int32, (1, rows), 1)
    live = position < live_end
    expert_row = jnp.concatenate([route_ref[0:1, :], route_ref[1:2, :]], axis=1)
    live_row = jnp.concatenate([live, live], axis=1)
    expert_index = lax.broadcasted_iota(jnp.int32, (expert_pad, pair_count), 0)
    hot = ((expert_index == expert_row) & live_row).astype(f32)
    hot_ref[...] = hot.astype(bf16)

    def count_step(index, counts):
        start = aligned(index * step, step)
        earlier = (ranks[pl.ds(start, step), 0:1] < rank_row).astype(f32).astype(bf16)
        return counts + dot_nn(hot_ref[:, pl.ds(start, step)], earlier)

    counts = lax.fori_loop(
        0, pair_count // step, count_step, jnp.zeros((expert_pad, pair_count), f32)
    )
    slot = jnp.sum(counts * hot, axis=0, keepdims=True).astype(jnp.int32)
    own = slot - (scalars[3] & 1) * part
    place = jnp.where(live_row & (own >= 0) & (own < part), expert_row * padded + own, -1)
    rows_ref[...] = jnp.full_like(rows_ref, -1)
    rows_ref[0:1, :] = place[:, 0:rows]
    rows_ref[1:2, :] = place[:, rows:]
    tall[...] = jnp.full_like(tall, -1.0)
    tall[0:1, :] = place[:, 0:rows].astype(f32)
    tall[1:2, :] = place[:, rows:].astype(f32)
    columns_ref[...] = tall[...].T.astype(jnp.int32)


def bias_kernel(table, bias_own, bias_next):
    key = lax.broadcasted_iota(jnp.int32, (8, tile), 0)
    query = lax.broadcasted_iota(jnp.int32, (8, tile), 1)
    heads = bias_own.shape[0]

    def bias_step(index, carry):
        start = aligned(index * 8, 8)
        for band, bias_ref in enumerate((bias_own, bias_next)):
            lag = band * tile + query - key - start
            found = [jnp.full((8, tile), table[0, head], f32) for head in range(heads)]
            for bucket, edge in enumerate(list(range(1, 17)) + list(bucket_edges), start=1):
                beyond = lag >= int(edge)
                found = [
                    jnp.where(beyond, table[bucket, head], found[head]) for head in range(heads)
                ]
            for head in range(heads):
                bias_ref[head, pl.ds(start, 8), :] = found[head]
        return carry

    lax.fori_loop(0, tile // 8, bias_step, 0)


def bias_tiles(table, heads):
    return pl.pallas_call(
        bias_kernel,
        out_shape=(shape((heads, tile, tile), f32),) * 2,
        in_specs=[SMEM],
        out_specs=(VMEM,) * 2,
        compiler_params=params(40),
        cost_estimate=cost(10**9, 2 * 2**20),
        name="bias_tiles",
    )(table)


def prepare(scalars, route_rows, order_row, expert_count, part, padded):
    rows = route_rows.shape[1]
    expert_pad = max(16, expert_count)
    return pl.pallas_call(
        functools.partial(prepare_kernel, part, padded),
        out_shape=(
            shape((8, rows), jnp.int32),
            shape((rows, 128), jnp.int32),
        ),
        in_specs=[SMEM, VMEM, VMEM],
        out_specs=(VMEM,) * 2,
        scratch_shapes=[
            pltpu.VMEM((2 * rows, 128), f32),
            pltpu.VMEM((expert_pad, 2 * rows), bf16),
            pltpu.VMEM((128, rows), f32),
        ],
        compiler_params=params(40),
        cost_estimate=cost(10 * 10**9, 3 * 2**20),
        name="prepare",
    )(scalars, route_rows, order_row)


def pack_kernel(query, key, value, output, gain_one, gain_two, router, block):
    size = query.shape[0]
    experts = router.shape[0]
    block[...] = jnp.zeros_like(block)
    block[:, 0:192] = query[...]
    gains = jnp.concatenate([gain_one[...], gain_two[...]], axis=0).astype(f32)
    block[:, 192:194] = gains.T.astype(bf16)
    block[:, 256:448] = key[...]
    block[:, 448:512] = value[:, 128:192]
    block[:, 512:640] = value[:, 0:128]
    block[:, 640:832] = output[...].astype(f32).T.astype(bf16)
    block[:, 832 : 832 + experts] = router[...].astype(f32).T.astype(bf16)


def pack_weights(query, key, value, output, gain_one, gain_two, router):
    size = query.shape[0]
    return pl.pallas_call(
        pack_kernel,
        out_shape=shape((size, 896), bf16),
        in_specs=[VMEM] * 7,
        out_specs=VMEM,
        compiler_params=params(60),
        cost_estimate=cost(0, 2**19),
        name="pack_weights",
    )(query, key, value, output, gain_one[None], gain_two[None], router.T)


def project_kernel(piece_count, offsets, token_ref, *rest):
    pieces = rest[:piece_count]
    hidden_ref, query_ref, kv_ref, weight_ref, output_ref, gain_ref = rest[piece_count:]
    for index, piece in enumerate(pieces):
        span = pl.ds(aligned(offsets[index], 16), piece.shape[0])
        weight_ref[span, :] = piece[:, 0:640]
        output_ref[span, :] = piece[:, 640:896]
    rows = token_ref.shape[0]
    gains = weight_ref[:, 128:256].astype(f32).T
    gain_ref[0:1, :] = gains[64:65, :]
    gain_ref[1:2, :] = gains[65:66, :]
    step = 256
    lane = lax.broadcasted_iota(jnp.int32, (step, 256), 1)
    for start in range(0, rows, step):
        inputs = token_ref[start : start + step, :].astype(f32)
        scale = lax.rsqrt(jnp.mean(inputs * inputs, axis=-1, keepdims=True) + epsilon)
        hidden = (inputs * scale * gain_ref[0:1, :]).astype(bf16)
        hidden_ref[start : start + step, :] = hidden
        queries = dot_nn(hidden, weight_ref[:, 0:256]).astype(bf16)
        query_ref[start : start + step, :] = jnp.where(
            lane < 192, queries * bf16(0.125), jnp.zeros_like(queries)
        )
        kv_ref[start : start + step, :] = dot_nn(hidden, weight_ref[:, 256:640]).astype(bf16)


def project(offsets, tokens, pieces):
    rows, model = tokens.shape
    return pl.pallas_call(
        functools.partial(project_kernel, len(pieces)),
        out_shape=(
            shape((rows, model), bf16),
            shape((rows, 256), bf16),
            shape((rows, 384), bf16),
            shape((model, 640), bf16),
            shape((model, 256), bf16),
            shape((8, model), f32),
        ),
        in_specs=[SMEM, VMEM] + [VMEM] * len(pieces),
        out_specs=(VMEM,) * 6,
        compiler_params=params(40),
        cost_estimate=cost(2 * rows * model * 640, 6 * 2**20),
        name="project",
    )(offsets, tokens, *pieces)


def assemble_kernel(piece_count, offsets, *rest):
    pieces = rest[:piece_count]
    out_ref = rest[piece_count]
    for index, piece in enumerate(pieces):
        size = piece.shape[0]
        out_ref[pl.ds(aligned(offsets[index], 16), size), :] = piece[...].astype(out_ref.dtype)


def assemble(offsets, pieces, dtype):
    total = sum(piece.shape[0] for piece in pieces)
    width = pieces[0].shape[1]
    return pl.pallas_call(
        functools.partial(assemble_kernel, len(pieces)),
        out_shape=shape((total, width), dtype),
        in_specs=[SMEM] + [VMEM] * len(pieces),
        out_specs=VMEM,
        compiler_params=params(40),
        cost_estimate=cost(0, 6 * total * width),
        name="assemble",
    )(offsets, *pieces)


def route_half(
    width, expert_count, part, token_ref, gain_ref, route_ref, attended, weights, packed, joined,
    hidden_ref, info_ref,
):
    half = packed.shape[1]
    quarter = half // 2
    lane_low = lax.broadcasted_iota(jnp.int32, (quarter, 128), 1)
    for source in range(4):
        piece = attended[source]
        middle = piece[:, 128:256].astype(f32)
        packed[source, 0:quarter, 0:128] = piece[:, 0:128]
        packed[source, 0:quarter, 128:256] = jnp.where(lane_low < width, middle, 0.0).astype(bf16)
        packed[source, quarter:, 0:128] = piece[:, 256:384]
        packed[source, quarter:, 128:256] = jnp.where(
            lane_low < width, pltpu.roll(middle, 64, 1), 0.0
        ).astype(bf16)
    step = quarter
    lane = lax.broadcasted_iota(jnp.int32, (step, 128), 1)
    valid = (lane >= 64) & (lane < 64 + expert_count)

    def token_step(index, carry):
        span = pl.ds(aligned(index * step, step), step)
        where = pl.ds(aligned(part * half + index * step, step), step)
        residual = token_ref[where, :].astype(f32)
        for source in range(4):
            residual = residual + dot_nt(packed[source, span, :], weights[source][...])
        joined[span, :] = residual
        scale = lax.rsqrt(jnp.mean(residual * residual, axis=-1, keepdims=True) + epsilon)
        hidden = (residual * scale * gain_ref[1:2, :]).astype(bf16)
        hidden_ref[span, :] = hidden
        logits = dot_nn(hidden, weights[0][:, 128:256])
        logits = jnp.where(valid, logits, masked_value)
        powers = jnp.where(valid, jnp.exp(logits - jnp.max(logits, axis=-1, keepdims=True)), 0.0)
        probs = powers / jnp.sum(powers, axis=-1, keepdims=True)
        first = jnp.sum(
            jnp.where(lane == route_ref[where, 0:1] + 64, probs, 0.0), axis=-1, keepdims=True
        )
        second = jnp.sum(
            jnp.where(lane == route_ref[where, 1:2] + 64, probs, 0.0), axis=-1, keepdims=True
        )
        total = first + second
        info_ref[span, :] = jnp.where(
            lane == 0,
            first / total,
            jnp.where(lane == 1, second / total, jnp.where(lane == 2, total, probs)),
        )
        return carry

    lax.fori_loop(0, half // step, token_step, 0)


def dispatch_kernel(
    width, expert_count, padded, scalars, token_ref, gain_ref, route_ref, row_place, *rest
):
    attended, weights = rest[0:4], rest[4:8]
    residual_ref, hidden_ref, info_ref, attended_ref, sent = rest[8:13]
    packed, joined, column = rest[13:]
    rows, model = token_ref.shape
    half, quarter = rows // 2, rows // 4
    for part in range(2):
        span = pl.ds(part * half, half)
        route_half(
            width, expert_count, part, token_ref, gain_ref, route_ref,
            [piece.at[pl.ds(part * quarter, quarter), :] for piece in attended], weights,
            packed.at[part], joined.at[span, :], hidden_ref.at[span, :], info_ref.at[span, :],
        )
    rank = scalars[3]
    here = aligned(lax.rem(rank, 2) * quarter, quarter)
    residual_ref[...] = joined[pl.ds(aligned(rank * quarter, quarter), quarter), :]
    for source in range(4):
        attended_ref[:, source * 256 : (source + 1) * 256] = packed[
            rank // 2, source, pl.ds(here, quarter), :
        ]
    gates = info_ref[...].T
    gate_one, gate_two = gates[0:1, :], gates[1:2, :]
    place_one, place_two = row_place[0:1, :], row_place[1:2, :]
    column[...] = jnp.zeros_like(column)

    taken = 4 * padded

    def expert_rows(index, carry):
        start = aligned(index * taken, 64)
        slot = start + lax.broadcasted_iota(jnp.int32, (taken, rows), 0)
        hit_one, hit_two = slot == place_one, slot == place_two
        picked = jnp.where(hit_one | hit_two, 1.0, 0.0).astype(bf16)
        sent[pl.ds(start, taken), :] = dot_nn(picked, hidden_ref[...]).astype(bf16)
        gate = jnp.where(hit_one, gate_one, jnp.where(hit_two, gate_two, 0.0))
        gate = jnp.sum(gate, axis=-1, keepdims=True)
        for chunk in range(4):
            write_digits(
                sent, column, start + chunk * padded, padded,
                gate[chunk * padded : (chunk + 1) * padded],
            )
        return carry

    lax.fori_loop(0, expert_count // 4, expert_rows, 0)


def write_digits(rows_ref, column, start, padded, values):
    column[0:padded, :] = jnp.broadcast_to(values, (padded, 128))
    row = column[...].T[0:1, :]
    high = row.astype(bf16).astype(f32)
    middle = (row - high).astype(bf16).astype(f32)
    low = row - high - middle
    size = row.shape[1]
    index = lax.broadcasted_iota(jnp.int32, (16, size), 0)
    block = jnp.where(
        index == 0, high, jnp.where(index == 1, middle, jnp.where(index == 2, low, 0.0))
    )
    span = pl.ds(aligned(start + padded - 16, 16), 16)
    rows_ref[span, 0:size] = block.astype(bf16)
    rows_ref[span, size:] = jnp.zeros((16, rows_ref.shape[1] - size), bf16)


def read_digits(rows_ref, start, padded):
    wide = (padded + 127) // 128 * 128
    span = pl.ds(aligned(start + padded - 16, 16), 16)
    return jnp.sum(rows_ref[span, 0:wide].astype(f32), axis=0, keepdims=True)


def dispatch(
    scalars, tokens, gains, routes, row_place, attended, weights, width, expert_count, padded
):
    rows, model = tokens.shape
    slots = expert_count * padded
    wide = (padded + 127) // 128 * 128
    return pl.pallas_call(
        functools.partial(dispatch_kernel, width, expert_count, padded),
        out_shape=(
            shape((rows // 4, model), f32),
            shape((rows, model), bf16),
            shape((rows, 128), f32),
            shape((rows // 4, 1024), bf16),
            shape((slots, model), bf16),
        ),
        in_specs=[SMEM] + [VMEM] * 12,
        out_specs=(VMEM,) * 5,
        scratch_shapes=[
            pltpu.VMEM((2, 4, rows // 2, 256), bf16),
            pltpu.VMEM((rows, model), f32),
            pltpu.VMEM((wide, 128), f32),
        ],
        compiler_params=params(60),
        cost_estimate=cost(2 * rows * model * (1024 + slots), 16 * 2**20),
        name="dispatch",
    )(scalars, tokens, gains, routes, row_place, *attended, *weights)


def scatter_kernel(value_ref, row_place, sent):
    rows = value_ref.shape[0]
    place_one, place_two = row_place[0:1, :], row_place[1:2, :]
    fill = sent.shape[0] // 2

    def slot_step(index, carry):
        start = aligned(index * fill, fill)
        slot = start + lax.broadcasted_iota(jnp.int32, (fill, rows), 0)
        picked = jnp.where((slot == place_one) | (slot == place_two), 1.0, 0.0).astype(bf16)
        sent[pl.ds(start, fill), :] = dot_nn(picked, value_ref[...]).astype(bf16)
        return carry

    lax.fori_loop(0, sent.shape[0] // fill, slot_step, 0)


def scatter_rows(values, row_place, slots):
    rows, model = values.shape
    return pl.pallas_call(
        scatter_kernel,
        out_shape=shape((slots, model), bf16),
        in_specs=[VMEM, VMEM],
        out_specs=VMEM,
        compiler_params=params(40),
        cost_estimate=cost(2 * rows * model * slots, 6 * 2**20),
        name="scatter_rows",
    )(values, row_place)


def expert_kernel(
    padded, in_own, in_partner, out_own, out_first, out_second, rows_ref, grads_ref, acted_ref,
    pre_ref, back_ref, column, gate_ref,
):
    hidden = in_own.shape[1]
    root, cubic = gelu_constants()
    wide = column.shape[0]
    column[...] = jnp.zeros_like(column)
    chunk_count = rows_ref.shape[0] // padded
    for chunk in range(chunk_count):
        gates = read_digits(rows_ref, chunk * padded, padded)
        gates = jnp.broadcast_to(gates, (128, wide)).T[0:padded, :]
        gate_ref[chunk * padded : (chunk + 1) * padded, :] = gates
    gate = jnp.concatenate([gate_ref[...], gate_ref[...]], axis=1)
    cut = out_first.shape[0]
    places = [(side, first) for side in range(2) for first in range(0, hidden, 256)]

    def products(side, first):
        part = slice(first, first + 256)
        if side == 0:
            inner, outer = in_own[:, part], out_own[part, :]
        elif first < cut:
            inner, outer = in_partner[:, part], out_first[part, :]
        else:
            inner, outer = in_partner[:, part], out_second[first - cut : first - cut + 256, :]
        return dot_nn(rows_ref[...], inner), dot_nt(grads_ref[...], outer)

    gate_part = None
    found = products(*places[0])
    for index, (side, first) in enumerate(places):
        pre, grad_acted = found
        if index + 1 < len(places):
            found = products(*places[index + 1])
        part = slice(first, first + 256)
        square = pre * pre
        share_on = 0.5 + 0.5 * jnp.tanh(pre * (root + root * cubic * square))
        acted = pre * share_on
        slope = share_on + acted * (1.0 - share_on) * (2.0 * root + 6.0 * root * cubic * square)
        acted_ref[side, :, part] = (acted * gate).astype(bf16)
        product = grad_acted * acted
        folded = product[:, 0:128] + product[:, 128:256]
        gate_part = folded if gate_part is None else gate_part + folded
        pre_ref[side, :, part] = (grad_acted * gate * slope).astype(bf16)
    back = dot_nt(pre_ref[0, :, :], in_own[...])
    back = back + dot_nt(pre_ref[1, :, :], in_partner[...])
    back_ref[:, :] = back.astype(bf16)
    gate_part = jnp.sum(gate_part, axis=-1, keepdims=True)
    for chunk in range(chunk_count):
        write_digits(
            back_ref, column, chunk * padded, padded,
            gate_part[chunk * padded : (chunk + 1) * padded],
        )


def expert_step(in_parts, out_parts, rows_in, grads_in, padded):
    slots, model = rows_in.shape
    hidden = in_parts[0].shape[1]
    wide = (padded + 127) // 128 * 128
    taken = 4 * padded

    def whole(value):
        return pl.BlockSpec(value.shape, lambda index: (0, 0), pipeline_mode=pl.Buffered(1))

    rows_spec = pl.BlockSpec((taken, model), lambda index: (index, 0))
    hidden_spec = pl.BlockSpec((2, taken, hidden), lambda index: (0, index, 0))
    return pl.pallas_call(
        functools.partial(expert_kernel, padded),
        grid=(slots // taken,),
        out_shape=(
            shape((2, slots, hidden), bf16),
            shape((2, slots, hidden), bf16),
            shape((slots, model), bf16),
        ),
        in_specs=[whole(part) for part in (*in_parts, *out_parts)] + [rows_spec] * 2,
        out_specs=(hidden_spec, hidden_spec, rows_spec),
        scratch_shapes=[pltpu.VMEM((wide, 128), f32), pltpu.VMEM((taken, 128), f32)],
        compiler_params=params(60),
        cost_estimate=cost(12 * slots * model * hidden, 24 * 2**20),
        name="expert_step",
    )(*in_parts, *out_parts, rows_in, grads_in)


def expert_out_kernel(acted_ref, out_own, out_first, out_second, out_ref):
    step = out_ref.shape[0] // 4
    cut = out_first.shape[0]

    def one(index, carry):
        span = pl.ds(aligned(index * step, 16), step)
        total = dot_nn(acted_ref[0, span, :], out_own[...])
        total = total + dot_nn(acted_ref[1, span, 0:cut], out_first[...])
        total = total + dot_nn(acted_ref[1, span, cut:], out_second[...])
        out_ref[span, :] = total.astype(bf16)
        return carry

    lax.fori_loop(0, 4, one, 0)


def expert_outputs(acted, out_parts):
    _, slots, hidden = acted.shape
    model = out_parts[0].shape[1]
    return pl.pallas_call(
        expert_out_kernel,
        out_shape=shape((slots, model), bf16),
        in_specs=[VMEM] * 4,
        out_specs=VMEM,
        compiler_params=params(60),
        cost_estimate=cost(4 * slots * model * hidden, 10 * 2**20),
        name="expert_outputs",
    )(acted, *out_parts)


def write_ring(scalars, joined, own, next_ref, last_ref, far_one, far_two):
    quarter = own.shape[0]
    eighth = quarter // 2
    rank = scalars[3]

    def rows_of(which):
        return aligned(lax.rem(rank + which, 4) * quarter, quarter)

    own[...] = joined[pl.ds(rows_of(0), quarter), :]
    next_ref[...] = joined[pl.ds(rows_of(1), quarter), :].astype(bf16)
    last_ref[...] = joined[pl.ds(rows_of(3), quarter), :].astype(bf16)
    far = rows_of(2)
    far_one[...] = joined[pl.ds(far, eighth), :].astype(bf16)
    far_two[...] = joined[pl.ds(aligned(far + eighth, eighth), eighth), :].astype(bf16)


def ring_shapes(rows, model):
    quarter, eighth = shape((rows // 4, model), bf16), shape((rows // 8, model), bf16)
    return (shape((rows // 4, model), f32), quarter, quarter, eighth, eighth)


def combine_grads_kernel(
    expert_count, padded, far, scalars, place_ref, info_ref, route_ref, router_ref, back_ref, *rest
):
    if far:
        logit_ref, far_one, far_two, digits = rest
    else:
        far_logits, digits, logit_ref, own, next_ref, last_ref = rest
    rows = place_ref.shape[0]
    quarter, eighth = rows // 4, rows // 8
    slots = back_ref.shape[0]
    rank = scalars[3]
    wide = (padded + 127) // 128 * 128
    lane_digit = lax.broadcasted_iota(jnp.int32, (padded, 128), 1)

    def column_step(expert, carry):
        start = aligned(expert * padded, 16)
        row = jnp.broadcast_to(read_digits(back_ref, start, padded), (128, wide))
        column = row.T[0:padded, :]
        high = column.astype(bf16).astype(f32)
        middle = (column - high).astype(bf16).astype(f32)
        digits[pl.ds(start, padded), :] = jnp.where(
            lane_digit == 0,
            high,
            jnp.where(lane_digit == 1, middle, jnp.where(lane_digit == 2, column - high - middle, 0.0)),
        ).astype(bf16)
        return carry

    if far:
        lax.fori_loop(0, expert_count, column_step, 0)
    lane = lax.broadcasted_iota(jnp.int32, (quarter, 128), 1)
    slot = lax.broadcasted_iota(jnp.int32, (quarter, slots), 1)

    def rows_of(which):
        return pl.ds(aligned(lax.rem(rank + which, 4) * quarter, quarter), quarter)

    def tokens(which):
        span = rows_of(which)
        info, place = info_ref[span, :], place_ref[span, :]
        hit_one, hit_two = slot == place[:, 0:1], slot == place[:, 1:2]
        ones = jnp.where(hit_one | hit_two, 1.0, 0.0).astype(bf16)
        total = dot_nn(ones, back_ref[...])
        signs = jnp.where(hit_one, 1.0, jnp.where(hit_two, -1.0, 0.0)).astype(bf16)
        difference = jnp.sum(dot_nn(signs, digits[...]), axis=-1, keepdims=True) / info[:, 2:3]
        picked = jnp.where(
            lane == route_ref[span, 0:1] + 64,
            info[:, 1:2] * difference,
            jnp.where(lane == route_ref[span, 1:2] + 64, -info[:, 0:1] * difference, 0.0),
        )
        probs = jnp.where((lane >= 64) & (lane < 64 + expert_count), info, 0.0)
        grads = probs * (picked - jnp.sum(probs * picked, axis=-1, keepdims=True))
        grads = grads.astype(bf16)
        return grads, total + dot_nt(grads, router_ref[:, 128:256])

    if far:
        grads, total = tokens(2)
        logit_ref[...] = grads
        far_one[...] = total[0:eighth].astype(bf16)
        far_two[...] = total[eighth:].astype(bf16)
    else:
        logit_ref[rows_of(2), :] = far_logits[...]
        for which, target in ((1, next_ref), (3, last_ref)):
            grads, total = tokens(which)
            logit_ref[rows_of(which), :] = grads
            target[...] = total.astype(bf16)
        grads, total = tokens(0)
        logit_ref[rows_of(0), :] = grads
        own[...] = total


def combine_grads(far, scalars, place, info, routes, router, back, given, expert_count, padded):
    rows = place.shape[0]
    model = router.shape[0]
    slots = back.shape[0]
    half = shape((rows // 8, model), bf16)
    if far:
        outs = (shape((rows // 4, 128), bf16), half, half, shape((slots, 128), bf16))
    else:
        outs = (shape((rows, 128), bf16), shape((rows // 4, model), f32))
        outs = outs + (shape((rows // 4, model), bf16),) * 2
    return pl.pallas_call(
        functools.partial(combine_grads_kernel, expert_count, padded, far),
        out_shape=outs,
        in_specs=[SMEM] + [VMEM] * (5 + len(given)),
        out_specs=(VMEM,) * len(outs),
        compiler_params=params(60),
        cost_estimate=cost(2 * rows * model * slots, 8 * 2**20),
        name="combine_grads",
    )(scalars, place, info, routes, router, back, *given)


def combine_outs_kernel(place_ref, rows_ref, out_ref):
    step = 512
    slot = lax.broadcasted_iota(jnp.int32, (step, rows_ref.shape[0]), 1)

    def token_step(index, carry):
        span = pl.ds(aligned(index * step, step), step)
        place = place_ref[span, :]
        hit = (slot == place[:, 0:1]) | (slot == place[:, 1:2])
        out_ref[span, :] = dot_nn(jnp.where(hit, 1.0, 0.0).astype(bf16), rows_ref[...]).astype(bf16)
        return carry

    lax.fori_loop(0, out_ref.shape[0] // step, token_step, 0)


def combine_outs(place, rows_in):
    rows = place.shape[0]
    slots, model = rows_in.shape
    return pl.pallas_call(
        combine_outs_kernel,
        out_shape=shape((rows, model), bf16),
        in_specs=[VMEM] * 2,
        out_specs=VMEM,
        compiler_params=params(60),
        cost_estimate=cost(2 * rows * model * slots, 8 * 2**20),
        name="combine_outs",
    )(place, rows_in)


def received(own, from_last, from_next):
    return own[...] + from_last[...].astype(f32) + from_next[...].astype(f32)


def norm_back_kernel(gain_index, has_bypass_rows, scalars, value_ref, gain_ref, bypass_ref, *rest):
    grads = received(*rest[:3])
    rest = rest[3:]
    weights = ()
    if gain_index == 1:
        weights, rest = rest[0:4], rest[4:]
    else:
        blocks_ref, rest = rest[0], rest[1:]
    full_ref, low_ref, gain_grad = rest[0:3]
    quarter = grads.shape[0]
    here = pl.ds(aligned(scalars[3] * quarter, quarter), quarter)
    values = (value_ref[here, :] if gain_index == 0 else value_ref[...]).astype(f32)
    bypass = (bypass_ref[here, :] if has_bypass_rows else bypass_ref[...]).astype(f32)
    scale = lax.rsqrt(jnp.mean(values * values, axis=-1, keepdims=True) + epsilon)
    normed = values * scale
    scaled = grads * gain_ref[gain_index : gain_index + 1, :]
    gain_grad[...] = jnp.broadcast_to(
        jnp.sum(grads * normed, axis=0, keepdims=True), gain_grad.shape
    )
    out = bypass + scale * (scaled - normed * jnp.mean(scaled * normed, axis=-1, keepdims=True))
    full_ref[...] = out
    low = out.astype(bf16)
    if weights:
        low_ref[...] = low
    else:
        low_ref[...] = low
        for place in range(4):
            target = scalars[3] ^ place
            rest[3][target] = blocks_ref[:, place * 256 : (place + 1) * 256].astype(bf16)
    lane = lax.broadcasted_iota(jnp.int32, (quarter, 256), 1)
    for weight, target in zip(weights, rest[3:]):
        target[...] = jnp.where(lane < 192, dot_nn(low, weight[...]), 0.0).astype(bf16)


def norm_back(gain_index, has_bypass_rows, scalars, values, gains, bypass, parts, weights=(), blocks=None):
    quarter, model = parts[0].shape
    low = shape((quarter, model), bf16)
    extra, more = tuple(weights), (shape((quarter, 256), bf16),) * len(weights)
    if blocks is not None:
        extra, more = (blocks,), (shape((4, blocks.shape[0], 256), bf16),)
    return pl.pallas_call(
        functools.partial(norm_back_kernel, gain_index, has_bypass_rows),
        out_shape=(shape((quarter, model), f32), low, shape((8, model), f32)) + more,
        in_specs=[SMEM] + [VMEM] * (6 + len(extra)),
        out_specs=(VMEM,) * (3 + len(more)),
        compiler_params=params(60),
        cost_estimate=cost(quarter * model * 16, 6 * 2**20),
        name="norm_back",
    )(scalars, values, gains, bypass, *parts, *extra)


def finish_kernel(residual_ref, part_ref, out_ref):
    total = residual_ref[...]
    quarter = total.shape[0]
    for source in range(4):
        total = total + part_ref[source * quarter : (source + 1) * quarter, :].astype(f32)
    out_ref[...] = total.astype(bf16)


def finish(residual, parts):
    quarter, model = residual.shape
    return pl.pallas_call(
        finish_kernel,
        out_shape=shape((quarter, model), bf16),
        in_specs=[VMEM] * 2,
        out_specs=VMEM,
        compiler_params=params(40),
        cost_estimate=cost(quarter * model * 4, 4 * 2**20),
        name="finish",
    )(residual, parts)


def hidden_grad_kernel(
    scalars, dq_ref, weight_ref, own, beside, across, dkv_ref, *rest
):
    ring, joined = rest[:5], rest[5]
    half = own.shape[0] // 2
    for part in range(2):
        span = slice(part * half, (part + 1) * half)
        total = own[span, :].astype(f32) + beside[span, :].astype(f32) + across[span, :].astype(f32)
        total = total.astype(bf16)
        dkv_ref[span, :] = total
        joined[span, :] = dot_nt(dq_ref[span, :], weight_ref[:, 0:256]) + dot_nt(
            total, weight_ref[:, 256:640]
        )
    write_ring(scalars, joined, *ring)


def hidden_grad(scalars, dq, weights, own, beside, across):
    rows = dq.shape[0]
    model = weights.shape[0]
    return pl.pallas_call(
        hidden_grad_kernel,
        out_shape=(shape((rows, 384), bf16),) + ring_shapes(rows, model),
        in_specs=[SMEM] + [VMEM] * 5,
        out_specs=(VMEM,) * 6,
        scratch_shapes=[pltpu.VMEM((rows, model), f32)],
        compiler_params=params(40),
        cost_estimate=cost(2 * rows * model * 640, 8 * 2**20),
        name="hidden_grad",
    )(scalars, dq, weights, own, beside, across)


def split_by_side(scalars, whole, mine, other):
    half = mine.shape[0]
    side = scalars[5]
    mine[...] = whole[pl.ds(aligned(side * half, 16), half), :]
    other[...] = whole[pl.ds(aligned((1 - side) * half, 16), half), :].astype(other.dtype)


def output_grad_kernel(scalars, branch_ref, attended_ref, hidden_ref, logit_ref, *rest):
    outs, whole = rest[:-1], rest[-1]
    whole[...] = dot_tn(branch_ref[...], attended_ref[...])
    router = dot_tn(hidden_ref[...], logit_ref[...])
    for source in range(4):
        whole[:, source * 256 + 128 : source * 256 + 256] += router
    if len(outs) == 1:
        outs[0][...] = whole[...]
    else:
        size = outs[0].shape[0] // 4
        context, side = scalars[0], scalars[5]
        for out, masks in zip(outs, ((0, 2), (1, 3))):
            for place, mask in enumerate(masks):
                for far in range(2):
                    start = aligned((4 * (side ^ far) + (context ^ mask)) * size, 16)
                    target = slice((2 * place + far) * size, (2 * place + far + 1) * size)
                    out[target, :] = whole[pl.ds(start, size), :].astype(out.dtype)


def output_grads(scalars, branch, attended, hidden, grad_logits, small):
    rows, model = hidden.shape
    outs = (shape((model, 1024), f32),)
    if small:
        outs = (shape((model // 2, 1024), f32), shape((model // 2, 1024), bf16))
    return pl.pallas_call(
        output_grad_kernel,
        out_shape=outs,
        in_specs=[SMEM] + [VMEM] * 4,
        out_specs=(VMEM,) * len(outs),
        scratch_shapes=[pltpu.VMEM((model, 1024), f32)],
        compiler_params=params(60),
        cost_estimate=cost(2 * rows * model * 384, 6 * 2**20),
        name="output_grads",
    )(scalars, branch, attended, hidden, grad_logits)


def projection_grad_kernel(scalars, hidden_ref, dq_ref, dkv_ref, gain_ref, fold_ref, *rest):
    outs, whole = rest[:-1], rest[-1]
    hidden = hidden_ref[...]
    whole[:, 0:256] = dot_tn(hidden, dq_ref[...])
    whole[:, 256:640] = dot_tn(hidden, dkv_ref[...])
    lane = lax.broadcasted_iota(jnp.int32, (whole.shape[0], 128), 1)
    column = jnp.broadcast_to(gain_ref[0:1, :], (128, whole.shape[0])).T
    whole[:, 128:256] = jnp.where(lane < 64, whole[:, 128:256], column)
    if len(outs) == 2:
        side = scalars[5]
        block = outs[0].shape[0] // 4
        size = block - 8
        for which, out in ((side, outs[0]), (1 - side, outs[1])):
            for context in range(4):
                start = aligned((which * 4 + context) * size, 8)
                out[context * block : context * block + size, :] = whole[pl.ds(start, size), :]
                tail = slice(context * block + size, (context + 1) * block)
                out[tail, 0:256] = fold_ref[...]
                out[tail, 256:640] = jnp.zeros((8, 384), f32)
    else:
        outs[0][...] = whole[...]


def projection_grads(scalars, hidden, dq, dkv, gain_grad, fold, small):
    rows, model = hidden.shape
    outs = (shape((model // 2 + 32, 640), f32),) * 2 if small else (shape((model, 640), f32),)
    return pl.pallas_call(
        projection_grad_kernel,
        out_shape=outs,
        in_specs=[SMEM] + [VMEM] * 5,
        out_specs=(VMEM,) * len(outs),
        scratch_shapes=[pltpu.VMEM((model, 640), f32)],
        compiler_params=params(40),
        cost_estimate=cost(2 * rows * model * 640, 6 * 2**20),
        name="projection_grads",
    )(scalars, hidden, dq, dkv, gain_grad, fold)


def add_arrived_kernel(beside, across, arrived_one, arrived_two, beside_out, across_out):
    half = arrived_one.shape[0]
    beside_out[0:half, :] = beside[0:half, :]
    beside_out[half:, :] = (beside[half:, :].astype(f32) + arrived_two[...].astype(f32)).astype(bf16)
    across_out[0:half, :] = (across[0:half, :].astype(f32) + arrived_one[...].astype(f32)).astype(bf16)
    across_out[half:, :] = across[half:, :]


def add_arrived(beside, across, arrived_one, arrived_two):
    return pl.pallas_call(
        add_arrived_kernel,
        out_shape=(shape(beside.shape, bf16),) * 2,
        in_specs=[VMEM] * 4,
        out_specs=(VMEM,) * 2,
        compiler_params=params(60),
        cost_estimate=cost(beside.size, 8 * beside.size),
        name="add_arrived",
    )(beside, across, arrived_one, arrived_two)


def share_kernel(scalars, mine, other, *outs):
    size = outs[0].shape[0]
    context = scalars[0]
    for mask, out in enumerate(outs):
        span = pl.ds(aligned((context ^ mask) * size, 8), size)
        total = mine[span, :] + other[span, :].astype(f32)
        out[...] = total.astype(out.dtype)


def share(scalars, mine, other):
    rows, width = mine.shape
    return pl.pallas_call(
        share_kernel,
        out_shape=(shape((rows // 4, width), f32),) + (shape((rows // 4, width), other.dtype),) * 3,
        in_specs=[SMEM, VMEM, VMEM],
        out_specs=(VMEM,) * 4,
        compiler_params=params(40),
        cost_estimate=cost(rows * width, 12 * rows * width),
        name="share",
    )(scalars, mine, other)


def shift(value, amount):
    size = lax.axis_size("tensor")
    return lax.ppermute(value, "tensor", [(i, (i + amount) % size) for i in range(size)])


def cross(value, mask):
    size = lax.axis_size("context")
    return lax.ppermute(value, "context", [(i, i ^ mask) for i in range(size)])


def trade(value, mask):
    return lax.ppermute(value, "tensor", [(i, i ^ mask) for i in range(lax.axis_size("tensor"))])


def spread(value):
    across, beside = trade(value, 2), trade(value, 1)
    return [value, beside, across, trade(across, 1)]


def sum_ranks(value):
    total = value
    for step in (1, 2, 3):
        total = total + shift(value, step)
    return total


def added(first, second):
    return (first.astype(f32) + second.astype(f32)).astype(bf16)


def ring_start(far_one, far_two):
    return shift(far_one, 1), shift(far_two, -1)


def with_first(whole, arrived):
    half = arrived.shape[0]
    return jnp.concatenate([added(whole[:half], arrived), whole[half:]], axis=0)


def with_second(whole, arrived):
    half = arrived.shape[0]
    return jnp.concatenate([whole[:half], added(whole[half:], arrived)], axis=0)


def ring_finish(next_block, last_block, arrived_one, arrived_two):
    last_block, next_block = add_arrived(last_block, next_block, arrived_one, arrived_two)
    return shift(next_block, 1), shift(last_block, -1)


ALL_ROWS = ("dp", "context")


def exchange(rows_out):
    return lax.all_to_all(rows_out, ALL_ROWS, split_axis=0, concat_axis=0, tiled=True)


def gather_weights(block, small, axis):
    size = block.shape[axis]
    if not small:
        whole = lax.all_gather(block, ALL_ROWS, axis=axis, tiled=True)
        return [whole], jnp.zeros((1,), jnp.int32)
    context, side = lax.axis_index("context"), lax.axis_index("dp")
    pieces = [block] + [cross(block, mask) for mask in (1, 2, 3)]
    pieces = pieces + [lax.ppermute(piece, "dp", [(0, 1), (1, 0)]) for piece in pieces]
    return pieces, jnp.stack(
        [((side ^ far) * 4 + (context ^ mask)) * size for far in range(2) for mask in range(4)]
    )


def swap_sides(parts):
    if len(parts) == 1:
        return parts
    return parts[0], lax.ppermute(parts[1], "dp", [(0, 1), (1, 0)])


def share_blocks(scalars, parts):
    return parts if len(parts) == 1 else share(scalars, *parts)


def halve(mine, arrived):
    total = mine + arrived.astype(f32)
    half = total.shape[0] // 2
    return total[:half], total[half:].astype(bf16)


def scatter_blocks(blocks):
    if len(blocks) == 1:
        return lax.psum_scatter(blocks[0], ALL_ROWS, scatter_dimension=0, tiled=True)
    total = blocks[0]
    for mask in (1, 2, 3):
        total = total + cross(blocks[mask], mask).astype(f32)
    return total


def on_device(
    tokens_in, query_weight, key_weight, value_weight, output_weight, bias_table, attention_gain,
    router_weight, expert_gain, expert_in, expert_out, routes, pair_order, seq_lengths, cotangent,
):
    rows, model = tokens_in.shape
    heads = bias_table.shape[1]
    width = query_weight.shape[1] // heads
    group_rows = rows * lax.axis_size("context")
    expert_count = router_weight.shape[1]
    capacity = (9 * rows + 4 * expert_count - 1) // (4 * expert_count)
    count = lax.axis_size("dp") * lax.axis_size("context")
    small = count == 8
    context, rank = lax.axis_index("context"), lax.axis_index("tensor")
    here = lax.axis_index("dp") * lax.axis_size("context") + context
    first_end = seq_lengths[0, 0]
    second_end = first_end + seq_lengths[0, 1]
    side = lax.axis_index("dp")
    scalars = jnp.stack([context, first_end, second_end, rank, here, side]).astype(jnp.int32)
    part = capacity // 2
    padded = (part + 15) // 16 * 16 + 16
    slots = expert_count * padded
    shard = query_weight.shape[0]
    block = pack_weights(
        query_weight, key_weight, value_weight, output_weight, attention_gain, expert_gain, router_weight
    )
    tie = lax.optimization_barrier
    half, quarter = rows // 2, rows // 4
    far_block = (context ^ 3) * rows
    kv_offsets = jnp.stack(
        [context * rows, (context ^ 1) * rows, (context ^ 2) * rows, far_block, far_block + half]
    )
    token_offsets = jnp.stack([(rank ^ mask) * quarter for mask in range(4)])
    far_bias = bias_table[-1]
    order_row = (pair_order & 1) * rows + (pair_order >> 1)
    pieces, offsets = gather_weights(block, small, 0)
    in_partner, out_first = trade(expert_in[0], 1), trade(expert_out[0, :256], 1)
    bias_own, bias_next = bias_tiles(bias_table, heads)
    offsets, bias_own, bias_next = tie((offsets, bias_own, bias_next))
    hidden_one, queries, kv_own, weights, output_own, gains = project(
        offsets, tokens_in, pieces
    )
    kv_beside, kv_across = cross(kv_own, 1), cross(kv_own, 2)
    output_across, output_beside = trade(output_own, 2), trade(output_own, 1)
    order_row, queries = tie((order_row, queries))
    row_place, column_place = prepare(
        scalars, routes.T, order_row, expert_count, part, padded
    )
    states = attention_near(
        scalars, far_bias, queries, bias_own, bias_next, kv_own, heads, width
    )
    kv_beside, kv_across, row_place, states = tie((kv_beside, kv_across, row_place, states))
    kv_far = cross(kv_beside[:half], 2), cross(kv_across[half:], 1)
    kv_pieces = (kv_own, kv_beside, kv_across) + kv_far
    cotangent_rows = scatter_rows(cotangent, row_place, slots)
    states, kv_pieces, cotangent_rows, in_partner, output_across, output_beside = tie(
        (states, kv_pieces, cotangent_rows, in_partner, output_across, output_beside)
    )
    output_parts = [output_own, output_beside, output_across, trade(output_across, 1)]
    packed, lse = attention_far(
        scalars, far_bias, kv_offsets, queries, bias_next, states, kv_pieces, group_rows, heads,
        width,
    )
    packed, output_parts, out_first, cotangent_rows = tie(
        (packed, output_parts, out_first, cotangent_rows)
    )
    attended = spread(packed)
    cotangent_rows = exchange(cotangent_rows)
    attended, cotangent_rows = tie((attended, cotangent_rows))
    out_second, attended = tie((expert_out[0, 256:], attended))
    out_second = trade(out_second, 1)
    residual, hidden_two, info, attended_here, rows_out = dispatch(
        scalars, tokens_in, gains, routes, row_place, attended, output_parts, width, expert_count,
        padded,
    )
    in_parts, out_parts = (expert_in[0], in_partner), (expert_out[0], out_first, out_second)
    expert_rows = exchange(rows_out)
    acted, grad_pre, back = expert_step(
        in_parts, out_parts, expert_rows, cotangent_rows, padded
    )
    back = exchange(back)
    in_grad_partner = dot_tn(expert_rows, grad_pre[1]).astype(bf16)
    out_grad_partner = dot_tn(acted[1], cotangent_rows).astype(bf16)
    in_grad_partner, out_grad_partner, acted, grad_pre = tie(
        (in_grad_partner, out_grad_partner, acted, grad_pre)
    )
    in_grad_partner = trade(in_grad_partner, 1)
    outs = expert_outputs(acted, out_parts)
    expert_out_grad = dot_tn(acted[0], cotangent_rows)
    expert_in_grad = dot_tn(expert_rows, grad_pre[0])
    back, outs, expert_out_grad, expert_in_grad = tie(
        (back, outs, expert_out_grad, expert_in_grad)
    )
    combine = (scalars, column_place, info, routes, output_own, back)
    far_logits, *far, digits = combine_grads(True, *combine, (), expert_count, padded)
    arrived = ring_start(*far)
    grad_logits, own, *ring = combine_grads(
        False, *combine, (far_logits, digits), expert_count, padded
    )
    arrived, ring, outs, in_grad_partner = tie((arrived, ring, outs, in_grad_partner))
    ring, outs = (own,) + ring_finish(*ring, *arrived), exchange(outs)
    ring, outs = tie((ring, outs))
    grad_one, grad_branch, gain_two_grad, *grad_heads = norm_back(
        1, True, scalars, residual, gains, cotangent, ring, output_parts
    )
    head_pieces = (grad_heads[0],) + tuple(trade(grad_heads[mask], mask) for mask in (1, 2, 3))
    outer = output_grads(scalars, grad_branch, attended_here, hidden_two, grad_logits, small)
    mixed = combine_outs(column_place, outs)
    head_pieces, mixed, out_grad_partner, outer = tie(
        (head_pieces, mixed, out_grad_partner, outer)
    )
    if small:
        outer = outer[0], cross(outer[1], 1)
    out_grad_partner = trade(out_grad_partner, 1)
    mixed = lax.all_to_all(mixed, "tensor", split_axis=0, concat_axis=0, tiled=True)
    shared = (scalars, far_bias, token_offsets, queries, bias_own, bias_next, lse)
    dout, deltas, dq_t, far_one, far_two, fold = attention_backward(
        (3,), *shared, kv_far, (packed, *head_pieces), 4, heads, width
    )
    arrived = cross(far_one, 1), cross(far_two, 2)
    dq_t, beside, across, fold = attention_backward(
        (1, 2), *shared, (kv_beside, kv_across), (dout, deltas, dq_t, fold), 0, heads, width
    )
    beside, across = add_arrived(beside, across, *arrived)
    dq_t, mixed, beside, across, outer = tie((dq_t, mixed, beside, across, outer))
    from_square = cross(beside, 1), cross(across, 2)
    layer_own = finish(residual, mixed)
    dq_t, layer_own = tie((dq_t, layer_own))
    layer_far, layer_beside = trade(layer_own, 2), trade(layer_own, 1)
    dq_t, own, dq, fold = attention_backward(
        (0,), *shared, (kv_own,), (dout, deltas, dq_t, fold), 0, heads, width
    )
    dq, from_square, outer, out_grad_partner, layer_beside = tie(
        (dq, from_square, outer, out_grad_partner, layer_beside)
    )
    layer_last = trade(layer_far, 1)
    dkv, own, *ring = hidden_grad(scalars, dq, weights, own, *from_square)
    arrived = ring_start(*ring[2:4])
    inner_parts = projection_grads(scalars, hidden_one, dq, dkv, gain_two_grad, fold, small)
    if small:
        outer = halve(*outer)
        outer = halve(outer[0], cross(outer[1], 2))
    arrived, inner_parts, outer, layer_last = tie((arrived, inner_parts, outer, layer_last))
    inner_parts = swap_sides(inner_parts)
    ring = (
        own,
        shift(with_first(ring[0], arrived[0]), 1),
        shift(with_second(ring[1], arrived[1]), -1),
    )
    if small:
        outer_grads = outer[0] + swap_sides(outer)[1].astype(f32)
    else:
        outer_grads = lax.psum_scatter(outer[0], ALL_ROWS, scatter_dimension=0, tiled=True)
    inner_parts = share_blocks(scalars, inner_parts)
    ring, outer_grads, inner_parts = tie((ring, outer_grads, inner_parts))
    _, input_low, _, outer_grads = norm_back(
        0, False, scalars, tokens_in, gains, grad_one, ring, blocks=outer_grads
    )
    input_far, input_beside = trade(input_low, 2), trade(input_low, 1)
    outer_grads = lax.all_to_all(outer_grads, "tensor", split_axis=0, concat_axis=0, tiled=True)
    layer_own, input_far = tie((layer_own, input_far))
    layer_out = assemble(
        token_offsets, [layer_own, layer_beside, layer_far, layer_last], bf16
    )
    projected = scatter_blocks(inner_parts)
    expert_out_grad, expert_in_grad, projected = tie((expert_out_grad, expert_in_grad, projected))
    input_pieces = [input_low, input_beside, input_far, trade(input_far, 1)]
    input_grad = assemble(token_offsets, input_pieces, f32)
    outer_grads = jnp.sum(outer_grads.astype(f32), axis=0)
    expert_out_grad = (expert_out_grad + out_grad_partner.astype(f32))[None]
    expert_in_grad = (expert_in_grad + in_grad_partner.astype(f32))[None]
    output_grad = outer_grads[:, :192].T
    router_grad = outer_grads[:, 192 : 192 + expert_count]
    fold = projected[shard:, :256] if small else lax.psum(fold, ALL_ROWS)
    projected = projected[:shard]
    query_grad, key_grad = projected[:, :192], projected[:, 256:448]
    value_grad = jnp.concatenate([projected[:, 512:], projected[:, 448:512]], axis=1)
    gain_one_grad = jnp.sum(
        query_weight.astype(f32) * query_grad
        + key_weight.astype(f32) * key_grad
        + value_weight.astype(f32) * value_grad,
        axis=1,
        keepdims=True,
    )
    gain_grads = sum_ranks(jnp.concatenate([gain_one_grad, projected[:, 192:193]], axis=1))
    bucket_row = jnp.asarray(bucket_tiles()[0, 0])
    bucket_hot = (bucket_row[None, :] == jnp.arange(bias_table.shape[0] - 1)[:, None]).astype(f32)
    near_grad = jnp.sum(bucket_hot[:, None, :] * fold[None, :heads, :], axis=-1)
    table_grad = jnp.concatenate([near_grad, -jnp.sum(near_grad, axis=0, keepdims=True)], axis=0)
    return (
        layer_out,
        input_grad,
        query_grad,
        key_grad,
        value_grad,
        output_grad,
        table_grad,
        gain_grads[:, 0] / attention_gain.astype(f32),
        router_grad,
        gain_grads[:, 1],
        expert_in_grad,
        expert_out_grad,
    )


def solution(mesh):
    rows = P(("dp", "context"), None)
    return jax.shard_map(
        on_device,
        mesh=mesh,
        in_specs=(
            rows,
            P(("dp", "context"), "tensor"),
            P(("dp", "context"), "tensor"),
            P(("dp", "context"), "tensor"),
            P("tensor", ("dp", "context")),
            P(None, "tensor"),
            P(("dp", "context")),
            rows,
            P(("dp", "context")),
            P(("dp", "context"), None, "tensor"),
            P(("dp", "context"), "tensor", None),
            rows,
            rows,
            P("dp", None),
            rows,
        ),
        out_specs=(
            rows,
            rows,
            P(("dp", "context"), "tensor"),
            P(("dp", "context"), "tensor"),
            P(("dp", "context"), "tensor"),
            P("tensor", ("dp", "context")),
            P(None, "tensor"),
            P(("dp", "context")),
            rows,
            P(("dp", "context")),
            P(("dp", "context"), None, "tensor"),
            P(("dp", "context"), "tensor", None),
        ),
        check_vma=False,
    )
```

```python
import functools
import jax
import jax.numpy as jnp
import numpy as np
from jax import lax
from jax.experimental import pallas as pl
from jax.experimental.pallas import tpu as pltpu
from jax.sharding import PartitionSpec as P

bf16 = jnp.bfloat16
f32 = jnp.float32
epsilon = 1e-06
masked_value = -1e30
tile = 256
VMEM = pl.BlockSpec(memory_space=pltpu.VMEM)
SMEM = pl.BlockSpec(memory_space=pltpu.SMEM)


def dot_nn(a, b):
    return lax.dot_general(a, b, (((1,), (0,)), ((), ())), preferred_element_type=f32)


def dot_nt(a, b):
    return lax.dot_general(a, b, (((1,), (1,)), ((), ())), preferred_element_type=f32)


def dot_tn(a, b):
    return lax.dot_general(a, b, (((0,), (0,)), ((), ())), preferred_element_type=f32)


def start_of(position, first_end, second_end):
    return jnp.where(
        position >= second_end, second_end, jnp.where(position >= first_end, first_end, 0)
    )


def aligned(value, size):
    return pl.multiple_of(value, size)


def transpose_values(source, source_start, values_t, start, width):
    span, target = pl.ds(source_start, tile), pl.ds(start, tile)
    upper = source[span, 256:384].astype(f32).T.astype(bf16)
    lower = source[span, 128:256].astype(f32).T.astype(bf16)
    for head, part in enumerate((upper[0:width], upper[width:], lower[width:])):
        values_t[head, 0:width, target] = part
        values_t[head, width:, target] = jnp.ones((16, tile), bf16)


def masked_heads(queries, heads, width):
    lane = lax.broadcasted_iota(jnp.int32, queries.shape, 1) // width
    return [jnp.where(lane == head, queries, jnp.zeros_like(queries)) for head in range(heads)]


def absorb(
    keys_values, values_t, bias_ref, far_bias, best, running, index, masked_queries, heads,
    key_start, size, key_first, positions, row_start, bias_index, masked, first_time,
):
    keys = keys_values[pl.ds(key_start, size), 0:256]
    if masked:
        key_positions = (
            key_first + key_start + lax.broadcasted_iota(jnp.int32, (size, tile), 0)
        )
        seen = key_positions >= row_start
        if bias_index == 0:
            seen = seen & (key_positions <= positions)
    shift_by = [far_bias[head] if bias_index is None else 0.0 for head in range(heads)]
    scores = [dot_nt(keys, masked_queries[head]) for head in range(heads)]
    if bias_index is not None:
        scores = [scores[head] + bias_ref[bias_index][head] for head in range(heads)]
    if masked:
        scores = [jnp.where(seen, part, masked_value) for part in scores]
    tops = [
        jnp.max(scores[head], axis=0, keepdims=True) + shift_by[head] for head in range(heads)
    ]
    if first_time:
        new = tops
    else:
        old = [best[index, head, 0:1] for head in range(heads)]
        new = [jnp.maximum(old[head], tops[head]) for head in range(heads)]
    weights = [
        jnp.exp(scores[head] - (new[head] - shift_by[head])).astype(bf16) for head in range(heads)
    ]
    sums = [
        dot_nn(values_t[head, :, pl.ds(key_start, size)], weights[head]) for head in range(heads)
    ]
    for head in range(heads):
        if first_time:
            running[index, head] = sums[head]
        else:
            running[index, head] = running[index, head] * jnp.exp(old[head] - new[head]) + sums[head]
        best[index, head] = jnp.broadcast_to(new[head], (8, tile))


def attention_near_kernel(
    heads, width, scalars, far_bias, query_ref, bias_own, bias_next, keys_values, running, best,
    values_t,
):
    rows = query_ref.shape[0]
    context, first_end, second_end = scalars[0], scalars[1], scalars[2]
    base = context * rows

    def values_step(index, carry):
        start = aligned(index * tile, tile)
        transpose_values(keys_values, start, values_t, start, width)
        return carry

    lax.fori_loop(0, rows // tile, values_step, 0)

    def query_tile(index, carry):
        local = aligned(index * tile, tile)
        positions = base + local + lax.broadcasted_iota(jnp.int32, (1, tile), 1)
        row_start = start_of(positions, first_end, second_end)
        masked_queries = masked_heads(query_ref[pl.ds(local, tile), :], heads, width)

        def take(key_start, bias_index, first_time):
            absorb(
                keys_values, values_t, (bias_own, bias_next), far_bias, best, running, index,
                masked_queries, heads, key_start, tile, base, positions, row_start, bias_index,
                True, first_time,
            )

        take(local, 0, True)

        @pl.when(index > 0)
        def _():
            take(aligned(local - tile, tile), 1, False)

        def far_step(step, inner):
            take(aligned(step * tile, tile), None, False)
            return inner

        lax.fori_loop(0, jnp.maximum(index - 1, 0), far_step, 0)
        return carry

    lax.fori_loop(0, rows // tile, query_tile, 0)


def attention_near(scalars, far_bias, queries, bias_own, bias_next, keys_values, heads, width):
    rows = queries.shape[0]
    tiles = rows // tile
    return pl.pallas_call(
        functools.partial(attention_near_kernel, heads, width),
        out_shape=(
            jax.ShapeDtypeStruct((tiles, heads, width + 16, tile), f32),
            jax.ShapeDtypeStruct((tiles, heads, 8, tile), f32),
        ),
        in_specs=[SMEM, SMEM] + [VMEM] * 4,
        out_specs=(VMEM,) * 2,
        scratch_shapes=[pltpu.VMEM((heads, width + 16, rows), bf16)],
        compiler_params=pltpu.CompilerParams(vmem_limit_bytes=40 * 2**20),
        cost_estimate=pl.CostEstimate(
            flops=2 * rows * rows * 256 * heads,
            bytes_accessed=4 * 2**20,
            transcendentals=rows * rows * heads // 2,
        ),
        name="attention_near",
    )(scalars, far_bias, queries, bias_own, bias_next, keys_values)


def attention_far_kernel(
    heads, width, piece_count, scalars, far_bias, offsets, query_ref, running_in, best_in,
    bias_next, *rest
):
    pieces = rest[:piece_count]
    packed, lse_ref, keys_values, values_t, running, best, side_one, side_two = rest[piece_count:]
    rows = query_ref.shape[0]
    half, quarter = rows // 2, rows // 4
    context, first_end, second_end = scalars[0], scalars[1], scalars[2]
    base = context * rows
    for index, piece in enumerate(pieces):
        size = piece.shape[0]
        keys_values[pl.ds(aligned(offsets[index], 128), size), :] = piece[...]

    def values_step(index, carry):
        start = aligned(index * tile, tile)
        transpose_values(keys_values, start, values_t, start, width)
        return carry

    lax.fori_loop(0, context * (rows // tile), values_step, 0)
    running[...] = running_in[...]
    best[...] = best_in[...]

    def query_tile(index, carry):
        local = aligned(index * tile, tile)
        first = base + local
        positions = first + lax.broadcasted_iota(jnp.int32, (1, tile), 1)
        row_start = start_of(positions, first_end, second_end)
        start_first = start_of(first, first_end, second_end)
        start_last = start_of(first + tile - 1, first_end, second_end)
        masked_queries = masked_heads(query_ref[pl.ds(local, tile), :], heads, width)

        def take(key_start, size, bias_index, masked):
            absorb(
                keys_values, values_t, (None, bias_next), far_bias, best, running, index,
                masked_queries, heads, key_start, size, 0, positions, row_start, bias_index,
                masked, False,
            )

        far_rows = jnp.where(index == 0, jnp.maximum(base - tile, 0), base)

        @pl.when((index == 0) & (context > 0))
        def _():
            take(aligned(base - tile, tile), tile, 1, True)

        big = 4 * tile
        big_count = far_rows // big
        low = jnp.minimum(start_first // big, big_count)
        middle = jnp.clip((start_last + big - 1) // big, low, big_count)

        def masked_step(step, inner):
            take(aligned(step * big, big), big, None, True)
            return inner

        def plain_step(step, inner):
            take(aligned(step * big, big), big, None, False)
            return inner

        lax.fori_loop(low, middle, masked_step, 0)
        lax.fori_loop(middle, big_count, plain_step, 0)

        def small_step(step, inner):
            take(aligned(step * tile, tile), tile, None, True)
            return inner

        lax.fori_loop(big_count * 4, far_rows // tile, small_step, 0)
        outs = []
        for head in range(heads):
            total = running[index, head, width : width + 1]
            outs.append(running[index, head, 0:width] / total)
            lse_ref[pl.ds(head, 1), pl.ds(aligned(index * tile, tile), tile)] = best[
                index, head, 0:1
            ] + jnp.log(total)
        span = pl.ds(aligned(index * tile, tile), tile)
        side_one[span, :] = jnp.concatenate([outs[0], outs[1]], axis=0).T
        side_two[span, :] = jnp.concatenate([outs[2], outs[2]], axis=0).T
        return carry

    lax.fori_loop(0, rows // tile, query_tile, 0)
    lane = lax.broadcasted_iota(jnp.int32, (quarter, 128), 1)
    for part in range(2):
        target = slice(part * quarter, (part + 1) * quarter)
        first_rows = slice(part * half, part * half + quarter)
        last_rows = slice(part * half + quarter, (part + 1) * half)
        packed[target, 0:128] = side_one[first_rows, :].astype(bf16)
        packed[target, 128:256] = jnp.where(
            lane < width, side_two[first_rows, :], side_two[last_rows, :]
        ).astype(bf16)
        packed[target, 256:384] = side_one[last_rows, :].astype(bf16)


def attention_far(
    scalars, far_bias, offsets, queries, bias_next, state, pieces, group_rows, heads, width
):
    rows = queries.shape[0]
    shape = jax.ShapeDtypeStruct
    return pl.pallas_call(
        functools.partial(attention_far_kernel, heads, width, len(pieces)),
        out_shape=(shape((rows // 2, 384), bf16), shape((8, rows), f32)),
        in_specs=[SMEM, SMEM, SMEM] + [VMEM] * (4 + len(pieces)),
        out_specs=(VMEM,) * 2,
        scratch_shapes=[
            pltpu.VMEM((group_rows, 384), bf16),
            pltpu.VMEM((heads, width + 16, group_rows), bf16),
            pltpu.VMEM((rows // tile, heads, width + 16, tile), f32),
            pltpu.VMEM((rows // tile, heads, 8, tile), f32),
            pltpu.VMEM((rows, 128), f32),
            pltpu.VMEM((rows, 128), f32),
        ],
        compiler_params=pltpu.CompilerParams(vmem_limit_bytes=60 * 2**20),
        cost_estimate=pl.CostEstimate(
            flops=4 * rows * group_rows * 256 * heads,
            bytes_accessed=8 * 2**20,
            transcendentals=rows * group_rows * heads,
        ),
        name="attention_far",
    )(scalars, far_bias, offsets, queries, *state, bias_next, *pieces)


def attention_backward_kernel(heads, width, masks, piece_count, scalars, far_bias, offsets, *rest):
    first_call, last_call = masks[0] == 3, masks[0] == 0
    block_count = 2 if first_call else len(masks)
    blocks, rest = rest[:block_count], rest[block_count:]
    query_ref, lse_ref, bias_next = rest[0:3]
    rest = rest[3:]
    bias_own = None
    if last_call:
        bias_own, rest = rest[0], rest[1:]
    bias_ref = (bias_own, bias_next)
    if first_call:
        packed_ref = rest[0]
        pieces = rest[1 : 1 + piece_count]
        rest = rest[1 + piece_count :]
        dout, deltas, dq_t = rest[0:3]
        rest = rest[3:]
    else:
        dout, deltas, dq_in, fold_in = rest[0:4]
        dq_t = rest[4]
        rest = rest[5:]
    out_count = 2 if first_call else len(masks)
    outs, rest = rest[:out_count], rest[out_count:]
    if last_call:
        dq_ref, rest = rest[0], rest[1:]
    fold_ref, masked_q, masked_o, keys_t, dkv, band_ref, keys_values, semaphores = rest
    copies = []
    for place, block_ref in enumerate(blocks):
        target = keys_values.at[place]
        if first_call:
            size = block_ref.shape[0]
            target = keys_values.at[0, pl.ds(place * size, size), :]
        copies.append(pltpu.make_async_copy(block_ref, target, semaphores.at[place]))
        copies[-1].start()
    rows = query_ref.shape[0]
    half, quarter = rows // 2, rows // 4
    context, first_end, second_end = scalars[0], scalars[1], scalars[2]
    tiles_here = rows // tile
    if first_call:
        for index, piece in enumerate(pieces):
            span = pl.ds(aligned(offsets[index], 128), piece.shape[0])
            dout[span, 0:128] = pltpu.roll(piece[:, 128:256].astype(f32), width, 1).astype(bf16)
            dout[span, 128:256] = piece[:, 0:128]
        head_row = lax.broadcasted_iota(jnp.int32, (16, 256), 0)
        head_lane = lax.broadcasted_iota(jnp.int32, (16, 256), 1) // width
        head_hot = (head_row == jnp.where(head_lane == 1, 2, head_lane - 2)).astype(bf16)
        for part in range(4):
            span = slice(part * quarter, (part + 1) * quarter)
            packed = packed_ref[part // 2 * quarter : (part // 2 + 1) * quarter, :]
            lower = packed[:, 128:256].astype(f32)
            if part % 2 == 0:
                upper, lower = packed[:, 0:128], pltpu.roll(lower, width, 1)
            else:
                upper = packed[:, 256:384]
            product = dout[span, :].astype(f32) * jnp.concatenate(
                [lower, upper.astype(f32)], axis=1
            )
            high = product.astype(bf16)
            rest_part = (product - high.astype(f32)).astype(bf16)
            deltas[:, span] = dot_nt(head_hot, high) + dot_nt(head_hot, rest_part)
        dq_t[...] = jnp.zeros_like(dq_t)
        fold_ref[...] = jnp.zeros_like(fold_ref)
    else:
        dq_t[...] = dq_in[...]
        fold_ref[...] = fold_in[...]
    lane = lax.broadcasted_iota(jnp.int32, (rows, 256), 1) // width
    for head in range(heads):
        masked_q[head] = jnp.where(lane == head, query_ref[...], jnp.zeros((rows, 256), bf16))
        slot = 1 if head == 2 else head + 2
        masked_o[head] = jnp.where(lane == slot, dout[...], jnp.zeros((rows, 256), bf16))
    first = context * rows
    all_positions = first + lax.broadcasted_iota(jnp.int32, (1, rows), 1)
    all_starts = start_of(all_positions, first_end, second_end)
    start_first = start_of(first, first_end, second_end)
    start_last = start_of(first + rows - 1, first_end, second_end)


    def block(place, key_start, base, query_start, bands, masked):
        size = rows - query_start
        here = pl.ds(aligned(key_start - base, tile), tile)
        keys = keys_values[place, here, 0:256]
        values = keys_values[place, here, 128:384]
        key_sum, value_sum = None, None
        if masked:
            key_positions = key_start + lax.broadcasted_iota(jnp.int32, (tile, size), 0)
            seen = key_positions >= all_starts[:, query_start:]
            if 0 in bands:
                seen = seen & (key_positions <= all_positions[:, query_start:])
        span = slice(query_start, rows)
        every = range(heads)
        queries = [masked_q[head, span, :] for head in every]
        grads = [masked_o[head, span, :] for head in every]
        scores = [dot_nt(keys, queries[head]) for head in every]
        grad_probs = [dot_nt(values, grads[head]) for head in every]
        lse = [lse_ref[head : head + 1, span] for head in every]
        if bands:
            for head in every:
                parts = [
                    scores[head][:, at * tile : (at + 1) * tile] + bias_ref[band][head]
                    for at, band in enumerate(bands)
                ]
                if size > len(bands) * tile:
                    parts.append(scores[head][:, len(bands) * tile :] + far_bias[head])
                scores[head] = jnp.concatenate(parts, axis=1)
        else:
            lse = [lse[head] - far_bias[head] for head in every]
        probs = [jnp.exp(scores[head] - lse[head]) for head in every]
        if masked:
            probs = [jnp.where(seen, part, 0.0) for part in probs]
        grad_scores = [
            probs[head] * (grad_probs[head] - deltas[head : head + 1, span]) for head in every
        ]
        for head in every:
            for at, band in enumerate(bands):
                band_ref[band, head] += grad_scores[head][:, at * tile : (at + 1) * tile]
        low_scores = [part.astype(bf16) for part in grad_scores]
        low_probs = [part.astype(bf16) for part in probs]
        for head in every:
            value_part = dot_nn(low_probs[head], grads[head])
            key_part = dot_nn(low_scores[head], queries[head])
            dq_t[head, :, span] += dot_nn(keys_t[head, :, here], low_scores[head])
            key_sum = key_part if key_sum is None else key_sum + key_part
            value_sum = value_part if value_sum is None else value_sum + value_part
        return key_sum, value_sum

    lane_tile = lax.broadcasted_iota(jnp.int32, (tile, 128), 1)

    def write(local, key_sum, value_sum):
        span = pl.ds(local, tile)
        dkv[span, 0:128] = key_sum[:, 0:128].astype(bf16)
        dkv[span, 128:256] = jnp.where(
            lane_tile < width, key_sum[:, 128:256], value_sum[:, 0:128]
        ).astype(bf16)
        dkv[span, 256:384] = value_sum[:, 128:256].astype(bf16)

    near = jnp.bool_(last_call)
    for mask in masks:
        near = near | ((context ^ mask) == context - 1)

    @pl.when(near)
    def _():
        band_ref[...] = jnp.zeros_like(band_ref)

    for place, mask in enumerate(masks):
        which = context ^ mask
        base = aligned(which * rows, rows)
        for copy in copies if first_call else copies[place : place + 1]:
            copy.wait()

        @pl.when((which > context) | (start_first > base))
        def _():
            dkv[...] = jnp.zeros_like(dkv)

        @pl.when(which <= context)
        def _():
            def transpose_keys(index, carry):
                target = pl.ds(aligned(index * tile, tile), tile)
                lower = keys_values[place, target, 0:128].astype(f32).T.astype(bf16)
                upper = keys_values[place, target, 128:256].astype(f32).T.astype(bf16)
                keys_t[0, :, target] = lower[0:width]
                keys_t[1, :, target] = lower[width:]
                keys_t[2, :, target] = upper[0:width]
                return carry

            lax.fori_loop(0, tiles_here, transpose_keys, 0)
            low_tile = which * tiles_here
            high_tile = low_tile + tiles_here
            if mask:
                far_end = jnp.minimum(high_tile, context * tiles_here - 1)
                low = jnp.clip(start_first // tile, low_tile, far_end)
                middle = jnp.clip((start_last + tile - 1) // tile, low, far_end)

                def masked_step(index, carry):
                    start = aligned(index * tile, tile)
                    found = block(place, start, base, 0, (), True)
                    write(aligned(start - base, tile), *found)
                    return carry

                def plain_step(index, carry):
                    start = aligned(index * tile, tile)
                    found = block(place, start, base, 0, (), False)
                    write(aligned(start - base, tile), *found)
                    return carry

                lax.fori_loop(low, middle, masked_step, 0)
                lax.fori_loop(middle, far_end, plain_step, 0)

                @pl.when(far_end < high_tile)
                def _():
                    start = aligned(far_end * tile, tile)
                    write(aligned(start - base, tile), *block(place, start, base, 0, (1,), True))

            else:
                for index in range(tiles_here):
                    start = aligned(base + index * tile, tile)
                    bands = (0, 1) if index + 1 < tiles_here else (0,)
                    write(index * tile, *block(place, start, base, index * tile, bands, True))

        if mask == 3:
            outs[0][...] = dkv[0:half, :]
            outs[1][...] = dkv[half:, :]
        else:
            outs[place][...] = dkv[...]

    @pl.when(near)
    def _():
        key_index = lax.broadcasted_iota(jnp.int32, (tile, tile), 0)
        query_index = lax.broadcasted_iota(jnp.int32, (tile, tile), 1)
        for head in range(heads):
            both = jnp.where(key_index > query_index, band_ref[1, head], band_ref[0, head])
            by_row = both[0:8]
            for first_row in range(8, tile, 8):
                by_row = by_row + pltpu.roll(both[first_row : first_row + 8], tile - first_row, 1)
            folded = by_row[0:1]
            for row in range(1, 8):
                folded = folded + pltpu.roll(by_row, tile - row, 1)[row : row + 1]
            fold_ref[head : head + 1, :] += folded

    if last_call:
        scale = width ** (-0.5)
        upper = jnp.concatenate([dq_t[0], dq_t[1]], axis=0)
        lower = jnp.concatenate([dq_t[2], jnp.zeros((width, rows), f32)], axis=0)
        dq_ref[:, 0:128] = (upper.T * scale).astype(bf16)
        dq_ref[:, 128:256] = (lower.T * scale).astype(bf16)


def attention_backward(
    masks, scalars, far_bias, offsets, queries, bias_own, bias_next, lse, blocks, given,
    piece_count, heads, width,
):
    rows = queries.shape[0]
    half = rows // 2
    shape = jax.ShapeDtypeStruct
    first_call, last_call = masks[0] == 3, masks[0] == 0
    if last_call:
        given = (bias_own,) + tuple(given)
    outs = (shape((heads, width, rows), f32),)
    if first_call:
        outs = (shape((rows, 256), bf16), shape((16, rows), f32)) + outs
    if first_call:
        outs = outs + (shape((half, 384), bf16),) * 2
    else:
        outs = outs + (shape((rows, 384), bf16),) * len(masks)
    if last_call:
        outs = outs + (shape((rows, 256), bf16),)
    outs = outs + (shape((8, tile), f32),)

    return pl.pallas_call(
        functools.partial(attention_backward_kernel, heads, width, masks, piece_count),
        out_shape=outs,
        in_specs=[SMEM, SMEM, SMEM]
        + [pl.BlockSpec(memory_space=pl.ANY)] * len(blocks)
        + [VMEM] * (3 + len(given)),
        out_specs=(VMEM,) * len(outs),
        scratch_shapes=[
            pltpu.VMEM((heads, rows, 256), bf16),
            pltpu.VMEM((heads, rows, 256), bf16),
            pltpu.VMEM((heads, width, rows), bf16),
            pltpu.VMEM((rows, 384), bf16),
            pltpu.VMEM((2, heads, tile, tile), f32),
            pltpu.VMEM((len(masks), rows, 384), bf16),
            pltpu.SemaphoreType.DMA((len(blocks),)),
        ],
        compiler_params=pltpu.CompilerParams(vmem_limit_bytes=60 * 2**20),
        cost_estimate=pl.CostEstimate(
            flops=10 * rows * rows * 256 * heads if first_call else 0,
            bytes_accessed=10 * 2**20 if first_call else 2**10,
            transcendentals=0,
        ),
        name="attention_backward",
    )(scalars, far_bias, offsets, *blocks, queries, lse, bias_next, *given)


bucket_edges = np.array(
    [19, 21, 24, 27, 31, 35, 40, 46, 52, 59, 67, 77, 87, 99, 113], dtype=np.int32
)


def bucket_tiles():
    key = np.arange(tile)[None, :, None]
    query = np.arange(tile)[None, None, :]
    lag = np.arange(3)[:, None, None] * tile + query - key
    clipped = np.maximum(lag, 0)
    counted = (clipped[..., None] >= bucket_edges).sum(-1)
    return np.where(clipped < 16, clipped, 16 + counted).astype(np.int32)


def shape(dims, dtype):
    return jax.ShapeDtypeStruct(dims, dtype)


def params(mebibytes):
    return pltpu.CompilerParams(vmem_limit_bytes=mebibytes * 2**20)


def cost(flops, bytes_accessed):
    return pl.CostEstimate(flops=flops, bytes_accessed=bytes_accessed, transcendentals=0)


def gelu_constants():
    return 0.7978845608028654, 0.044715


def prepare_kernel(
    part, padded, scalars, route_ref, order_ref, rows_ref, columns_ref, ranks, hot_ref, tall,
):
    pair_count = order_ref.shape[1]
    rows = pair_count // 2
    expert_pad = hot_ref.shape[0]
    step = 256
    live_end = scalars[2] - scalars[0] * rows
    order = order_ref[...]
    index_row = lax.broadcasted_iota(jnp.int32, (pair_count, 128), 0)
    index_lane = lax.broadcasted_iota(jnp.int32, (pair_count, 128), 1)
    digits = jnp.where(
        index_lane == 0, index_row // 64, jnp.where(index_lane == 1, index_row % 64, 0)
    ).astype(f32).astype(bf16)

    def rank_step(index, carry):
        start = aligned(index * step, step)
        pair = start + lax.broadcasted_iota(jnp.int32, (step, pair_count), 0)
        hit = (pair == order).astype(f32).astype(bf16)
        found = dot_nn(hit, digits)
        position = found[:, 0:1] * 64.0 + found[:, 1:2]
        ranks[pl.ds(start, step), :] = jnp.broadcast_to(position, (step, 128))
        return carry

    lax.fori_loop(0, pair_count // step, rank_step, 0)
    rank_row = ranks[...].T[0:1, :]
    position = lax.broadcasted_iota(jnp.int32, (1, rows), 1)
    live = position < live_end
    expert_row = jnp.concatenate([route_ref[0:1, :], route_ref[1:2, :]], axis=1)
    live_row = jnp.concatenate([live, live], axis=1)
    expert_index = lax.broadcasted_iota(jnp.int32, (expert_pad, pair_count), 0)
    hot = ((expert_index == expert_row) & live_row).astype(f32)
    hot_ref[...] = hot.astype(bf16)

    def count_step(index, counts):
        start = aligned(index * step, step)
        earlier = (ranks[pl.ds(start, step), 0:1] < rank_row).astype(f32).astype(bf16)
        return counts + dot_nn(hot_ref[:, pl.ds(start, step)], earlier)

    counts = lax.fori_loop(
        0, pair_count // step, count_step, jnp.zeros((expert_pad, pair_count), f32)
    )
    slot = jnp.sum(counts * hot, axis=0, keepdims=True).astype(jnp.int32)
    own = slot - (scalars[3] & 1) * part
    place = jnp.where(live_row & (own >= 0) & (own < part), expert_row * padded + own, -1)
    rows_ref[...] = jnp.full_like(rows_ref, -1)
    rows_ref[0:1, :] = place[:, 0:rows]
    rows_ref[1:2, :] = place[:, rows:]
    tall[...] = jnp.full_like(tall, -1.0)
    tall[0:1, :] = place[:, 0:rows].astype(f32)
    tall[1:2, :] = place[:, rows:].astype(f32)
    columns_ref[...] = tall[...].T.astype(jnp.int32)


def bias_kernel(table, bias_own, bias_next):
    key = lax.broadcasted_iota(jnp.int32, (8, tile), 0)
    query = lax.broadcasted_iota(jnp.int32, (8, tile), 1)
    heads = bias_own.shape[0]

    def bias_step(index, carry):
        start = aligned(index * 8, 8)
        for band, bias_ref in enumerate((bias_own, bias_next)):
            lag = band * tile + query - key - start
            found = [jnp.full((8, tile), table[0, head], f32) for head in range(heads)]
            for bucket, edge in enumerate(list(range(1, 17)) + list(bucket_edges), start=1):
                beyond = lag >= int(edge)
                found = [
                    jnp.where(beyond, table[bucket, head], found[head]) for head in range(heads)
                ]
            for head in range(heads):
                bias_ref[head, pl.ds(start, 8), :] = found[head]
        return carry

    lax.fori_loop(0, tile // 8, bias_step, 0)


def bias_tiles(table, heads):
    return pl.pallas_call(
        bias_kernel,
        out_shape=(shape((heads, tile, tile), f32),) * 2,
        in_specs=[SMEM],
        out_specs=(VMEM,) * 2,
        compiler_params=params(40),
        cost_estimate=cost(10**9, 2 * 2**20),
        name="bias_tiles",
    )(table)


def prepare(scalars, route_rows, order_row, expert_count, part, padded):
    rows = route_rows.shape[1]
    expert_pad = max(16, expert_count)
    return pl.pallas_call(
        functools.partial(prepare_kernel, part, padded),
        out_shape=(
            shape((8, rows), jnp.int32),
            shape((rows, 128), jnp.int32),
        ),
        in_specs=[SMEM, VMEM, VMEM],
        out_specs=(VMEM,) * 2,
        scratch_shapes=[
            pltpu.VMEM((2 * rows, 128), f32),
            pltpu.VMEM((expert_pad, 2 * rows), bf16),
            pltpu.VMEM((128, rows), f32),
        ],
        compiler_params=params(40),
        cost_estimate=cost(10 * 10**9, 3 * 2**20),
        name="prepare",
    )(scalars, route_rows, order_row)


def pack_kernel(query, key, value, output, gain_one, gain_two, router, block):
    size = query.shape[0]
    experts = router.shape[0]
    block[...] = jnp.zeros_like(block)
    block[:, 0:192] = query[...]
    gains = jnp.concatenate([gain_one[...], gain_two[...]], axis=0).astype(f32)
    block[:, 192:194] = gains.T.astype(bf16)
    block[:, 256:448] = key[...]
    block[:, 448:512] = value[:, 128:192]
    block[:, 512:640] = value[:, 0:128]
    block[:, 640:832] = output[...].astype(f32).T.astype(bf16)
    block[:, 832 : 832 + experts] = router[...].astype(f32).T.astype(bf16)


def pack_weights(query, key, value, output, gain_one, gain_two, router):
    size = query.shape[0]
    return pl.pallas_call(
        pack_kernel,
        out_shape=shape((size, 896), bf16),
        in_specs=[VMEM] * 7,
        out_specs=VMEM,
        compiler_params=params(60),
        cost_estimate=cost(0, 2**19),
        name="pack_weights",
    )(query, key, value, output, gain_one[None], gain_two[None], router.T)


def project_kernel(piece_count, offsets, token_ref, *rest):
    pieces = rest[:piece_count]
    hidden_ref, query_ref, kv_ref, weight_ref, output_ref, gain_ref = rest[piece_count:]
    for index, piece in enumerate(pieces):
        span = pl.ds(aligned(offsets[index], 16), piece.shape[0])
        weight_ref[span, :] = piece[:, 0:640]
        output_ref[span, :] = piece[:, 640:896]
    rows = token_ref.shape[0]
    gains = weight_ref[:, 128:256].astype(f32).T
    gain_ref[0:1, :] = gains[64:65, :]
    gain_ref[1:2, :] = gains[65:66, :]
    step = 256
    lane = lax.broadcasted_iota(jnp.int32, (step, 256), 1)
    for start in range(0, rows, step):
        inputs = token_ref[start : start + step, :].astype(f32)
        scale = lax.rsqrt(jnp.mean(inputs * inputs, axis=-1, keepdims=True) + epsilon)
        hidden = (inputs * scale * gain_ref[0:1, :]).astype(bf16)
        hidden_ref[start : start + step, :] = hidden
        queries = dot_nn(hidden, weight_ref[:, 0:256]).astype(bf16)
        query_ref[start : start + step, :] = jnp.where(
            lane < 192, queries * bf16(0.125), jnp.zeros_like(queries)
        )
        kv_ref[start : start + step, :] = dot_nn(hidden, weight_ref[:, 256:640]).astype(bf16)


def project(offsets, tokens, pieces):
    rows, model = tokens.shape
    return pl.pallas_call(
        functools.partial(project_kernel, len(pieces)),
        out_shape=(
            shape((rows, model), bf16),
            shape((rows, 256), bf16),
            shape((rows, 384), bf16),
            shape((model, 640), bf16),
            shape((model, 256), bf16),
            shape((8, model), f32),
        ),
        in_specs=[SMEM, VMEM] + [VMEM] * len(pieces),
        out_specs=(VMEM,) * 6,
        compiler_params=params(40),
        cost_estimate=cost(2 * rows * model * 640, 6 * 2**20),
        name="project",
    )(offsets, tokens, *pieces)


def assemble_kernel(piece_count, offsets, *rest):
    pieces = rest[:piece_count]
    out_ref = rest[piece_count]
    for index, piece in enumerate(pieces):
        size = piece.shape[0]
        out_ref[pl.ds(aligned(offsets[index], 16), size), :] = piece[...].astype(out_ref.dtype)


def assemble(offsets, pieces, dtype):
    total = sum(piece.shape[0] for piece in pieces)
    width = pieces[0].shape[1]
    return pl.pallas_call(
        functools.partial(assemble_kernel, len(pieces)),
        out_shape=shape((total, width), dtype),
        in_specs=[SMEM] + [VMEM] * len(pieces),
        out_specs=VMEM,
        compiler_params=params(40),
        cost_estimate=cost(0, 6 * total * width),
        name="assemble",
    )(offsets, *pieces)


def route_half(
    width, expert_count, part, token_ref, gain_ref, route_ref, attended, weights, packed, joined,
    hidden_ref, info_ref,
):
    half = packed.shape[1]
    quarter = half // 2
    lane_low = lax.broadcasted_iota(jnp.int32, (quarter, 128), 1)
    for source in range(4):
        piece = attended[source]
        middle = piece[:, 128:256].astype(f32)
        packed[source, 0:quarter, 0:128] = piece[:, 0:128]
        packed[source, 0:quarter, 128:256] = jnp.where(lane_low < width, middle, 0.0).astype(bf16)
        packed[source, quarter:, 0:128] = piece[:, 256:384]
        packed[source, quarter:, 128:256] = jnp.where(
            lane_low < width, pltpu.roll(middle, 64, 1), 0.0
        ).astype(bf16)
    step = half
    lane = lax.broadcasted_iota(jnp.int32, (step, 128), 1)
    valid = (lane >= 64) & (lane < 64 + expert_count)

    def token_step(index, carry):
        span = pl.ds(aligned(index * step, step), step)
        where = pl.ds(aligned(part * half + index * step, step), step)
        residual = token_ref[where, :].astype(f32)
        for source in range(4):
            residual = residual + dot_nt(packed[source, span, :], weights[source][...])
        joined[span, :] = residual
        scale = lax.rsqrt(jnp.mean(residual * residual, axis=-1, keepdims=True) + epsilon)
        hidden = (residual * scale * gain_ref[1:2, :]).astype(bf16)
        hidden_ref[span, :] = hidden
        logits = dot_nn(hidden, weights[0][:, 128:256])
        logits = jnp.where(valid, logits, masked_value)
        powers = jnp.where(valid, jnp.exp(logits - jnp.max(logits, axis=-1, keepdims=True)), 0.0)
        probs = powers / jnp.sum(powers, axis=-1, keepdims=True)
        first = jnp.sum(
            jnp.where(lane == route_ref[where, 0:1] + 64, probs, 0.0), axis=-1, keepdims=True
        )
        second = jnp.sum(
            jnp.where(lane == route_ref[where, 1:2] + 64, probs, 0.0), axis=-1, keepdims=True
        )
        total = first + second
        info_ref[span, :] = jnp.where(
            lane == 0,
            first / total,
            jnp.where(lane == 1, second / total, jnp.where(lane == 2, total, probs)),
        )
        return carry

    lax.fori_loop(0, half // step, token_step, 0)


def dispatch_kernel(
    width, expert_count, padded, scalars, token_ref, gain_ref, route_ref, row_place, *rest
):
    attended, weights = rest[0:4], rest[4:8]
    residual_ref, hidden_ref, info_ref, attended_ref, sent = rest[8:13]
    packed, joined, column = rest[13:]
    rows, model = token_ref.shape
    half, quarter = rows // 2, rows // 4
    for part in range(2):
        span = pl.ds(part * half, half)
        route_half(
            width, expert_count, part, token_ref, gain_ref, route_ref,
            [piece.at[pl.ds(part * quarter, quarter), :] for piece in attended], weights,
            packed.at[part], joined.at[span, :], hidden_ref.at[span, :], info_ref.at[span, :],
        )
    rank = scalars[3]
    here = aligned(lax.rem(rank, 2) * quarter, quarter)
    residual_ref[...] = joined[pl.ds(aligned(rank * quarter, quarter), quarter), :]
    for source in range(4):
        attended_ref[:, source * 256 : (source + 1) * 256] = packed[
            rank // 2, source, pl.ds(here, quarter), :
        ]
    gates = info_ref[...].T
    gate_one, gate_two = gates[0:1, :], gates[1:2, :]
    place_one, place_two = row_place[0:1, :], row_place[1:2, :]
    column[...] = jnp.zeros_like(column)

    taken = 4 * padded

    def expert_rows(index, carry):
        start = aligned(index * taken, 64)
        slot = start + lax.broadcasted_iota(jnp.int32, (taken, rows), 0)
        hit_one, hit_two = slot == place_one, slot == place_two
        picked = jnp.where(hit_one | hit_two, 1.0, 0.0).astype(bf16)
        sent[pl.ds(start, taken), :] = dot_nn(picked, hidden_ref[...]).astype(bf16)
        gate = jnp.where(hit_one, gate_one, jnp.where(hit_two, gate_two, 0.0))
        gate = jnp.sum(gate, axis=-1, keepdims=True)
        for chunk in range(4):
            write_digits(
                sent, column, start + chunk * padded, padded,
                gate[chunk * padded : (chunk + 1) * padded],
            )
        return carry

    lax.fori_loop(0, expert_count // 4, expert_rows, 0)


def write_digits(rows_ref, column, start, padded, values):
    column[0:padded, :] = jnp.broadcast_to(values, (padded, 128))
    row = column[...].T[0:1, :]
    high = row.astype(bf16).astype(f32)
    middle = (row - high).astype(bf16).astype(f32)
    low = row - high - middle
    size = row.shape[1]
    index = lax.broadcasted_iota(jnp.int32, (16, size), 0)
    block = jnp.where(
        index == 0, high, jnp.where(index == 1, middle, jnp.where(index == 2, low, 0.0))
    )
    span = pl.ds(aligned(start + padded - 16, 16), 16)
    rows_ref[span, 0:size] = block.astype(bf16)
    rows_ref[span, size:] = jnp.zeros((16, rows_ref.shape[1] - size), bf16)


def read_digits(rows_ref, start, padded):
    wide = (padded + 127) // 128 * 128
    span = pl.ds(aligned(start + padded - 16, 16), 16)
    return jnp.sum(rows_ref[span, 0:wide].astype(f32), axis=0, keepdims=True)


def dispatch(
    scalars, tokens, gains, routes, row_place, attended, weights, width, expert_count, padded
):
    rows, model = tokens.shape
    slots = expert_count * padded
    wide = (padded + 127) // 128 * 128
    return pl.pallas_call(
        functools.partial(dispatch_kernel, width, expert_count, padded),
        out_shape=(
            shape((rows // 4, model), f32),
            shape((rows, model), bf16),
            shape((rows, 128), f32),
            shape((rows // 4, 1024), bf16),
            shape((slots, model), bf16),
        ),
        in_specs=[SMEM] + [VMEM] * 12,
        out_specs=(VMEM,) * 5,
        scratch_shapes=[
            pltpu.VMEM((2, 4, rows // 2, 256), bf16),
            pltpu.VMEM((rows, model), f32),
            pltpu.VMEM((wide, 128), f32),
        ],
        compiler_params=params(60),
        cost_estimate=cost(2 * rows * model * (1024 + slots), 16 * 2**20),
        name="dispatch",
    )(scalars, tokens, gains, routes, row_place, *attended, *weights)


def scatter_kernel(value_ref, row_place, sent):
    rows = value_ref.shape[0]
    place_one, place_two = row_place[0:1, :], row_place[1:2, :]
    fill = sent.shape[0] // 2

    def slot_step(index, carry):
        start = aligned(index * fill, fill)
        slot = start + lax.broadcasted_iota(jnp.int32, (fill, rows), 0)
        picked = jnp.where((slot == place_one) | (slot == place_two), 1.0, 0.0).astype(bf16)
        sent[pl.ds(start, fill), :] = dot_nn(picked, value_ref[...]).astype(bf16)
        return carry

    lax.fori_loop(0, sent.shape[0] // fill, slot_step, 0)


def scatter_rows(values, row_place, slots):
    rows, model = values.shape
    return pl.pallas_call(
        scatter_kernel,
        out_shape=shape((slots, model), bf16),
        in_specs=[VMEM, VMEM],
        out_specs=VMEM,
        compiler_params=params(40),
        cost_estimate=cost(2 * rows * model * slots, 6 * 2**20),
        name="scatter_rows",
    )(values, row_place)


def expert_kernel(
    padded, in_own, in_partner, out_own, out_first, out_second, rows_ref, grads_ref, acted_ref,
    pre_ref, back_ref, column, gate_ref,
):
    hidden = in_own.shape[1]
    root, cubic = gelu_constants()
    wide = column.shape[0]
    column[...] = jnp.zeros_like(column)
    chunk_count = rows_ref.shape[0] // padded
    for chunk in range(chunk_count):
        gates = read_digits(rows_ref, chunk * padded, padded)
        gates = jnp.broadcast_to(gates, (128, wide)).T[0:padded, :]
        gate_ref[chunk * padded : (chunk + 1) * padded, :] = gates
    gate = jnp.concatenate([gate_ref[...], gate_ref[...]], axis=1)
    cut = out_first.shape[0]
    places = [(side, first) for side in range(2) for first in range(0, hidden, 256)]

    def products(side, first):
        part = slice(first, first + 256)
        if side == 0:
            inner, outer = in_own[:, part], out_own[part, :]
        elif first < cut:
            inner, outer = in_partner[:, part], out_first[part, :]
        else:
            inner, outer = in_partner[:, part], out_second[first - cut : first - cut + 256, :]
        return dot_nn(rows_ref[...], inner), dot_nt(grads_ref[...], outer)

    gate_part = None
    found = products(*places[0])
    for index, (side, first) in enumerate(places):
        pre, grad_acted = found
        if index + 1 < len(places):
            found = products(*places[index + 1])
        part = slice(first, first + 256)
        square = pre * pre
        share_on = 0.5 + 0.5 * jnp.tanh(pre * (root + root * cubic * square))
        acted = pre * share_on
        slope = share_on + acted * (1.0 - share_on) * (2.0 * root + 6.0 * root * cubic * square)
        acted_ref[side, :, part] = (acted * gate).astype(bf16)
        product = grad_acted * acted
        folded = product[:, 0:128] + product[:, 128:256]
        gate_part = folded if gate_part is None else gate_part + folded
        pre_ref[side, :, part] = (grad_acted * gate * slope).astype(bf16)
    back = dot_nt(pre_ref[0, :, :], in_own[...])
    back = back + dot_nt(pre_ref[1, :, :], in_partner[...])
    back_ref[:, :] = back.astype(bf16)
    gate_part = jnp.sum(gate_part, axis=-1, keepdims=True)
    for chunk in range(chunk_count):
        write_digits(
            back_ref, column, chunk * padded, padded,
            gate_part[chunk * padded : (chunk + 1) * padded],
        )


def expert_step(in_parts, out_parts, rows_in, grads_in, padded):
    slots, model = rows_in.shape
    hidden = in_parts[0].shape[1]
    wide = (padded + 127) // 128 * 128
    taken = 4 * padded

    def whole(value):
        return pl.BlockSpec(value.shape, lambda index: (0, 0), pipeline_mode=pl.Buffered(1))

    rows_spec = pl.BlockSpec((taken, model), lambda index: (index, 0))
    hidden_spec = pl.BlockSpec((2, taken, hidden), lambda index: (0, index, 0))
    return pl.pallas_call(
        functools.partial(expert_kernel, padded),
        grid=(slots // taken,),
        out_shape=(
            shape((2, slots, hidden), bf16),
            shape((2, slots, hidden), bf16),
            shape((slots, model), bf16),
        ),
        in_specs=[whole(part) for part in (*in_parts, *out_parts)] + [rows_spec] * 2,
        out_specs=(hidden_spec, hidden_spec, rows_spec),
        scratch_shapes=[pltpu.VMEM((wide, 128), f32), pltpu.VMEM((taken, 128), f32)],
        compiler_params=params(60),
        cost_estimate=cost(12 * slots * model * hidden, 24 * 2**20),
        name="expert_step",
    )(*in_parts, *out_parts, rows_in, grads_in)


def expert_out_kernel(acted_ref, out_own, out_first, out_second, out_ref):
    step = out_ref.shape[0] // 4
    cut = out_first.shape[0]

    def one(index, carry):
        span = pl.ds(aligned(index * step, 16), step)
        total = dot_nn(acted_ref[0, span, :], out_own[...])
        total = total + dot_nn(acted_ref[1, span, 0:cut], out_first[...])
        total = total + dot_nn(acted_ref[1, span, cut:], out_second[...])
        out_ref[span, :] = total.astype(bf16)
        return carry

    lax.fori_loop(0, 4, one, 0)


def expert_outputs(acted, out_parts):
    _, slots, hidden = acted.shape
    model = out_parts[0].shape[1]
    return pl.pallas_call(
        expert_out_kernel,
        out_shape=shape((slots, model), bf16),
        in_specs=[VMEM] * 4,
        out_specs=VMEM,
        compiler_params=params(60),
        cost_estimate=cost(4 * slots * model * hidden, 10 * 2**20),
        name="expert_outputs",
    )(acted, *out_parts)


def write_ring(scalars, joined, own, next_ref, last_ref, far_one, far_two):
    quarter = own.shape[0]
    eighth = quarter // 2
    rank = scalars[3]

    def rows_of(which):
        return aligned(lax.rem(rank + which, 4) * quarter, quarter)

    own[...] = joined[pl.ds(rows_of(0), quarter), :]
    next_ref[...] = joined[pl.ds(rows_of(1), quarter), :].astype(bf16)
    last_ref[...] = joined[pl.ds(rows_of(3), quarter), :].astype(bf16)
    far = rows_of(2)
    far_one[...] = joined[pl.ds(far, eighth), :].astype(bf16)
    far_two[...] = joined[pl.ds(aligned(far + eighth, eighth), eighth), :].astype(bf16)


def ring_shapes(rows, model):
    quarter, eighth = shape((rows // 4, model), bf16), shape((rows // 8, model), bf16)
    return (shape((rows // 4, model), f32), quarter, quarter, eighth, eighth)


def combine_grads_kernel(
    expert_count, padded, far, scalars, place_ref, info_ref, route_ref, router_ref, back_ref, *rest
):
    if far:
        logit_ref, far_one, far_two, digits = rest
    else:
        far_logits, digits, logit_ref, own, next_ref, last_ref = rest
    rows = place_ref.shape[0]
    quarter, eighth = rows // 4, rows // 8
    slots = back_ref.shape[0]
    rank = scalars[3]
    wide = (padded + 127) // 128 * 128
    lane_digit = lax.broadcasted_iota(jnp.int32, (padded, 128), 1)

    def column_step(expert, carry):
        start = aligned(expert * padded, 16)
        row = jnp.broadcast_to(read_digits(back_ref, start, padded), (128, wide))
        column = row.T[0:padded, :]
        high = column.astype(bf16).astype(f32)
        middle = (column - high).astype(bf16).astype(f32)
        digits[pl.ds(start, padded), :] = jnp.where(
            lane_digit == 0,
            high,
            jnp.where(lane_digit == 1, middle, jnp.where(lane_digit == 2, column - high - middle, 0.0)),
        ).astype(bf16)
        return carry

    if far:
        lax.fori_loop(0, expert_count, column_step, 0)
    lane = lax.broadcasted_iota(jnp.int32, (quarter, 128), 1)
    slot = lax.broadcasted_iota(jnp.int32, (quarter, slots), 1)

    def rows_of(which):
        return pl.ds(aligned(lax.rem(rank + which, 4) * quarter, quarter), quarter)

    def tokens(which):
        span = rows_of(which)
        info, place = info_ref[span, :], place_ref[span, :]
        hit_one, hit_two = slot == place[:, 0:1], slot == place[:, 1:2]
        ones = jnp.where(hit_one | hit_two, 1.0, 0.0).astype(bf16)
        total = dot_nn(ones, back_ref[...])
        signs = jnp.where(hit_one, 1.0, jnp.where(hit_two, -1.0, 0.0)).astype(bf16)
        difference = jnp.sum(dot_nn(signs, digits[...]), axis=-1, keepdims=True) / info[:, 2:3]
        picked = jnp.where(
            lane == route_ref[span, 0:1] + 64,
            info[:, 1:2] * difference,
            jnp.where(lane == route_ref[span, 1:2] + 64, -info[:, 0:1] * difference, 0.0),
        )
        probs = jnp.where((lane >= 64) & (lane < 64 + expert_count), info, 0.0)
        grads = probs * (picked - jnp.sum(probs * picked, axis=-1, keepdims=True))
        grads = grads.astype(bf16)
        return grads, total + dot_nt(grads, router_ref[:, 128:256])

    if far:
        grads, total = tokens(2)
        logit_ref[...] = grads
        far_one[...] = total[0:eighth].astype(bf16)
        far_two[...] = total[eighth:].astype(bf16)
    else:
        logit_ref[rows_of(2), :] = far_logits[...]
        for which, target in ((1, next_ref), (3, last_ref)):
            grads, total = tokens(which)
            logit_ref[rows_of(which), :] = grads
            target[...] = total.astype(bf16)
        grads, total = tokens(0)
        logit_ref[rows_of(0), :] = grads
        own[...] = total


def combine_grads(far, scalars, place, info, routes, router, back, given, expert_count, padded):
    rows = place.shape[0]
    model = router.shape[0]
    slots = back.shape[0]
    half = shape((rows // 8, model), bf16)
    if far:
        outs = (shape((rows // 4, 128), bf16), half, half, shape((slots, 128), bf16))
    else:
        outs = (shape((rows, 128), bf16), shape((rows // 4, model), f32))
        outs = outs + (shape((rows // 4, model), bf16),) * 2
    return pl.pallas_call(
        functools.partial(combine_grads_kernel, expert_count, padded, far),
        out_shape=outs,
        in_specs=[SMEM] + [VMEM] * (5 + len(given)),
        out_specs=(VMEM,) * len(outs),
        compiler_params=params(60),
        cost_estimate=cost(2 * rows * model * slots, 8 * 2**20),
        name="combine_grads",
    )(scalars, place, info, routes, router, back, *given)


def combine_outs_kernel(place_ref, rows_ref, out_ref):
    step = 512
    slot = lax.broadcasted_iota(jnp.int32, (step, rows_ref.shape[0]), 1)

    def token_step(index, carry):
        span = pl.ds(aligned(index * step, step), step)
        place = place_ref[span, :]
        hit = (slot == place[:, 0:1]) | (slot == place[:, 1:2])
        out_ref[span, :] = dot_nn(jnp.where(hit, 1.0, 0.0).astype(bf16), rows_ref[...]).astype(bf16)
        return carry

    lax.fori_loop(0, out_ref.shape[0] // step, token_step, 0)


def combine_outs(place, rows_in):
    rows = place.shape[0]
    slots, model = rows_in.shape
    return pl.pallas_call(
        combine_outs_kernel,
        out_shape=shape((rows, model), bf16),
        in_specs=[VMEM] * 2,
        out_specs=VMEM,
        compiler_params=params(60),
        cost_estimate=cost(2 * rows * model * slots, 8 * 2**20),
        name="combine_outs",
    )(place, rows_in)


def received(own, from_last, from_next):
    return own[...] + from_last[...].astype(f32) + from_next[...].astype(f32)


def norm_back_kernel(gain_index, has_bypass_rows, scalars, value_ref, gain_ref, bypass_ref, *rest):
    grads = received(*rest[:3])
    rest = rest[3:]
    weights = ()
    if gain_index == 1:
        weights, rest = rest[0:4], rest[4:]
    else:
        blocks_ref, rest = rest[0], rest[1:]
    full_ref, low_ref, gain_grad = rest[0:3]
    quarter = grads.shape[0]
    here = pl.ds(aligned(scalars[3] * quarter, quarter), quarter)
    values = (value_ref[here, :] if gain_index == 0 else value_ref[...]).astype(f32)
    bypass = (bypass_ref[here, :] if has_bypass_rows else bypass_ref[...]).astype(f32)
    scale = lax.rsqrt(jnp.mean(values * values, axis=-1, keepdims=True) + epsilon)
    normed = values * scale
    scaled = grads * gain_ref[gain_index : gain_index + 1, :]
    gain_grad[...] = jnp.broadcast_to(
        jnp.sum(grads * normed, axis=0, keepdims=True), gain_grad.shape
    )
    out = bypass + scale * (scaled - normed * jnp.mean(scaled * normed, axis=-1, keepdims=True))
    full_ref[...] = out
    low = out.astype(bf16)
    if weights:
        low_ref[...] = low
    else:
        low_ref[...] = low
        for place in range(4):
            target = scalars[3] ^ place
            rest[3][target] = blocks_ref[:, place * 256 : (place + 1) * 256].astype(bf16)
    lane = lax.broadcasted_iota(jnp.int32, (quarter, 256), 1)
    for weight, target in zip(weights, rest[3:]):
        target[...] = jnp.where(lane < 192, dot_nn(low, weight[...]), 0.0).astype(bf16)


def norm_back(gain_index, has_bypass_rows, scalars, values, gains, bypass, parts, weights=(), blocks=None):
    quarter, model = parts[0].shape
    low = shape((quarter, model), bf16)
    extra, more = tuple(weights), (shape((quarter, 256), bf16),) * len(weights)
    if blocks is not None:
        extra, more = (blocks,), (shape((4, blocks.shape[0], 256), bf16),)
    return pl.pallas_call(
        functools.partial(norm_back_kernel, gain_index, has_bypass_rows),
        out_shape=(shape((quarter, model), f32), low, shape((8, model), f32)) + more,
        in_specs=[SMEM] + [VMEM] * (6 + len(extra)),
        out_specs=(VMEM,) * (3 + len(more)),
        compiler_params=params(60),
        cost_estimate=cost(quarter * model * 16, 6 * 2**20),
        name="norm_back",
    )(scalars, values, gains, bypass, *parts, *extra)


def finish_kernel(residual_ref, part_ref, out_ref):
    total = residual_ref[...]
    quarter = total.shape[0]
    for source in range(4):
        total = total + part_ref[source * quarter : (source + 1) * quarter, :].astype(f32)
    out_ref[...] = total.astype(bf16)


def finish(residual, parts):
    quarter, model = residual.shape
    return pl.pallas_call(
        finish_kernel,
        out_shape=shape((quarter, model), bf16),
        in_specs=[VMEM] * 2,
        out_specs=VMEM,
        compiler_params=params(40),
        cost_estimate=cost(quarter * model * 4, 4 * 2**20),
        name="finish",
    )(residual, parts)


def hidden_grad_kernel(
    scalars, dq_ref, weight_ref, own, beside, across, dkv_ref, *rest
):
    ring, joined = rest[:5], rest[5]
    half = own.shape[0] // 2
    for part in range(2):
        span = slice(part * half, (part + 1) * half)
        total = own[span, :].astype(f32) + beside[span, :].astype(f32) + across[span, :].astype(f32)
        total = total.astype(bf16)
        dkv_ref[span, :] = total
        joined[span, :] = dot_nt(dq_ref[span, :], weight_ref[:, 0:256]) + dot_nt(
            total, weight_ref[:, 256:640]
        )
    write_ring(scalars, joined, *ring)


def hidden_grad(scalars, dq, weights, own, beside, across):
    rows = dq.shape[0]
    model = weights.shape[0]
    return pl.pallas_call(
        hidden_grad_kernel,
        out_shape=(shape((rows, 384), bf16),) + ring_shapes(rows, model),
        in_specs=[SMEM] + [VMEM] * 5,
        out_specs=(VMEM,) * 6,
        scratch_shapes=[pltpu.VMEM((rows, model), f32)],
        compiler_params=params(40),
        cost_estimate=cost(2 * rows * model * 640, 8 * 2**20),
        name="hidden_grad",
    )(scalars, dq, weights, own, beside, across)


def split_by_side(scalars, whole, mine, other):
    half = mine.shape[0]
    side = scalars[5]
    mine[...] = whole[pl.ds(aligned(side * half, 16), half), :]
    other[...] = whole[pl.ds(aligned((1 - side) * half, 16), half), :].astype(other.dtype)


def output_grad_kernel(scalars, branch_ref, attended_ref, hidden_ref, logit_ref, *rest):
    outs, whole = rest[:-1], rest[-1]
    whole[...] = dot_tn(branch_ref[...], attended_ref[...])
    router = dot_tn(hidden_ref[...], logit_ref[...])
    for source in range(4):
        whole[:, source * 256 + 128 : source * 256 + 256] += router
    if len(outs) == 1:
        outs[0][...] = whole[...]
    else:
        size = outs[0].shape[0] // 4
        context, side = scalars[0], scalars[5]
        for out, masks in zip(outs, ((0, 2), (1, 3))):
            for place, mask in enumerate(masks):
                for far in range(2):
                    start = aligned((4 * (side ^ far) + (context ^ mask)) * size, 16)
                    target = slice((2 * place + far) * size, (2 * place + far + 1) * size)
                    out[target, :] = whole[pl.ds(start, size), :].astype(out.dtype)


def output_grads(scalars, branch, attended, hidden, grad_logits, small):
    rows, model = hidden.shape
    outs = (shape((model, 1024), f32),)
    if small:
        outs = (shape((model // 2, 1024), f32), shape((model // 2, 1024), bf16))
    return pl.pallas_call(
        output_grad_kernel,
        out_shape=outs,
        in_specs=[SMEM] + [VMEM] * 4,
        out_specs=(VMEM,) * len(outs),
        scratch_shapes=[pltpu.VMEM((model, 1024), f32)],
        compiler_params=params(60),
        cost_estimate=cost(2 * rows * model * 384, 6 * 2**20),
        name="output_grads",
    )(scalars, branch, attended, hidden, grad_logits)


def projection_grad_kernel(scalars, hidden_ref, dq_ref, dkv_ref, gain_ref, fold_ref, *rest):
    outs, whole = rest[:-1], rest[-1]
    hidden = hidden_ref[...]
    whole[:, 0:256] = dot_tn(hidden, dq_ref[...])
    whole[:, 256:640] = dot_tn(hidden, dkv_ref[...])
    lane = lax.broadcasted_iota(jnp.int32, (whole.shape[0], 128), 1)
    column = jnp.broadcast_to(gain_ref[0:1, :], (128, whole.shape[0])).T
    whole[:, 128:256] = jnp.where(lane < 64, whole[:, 128:256], column)
    if len(outs) == 2:
        side = scalars[5]
        block = outs[0].shape[0] // 4
        size = block - 8
        for which, out in ((side, outs[0]), (1 - side, outs[1])):
            for context in range(4):
                start = aligned((which * 4 + context) * size, 8)
                out[context * block : context * block + size, :] = whole[pl.ds(start, size), :]
                tail = slice(context * block + size, (context + 1) * block)
                out[tail, 0:256] = fold_ref[...]
                out[tail, 256:640] = jnp.zeros((8, 384), f32)
    else:
        outs[0][...] = whole[...]


def projection_grads(scalars, hidden, dq, dkv, gain_grad, fold, small):
    rows, model = hidden.shape
    outs = (shape((model // 2 + 32, 640), f32),) * 2 if small else (shape((model, 640), f32),)
    return pl.pallas_call(
        projection_grad_kernel,
        out_shape=outs,
        in_specs=[SMEM] + [VMEM] * 5,
        out_specs=(VMEM,) * len(outs),
        scratch_shapes=[pltpu.VMEM((model, 640), f32)],
        compiler_params=params(40),
        cost_estimate=cost(2 * rows * model * 640, 6 * 2**20),
        name="projection_grads",
    )(scalars, hidden, dq, dkv, gain_grad, fold)


def add_arrived_kernel(beside, across, arrived_one, arrived_two, beside_out, across_out):
    half = arrived_one.shape[0]
    beside_out[0:half, :] = beside[0:half, :]
    beside_out[half:, :] = (beside[half:, :].astype(f32) + arrived_two[...].astype(f32)).astype(bf16)
    across_out[0:half, :] = (across[0:half, :].astype(f32) + arrived_one[...].astype(f32)).astype(bf16)
    across_out[half:, :] = across[half:, :]


def add_arrived(beside, across, arrived_one, arrived_two):
    return pl.pallas_call(
        add_arrived_kernel,
        out_shape=(shape(beside.shape, bf16),) * 2,
        in_specs=[VMEM] * 4,
        out_specs=(VMEM,) * 2,
        compiler_params=params(60),
        cost_estimate=cost(beside.size, 8 * beside.size),
        name="add_arrived",
    )(beside, across, arrived_one, arrived_two)


def share_kernel(scalars, mine, other, *outs):
    size = outs[0].shape[0]
    context = scalars[0]
    for mask, out in enumerate(outs):
        span = pl.ds(aligned((context ^ mask) * size, 8), size)
        total = mine[span, :] + other[span, :].astype(f32)
        out[...] = total.astype(out.dtype)


def share(scalars, mine, other):
    rows, width = mine.shape
    return pl.pallas_call(
        share_kernel,
        out_shape=(shape((rows // 4, width), f32),) + (shape((rows // 4, width), other.dtype),) * 3,
        in_specs=[SMEM, VMEM, VMEM],
        out_specs=(VMEM,) * 4,
        compiler_params=params(40),
        cost_estimate=cost(rows * width, 12 * rows * width),
        name="share",
    )(scalars, mine, other)


def shift(value, amount):
    size = lax.axis_size("tensor")
    return lax.ppermute(value, "tensor", [(i, (i + amount) % size) for i in range(size)])


def cross(value, mask):
    size = lax.axis_size("context")
    return lax.ppermute(value, "context", [(i, i ^ mask) for i in range(size)])


def trade(value, mask):
    return lax.ppermute(value, "tensor", [(i, i ^ mask) for i in range(lax.axis_size("tensor"))])


def spread(value):
    across, beside = trade(value, 2), trade(value, 1)
    return [value, beside, across, trade(across, 1)]


def sum_ranks(value):
    total = value
    for step in (1, 2, 3):
        total = total + shift(value, step)
    return total


def added(first, second):
    return (first.astype(f32) + second.astype(f32)).astype(bf16)


def ring_start(far_one, far_two):
    return shift(far_one, 1), shift(far_two, -1)


def with_first(whole, arrived):
    half = arrived.shape[0]
    return jnp.concatenate([added(whole[:half], arrived), whole[half:]], axis=0)


def with_second(whole, arrived):
    half = arrived.shape[0]
    return jnp.concatenate([whole[:half], added(whole[half:], arrived)], axis=0)


def ring_finish(next_block, last_block, arrived_one, arrived_two):
    last_block, next_block = add_arrived(last_block, next_block, arrived_one, arrived_two)
    return shift(next_block, 1), shift(last_block, -1)


ALL_ROWS = ("dp", "context")


def exchange(rows_out):
    return lax.all_to_all(rows_out, ALL_ROWS, split_axis=0, concat_axis=0, tiled=True)


def gather_weights(block, small, axis):
    size = block.shape[axis]
    if not small:
        whole = lax.all_gather(block, ALL_ROWS, axis=axis, tiled=True)
        return [whole], jnp.zeros((1,), jnp.int32)
    context, side = lax.axis_index("context"), lax.axis_index("dp")
    pieces = [block] + [cross(block, mask) for mask in (1, 2, 3)]
    pieces = pieces + [lax.ppermute(piece, "dp", [(0, 1), (1, 0)]) for piece in pieces]
    return pieces, jnp.stack(
        [((side ^ far) * 4 + (context ^ mask)) * size for far in range(2) for mask in range(4)]
    )


def swap_sides(parts):
    if len(parts) == 1:
        return parts
    return parts[0], lax.ppermute(parts[1], "dp", [(0, 1), (1, 0)])


def share_blocks(scalars, parts):
    return parts if len(parts) == 1 else share(scalars, *parts)


def halve(mine, arrived):
    total = mine + arrived.astype(f32)
    half = total.shape[0] // 2
    return total[:half], total[half:].astype(bf16)


def scatter_blocks(blocks):
    if len(blocks) == 1:
        return lax.psum_scatter(blocks[0], ALL_ROWS, scatter_dimension=0, tiled=True)
    total = blocks[0]
    for mask in (1, 2, 3):
        total = total + cross(blocks[mask], mask).astype(f32)
    return total


def on_device(
    tokens_in, query_weight, key_weight, value_weight, output_weight, bias_table, attention_gain,
    router_weight, expert_gain, expert_in, expert_out, routes, pair_order, seq_lengths, cotangent,
):
    rows, model = tokens_in.shape
    heads = bias_table.shape[1]
    width = query_weight.shape[1] // heads
    group_rows = rows * lax.axis_size("context")
    expert_count = router_weight.shape[1]
    capacity = (9 * rows + 4 * expert_count - 1) // (4 * expert_count)
    count = lax.axis_size("dp") * lax.axis_size("context")
    small = count == 8
    context, rank = lax.axis_index("context"), lax.axis_index("tensor")
    here = lax.axis_index("dp") * lax.axis_size("context") + context
    first_end = seq_lengths[0, 0]
    second_end = first_end + seq_lengths[0, 1]
    side = lax.axis_index("dp")
    scalars = jnp.stack([context, first_end, second_end, rank, here, side]).astype(jnp.int32)
    part = capacity // 2
    padded = (part + 15) // 16 * 16 + 16
    slots = expert_count * padded
    shard = query_weight.shape[0]
    block = pack_weights(
        query_weight, key_weight, value_weight, output_weight, attention_gain, expert_gain, router_weight
    )
    tie = lax.optimization_barrier
    half, quarter = rows // 2, rows // 4
    far_block = (context ^ 3) * rows
    kv_offsets = jnp.stack(
        [context * rows, (context ^ 1) * rows, (context ^ 2) * rows, far_block, far_block + half]
    )
    token_offsets = jnp.stack([(rank ^ mask) * quarter for mask in range(4)])
    far_bias = bias_table[-1]
    order_row = (pair_order & 1) * rows + (pair_order >> 1)
    pieces, offsets = gather_weights(block, small, 0)
    in_partner, out_first = trade(expert_in[0], 1), trade(expert_out[0, :256], 1)
    bias_own, bias_next = bias_tiles(bias_table, heads)
    offsets, bias_own, bias_next = tie((offsets, bias_own, bias_next))
    hidden_one, queries, kv_own, weights, output_own, gains = project(
        offsets, tokens_in, pieces
    )
    kv_beside, kv_across = cross(kv_own, 1), cross(kv_own, 2)
    output_across, output_beside = trade(output_own, 2), trade(output_own, 1)
    order_row, queries = tie((order_row, queries))
    row_place, column_place = prepare(
        scalars, routes.T, order_row, expert_count, part, padded
    )
    states = attention_near(
        scalars, far_bias, queries, bias_own, bias_next, kv_own, heads, width
    )
    kv_beside, kv_across, row_place, states = tie((kv_beside, kv_across, row_place, states))
    kv_far = cross(kv_beside[:half], 2), cross(kv_across[half:], 1)
    kv_pieces = (kv_own, kv_beside, kv_across) + kv_far
    cotangent_rows = scatter_rows(cotangent, row_place, slots)
    states, kv_pieces, cotangent_rows, in_partner, output_across, output_beside = tie(
        (states, kv_pieces, cotangent_rows, in_partner, output_across, output_beside)
    )
    output_parts = [output_own, output_beside, output_across, trade(output_across, 1)]
    packed, lse = attention_far(
        scalars, far_bias, kv_offsets, queries, bias_next, states, kv_pieces, group_rows, heads,
        width,
    )
    packed, output_parts, out_first, cotangent_rows = tie(
        (packed, output_parts, out_first, cotangent_rows)
    )
    attended = spread(packed)
    cotangent_rows = exchange(cotangent_rows)
    attended, cotangent_rows = tie((attended, cotangent_rows))
    out_second, attended = tie((expert_out[0, 256:], attended))
    out_second = trade(out_second, 1)
    residual, hidden_two, info, attended_here, rows_out = dispatch(
        scalars, tokens_in, gains, routes, row_place, attended, output_parts, width, expert_count,
        padded,
    )
    in_parts, out_parts = (expert_in[0], in_partner), (expert_out[0], out_first, out_second)
    expert_rows = exchange(rows_out)
    acted, grad_pre, back = expert_step(
        in_parts, out_parts, expert_rows, cotangent_rows, padded
    )
    back = exchange(back)
    in_grad_partner = dot_tn(expert_rows, grad_pre[1]).astype(bf16)
    out_grad_partner = dot_tn(acted[1], cotangent_rows).astype(bf16)
    in_grad_partner, out_grad_partner, acted, grad_pre = tie(
        (in_grad_partner, out_grad_partner, acted, grad_pre)
    )
    in_grad_partner = trade(in_grad_partner, 1)
    outs = expert_outputs(acted, out_parts)
    expert_out_grad = dot_tn(acted[0], cotangent_rows)
    expert_in_grad = dot_tn(expert_rows, grad_pre[0])
    back, outs, expert_out_grad, expert_in_grad = tie(
        (back, outs, expert_out_grad, expert_in_grad)
    )
    combine = (scalars, column_place, info, routes, output_own, back)
    far_logits, *far, digits = combine_grads(True, *combine, (), expert_count, padded)
    arrived = ring_start(*far)
    grad_logits, own, *ring = combine_grads(
        False, *combine, (far_logits, digits), expert_count, padded
    )
    arrived, ring, outs, in_grad_partner = tie((arrived, ring, outs, in_grad_partner))
    ring, outs = (own,) + ring_finish(*ring, *arrived), exchange(outs)
    ring, outs = tie((ring, outs))
    grad_one, grad_branch, gain_two_grad, *grad_heads = norm_back(
        1, True, scalars, residual, gains, cotangent, ring, output_parts
    )
    head_pieces = (grad_heads[0],) + tuple(trade(grad_heads[mask], mask) for mask in (1, 2, 3))
    outer = output_grads(scalars, grad_branch, attended_here, hidden_two, grad_logits, small)
    mixed = combine_outs(column_place, outs)
    head_pieces, mixed, out_grad_partner, outer = tie(
        (head_pieces, mixed, out_grad_partner, outer)
    )
    if small:
        outer = outer[0], cross(outer[1], 1)
    out_grad_partner = trade(out_grad_partner, 1)
    mixed = lax.all_to_all(mixed, "tensor", split_axis=0, concat_axis=0, tiled=True)
    shared = (scalars, far_bias, token_offsets, queries, bias_own, bias_next, lse)
    dout, deltas, dq_t, far_one, far_two, fold = attention_backward(
        (3,), *shared, kv_far, (packed, *head_pieces), 4, heads, width
    )
    arrived = cross(far_one, 1), cross(far_two, 2)
    dq_t, beside, across, fold = attention_backward(
        (1, 2), *shared, (kv_beside, kv_across), (dout, deltas, dq_t, fold), 0, heads, width
    )
    beside, across = add_arrived(beside, across, *arrived)
    dq_t, mixed, beside, across, outer = tie((dq_t, mixed, beside, across, outer))
    from_square = cross(beside, 1), cross(across, 2)
    layer_own = finish(residual, mixed)
    dq_t, layer_own = tie((dq_t, layer_own))
    layer_far, layer_beside = trade(layer_own, 2), trade(layer_own, 1)
    dq_t, own, dq, fold = attention_backward(
        (0,), *shared, (kv_own,), (dout, deltas, dq_t, fold), 0, heads, width
    )
    dq, from_square, outer, out_grad_partner, layer_beside = tie(
        (dq, from_square, outer, out_grad_partner, layer_beside)
    )
    layer_last = trade(layer_far, 1)
    dkv, own, *ring = hidden_grad(scalars, dq, weights, own, *from_square)
    arrived = ring_start(*ring[2:4])
    inner_parts = projection_grads(scalars, hidden_one, dq, dkv, gain_two_grad, fold, small)
    if small:
        outer = halve(*outer)
        outer = halve(outer[0], cross(outer[1], 2))
    arrived, inner_parts, outer, layer_last = tie((arrived, inner_parts, outer, layer_last))
    inner_parts = swap_sides(inner_parts)
    ring = (
        own,
        shift(with_first(ring[0], arrived[0]), 1),
        shift(with_second(ring[1], arrived[1]), -1),
    )
    if small:
        outer_grads = outer[0] + swap_sides(outer)[1].astype(f32)
    else:
        outer_grads = lax.psum_scatter(outer[0], ALL_ROWS, scatter_dimension=0, tiled=True)
    inner_parts = share_blocks(scalars, inner_parts)
    ring, outer_grads, inner_parts = tie((ring, outer_grads, inner_parts))
    _, input_low, _, outer_grads = norm_back(
        0, False, scalars, tokens_in, gains, grad_one, ring, blocks=outer_grads
    )
    input_far, input_beside = trade(input_low, 2), trade(input_low, 1)
    outer_grads = lax.all_to_all(outer_grads, "tensor", split_axis=0, concat_axis=0, tiled=True)
    layer_own, input_far = tie((layer_own, input_far))
    layer_out = assemble(
        token_offsets, [layer_own, layer_beside, layer_far, layer_last], bf16
    )
    projected = scatter_blocks(inner_parts)
    expert_out_grad, expert_in_grad, projected = tie((expert_out_grad, expert_in_grad, projected))
    input_pieces = [input_low, input_beside, input_far, trade(input_far, 1)]
    input_grad = assemble(token_offsets, input_pieces, f32)
    outer_grads = jnp.sum(outer_grads.astype(f32), axis=0)
    expert_out_grad = (expert_out_grad + out_grad_partner.astype(f32))[None]
    expert_in_grad = (expert_in_grad + in_grad_partner.astype(f32))[None]
    output_grad = outer_grads[:, :192].T
    router_grad = outer_grads[:, 192 : 192 + expert_count]
    fold = projected[shard:, :256] if small else lax.psum(fold, ALL_ROWS)
    projected = projected[:shard]
    query_grad, key_grad = projected[:, :192], projected[:, 256:448]
    value_grad = jnp.concatenate([projected[:, 512:], projected[:, 448:512]], axis=1)
    gain_one_grad = jnp.sum(
        query_weight.astype(f32) * query_grad
        + key_weight.astype(f32) * key_grad
        + value_weight.astype(f32) * value_grad,
        axis=1,
        keepdims=True,
    )
    gain_grads = sum_ranks(jnp.concatenate([gain_one_grad, projected[:, 192:193]], axis=1))
    bucket_row = jnp.asarray(bucket_tiles()[0, 0])
    bucket_hot = (bucket_row[None, :] == jnp.arange(bias_table.shape[0] - 1)[:, None]).astype(f32)
    near_grad = jnp.sum(bucket_hot[:, None, :] * fold[None, :heads, :], axis=-1)
    table_grad = jnp.concatenate([near_grad, -jnp.sum(near_grad, axis=0, keepdims=True)], axis=0)
    return (
        layer_out,
        input_grad,
        query_grad,
        key_grad,
        value_grad,
        output_grad,
        table_grad,
        gain_grads[:, 0] / attention_gain.astype(f32),
        router_grad,
        gain_grads[:, 1],
        expert_in_grad,
        expert_out_grad,
    )


def solution(mesh):
    rows = P(("dp", "context"), None)
    return jax.shard_map(
        on_device,
        mesh=mesh,
        in_specs=(
            rows,
            P(("dp", "context"), "tensor"),
            P(("dp", "context"), "tensor"),
            P(("dp", "context"), "tensor"),
            P("tensor", ("dp", "context")),
            P(None, "tensor"),
            P(("dp", "context")),
            rows,
            P(("dp", "context")),
            P(("dp", "context"), None, "tensor"),
            P(("dp", "context"), "tensor", None),
            rows,
            rows,
            P("dp", None),
            rows,
        ),
        out_specs=(
            rows,
            rows,
            P(("dp", "context"), "tensor"),
            P(("dp", "context"), "tensor"),
            P(("dp", "context"), "tensor"),
            P("tensor", ("dp", "context")),
            P(None, "tensor"),
            P(("dp", "context")),
            rows,
            P(("dp", "context")),
            P(("dp", "context"), None, "tensor"),
            P(("dp", "context"), "tensor", None),
        ),
        check_vma=False,
    )
```
